128 devices in a mesh: dp: 16 (over x, y), tensor: 8 (over z, core).
Axes of the slice: x: 4, y: 4, z: 4, core: 2. Of those that a mesh axis runs over, the one named last changes fastest.
Arguments:
- queries: bfloat16 [4, 128, 8192], P(None, 'dp', 'tensor'), may hold values from -16 to 16
- new_kv: bfloat16 [4, 128, 2048], P(None, 'dp', 'tensor'), may hold values from -8 to 8
- kv_pool: bfloat16 [1024, 128, 2048], P('dp', None, 'tensor'), may hold values from -4 to 4
- page_tables: int32 [128, 8], P('dp'), may hold values from 0 to 63
- lengths: int32 [128], replicated, may hold values from 1 to 1020, as said below
- parents: int32 [128], replicated, may hold values from 0 to 127, as said below
- out_weight: bfloat16 [8192, 8192], P('tensor'), may hold values from -0.09375 to 0.09375
Outputs:
- projected: bfloat16 [4, 128, 8192], P(None, 'dp', 'tensor')
- child_cache: bfloat16 [128, 1024, 2048], P('dp', None, 'tensor')
The draws below stay inside these ranges and needn't reach their ends.
Inputs may be any that keep to these rules, and one draw needn't show every extreme that they name: Child c and old beam b are held by indices c // 8 and b // 8 of dp; a problem's beams sit on 4 aligned indices of dp (indices g with equal g // 4). Every parent belongs to its child's problem, and for every index of dp and every index of its problem, exactly 2 children held by the first have parents held by the second. `lengths`: every cache leaves room for the 4 new tokens. `page_tables`: pages may be shared between beams.
All inputs are finite; a program needn't handle non-finite values.
Results may differ from the reference program's by a relative error of at most 0.0058.
Values may be sent and summed in bfloat16 or wider, within the bound.
A program may use at most 128 MiB of HBM per device.

```python
import jax
import jax.numpy as jnp
from jax import lax

D = 8192
QH = 64
KVH = 8
HD = 128
CTX = 1024
BEAM_DEV = 8
STEPS = 4
PAGE = 128
SPAN = 4
MOST = 2
PAGES = 8
POOL_DEV = 64
BEAMS = 128
N_DP = 16


def draw_queries(key, part):
    key = jax.random.fold_in(key, 5)
    key_drawn = jax.random.fold_in(key, 0)
    drawn = jnp.clip(jax.random.normal(key_drawn, (STEPS, BEAMS, QH, HD), jnp.float32), -4.0, 4.0)
    return drawn.reshape(STEPS, BEAMS, QH * HD).astype(jnp.bfloat16)


def draw_new_kv(key, part):
    key = jax.random.fold_in(key, 3)
    key_drawn = jax.random.fold_in(key, 0)
    drawn = jnp.clip(jax.random.normal(key_drawn, (STEPS, BEAMS, KVH, 2, HD), jnp.float32), -4.0, 4.0)
    return drawn.reshape(STEPS, BEAMS, KVH * 2 * HD).astype(jnp.bfloat16)


def draw_lengths(key, part):
    key = jax.random.fold_in(key, 7)
    key_value, key_order = jax.random.split(key)
    drawn = jax.random.randint(key_value, (BEAMS,), 1, CTX - STEPS + 1, jnp.int32)
    order = jax.random.permutation(key_order, BEAMS)
    drawn = drawn.at[order[0]].set(CTX - STEPS)
    drawn = drawn.at[order[1]].set(1)
    return drawn.astype(jnp.int32)


def draw_parents(key, part):
    key = jax.random.fold_in(key, 9)
    key_order, key_within = jax.random.split(key)
    groups = BEAMS // BEAM_DEV
    pattern = jnp.tile(jnp.arange(SPAN, dtype=jnp.int32), MOST)
    table = jnp.broadcast_to(pattern[None, :], (groups, BEAM_DEV))
    senders = jax.random.permutation(key_order, table, axis=1, independent=True).astype(jnp.int32)
    group_ids = jnp.arange(groups, dtype=jnp.int32)
    sources = (group_ids // SPAN * SPAN)[:, None] + senders
    within = jax.random.randint(key_within, (groups, BEAM_DEV), 0, BEAM_DEV, jnp.int32)
    return (sources * BEAM_DEV + within).reshape(BEAMS).astype(jnp.int32)


def with_ends(values, rng, smallest, high):
    spot = [jax.random.randint(jax.random.fold_in(rng, axis), (), 0, length) for axis, length in enumerate(values.shape)]
    widest = values.shape.index(max(values.shape))
    next_to = spot[:widest] + [(spot[widest] + 1) % values.shape[widest]] + spot[widest + 1:]
    return values.at[tuple(spot)].set(smallest).at[tuple(next_to)].set(high)


def raised(entries, rng, source, target, shards_of, factor):
    def block_of(dim):
        return (jnp.arange(entries.shape[dim]) // (entries.shape[dim] // shards_of)).reshape((-1,) + (1,) * (entries.ndim - 1 - dim))

    near = jax.random.permutation(rng, shards_of)[block_of(target)]
    far = (block_of(target) + shards_of // 2) % shards_of
    return jnp.where((block_of(source) == near) | (block_of(source) == far), factor * entries, entries)


def block_levels(own_key, shape, cuts, least, largest):
    gain = 1.0
    for axis_at, parts in cuts:
        draws = jax.random.uniform(jax.random.fold_in(jax.random.fold_in(own_key, 6), axis_at), (parts,), jnp.float32, least / len(cuts), largest / len(cuts))
        gain = gain * jnp.repeat(jnp.exp(draws), shape[axis_at] // parts).reshape((-1,) + (1,) * (len(shape) - 1 - axis_at))
    return gain


def normal_values(stream_key, dims, deviation, limit, cuts=(), kind=jnp.bfloat16):
    result = jax.random.normal(stream_key, dims, jnp.float32) * deviation
    if len(cuts) > 0:
        result = block_levels(stream_key, dims, cuts, -0.22, 0.18) * result
    return jnp.clip(result, min=-limit, max=limit).astype(kind)


def bell_draw_with(stream_key, dims, scale, most, cuts, heavy, held_as=jnp.bfloat16):
    result = scale * jax.random.normal(stream_key, dims, jnp.float32)
    if cuts:
        result = result * block_levels(stream_key, dims, cuts, -0.22, 0.18)
    return jnp.clip(raised(result, jax.random.fold_in(stream_key, 3), *heavy), -most, most).astype(held_as)


def setup_inputs(seed: int = 0) -> dict:
    seeds = jax.random.split(jax.random.key(seed), 8)
    queries = draw_queries(jax.random.fold_in(seeds[7], 71), 0)
    new_kv = draw_new_kv(jax.random.fold_in(seeds[7], 71), 0)
    kv_pool = normal_values(seeds[2], (POOL_DEV * N_DP, PAGE, 2 * KVH * HD), 1.0, 4.0, ((0, 16), (2, 8)))
    page_tables = with_ends(jax.random.randint(seeds[3], (BEAMS, PAGES), 0, POOL_DEV), jax.random.fold_in(seeds[3], 1), 0, POOL_DEV - 1).astype(jnp.int32)
    lengths = draw_lengths(jax.random.fold_in(seeds[7], 71), 0)
    parents = draw_parents(jax.random.fold_in(seeds[7], 71), 0)
    out_weight = bell_draw_with(seeds[6], (QH * HD, D), (QH * HD) ** -0.5, 0.09375, ((0, 8),), (0, 1, 8, 2.0))
    return {"queries": queries, "new_kv": new_kv, "kv_pool": kv_pool, "page_tables": page_tables, "lengths": lengths, "parents": parents, "out_weight": out_weight}


def softmax_weights(scores):
    shifted = scores - jnp.max(scores, axis=-1, keepdims=True)
    exp_scores = jnp.exp(shifted)
    return exp_scores / jnp.sum(exp_scores, axis=-1, keepdims=True)


def reference(queries, new_kv, kv_pool, page_tables, lengths, parents, out_weight):
    owner_group = parents // BEAM_DEV
    page_rows = page_tables[parents] + (owner_group * POOL_DEV)[:, None]
    fetched = kv_pool[page_rows].reshape(BEAMS, CTX, KVH * 2 * HD)
    parent_len = lengths[parents]
    position = jnp.arange(CTX, dtype=jnp.int32)
    kv_cache = jnp.where(position[None, :, None] < parent_len[:, None, None], fetched, jnp.zeros((), jnp.bfloat16))
    for step_index in range(STEPS):
        target = (position[None, :] == parent_len[:, None] + step_index)[:, :, None]
        kv_cache = jnp.where(target, new_kv[step_index][:, None, :], kv_cache)
    limits = parent_len[None, :] + jnp.arange(STEPS, dtype=jnp.int32)[:, None]
    visible = position[None, None, :] <= limits[:, :, None]
    group_size = QH // KVH
    outputs = []
    for head_index in range(KVH):
        key_part = kv_cache[:, :, 2 * head_index * HD:(2 * head_index + 1) * HD].astype(jnp.float32)
        value_part = kv_cache[:, :, (2 * head_index + 1) * HD:(2 * head_index + 2) * HD].astype(jnp.float32)
        q_part = queries[:, :, head_index * group_size * HD:(head_index + 1) * group_size * HD]
        q_part = q_part.reshape(STEPS, BEAMS, group_size, HD).astype(jnp.float32)
        scores = jnp.einsum("tbgd,bcd->tbgc", q_part, key_part) * (HD ** -0.5)
        scores = jnp.where(visible[:, :, None, :], scores, -1e30)
        weights = softmax_weights(scores).astype(jnp.bfloat16)
        weights = lax.optimization_barrier(weights).astype(jnp.float32)
        head_out = jnp.einsum("tbgc,bcd->tbgd", weights, value_part).astype(jnp.bfloat16)
        outputs.append(head_out.reshape(STEPS, BEAMS, group_size * HD))
    attended = jnp.concatenate(outputs, axis=2)
    projected = jnp.dot(attended.reshape(STEPS * BEAMS, QH * HD), out_weight, preferred_element_type=jnp.float32)
    return projected.astype(jnp.bfloat16).reshape(STEPS, BEAMS, D), kv_cache
```

```python
import functools

import jax
import jax.numpy as jnp
from jax import lax
from jax.experimental import pallas as pl
from jax.experimental.pallas import tpu as pltpu
from jax.sharding import PartitionSpec as P

HD = 128
SPAN = 4
MOST = 2
BEAMS = 8
STEPS = 4
PAGE = 128
MESH = pl.DeviceIdType.MESH


def slots_of_children(parents, me):
    taken = [jnp.int32(0) for _ in range(SPAN)]
    slots, owners = [], []
    for child in range(BEAMS):
        parent = parents[me * BEAMS + child]
        apart = jnp.bitwise_and(parent // BEAMS - me, SPAN - 1)
        slot = jnp.int32(0)
        for distance in range(SPAN):
            hit = apart == distance
            slot = jnp.where(hit, distance * MOST + taken[distance], slot)
            taken[distance] = taken[distance] + hit.astype(jnp.int32)
        slots.append(slot)
        owners.append(parent)
    return slots, owners


def served_beams(parents, me, target):
    count = jnp.int32(0)
    beams = [jnp.int32(0) for _ in range(MOST)]
    for child in range(BEAMS):
        parent = parents[target * BEAMS + child]
        hit = parent // BEAMS == me
        for rank in range(MOST):
            beams[rank] = jnp.where(hit & (count == rank), parent % BEAMS, beams[rank])
        count = count + hit.astype(jnp.int32)
    return beams


def exchange_kernel(
    q_ref, new_ref, pool_ref, table_ref, len_ref, par_ref, w_ref,
    recv_ref, proj_ref,
    pool_v, w_v, stage, q_send, q_recv, att, p_send, p_recv, r_send, lens,
    pool_sem, w_sem, own_sem, qs_sem, qr_sem, bs_sem, br_sem, ps_sem, pr_sem, rs_sem, rr_sem,
):
    me = lax.axis_index("dp")
    mine = lax.axis_index("tensor")
    shards = lax.axis_size("tensor")
    y = lax.rem(me, SPAN)
    base = me - y
    context = stage.shape[1] // MOST
    wide = q_ref.shape[2]
    heads = wide // HD
    rows = MOST * STEPS

    def peer(distance):
        return base + lax.rem(y + distance, SPAN)

    pool_copy = pltpu.make_async_copy(pool_ref, pool_v, pool_sem)
    pool_copy.start()
    barrier = pltpu.get_barrier_semaphore()
    for distance in range(1, SPAN):
        pl.semaphore_signal(barrier, inc=1, device_id={"dp": peer(distance)}, device_id_type=MESH)
    for other in range(1, shards):
        pl.semaphore_signal(barrier, inc=1, device_id={"tensor": lax.rem(mine + other, shards)}, device_id_type=MESH)
    w_copies = []
    for block in range(shards):
        copy = pltpu.make_async_copy(w_ref.at[:, pl.ds(block * wide, wide)], w_v.at[block], w_sem.at[block])
        copy.start()
        w_copies.append(copy)

    slots, _ = slots_of_children(par_ref, me)
    row = lax.broadcasted_iota(jnp.int32, (SPAN * rows, BEAMS), 0)
    col = lax.broadcasted_iota(jnp.int32, (SPAN * rows, BEAMS), 1)
    slot_at = jnp.zeros_like(col)
    for child in range(BEAMS):
        slot_at = jnp.where(col == child, slots[child], slot_at)
    q_sorted = jnp.zeros((SPAN * rows, wide), jnp.float32)
    new_sorted = jnp.zeros((SPAN * rows, 2 * HD), jnp.float32)
    for step in range(STEPS):
        pick = jnp.where((row // STEPS == slot_at) & (row % STEPS == step), 1.0, 0.0).astype(jnp.bfloat16)
        q_sorted += jnp.dot(pick, q_ref[step], preferred_element_type=jnp.float32)
        new_sorted += jnp.dot(pick, new_ref[step], preferred_element_type=jnp.float32)
    both = jnp.concatenate([q_sorted, new_sorted], axis=1)
    half = both.shape[1] // 2
    for distance in range(SPAN):
        part = both[distance * rows:(distance + 1) * rows]
        part = jnp.concatenate([part[:, :half], part[:, half:]], axis=0).astype(jnp.bfloat16)
        if distance == 0:
            q_recv[0] = part
        else:
            q_send[distance] = part

    pl.semaphore_wait(barrier, SPAN - 1 + shards - 1)

    q_copies = []
    for distance in range(1, SPAN):
        copy = pltpu.make_async_remote_copy(
            src_ref=q_send.at[distance], dst_ref=q_recv.at[distance],
            send_sem=qs_sem.at[distance], recv_sem=qr_sem.at[distance],
            device_id={"dp": peer(distance)}, device_id_type=MESH,
        )
        copy.start()
        q_copies.append(copy)

    pool_copy.wait()
    served = {}
    for distance in range(SPAN):
        served[distance] = served_beams(par_ref, me, peer(SPAN - distance))
        for rank in range(MOST):
            lens[distance * MOST + rank] = len_ref[me * BEAMS + served[distance][rank]]

    b_copies = []
    for rank in range(MOST):
        for distance in (2, 1, 3, 0):
            beam = served[distance][rank]

            def put(index, carry, distance=distance, rank=rank, beam=beam):
                at = pl.multiple_of(rank * context + index * PAGE, PAGE)
                stage[distance, pl.ds(at, PAGE), :] = pool_v[table_ref[beam, index]]
                return carry

            lax.fori_loop(0, context // PAGE, put, 0)
            span = pl.ds(rank * context, context)
            if distance == 0:
                copy = pltpu.make_async_copy(stage.at[0, span], recv_ref.at[0, span], own_sem.at[rank])
            else:
                copy = pltpu.make_async_remote_copy(
                    src_ref=stage.at[distance, span], dst_ref=recv_ref.at[distance, span],
                    send_sem=bs_sem.at[distance * MOST + rank], recv_sem=br_sem.at[distance * MOST + rank],
                    device_id={"dp": peer(SPAN - distance)}, device_id_type=MESH,
                )
            copy.start()
            b_copies.append(copy)

    for copy in q_copies:
        copy.wait()

    def attend(distance, carry):
        message = q_recv[distance].astype(jnp.float32)
        message = jnp.concatenate([message[:rows], message[rows:]], axis=1)
        q_rows = jnp.concatenate([message[:, h * HD:(h + 1) * HD] for h in range(heads)], axis=0).astype(jnp.bfloat16)
        fresh = message[:, wide:].astype(jnp.bfloat16)
        old_len = lens[distance * MOST]
        last_len = lens[distance * MOST + 1]
        contract = (((1,), (1,)), ((), ()))
        scale = HD ** -0.5
        scores = lax.dot_general(q_rows, stage[distance, :, 0:HD], contract, preferred_element_type=jnp.float32) * scale
        fresh_scores = lax.dot_general(q_rows, fresh[:, :HD], contract, preferred_element_type=jnp.float32) * scale
        rank_at = lax.broadcasted_iota(jnp.int32, scores.shape, 0) // STEPS % MOST
        position = lax.broadcasted_iota(jnp.int32, scores.shape, 1) - rank_at * context
        limit = jnp.where(rank_at == 0, old_len, last_len)
        scores = jnp.where((position >= 0) & (position < limit), scores, -1e30)
        f_row = lax.broadcasted_iota(jnp.int32, fresh_scores.shape, 0)
        f_col = lax.broadcasted_iota(jnp.int32, fresh_scores.shape, 1)
        seen = (f_row // STEPS % MOST == f_col // STEPS) & (f_col % STEPS <= f_row % STEPS)
        fresh_scores = jnp.where(seen, fresh_scores, -1e30)
        top = jnp.maximum(jnp.max(scores, axis=1, keepdims=True), jnp.max(fresh_scores, axis=1, keepdims=True))
        exp_old = jnp.exp(scores - top)
        exp_new = jnp.exp(fresh_scores - top)
        total = jnp.sum(exp_old, axis=1, keepdims=True) + jnp.sum(exp_new, axis=1, keepdims=True)
        w_old = (exp_old / total).astype(jnp.bfloat16)
        w_new = (exp_new / total).astype(jnp.bfloat16)
        out = jnp.dot(w_old, stage[distance, :, HD:2 * HD], preferred_element_type=jnp.float32)
        out += jnp.dot(w_new, fresh[:, HD:], preferred_element_type=jnp.float32)
        out = jnp.concatenate([out[h * rows:(h + 1) * rows] for h in range(heads)], axis=1)
        att[pl.ds(pl.multiple_of(distance * rows, rows), rows), :] = out
        return carry

    lax.fori_loop(0, SPAN, attend, 0)
    attended = att[...].astype(jnp.bfloat16)
    for copy in w_copies:
        copy.wait()

    def p_copy(other):
        return pltpu.make_async_remote_copy(
            src_ref=p_send.at[other], dst_ref=p_recv.at[other],
            send_sem=ps_sem.at[other], recv_sem=pr_sem.at[other],
            device_id={"tensor": lax.rem(mine + other, shards)}, device_id_type=MESH,
        )

    def project(other, carry):
        product = jnp.dot(attended, w_v[lax.rem(mine + other, shards)], preferred_element_type=jnp.float32)
        p_send[other] = product.astype(jnp.bfloat16)
        p_copy(other).start()
        return carry

    lax.fori_loop(1, shards, project, 0)
    own = jnp.dot(attended, w_v[mine], preferred_element_type=jnp.float32)

    def gather_sums(other, total):
        p_copy(other).wait()
        return total + p_recv[other].astype(jnp.float32)

    summed = lax.fori_loop(1, shards, gather_sums, own)
    half = wide // 2
    r_copies = []
    for distance in range(SPAN):
        part = summed[distance * rows:(distance + 1) * rows]
        r_send[distance] = jnp.concatenate([part[:, :half], part[:, half:]], axis=0).astype(jnp.bfloat16)
        if distance == 0:
            copy = pltpu.make_async_copy(r_send.at[0], proj_ref.at[0], own_sem.at[MOST])
        else:
            copy = pltpu.make_async_remote_copy(
                src_ref=r_send.at[distance], dst_ref=proj_ref.at[distance],
                send_sem=rs_sem.at[distance], recv_sem=rr_sem.at[distance],
                device_id={"dp": peer(SPAN - distance)}, device_id_type=MESH,
            )
        copy.start()
        r_copies.append(copy)
    for copy in r_copies:
        copy.wait()
    for copy in b_copies:
        copy.wait()


def finish_kernel(recv_ref, raw_ref, new_ref, len_ref, par_ref, proj_ref, cache_ref, held, in_sem, out_sem):
    me = lax.axis_index("dp")
    context = held.shape[1]
    slots, owners = slots_of_children(par_ref, me)

    def fetch(child):
        return pltpu.make_async_copy(recv_ref.at[slots[child]], held.at[child], in_sem.at[child])

    def put(child):
        return pltpu.make_async_copy(held.at[child], cache_ref.at[child], out_sem.at[child])

    for child in range(BEAMS):
        fetch(child).start()
    fresh = [new_ref[step].astype(jnp.float32) for step in range(STEPS)]
    for child in range(BEAMS):
        fetch(child).wait()
        length = len_ref[owners[child]]

        def fix(index, carry, child=child, length=length):
            at = pl.multiple_of(index * PAGE, PAGE)
            position = at + lax.broadcasted_iota(jnp.int32, (PAGE, 2 * HD), 0)
            page = held[child, pl.ds(at, PAGE), :].astype(jnp.float32)
            page = jnp.where(position < length, page, 0.0)
            for step in range(STEPS):
                page = jnp.where(position == length + step, fresh[step][child:child + 1], page)
            held[child, pl.ds(at, PAGE), :] = page.astype(jnp.bfloat16)
            return carry

        lax.fori_loop(length // PAGE, context // PAGE, fix, 0)
        put(child).start()

    rows = MOST * STEPS
    raw = []
    for distance in range(SPAN):
        part = raw_ref[distance].astype(jnp.float32)
        raw.append(jnp.concatenate([part[:rows], part[rows:]], axis=1))
    raw = jnp.concatenate(raw, axis=0).astype(jnp.bfloat16)
    row = lax.broadcasted_iota(jnp.int32, (BEAMS, SPAN * rows), 0)
    col = lax.broadcasted_iota(jnp.int32, (BEAMS, SPAN * rows), 1)
    slot_at = jnp.zeros_like(col)
    for child in range(BEAMS):
        slot_at = jnp.where(row == child, slots[child], slot_at)
    for step in range(STEPS):
        pick = jnp.where(col == slot_at * STEPS + step, 1.0, 0.0).astype(jnp.bfloat16)
        proj_ref[step] = jnp.dot(pick, raw, preferred_element_type=jnp.float32).astype(jnp.bfloat16)
    for child in range(BEAMS):
        put(child).wait()


def local(shards, queries, new_kv, kv_pool, page_tables, lengths, parents, out_weight):
    wide = queries.shape[2]
    channels = kv_pool.shape[2]
    context = page_tables.shape[1] * kv_pool.shape[1]
    rows = MOST * STEPS
    vmem = pl.BlockSpec(memory_space=pltpu.VMEM)
    smem = pl.BlockSpec(memory_space=pltpu.SMEM)
    hbm = pl.BlockSpec(memory_space=pl.ANY)
    dma = pltpu.SemaphoreType.DMA
    bf16 = jnp.bfloat16
    with jax.named_scope("exchange"):
        recv, raw = pl.pallas_call(
            exchange_kernel,
            out_shape=(
                jax.ShapeDtypeStruct((SPAN, MOST * context, channels), bf16),
                jax.ShapeDtypeStruct((SPAN, 2 * rows, wide // 2), bf16),
            ),
            in_specs=[vmem, vmem, hbm, smem, smem, smem, hbm],
            out_specs=(hbm, hbm),
            scratch_shapes=[
                pltpu.VMEM(kv_pool.shape, bf16),
                pltpu.VMEM((shards, out_weight.shape[0], wide), bf16),
                pltpu.VMEM((SPAN, MOST * context, channels), bf16),
                pltpu.VMEM((SPAN, 2 * rows, (wide + channels) // 2), bf16),
                pltpu.VMEM((SPAN, 2 * rows, (wide + channels) // 2), bf16),
                pltpu.VMEM((SPAN * rows, wide), jnp.float32),
                pltpu.VMEM((shards, SPAN * rows, wide), bf16),
                pltpu.VMEM((shards, SPAN * rows, wide), bf16),
                pltpu.VMEM((SPAN, 2 * rows, wide // 2), bf16),
                pltpu.SMEM((SPAN * MOST,), jnp.int32),
                dma, dma((shards,)), dma((MOST + 1,)),
                dma((SPAN,)), dma((SPAN,)),
                dma((SPAN * MOST,)), dma((SPAN * MOST,)),
                dma((shards,)), dma((shards,)),
                dma((SPAN,)), dma((SPAN,)),
            ],
            compiler_params=pltpu.CompilerParams(
                collective_id=0, has_side_effects=True, vmem_limit_bytes=48 * 1024 * 1024
            ),
            name="exchange",
        )(queries, new_kv, kv_pool, page_tables, lengths, parents, out_weight)
    with jax.named_scope("finish"):
        return pl.pallas_call(
            finish_kernel,
            out_shape=(
                jax.ShapeDtypeStruct(queries.shape, bf16),
                jax.ShapeDtypeStruct((BEAMS, context, channels), bf16),
            ),
            in_specs=[hbm, vmem, vmem, smem, smem],
            out_specs=(vmem, hbm),
            scratch_shapes=[pltpu.VMEM((BEAMS, context, channels), bf16), dma((BEAMS,)), dma((BEAMS,))],
            compiler_params=pltpu.CompilerParams(vmem_limit_bytes=24 * 1024 * 1024),
            name="finish",
        )(recv.reshape(BEAMS, context, channels), raw, new_kv, lengths, parents)


def solution(mesh):
    in_specs = (
        P(None, "dp", "tensor"),
        P(None, "dp", "tensor"),
        P("dp", None, "tensor"),
        P("dp", None),
        P(),
        P(),
        P("tensor", None),
    )
    out_specs = (P(None, "dp", "tensor"), P("dp", None, "tensor"))
    body = functools.partial(local, mesh.shape["tensor"])
    return jax.shard_map(body, mesh=mesh, in_specs=in_specs, out_specs=out_specs, check_vma=False)
```

```python
import functools

import jax
import jax.numpy as jnp
from jax import lax
from jax.experimental import pallas as pl
from jax.experimental.pallas import tpu as pltpu
from jax.sharding import PartitionSpec as P

HD = 128
SPAN = 4
MOST = 2
BEAMS = 8
STEPS = 4
PAGE = 128
MESH = pl.DeviceIdType.MESH


def slots_of_children(parents, me):
    taken = [jnp.int32(0) for _ in range(SPAN)]
    slots, owners = [], []
    for child in range(BEAMS):
        parent = parents[me * BEAMS + child]
        apart = jnp.bitwise_and(parent // BEAMS - me, SPAN - 1)
        slot = jnp.int32(0)
        for distance in range(SPAN):
            hit = apart == distance
            slot = jnp.where(hit, distance * MOST + taken[distance], slot)
            taken[distance] = taken[distance] + hit.astype(jnp.int32)
        slots.append(slot)
        owners.append(parent)
    return slots, owners


def served_beams(parents, me, target):
    count = jnp.int32(0)
    beams = [jnp.int32(0) for _ in range(MOST)]
    for child in range(BEAMS):
        parent = parents[target * BEAMS + child]
        hit = parent // BEAMS == me
        for rank in range(MOST):
            beams[rank] = jnp.where(hit & (count == rank), parent % BEAMS, beams[rank])
        count = count + hit.astype(jnp.int32)
    return beams


def exchange_kernel(
    q_hbm, new_hbm, pool_ref, table_hbm, len_hbm, par_hbm, w_ref,
    recv_ref, proj_ref,
    q_ref, new_ref, table_ref, len_ref, par_ref,
    pool_v, w_v, stage, q_send, q_recv, att, p_send, p_recv, r_send, lens,
    in_sem, pool_sem, w_sem, own_sem, qs_sem, qr_sem, bs_sem, br_sem, ps_sem, pr_sem, rs_sem, rr_sem,
):
    me = lax.axis_index("dp")
    mine = lax.axis_index("tensor")
    shards = lax.axis_size("tensor")
    y = lax.rem(me, SPAN)
    base = me - y
    context = stage.shape[1] // MOST
    wide = q_hbm.shape[2]
    heads = wide // HD
    rows = MOST * STEPS

    def peer(distance):
        return base + lax.rem(y + distance, SPAN)

    in_copies = []
    operands = ((par_hbm, par_ref), (q_hbm, q_ref), (new_hbm, new_ref), (table_hbm, table_ref), (len_hbm, len_ref))
    for at, (source, target) in enumerate(operands):
        copy = pltpu.make_async_copy(source, target, in_sem.at[at])
        copy.start()
        in_copies.append(copy)
    pool_copy = pltpu.make_async_copy(pool_ref, pool_v, pool_sem)
    pool_copy.start()
    barrier = pltpu.get_barrier_semaphore()
    for distance in range(1, SPAN):
        pl.semaphore_signal(barrier, inc=1, device_id={"dp": peer(distance)}, device_id_type=MESH)
    for other in range(1, shards):
        pl.semaphore_signal(barrier, inc=1, device_id={"tensor": lax.rem(mine + other, shards)}, device_id_type=MESH)
    for copy in in_copies:
        copy.wait()

    slots, _ = slots_of_children(par_ref, me)
    row = lax.broadcasted_iota(jnp.int32, (SPAN * rows, BEAMS), 0)
    col = lax.broadcasted_iota(jnp.int32, (SPAN * rows, BEAMS), 1)
    slot_at = jnp.zeros_like(col)
    for child in range(BEAMS):
        slot_at = jnp.where(col == child, slots[child], slot_at)
    q_sorted = jnp.zeros((SPAN * rows, wide), jnp.float32)
    new_sorted = jnp.zeros((SPAN * rows, 2 * HD), jnp.float32)
    for step in range(STEPS):
        pick = jnp.where((row // STEPS == slot_at) & (row % STEPS == step), 1.0, 0.0).astype(jnp.bfloat16)
        q_sorted += jnp.dot(pick, q_ref[step], preferred_element_type=jnp.float32)
        new_sorted += jnp.dot(pick, new_ref[step], preferred_element_type=jnp.float32)
    both = jnp.concatenate([q_sorted, new_sorted], axis=1)
    half = both.shape[1] // 2
    for distance in range(SPAN):
        part = both[distance * rows:(distance + 1) * rows]
        part = jnp.concatenate([part[:, :half], part[:, half:]], axis=0).astype(jnp.bfloat16)
        if distance == 0:
            q_recv[0] = part
        else:
            q_send[distance] = part

    pl.semaphore_wait(barrier, SPAN - 1 + shards - 1)

    q_copies = []
    for distance in range(1, SPAN):
        copy = pltpu.make_async_remote_copy(
            src_ref=q_send.at[distance], dst_ref=q_recv.at[distance],
            send_sem=qs_sem.at[distance], recv_sem=qr_sem.at[distance],
            device_id={"dp": peer(distance)}, device_id_type=MESH,
        )
        copy.start()
        q_copies.append(copy)

    pool_copy.wait()
    w_copies = []
    for block in range(shards):
        copy = pltpu.make_async_copy(w_ref.at[:, pl.ds(block * wide, wide)], w_v.at[block], w_sem.at[block])
        copy.start()
        w_copies.append(copy)
    served = {}
    for distance in range(SPAN):
        served[distance] = served_beams(par_ref, me, peer(SPAN - distance))
        for rank in range(MOST):
            lens[distance * MOST + rank] = len_ref[me * BEAMS + served[distance][rank]]

    b_copies = []
    for rank in range(MOST):
        for distance in (2, 1, 3, 0):
            beam = served[distance][rank]

            def put(index, carry, distance=distance, rank=rank, beam=beam):
                at = pl.multiple_of(rank * context + index * PAGE, PAGE)
                stage[distance, pl.ds(at, PAGE), :] = pool_v[table_ref[beam, index]]
                return carry

            lax.fori_loop(0, context // PAGE, put, 0)
            span = pl.ds(rank * context, context)
            if distance == 0:
                copy = pltpu.make_async_copy(stage.at[0, span], recv_ref.at[0, span], own_sem.at[rank])
            else:
                copy = pltpu.make_async_remote_copy(
                    src_ref=stage.at[distance, span], dst_ref=recv_ref.at[distance, span],
                    send_sem=bs_sem.at[distance * MOST + rank], recv_sem=br_sem.at[distance * MOST + rank],
                    device_id={"dp": peer(SPAN - distance)}, device_id_type=MESH,
                )
            copy.start()
            b_copies.append(copy)

    for copy in q_copies:
        copy.wait()

    def attend(distance, carry):
        message = q_recv[distance].astype(jnp.float32)
        message = jnp.concatenate([message[:rows], message[rows:]], axis=1)
        q_rows = jnp.concatenate([message[:, h * HD:(h + 1) * HD] for h in range(heads)], axis=0).astype(jnp.bfloat16)
        fresh = message[:, wide:].astype(jnp.bfloat16)
        old_len = lens[distance * MOST]
        last_len = lens[distance * MOST + 1]
        contract = (((1,), (1,)), ((), ()))
        scale = HD ** -0.5
        scores = lax.dot_general(q_rows, stage[distance, :, 0:HD], contract, preferred_element_type=jnp.float32) * scale
        fresh_scores = lax.dot_general(q_rows, fresh[:, :HD], contract, preferred_element_type=jnp.float32) * scale
        rank_at = lax.broadcasted_iota(jnp.int32, scores.shape, 0) // STEPS % MOST
        position = lax.broadcasted_iota(jnp.int32, scores.shape, 1) - rank_at * context
        limit = jnp.where(rank_at == 0, old_len, last_len)
        scores = jnp.where((position >= 0) & (position < limit), scores, -1e30)
        f_row = lax.broadcasted_iota(jnp.int32, fresh_scores.shape, 0)
        f_col = lax.broadcasted_iota(jnp.int32, fresh_scores.shape, 1)
        seen = (f_row // STEPS % MOST == f_col // STEPS) & (f_col % STEPS <= f_row % STEPS)
        fresh_scores = jnp.where(seen, fresh_scores, -1e30)
        top = jnp.maximum(jnp.max(scores, axis=1, keepdims=True), jnp.max(fresh_scores, axis=1, keepdims=True))
        exp_old = jnp.exp(scores - top)
        exp_new = jnp.exp(fresh_scores - top)
        total = jnp.sum(exp_old, axis=1, keepdims=True) + jnp.sum(exp_new, axis=1, keepdims=True)
        w_old = (exp_old / total).astype(jnp.bfloat16)
        w_new = (exp_new / total).astype(jnp.bfloat16)
        out = jnp.dot(w_old, stage[distance, :, HD:2 * HD], preferred_element_type=jnp.float32)
        out += jnp.dot(w_new, fresh[:, HD:], preferred_element_type=jnp.float32)
        out = jnp.concatenate([out[h * rows:(h + 1) * rows] for h in range(heads)], axis=1)
        att[pl.ds(pl.multiple_of(distance * rows, rows), rows), :] = out
        return carry

    lax.fori_loop(0, SPAN, attend, 0)
    attended = att[...].astype(jnp.bfloat16)
    for copy in w_copies:
        copy.wait()

    def p_copy(other):
        return pltpu.make_async_remote_copy(
            src_ref=p_send.at[other], dst_ref=p_recv.at[other],
            send_sem=ps_sem.at[other], recv_sem=pr_sem.at[other],
            device_id={"tensor": lax.rem(mine + other, shards)}, device_id_type=MESH,
        )

    def project(other, carry):
        product = jnp.dot(attended, w_v[lax.rem(mine + other, shards)], preferred_element_type=jnp.float32)
        p_send[other] = product.astype(jnp.bfloat16)
        p_copy(other).start()
        return carry

    lax.fori_loop(1, shards, project, 0)
    own = jnp.dot(attended, w_v[mine], preferred_element_type=jnp.float32)

    def gather_sums(other, total):
        p_copy(other).wait()
        return total + p_recv[other].astype(jnp.float32)

    summed = lax.fori_loop(1, shards, gather_sums, own)
    half = wide // 2
    r_copies = []
    for distance in range(SPAN):
        part = summed[distance * rows:(distance + 1) * rows]
        r_send[distance] = jnp.concatenate([part[:, :half], part[:, half:]], axis=0).astype(jnp.bfloat16)
        if distance == 0:
            copy = pltpu.make_async_copy(r_send.at[0], proj_ref.at[0], own_sem.at[MOST])
        else:
            copy = pltpu.make_async_remote_copy(
                src_ref=r_send.at[distance], dst_ref=proj_ref.at[distance],
                send_sem=rs_sem.at[distance], recv_sem=rr_sem.at[distance],
                device_id={"dp": peer(SPAN - distance)}, device_id_type=MESH,
            )
        copy.start()
        r_copies.append(copy)
    for copy in r_copies:
        copy.wait()
    for copy in b_copies:
        copy.wait()


def finish_kernel(recv_ref, raw_ref, new_hbm, len_hbm, par_hbm, proj_ref, cache_ref, new_ref, len_ref, par_ref, edge, zeros, in_sem, out_sem):
    me = lax.axis_index("dp")
    pages = recv_ref.shape[1] // PAGE
    operands = ((par_hbm, par_ref), (len_hbm, len_ref), (new_hbm, new_ref))
    in_copies = [pltpu.make_async_copy(source, target, in_sem.at[at]) for at, (source, target) in enumerate(operands)]
    for copy in in_copies:
        copy.start()
    zeros[...] = jnp.zeros_like(zeros)
    for copy in in_copies:
        copy.wait()
    slots, owners = slots_of_children(par_ref, me)
    fresh = [new_ref[step].astype(jnp.float32) for step in range(STEPS)]
    for child in range(BEAMS):
        slot = slots[child]
        length = len_ref[owners[child]]
        first = length // PAGE
        last = (length + STEPS - 1) // PAGE

        def whole(index, carry, child=child, slot=slot):
            span = pl.ds(pl.multiple_of(index * PAGE, PAGE), PAGE)
            pltpu.make_async_copy(recv_ref.at[slot, span], cache_ref.at[child, span], out_sem).start()
            return carry

        def clear(index, carry, child=child):
            span = pl.ds(pl.multiple_of(index * PAGE, PAGE), PAGE)
            pltpu.make_async_copy(zeros, cache_ref.at[child, span], out_sem).start()
            return carry

        def fix(index, carry, child=child, slot=slot, length=length, first=first):
            at = pl.multiple_of(index * PAGE, PAGE)
            position = at + lax.broadcasted_iota(jnp.int32, (PAGE, 2 * HD), 0)
            page = recv_ref[slot, pl.ds(at, PAGE), :].astype(jnp.float32)
            page = jnp.where(position < length, page, 0.0)
            for step in range(STEPS):
                page = jnp.where(position == length + step, fresh[step][child:child + 1], page)
            edge[child * 2 + index - first] = page.astype(jnp.bfloat16)
            pltpu.make_async_copy(edge.at[child * 2 + index - first], cache_ref.at[child, pl.ds(at, PAGE)], out_sem).start()
            return carry

        lax.fori_loop(0, first, whole, 0)
        lax.fori_loop(last + 1, pages, clear, 0)
        lax.fori_loop(first, last + 1, fix, 0)

    rows = MOST * STEPS
    raw = []
    for distance in range(SPAN):
        part = raw_ref[distance].astype(jnp.float32)
        raw.append(jnp.concatenate([part[:rows], part[rows:]], axis=1))
    raw = jnp.concatenate(raw, axis=0).astype(jnp.bfloat16)
    row = lax.broadcasted_iota(jnp.int32, (BEAMS, SPAN * rows), 0)
    col = lax.broadcasted_iota(jnp.int32, (BEAMS, SPAN * rows), 1)
    slot_at = jnp.zeros_like(col)
    for child in range(BEAMS):
        slot_at = jnp.where(row == child, slots[child], slot_at)
    for step in range(STEPS):
        pick = jnp.where(col == slot_at * STEPS + step, 1.0, 0.0).astype(jnp.bfloat16)
        proj_ref[step] = jnp.dot(pick, raw, preferred_element_type=jnp.float32).astype(jnp.bfloat16)
    pltpu.make_async_copy(recv_ref, cache_ref, out_sem).wait()


def local(shards, queries, new_kv, kv_pool, page_tables, lengths, parents, out_weight):
    wide = queries.shape[2]
    channels = kv_pool.shape[2]
    context = page_tables.shape[1] * kv_pool.shape[1]
    rows = MOST * STEPS
    vmem = pl.BlockSpec(memory_space=pltpu.VMEM)
    hbm = pl.BlockSpec(memory_space=pltpu.HBM)
    free = pl.BlockSpec(memory_space=pl.ANY)
    dma = pltpu.SemaphoreType.DMA
    bf16 = jnp.bfloat16
    with jax.named_scope("exchange"):
        recv, raw = pl.pallas_call(
            exchange_kernel,
            out_shape=(
                jax.ShapeDtypeStruct((SPAN, MOST * context, channels), bf16),
                jax.ShapeDtypeStruct((SPAN, 2 * rows, wide // 2), bf16),
            ),
            in_specs=[hbm] * 7,
            out_specs=(free, free),
            scratch_shapes=[
                pltpu.VMEM(queries.shape, bf16),
                pltpu.VMEM(new_kv.shape, bf16),
                pltpu.SMEM(page_tables.shape, jnp.int32),
                pltpu.SMEM(lengths.shape, jnp.int32),
                pltpu.SMEM(parents.shape, jnp.int32),
                pltpu.VMEM(kv_pool.shape, bf16),
                pltpu.VMEM((shards, out_weight.shape[0], wide), bf16),
                pltpu.VMEM((SPAN, MOST * context, channels), bf16),
                pltpu.VMEM((SPAN, 2 * rows, (wide + channels) // 2), bf16),
                pltpu.VMEM((SPAN, 2 * rows, (wide + channels) // 2), bf16),
                pltpu.VMEM((SPAN * rows, wide), jnp.float32),
                pltpu.VMEM((shards, SPAN * rows, wide), bf16),
                pltpu.VMEM((shards, SPAN * rows, wide), bf16),
                pltpu.VMEM((SPAN, 2 * rows, wide // 2), bf16),
                pltpu.SMEM((SPAN * MOST,), jnp.int32),
                dma((5,)), dma, dma((shards,)), dma((MOST + 1,)),
                dma((SPAN,)), dma((SPAN,)),
                dma((SPAN * MOST,)), dma((SPAN * MOST,)),
                dma((shards,)), dma((shards,)),
                dma((SPAN,)), dma((SPAN,)),
            ],
            compiler_params=pltpu.CompilerParams(
                collective_id=0, has_side_effects=True, vmem_limit_bytes=48 * 1024 * 1024
            ),
            name="exchange",
        )(queries, new_kv, kv_pool, page_tables, lengths, parents, out_weight)
    with jax.named_scope("finish"):
        return pl.pallas_call(
            finish_kernel,
            out_shape=(
                jax.ShapeDtypeStruct(queries.shape, bf16),
                jax.ShapeDtypeStruct((BEAMS, context, channels), bf16),
            ),
            in_specs=[vmem, vmem, hbm, hbm, hbm],
            out_specs=(vmem, hbm),
            scratch_shapes=[
                pltpu.VMEM(new_kv.shape, bf16),
                pltpu.SMEM(lengths.shape, jnp.int32),
                pltpu.SMEM(parents.shape, jnp.int32),
                pltpu.VMEM((2 * BEAMS, PAGE, channels), bf16),
                pltpu.VMEM((PAGE, channels), bf16),
                dma((3,)), dma,
            ],
            compiler_params=pltpu.CompilerParams(vmem_limit_bytes=24 * 1024 * 1024),
            name="finish",
        )(recv.reshape(BEAMS, context, channels), raw, new_kv, lengths, parents)


def solution(mesh):
    in_specs = (
        P(None, "dp", "tensor"),
        P(None, "dp", "tensor"),
        P("dp", None, "tensor"),
        P("dp", None),
        P(),
        P(),
        P("tensor", None),
    )
    out_specs = (P(None, "dp", "tensor"), P("dp", None, "tensor"))
    body = functools.partial(local, mesh.shape["tensor"])
    return jax.shard_map(body, mesh=mesh, in_specs=in_specs, out_specs=out_specs, check_vma=False)
```

```python
import functools

import jax
import jax.numpy as jnp
from jax import lax
from jax.experimental import pallas as pl
from jax.experimental.pallas import tpu as pltpu
from jax.sharding import PartitionSpec as P

HD = 128
SPAN = 4
MOST = 2
BEAMS = 8
STEPS = 4
PAGE = 128
MESH = pl.DeviceIdType.MESH


def slots_of_children(parents, me):
    taken = [jnp.int32(0) for _ in range(SPAN)]
    slots, owners = [], []
    for child in range(BEAMS):
        parent = parents[me * BEAMS + child]
        apart = jnp.bitwise_and(parent // BEAMS - me, SPAN - 1)
        slot = jnp.int32(0)
        for distance in range(SPAN):
            hit = apart == distance
            slot = jnp.where(hit, distance * MOST + taken[distance], slot)
            taken[distance] = taken[distance] + hit.astype(jnp.int32)
        slots.append(slot)
        owners.append(parent)
    return slots, owners


def served_beams(parents, me, target):
    count = jnp.int32(0)
    beams = [jnp.int32(0) for _ in range(MOST)]
    for child in range(BEAMS):
        parent = parents[target * BEAMS + child]
        hit = parent // BEAMS == me
        for rank in range(MOST):
            beams[rank] = jnp.where(hit & (count == rank), parent % BEAMS, beams[rank])
        count = count + hit.astype(jnp.int32)
    return beams


def exchange_kernel(
    q_hbm, new_hbm, pool_ref, table_hbm, len_hbm, par_hbm, w_ref,
    recv_ref, proj_ref,
    q_ref, new_ref, table_ref, len_ref, par_ref,
    pool_v, w_v, stage, q_send, q_recv, att, p_send, p_recv, r_send, lens,
    in_sem, pool_sem, w_sem, own_sem, qs_sem, qr_sem, bs_sem, br_sem, ps_sem, pr_sem, rs_sem, rr_sem,
):
    me = lax.axis_index("dp")
    mine = lax.axis_index("tensor")
    shards = lax.axis_size("tensor")
    y = lax.rem(me, SPAN)
    base = me - y
    context = stage.shape[1] // MOST
    wide = q_hbm.shape[2]
    heads = wide // HD
    rows = MOST * STEPS

    def peer(distance):
        return base + lax.rem(y + distance, SPAN)

    barrier = pltpu.get_barrier_semaphore()
    for distance in range(1, SPAN):
        pl.semaphore_signal(barrier, inc=1, device_id={"dp": peer(distance)}, device_id_type=MESH)
    for other in range(1, shards):
        pl.semaphore_signal(barrier, inc=1, device_id={"tensor": lax.rem(mine + other, shards)}, device_id_type=MESH)
    in_copies = []
    operands = ((par_hbm, par_ref), (q_hbm, q_ref), (new_hbm, new_ref), (table_hbm, table_ref), (len_hbm, len_ref))
    for at, (source, target) in enumerate(operands):
        copy = pltpu.make_async_copy(source, target, in_sem.at[at])
        copy.start()
        in_copies.append(copy)
    pool_copy = pltpu.make_async_copy(pool_ref, pool_v, pool_sem)
    pool_copy.start()
    for copy in in_copies:
        copy.wait()

    slots, _ = slots_of_children(par_ref, me)
    row = lax.broadcasted_iota(jnp.int32, (SPAN * rows, BEAMS), 0)
    col = lax.broadcasted_iota(jnp.int32, (SPAN * rows, BEAMS), 1)
    slot_at = jnp.zeros_like(col)
    for child in range(BEAMS):
        slot_at = jnp.where(col == child, slots[child], slot_at)
    q_sorted = jnp.zeros((SPAN * rows, wide), jnp.float32)
    new_sorted = jnp.zeros((SPAN * rows, 2 * HD), jnp.float32)
    for step in range(STEPS):
        pick = jnp.where((row // STEPS == slot_at) & (row % STEPS == step), 1.0, 0.0).astype(jnp.bfloat16)
        q_sorted += jnp.dot(pick, q_ref[step], preferred_element_type=jnp.float32)
        new_sorted += jnp.dot(pick, new_ref[step], preferred_element_type=jnp.float32)
    both = jnp.concatenate([q_sorted, new_sorted], axis=1)
    half = both.shape[1] // 2
    for distance in range(SPAN):
        part = both[distance * rows:(distance + 1) * rows]
        part = jnp.concatenate([part[:, :half], part[:, half:]], axis=0).astype(jnp.bfloat16)
        if distance == 0:
            q_recv[0] = part
        else:
            q_send[distance] = part

    pl.semaphore_wait(barrier, SPAN - 1 + shards - 1)

    q_copies = []
    for distance in range(1, SPAN):
        copy = pltpu.make_async_remote_copy(
            src_ref=q_send.at[distance], dst_ref=q_recv.at[distance],
            send_sem=qs_sem.at[distance], recv_sem=qr_sem.at[distance],
            device_id={"dp": peer(distance)}, device_id_type=MESH,
        )
        copy.start()
        q_copies.append(copy)

    pool_copy.wait()
    w_copies = []
    for block in range(shards):
        copy = pltpu.make_async_copy(w_ref.at[:, pl.ds(block * wide, wide)], w_v.at[block], w_sem.at[block])
        copy.start()
        w_copies.append(copy)
    served = {}
    for distance in range(SPAN):
        served[distance] = served_beams(par_ref, me, peer(SPAN - distance))
        for rank in range(MOST):
            lens[distance * MOST + rank] = len_ref[me * BEAMS + served[distance][rank]]

    b_copies = []
    for rank in range(MOST):
        for distance in (2, 1, 3, 0):
            beam = served[distance][rank]

            def put(index, carry, distance=distance, rank=rank, beam=beam):
                at = pl.multiple_of(rank * context + index * PAGE, PAGE)
                stage[distance, pl.ds(at, PAGE), :] = pool_v[table_ref[beam, index]]
                return carry

            lax.fori_loop(0, context // PAGE, put, 0)
            span = pl.ds(rank * context, context)
            if distance == 0:
                copy = pltpu.make_async_copy(stage.at[0, span], recv_ref.at[0, span], own_sem.at[rank])
            else:
                copy = pltpu.make_async_remote_copy(
                    src_ref=stage.at[distance, span], dst_ref=recv_ref.at[distance, span],
                    send_sem=bs_sem.at[distance * MOST + rank], recv_sem=br_sem.at[distance * MOST + rank],
                    device_id={"dp": peer(SPAN - distance)}, device_id_type=MESH,
                )
            copy.start()
            b_copies.append(copy)

    for copy in q_copies:
        copy.wait()

    def attend(distance, carry):
        message = q_recv[distance].astype(jnp.float32)
        message = jnp.concatenate([message[:rows], message[rows:]], axis=1)
        q_rows = jnp.concatenate([message[:, h * HD:(h + 1) * HD] for h in range(heads)], axis=0).astype(jnp.bfloat16)
        fresh = message[:, wide:].astype(jnp.bfloat16)
        old_len = lens[distance * MOST]
        last_len = lens[distance * MOST + 1]
        contract = (((1,), (1,)), ((), ()))
        scale = HD ** -0.5
        scores = lax.dot_general(q_rows, stage[distance, :, 0:HD], contract, preferred_element_type=jnp.float32) * scale
        fresh_scores = lax.dot_general(q_rows, fresh[:, :HD], contract, preferred_element_type=jnp.float32) * scale
        rank_at = lax.broadcasted_iota(jnp.int32, scores.shape, 0) // STEPS % MOST
        position = lax.broadcasted_iota(jnp.int32, scores.shape, 1) - rank_at * context
        limit = jnp.where(rank_at == 0, old_len, last_len)
        scores = jnp.where((position >= 0) & (position < limit), scores, -1e30)
        f_row = lax.broadcasted_iota(jnp.int32, fresh_scores.shape, 0)
        f_col = lax.broadcasted_iota(jnp.int32, fresh_scores.shape, 1)
        seen = (f_row // STEPS % MOST == f_col // STEPS) & (f_col % STEPS <= f_row % STEPS)
        fresh_scores = jnp.where(seen, fresh_scores, -1e30)
        top = jnp.maximum(jnp.max(scores, axis=1, keepdims=True), jnp.max(fresh_scores, axis=1, keepdims=True))
        exp_old = jnp.exp(scores - top)
        exp_new = jnp.exp(fresh_scores - top)
        total = jnp.sum(exp_old, axis=1, keepdims=True) + jnp.sum(exp_new, axis=1, keepdims=True)
        w_old = (exp_old / total).astype(jnp.bfloat16)
        w_new = (exp_new / total).astype(jnp.bfloat16)
        out = jnp.dot(w_old, stage[distance, :, HD:2 * HD], preferred_element_type=jnp.float32)
        out += jnp.dot(w_new, fresh[:, HD:], preferred_element_type=jnp.float32)
        out = jnp.concatenate([out[h * rows:(h + 1) * rows] for h in range(heads)], axis=1)
        att[pl.ds(pl.multiple_of(distance * rows, rows), rows), :] = out
        return carry

    lax.fori_loop(0, SPAN, attend, 0)
    attended = att[...].astype(jnp.bfloat16)
    for copy in w_copies:
        copy.wait()

    def p_copy(other):
        return pltpu.make_async_remote_copy(
            src_ref=p_send.at[other], dst_ref=p_recv.at[other],
            send_sem=ps_sem.at[other], recv_sem=pr_sem.at[other],
            device_id={"tensor": lax.rem(mine + other, shards)}, device_id_type=MESH,
        )

    def project(other, carry):
        product = jnp.dot(attended, w_v[lax.rem(mine + other, shards)], preferred_element_type=jnp.float32)
        p_send[other] = product.astype(jnp.bfloat16)
        p_copy(other).start()
        return carry

    lax.fori_loop(1, shards, project, 0)
    own = jnp.dot(attended, w_v[mine], preferred_element_type=jnp.float32)

    def gather_sums(other, total):
        p_copy(other).wait()
        return total + p_recv[other].astype(jnp.float32)

    summed = lax.fori_loop(1, shards, gather_sums, own)
    half = wide // 2
    r_copies = []
    for distance in range(SPAN):
        part = summed[distance * rows:(distance + 1) * rows]
        r_send[distance] = jnp.concatenate([part[:, :half], part[:, half:]], axis=0).astype(jnp.bfloat16)
        if distance == 0:
            copy = pltpu.make_async_copy(r_send.at[0], proj_ref.at[0], own_sem.at[MOST])
        else:
            copy = pltpu.make_async_remote_copy(
                src_ref=r_send.at[distance], dst_ref=proj_ref.at[distance],
                send_sem=rs_sem.at[distance], recv_sem=rr_sem.at[distance],
                device_id={"dp": peer(SPAN - distance)}, device_id_type=MESH,
            )
        copy.start()
        r_copies.append(copy)
    for copy in r_copies:
        copy.wait()
    for copy in b_copies:
        copy.wait()


def finish_kernel(recv_ref, raw_ref, new_hbm, len_hbm, par_hbm, proj_ref, cache_ref, new_ref, len_ref, par_ref, edge, zeros, in_sem, out_sem):
    me = lax.axis_index("dp")
    pages = recv_ref.shape[1] // PAGE
    operands = ((par_hbm, par_ref), (len_hbm, len_ref), (new_hbm, new_ref))
    in_copies = [pltpu.make_async_copy(source, target, in_sem.at[at]) for at, (source, target) in enumerate(operands)]
    for copy in in_copies:
        copy.start()
    zeros[...] = jnp.zeros_like(zeros)
    for copy in in_copies:
        copy.wait()
    slots, owners = slots_of_children(par_ref, me)
    fresh = [new_ref[step].astype(jnp.float32) for step in range(STEPS)]
    for child in range(BEAMS):
        slot = slots[child]
        length = len_ref[owners[child]]
        first = length // PAGE
        last = (length + STEPS - 1) // PAGE

        def whole(index, carry, child=child, slot=slot):
            span = pl.ds(pl.multiple_of(index * PAGE, PAGE), PAGE)
            pltpu.make_async_copy(recv_ref.at[slot, span], cache_ref.at[child, span], out_sem).start()
            return carry

        def clear(index, carry, child=child):
            span = pl.ds(pl.multiple_of(index * PAGE, PAGE), PAGE)
            pltpu.make_async_copy(zeros, cache_ref.at[child, span], out_sem).start()
            return carry

        def fix(index, carry, child=child, slot=slot, length=length, first=first):
            at = pl.multiple_of(index * PAGE, PAGE)
            position = at + lax.broadcasted_iota(jnp.int32, (PAGE, 2 * HD), 0)
            page = recv_ref[slot, pl.ds(at, PAGE), :].astype(jnp.float32)
            page = jnp.where(position < length, page, 0.0)
            for step in range(STEPS):
                page = jnp.where(position == length + step, fresh[step][child:child + 1], page)
            edge[child * 2 + index - first] = page.astype(jnp.bfloat16)
            pltpu.make_async_copy(edge.at[child * 2 + index - first], cache_ref.at[child, pl.ds(at, PAGE)], out_sem).start()
            return carry

        lax.fori_loop(0, first, whole, 0)
        lax.fori_loop(last + 1, pages, clear, 0)
        lax.fori_loop(first, last + 1, fix, 0)

    rows = MOST * STEPS
    raw = []
    for distance in range(SPAN):
        part = raw_ref[distance].astype(jnp.float32)
        raw.append(jnp.concatenate([part[:rows], part[rows:]], axis=1))
    raw = jnp.concatenate(raw, axis=0).astype(jnp.bfloat16)
    row = lax.broadcasted_iota(jnp.int32, (BEAMS, SPAN * rows), 0)
    col = lax.broadcasted_iota(jnp.int32, (BEAMS, SPAN * rows), 1)
    slot_at = jnp.zeros_like(col)
    for child in range(BEAMS):
        slot_at = jnp.where(row == child, slots[child], slot_at)
    for step in range(STEPS):
        pick = jnp.where(col == slot_at * STEPS + step, 1.0, 0.0).astype(jnp.bfloat16)
        proj_ref[step] = jnp.dot(pick, raw, preferred_element_type=jnp.float32).astype(jnp.bfloat16)
    pltpu.make_async_copy(recv_ref, cache_ref, out_sem).wait()


def local(shards, queries, new_kv, kv_pool, page_tables, lengths, parents, out_weight):
    wide = queries.shape[2]
    channels = kv_pool.shape[2]
    context = page_tables.shape[1] * kv_pool.shape[1]
    rows = MOST * STEPS
    vmem = pl.BlockSpec(memory_space=pltpu.VMEM)
    hbm = pl.BlockSpec(memory_space=pltpu.HBM)
    free = pl.BlockSpec(memory_space=pl.ANY)
    dma = pltpu.SemaphoreType.DMA
    bf16 = jnp.bfloat16
    with jax.named_scope("exchange"):
        recv, raw = pl.pallas_call(
            exchange_kernel,
            out_shape=(
                jax.ShapeDtypeStruct((SPAN, MOST * context, channels), bf16),
                jax.ShapeDtypeStruct((SPAN, 2 * rows, wide // 2), bf16),
            ),
            in_specs=[hbm] * 7,
            out_specs=(free, free),
            scratch_shapes=[
                pltpu.VMEM(queries.shape, bf16),
                pltpu.VMEM(new_kv.shape, bf16),
                pltpu.SMEM(page_tables.shape, jnp.int32),
                pltpu.SMEM(lengths.shape, jnp.int32),
                pltpu.SMEM(parents.shape, jnp.int32),
                pltpu.VMEM(kv_pool.shape, bf16),
                pltpu.VMEM((shards, out_weight.shape[0], wide), bf16),
                pltpu.VMEM((SPAN, MOST * context, channels), bf16),
                pltpu.VMEM((SPAN, 2 * rows, (wide + channels) // 2), bf16),
                pltpu.VMEM((SPAN, 2 * rows, (wide + channels) // 2), bf16),
                pltpu.VMEM((SPAN * rows, wide), jnp.float32),
                pltpu.VMEM((shards, SPAN * rows, wide), bf16),
                pltpu.VMEM((shards, SPAN * rows, wide), bf16),
                pltpu.VMEM((SPAN, 2 * rows, wide // 2), bf16),
                pltpu.SMEM((SPAN * MOST,), jnp.int32),
                dma((5,)), dma, dma((shards,)), dma((MOST + 1,)),
                dma((SPAN,)), dma((SPAN,)),
                dma((SPAN * MOST,)), dma((SPAN * MOST,)),
                dma((shards,)), dma((shards,)),
                dma((SPAN,)), dma((SPAN,)),
            ],
            compiler_params=pltpu.CompilerParams(
                collective_id=0, has_side_effects=True, vmem_limit_bytes=48 * 1024 * 1024
            ),
            name="exchange",
        )(*(
            pltpu.with_memory_space_constraint(operand, pltpu.HBM)
            for operand in (queries, new_kv, kv_pool, page_tables, lengths, parents, out_weight)
        ))
    with jax.named_scope("finish"):
        return pl.pallas_call(
            finish_kernel,
            out_shape=(
                jax.ShapeDtypeStruct(queries.shape, bf16),
                jax.ShapeDtypeStruct((BEAMS, context, channels), bf16),
            ),
            in_specs=[vmem, vmem, hbm, hbm, hbm],
            out_specs=(vmem, hbm),
            scratch_shapes=[
                pltpu.VMEM(new_kv.shape, bf16),
                pltpu.SMEM(lengths.shape, jnp.int32),
                pltpu.SMEM(parents.shape, jnp.int32),
                pltpu.VMEM((2 * BEAMS, PAGE, channels), bf16),
                pltpu.VMEM((PAGE, channels), bf16),
                dma((3,)), dma,
            ],
            compiler_params=pltpu.CompilerParams(vmem_limit_bytes=24 * 1024 * 1024),
            name="finish",
        )(recv.reshape(BEAMS, context, channels), raw, new_kv, lengths, parents)


def solution(mesh):
    in_specs = (
        P(None, "dp", "tensor"),
        P(None, "dp", "tensor"),
        P("dp", None, "tensor"),
        P("dp", None),
        P(),
        P(),
        P("tensor", None),
    )
    out_specs = (P(None, "dp", "tensor"), P("dp", None, "tensor"))
    body = functools.partial(local, mesh.shape["tensor"])
    return jax.shard_map(body, mesh=mesh, in_specs=in_specs, out_specs=out_specs, check_vma=False)
```

```python
import functools

import jax
import jax.numpy as jnp
from jax import lax
from jax.experimental import pallas as pl
from jax.experimental.pallas import tpu as pltpu
from jax.sharding import PartitionSpec as P

HD = 128
SPAN = 4
MOST = 2
BEAMS = 8
STEPS = 4
PAGE = 128
MESH = pl.DeviceIdType.MESH


def slots_of_children(parents, me):
    taken = [jnp.int32(0) for _ in range(SPAN)]
    slots, owners = [], []
    for child in range(BEAMS):
        parent = parents[me * BEAMS + child]
        apart = jnp.bitwise_and(parent // BEAMS - me, SPAN - 1)
        slot = jnp.int32(0)
        for distance in range(SPAN):
            hit = apart == distance
            slot = jnp.where(hit, distance * MOST + taken[distance], slot)
            taken[distance] = taken[distance] + hit.astype(jnp.int32)
        slots.append(slot)
        owners.append(parent)
    return slots, owners


def served_beams(parents, me, target):
    count = jnp.int32(0)
    beams = [jnp.int32(0) for _ in range(MOST)]
    for child in range(BEAMS):
        parent = parents[target * BEAMS + child]
        hit = parent // BEAMS == me
        for rank in range(MOST):
            beams[rank] = jnp.where(hit & (count == rank), parent % BEAMS, beams[rank])
        count = count + hit.astype(jnp.int32)
    return beams


def exchange_kernel(
    q_hbm, new_hbm, pool_ref, table_hbm, len_hbm, par_hbm, w_ref,
    recv_ref, proj_ref,
    q_ref, new_ref, table_ref, len_ref, par_ref,
    pool_v, w_v, stage, q_send, q_recv, att, p_send, p_recv, r_send, lens,
    in_sem, pool_sem, w_sem, own_sem, qs_sem, qr_sem, bs_sem, br_sem, ps_sem, pr_sem, rs_sem, rr_sem, here_sem,
):
    me = lax.axis_index("dp")
    mine = lax.axis_index("tensor")
    shards = lax.axis_size("tensor")
    y = lax.rem(me, SPAN)
    base = me - y
    context = stage.shape[1] // MOST
    wide = q_hbm.shape[2]
    heads = wide // HD
    rows = MOST * STEPS

    def peer(distance):
        return base + lax.rem(y + distance, SPAN)

    barrier = pltpu.get_barrier_semaphore()
    for distance in range(1, SPAN):
        pl.semaphore_signal(barrier, inc=1, device_id={"dp": peer(distance)}, device_id_type=MESH)
    for other in range(1, shards):
        @pl.when(mine + other < shards)
        def _(other=other):
            pl.semaphore_signal(barrier, inc=1, device_id={"tensor": mine + other}, device_id_type=MESH)
    in_copies = []
    operands = ((par_hbm, par_ref), (q_hbm, q_ref), (new_hbm, new_ref), (table_hbm, table_ref), (len_hbm, len_ref))
    for at, (source, target) in enumerate(operands):
        copy = pltpu.make_async_copy(source, target, in_sem.at[at])
        copy.start()
        in_copies.append(copy)
    pool_copy = pltpu.make_async_copy(pool_ref, pool_v, pool_sem)
    pool_copy.start()
    for copy in in_copies:
        copy.wait()

    slots, _ = slots_of_children(par_ref, me)
    row = lax.broadcasted_iota(jnp.int32, (SPAN * rows, BEAMS), 0)
    col = lax.broadcasted_iota(jnp.int32, (SPAN * rows, BEAMS), 1)
    slot_at = jnp.zeros_like(col)
    for child in range(BEAMS):
        slot_at = jnp.where(col == child, slots[child], slot_at)
    q_sorted = jnp.zeros((SPAN * rows, wide), jnp.float32)
    new_sorted = jnp.zeros((SPAN * rows, 2 * HD), jnp.float32)
    for step in range(STEPS):
        pick = jnp.where((row // STEPS == slot_at) & (row % STEPS == step), 1.0, 0.0).astype(jnp.bfloat16)
        q_sorted += jnp.dot(pick, q_ref[step], preferred_element_type=jnp.float32)
        new_sorted += jnp.dot(pick, new_ref[step], preferred_element_type=jnp.float32)
    both = jnp.concatenate([q_sorted, new_sorted], axis=1)
    half = both.shape[1] // 2
    for distance in range(SPAN):
        part = both[distance * rows:(distance + 1) * rows]
        part = jnp.concatenate([part[:, :half], part[:, half:]], axis=0).astype(jnp.bfloat16)
        if distance == 0:
            q_recv[0] = part
        else:
            q_send[distance] = part

    pl.semaphore_wait(barrier, SPAN - 1 + mine)
    for other in range(1, shards):
        @pl.when(mine >= other)
        def _(other=other):
            pl.semaphore_signal(here_sem, inc=1, device_id={"tensor": mine - other}, device_id_type=MESH)

    q_copies = []
    for distance in range(1, SPAN):
        copy = pltpu.make_async_remote_copy(
            src_ref=q_send.at[distance], dst_ref=q_recv.at[distance],
            send_sem=qs_sem.at[distance], recv_sem=qr_sem.at[distance],
            device_id={"dp": peer(distance)}, device_id_type=MESH,
        )
        copy.start()
        q_copies.append(copy)

    pool_copy.wait()
    w_copies = []
    for block in range(shards):
        copy = pltpu.make_async_copy(w_ref.at[:, pl.ds(block * wide, wide)], w_v.at[block], w_sem.at[block])
        copy.start()
        w_copies.append(copy)
    served = {}
    for distance in range(SPAN):
        served[distance] = served_beams(par_ref, me, peer(SPAN - distance))
        for rank in range(MOST):
            lens[distance * MOST + rank] = len_ref[me * BEAMS + served[distance][rank]]

    b_copies = []
    for rank in range(MOST):
        for distance in (2, 1, 3, 0):
            beam = served[distance][rank]

            def put(index, carry, distance=distance, rank=rank, beam=beam):
                at = pl.multiple_of(rank * context + index * PAGE, PAGE)
                stage[distance, pl.ds(at, PAGE), :] = pool_v[table_ref[beam, index]]
                return carry

            lax.fori_loop(0, context // PAGE, put, 0)
            span = pl.ds(rank * context, context)
            if distance == 0:
                copy = pltpu.make_async_copy(stage.at[0, span], recv_ref.at[0, span], own_sem.at[rank])
            else:
                copy = pltpu.make_async_remote_copy(
                    src_ref=stage.at[distance, span], dst_ref=recv_ref.at[distance, span],
                    send_sem=bs_sem.at[distance * MOST + rank], recv_sem=br_sem.at[distance * MOST + rank],
                    device_id={"dp": peer(SPAN - distance)}, device_id_type=MESH,
                )
            copy.start()
            b_copies.append(copy)

    for copy in q_copies:
        copy.wait()

    def attend(distance, carry):
        message = q_recv[distance].astype(jnp.float32)
        message = jnp.concatenate([message[:rows], message[rows:]], axis=1)
        q_rows = jnp.concatenate([message[:, h * HD:(h + 1) * HD] for h in range(heads)], axis=0).astype(jnp.bfloat16)
        fresh = message[:, wide:].astype(jnp.bfloat16)
        old_len = lens[distance * MOST]
        last_len = lens[distance * MOST + 1]
        contract = (((1,), (1,)), ((), ()))
        scale = HD ** -0.5
        scores = lax.dot_general(q_rows, stage[distance, :, 0:HD], contract, preferred_element_type=jnp.float32) * scale
        fresh_scores = lax.dot_general(q_rows, fresh[:, :HD], contract, preferred_element_type=jnp.float32) * scale
        rank_at = lax.broadcasted_iota(jnp.int32, scores.shape, 0) // STEPS % MOST
        position = lax.broadcasted_iota(jnp.int32, scores.shape, 1) - rank_at * context
        limit = jnp.where(rank_at == 0, old_len, last_len)
        scores = jnp.where((position >= 0) & (position < limit), scores, -1e30)
        f_row = lax.broadcasted_iota(jnp.int32, fresh_scores.shape, 0)
        f_col = lax.broadcasted_iota(jnp.int32, fresh_scores.shape, 1)
        seen = (f_row // STEPS % MOST == f_col // STEPS) & (f_col % STEPS <= f_row % STEPS)
        fresh_scores = jnp.where(seen, fresh_scores, -1e30)
        top = jnp.maximum(jnp.max(scores, axis=1, keepdims=True), jnp.max(fresh_scores, axis=1, keepdims=True))
        exp_old = jnp.exp(scores - top)
        exp_new = jnp.exp(fresh_scores - top)
        total = jnp.sum(exp_old, axis=1, keepdims=True) + jnp.sum(exp_new, axis=1, keepdims=True)
        w_old = (exp_old / total).astype(jnp.bfloat16)
        w_new = (exp_new / total).astype(jnp.bfloat16)
        out = jnp.dot(w_old, stage[distance, :, HD:2 * HD], preferred_element_type=jnp.float32)
        out += jnp.dot(w_new, fresh[:, HD:], preferred_element_type=jnp.float32)
        out = jnp.concatenate([out[h * rows:(h + 1) * rows] for h in range(heads)], axis=1)
        att[pl.ds(pl.multiple_of(distance * rows, rows), rows), :] = out
        return carry

    lax.fori_loop(0, SPAN, attend, 0)
    attended = att[...].astype(jnp.bfloat16)
    for copy in w_copies:
        copy.wait()

    def p_copy(other):
        return pltpu.make_async_remote_copy(
            src_ref=p_send.at[other], dst_ref=p_recv.at[other],
            send_sem=ps_sem.at[other], recv_sem=pr_sem.at[other],
            device_id={"tensor": lax.rem(mine + other, shards)}, device_id_type=MESH,
        )

    def project(other, carry):
        product = jnp.dot(attended, w_v[lax.rem(mine + other, shards)], preferred_element_type=jnp.float32)
        p_send[other] = product.astype(jnp.bfloat16)
        p_copy(other).start()
        return carry

    @pl.when(mine < shards - 1)
    def _():
        pl.semaphore_wait(here_sem, shards - 1 - mine)

    lax.fori_loop(1, shards, project, 0)
    own = jnp.dot(attended, w_v[mine], preferred_element_type=jnp.float32)

    def gather_sums(other, total):
        p_copy(other).wait()
        return total + p_recv[other].astype(jnp.float32)

    summed = lax.fori_loop(1, shards, gather_sums, own)
    half = wide // 2
    r_copies = []
    for distance in range(SPAN):
        part = summed[distance * rows:(distance + 1) * rows]
        r_send[distance] = jnp.concatenate([part[:, :half], part[:, half:]], axis=0).astype(jnp.bfloat16)
        if distance == 0:
            copy = pltpu.make_async_copy(r_send.at[0], proj_ref.at[0], own_sem.at[MOST])
        else:
            copy = pltpu.make_async_remote_copy(
                src_ref=r_send.at[distance], dst_ref=proj_ref.at[distance],
                send_sem=rs_sem.at[distance], recv_sem=rr_sem.at[distance],
                device_id={"dp": peer(SPAN - distance)}, device_id_type=MESH,
            )
        copy.start()
        r_copies.append(copy)
    for copy in r_copies:
        copy.wait()
    for copy in b_copies:
        copy.wait()


def finish_kernel(recv_ref, raw_ref, new_hbm, len_hbm, par_hbm, proj_ref, cache_ref, new_ref, len_ref, par_ref, edge, zeros, in_sem, out_sem):
    me = lax.axis_index("dp")
    pages = recv_ref.shape[1] // PAGE
    operands = ((par_hbm, par_ref), (len_hbm, len_ref), (new_hbm, new_ref))
    in_copies = [pltpu.make_async_copy(source, target, in_sem.at[at]) for at, (source, target) in enumerate(operands)]
    for copy in in_copies:
        copy.start()
    zeros[...] = jnp.zeros_like(zeros)
    for copy in in_copies:
        copy.wait()
    slots, owners = slots_of_children(par_ref, me)
    fresh = [new_ref[step].astype(jnp.float32) for step in range(STEPS)]
    for child in range(BEAMS):
        slot = slots[child]
        length = len_ref[owners[child]]
        first = length // PAGE
        last = (length + STEPS - 1) // PAGE

        def whole(index, carry, child=child, slot=slot):
            span = pl.ds(pl.multiple_of(index * PAGE, PAGE), PAGE)
            pltpu.make_async_copy(recv_ref.at[slot, span], cache_ref.at[child, span], out_sem).start()
            return carry

        def clear(index, carry, child=child):
            span = pl.ds(pl.multiple_of(index * PAGE, PAGE), PAGE)
            pltpu.make_async_copy(zeros, cache_ref.at[child, span], out_sem).start()
            return carry

        def fix(index, carry, child=child, slot=slot, length=length, first=first):
            at = pl.multiple_of(index * PAGE, PAGE)
            position = at + lax.broadcasted_iota(jnp.int32, (PAGE, 2 * HD), 0)
            page = recv_ref[slot, pl.ds(at, PAGE), :].astype(jnp.float32)
            page = jnp.where(position < length, page, 0.0)
            for step in range(STEPS):
                page = jnp.where(position == length + step, fresh[step][child:child + 1], page)
            edge[child * 2 + index - first] = page.astype(jnp.bfloat16)
            pltpu.make_async_copy(edge.at[child * 2 + index - first], cache_ref.at[child, pl.ds(at, PAGE)], out_sem).start()
            return carry

        lax.fori_loop(0, first, whole, 0)
        lax.fori_loop(last + 1, pages, clear, 0)
        lax.fori_loop(first, last + 1, fix, 0)

    rows = MOST * STEPS
    raw = []
    for distance in range(SPAN):
        part = raw_ref[distance].astype(jnp.float32)
        raw.append(jnp.concatenate([part[:rows], part[rows:]], axis=1))
    raw = jnp.concatenate(raw, axis=0).astype(jnp.bfloat16)
    row = lax.broadcasted_iota(jnp.int32, (BEAMS, SPAN * rows), 0)
    col = lax.broadcasted_iota(jnp.int32, (BEAMS, SPAN * rows), 1)
    slot_at = jnp.zeros_like(col)
    for child in range(BEAMS):
        slot_at = jnp.where(row == child, slots[child], slot_at)
    for step in range(STEPS):
        pick = jnp.where(col == slot_at * STEPS + step, 1.0, 0.0).astype(jnp.bfloat16)
        proj_ref[step] = jnp.dot(pick, raw, preferred_element_type=jnp.float32).astype(jnp.bfloat16)
    pltpu.make_async_copy(recv_ref, cache_ref, out_sem).wait()


def local(shards, queries, new_kv, kv_pool, page_tables, lengths, parents, out_weight):
    wide = queries.shape[2]
    channels = kv_pool.shape[2]
    context = page_tables.shape[1] * kv_pool.shape[1]
    rows = MOST * STEPS
    vmem = pl.BlockSpec(memory_space=pltpu.VMEM)
    hbm = pl.BlockSpec(memory_space=pltpu.HBM)
    free = pl.BlockSpec(memory_space=pl.ANY)
    dma = pltpu.SemaphoreType.DMA
    bf16 = jnp.bfloat16
    with jax.named_scope("exchange"):
        recv, raw = pl.pallas_call(
            exchange_kernel,
            out_shape=(
                jax.ShapeDtypeStruct((SPAN, MOST * context, channels), bf16),
                jax.ShapeDtypeStruct((SPAN, 2 * rows, wide // 2), bf16),
            ),
            in_specs=[hbm] * 7,
            out_specs=(free, free),
            scratch_shapes=[
                pltpu.VMEM(queries.shape, bf16),
                pltpu.VMEM(new_kv.shape, bf16),
                pltpu.SMEM(page_tables.shape, jnp.int32),
                pltpu.SMEM(lengths.shape, jnp.int32),
                pltpu.SMEM(parents.shape, jnp.int32),
                pltpu.VMEM(kv_pool.shape, bf16),
                pltpu.VMEM((shards, out_weight.shape[0], wide), bf16),
                pltpu.VMEM((SPAN, MOST * context, channels), bf16),
                pltpu.VMEM((SPAN, 2 * rows, (wide + channels) // 2), bf16),
                pltpu.VMEM((SPAN, 2 * rows, (wide + channels) // 2), bf16),
                pltpu.VMEM((SPAN * rows, wide), jnp.float32),
                pltpu.VMEM((shards, SPAN * rows, wide), bf16),
                pltpu.VMEM((shards, SPAN * rows, wide), bf16),
                pltpu.VMEM((SPAN, 2 * rows, wide // 2), bf16),
                pltpu.SMEM((SPAN * MOST,), jnp.int32),
                dma((5,)), dma, dma((shards,)), dma((MOST + 1,)),
                dma((SPAN,)), dma((SPAN,)),
                dma((SPAN * MOST,)), dma((SPAN * MOST,)),
                dma((shards,)), dma((shards,)),
                dma((SPAN,)), dma((SPAN,)),
                pltpu.SemaphoreType.REGULAR,
            ],
            compiler_params=pltpu.CompilerParams(
                collective_id=0, has_side_effects=True, vmem_limit_bytes=48 * 1024 * 1024
            ),
            name="exchange",
        )(*(
            pltpu.with_memory_space_constraint(operand, pltpu.HBM)
            for operand in (queries, new_kv, kv_pool, page_tables, lengths, parents, out_weight)
        ))
    with jax.named_scope("finish"):
        return pl.pallas_call(
            finish_kernel,
            out_shape=(
                jax.ShapeDtypeStruct(queries.shape, bf16),
                jax.ShapeDtypeStruct((BEAMS, context, channels), bf16),
            ),
            in_specs=[vmem, vmem, hbm, hbm, hbm],
            out_specs=(vmem, hbm),
            scratch_shapes=[
                pltpu.VMEM(new_kv.shape, bf16),
                pltpu.SMEM(lengths.shape, jnp.int32),
                pltpu.SMEM(parents.shape, jnp.int32),
                pltpu.VMEM((2 * BEAMS, PAGE, channels), bf16),
                pltpu.VMEM((PAGE, channels), bf16),
                dma((3,)), dma,
            ],
            compiler_params=pltpu.CompilerParams(vmem_limit_bytes=24 * 1024 * 1024),
            name="finish",
        )(recv.reshape(BEAMS, context, channels), raw, new_kv, lengths, parents)


def solution(mesh):
    in_specs = (
        P(None, "dp", "tensor"),
        P(None, "dp", "tensor"),
        P("dp", None, "tensor"),
        P("dp", None),
        P(),
        P(),
        P("tensor", None),
    )
    out_specs = (P(None, "dp", "tensor"), P("dp", None, "tensor"))
    body = functools.partial(local, mesh.shape["tensor"])
    return jax.shard_map(body, mesh=mesh, in_specs=in_specs, out_specs=out_specs, check_vma=False)
```

```python
import functools

import jax
import jax.numpy as jnp
from jax import lax
from jax.experimental import pallas as pl
from jax.experimental.pallas import tpu as pltpu
from jax.sharding import PartitionSpec as P

HD = 128
SPAN = 4
MOST = 2
BEAMS = 8
STEPS = 4
PAGE = 128
CUTS = 4
CUT = PAGE // CUTS
MESH = pl.DeviceIdType.MESH


def slots_of_children(parents, me):
    taken = [jnp.int32(0) for _ in range(SPAN)]
    slots, owners = [], []
    for child in range(BEAMS):
        parent = parents[me * BEAMS + child]
        apart = jnp.bitwise_and(parent // BEAMS - me, SPAN - 1)
        slot = jnp.int32(0)
        for distance in range(SPAN):
            hit = apart == distance
            slot = jnp.where(hit, distance * MOST + taken[distance], slot)
            taken[distance] = taken[distance] + hit.astype(jnp.int32)
        slots.append(slot)
        owners.append(parent)
    return slots, owners


def served_beams(parents, me, target):
    count = jnp.int32(0)
    beams = [jnp.int32(0) for _ in range(MOST)]
    for child in range(BEAMS):
        parent = parents[target * BEAMS + child]
        hit = parent // BEAMS == me
        for rank in range(MOST):
            beams[rank] = jnp.where(hit & (count == rank), parent % BEAMS, beams[rank])
        count = count + hit.astype(jnp.int32)
    return beams


def exchange_kernel(
    q_hbm, new_hbm, pool_ref, table_hbm, len_hbm, par_hbm, w_ref,
    recv_ref, proj_ref,
    q_ref, new_ref, table_ref, len_ref, par_ref,
    pool_0, pool_1, pool_2, pool_3, w_v, stage, q_send, q_recv, att, p_send, p_recv, r_send, lens, beams,
    in_sem, pool_sem, w_sem, own_sem, qs_sem, qr_sem, bs_sem, br_sem, ps_sem, pr_sem, rs_sem, rr_sem, here_sem,
):
    me = lax.axis_index("dp")
    mine = lax.axis_index("tensor")
    shards = lax.axis_size("tensor")
    y = lax.rem(me, SPAN)
    base = me - y
    pages = stage.shape[1] // MOST
    context = pages * PAGE
    pools = (pool_0, pool_1, pool_2, pool_3)
    wide = q_hbm.shape[2]
    heads = wide // HD
    rows = MOST * STEPS

    def peer(distance):
        return base + lax.rem(y + distance, SPAN)

    barrier = pltpu.get_barrier_semaphore()
    for distance in range(1, SPAN):
        pl.semaphore_signal(barrier, inc=1, device_id={"dp": peer(distance)}, device_id_type=MESH)
    for other in range(1, shards):
        @pl.when(mine + other < shards)
        def _(other=other):
            pl.semaphore_signal(barrier, inc=1, device_id={"tensor": mine + other}, device_id_type=MESH)
    in_copies = []
    operands = ((par_hbm, par_ref), (q_hbm, q_ref), (new_hbm, new_ref), (table_hbm, table_ref), (len_hbm, len_ref))
    for at, (source, target) in enumerate(operands):
        copy = pltpu.make_async_copy(source, target, in_sem.at[at])
        copy.start()
        in_copies.append(copy)
    pool_copies = []
    for cut in range(CUTS):
        copy = pltpu.make_async_copy(pool_ref.at[:, pl.ds(cut * CUT, CUT), :], pools[cut], pool_sem.at[cut])
        copy.start()
        pool_copies.append(copy)
    for copy in in_copies:
        copy.wait()

    slots, _ = slots_of_children(par_ref, me)
    row = lax.broadcasted_iota(jnp.int32, (SPAN * rows, BEAMS), 0)
    col = lax.broadcasted_iota(jnp.int32, (SPAN * rows, BEAMS), 1)
    slot_at = jnp.zeros_like(col)
    for child in range(BEAMS):
        slot_at = jnp.where(col == child, slots[child], slot_at)
    q_sorted = jnp.zeros((SPAN * rows, wide), jnp.float32)
    new_sorted = jnp.zeros((SPAN * rows, 2 * HD), jnp.float32)
    for step in range(STEPS):
        pick = jnp.where((row // STEPS == slot_at) & (row % STEPS == step), 1.0, 0.0).astype(jnp.bfloat16)
        q_sorted += jnp.dot(pick, q_ref[step], preferred_element_type=jnp.float32)
        new_sorted += jnp.dot(pick, new_ref[step], preferred_element_type=jnp.float32)
    both = jnp.concatenate([q_sorted, new_sorted], axis=1)
    half = both.shape[1] // 2
    for distance in range(SPAN):
        part = both[distance * rows:(distance + 1) * rows]
        part = jnp.concatenate([part[:, :half], part[:, half:]], axis=0).astype(jnp.bfloat16)
        if distance == 0:
            q_recv[0] = part
        else:
            q_send[distance] = part

    pl.semaphore_wait(barrier, SPAN - 1 + mine)
    for other in range(1, shards):
        @pl.when(mine >= other)
        def _(other=other):
            pl.semaphore_signal(here_sem, inc=1, device_id={"tensor": mine - other}, device_id_type=MESH)

    q_copies = []
    for distance in range(1, SPAN):
        copy = pltpu.make_async_remote_copy(
            src_ref=q_send.at[distance], dst_ref=q_recv.at[distance],
            send_sem=qs_sem.at[distance], recv_sem=qr_sem.at[distance],
            device_id={"dp": peer(distance)}, device_id_type=MESH,
        )
        copy.start()
        q_copies.append(copy)

    for distance in range(SPAN):
        served = served_beams(par_ref, me, peer(SPAN - distance))
        for rank in range(MOST):
            beams[distance * MOST + rank] = served[rank]
            lens[distance * MOST + rank] = len_ref[me * BEAMS + served[rank]]

    def put(distance, cut):
        def body(index, carry):
            beam = beams[distance * MOST + index // pages]
            stage[distance, index, pl.ds(cut * CUT, CUT), :] = pools[cut][table_ref[beam, lax.rem(index, pages)]]
            return carry

        lax.fori_loop(0, MOST * pages, body, 0)

    b_copies = []
    for cut in range(CUTS):
        pool_copies[cut].wait()
        rows_at = pl.ds(cut * CUT, CUT)
        for distance in (2, 1, 3):
            put(distance, cut)
            copy = pltpu.make_async_remote_copy(
                src_ref=stage.at[distance, :, rows_at], dst_ref=recv_ref.at[distance, :, rows_at],
                send_sem=bs_sem.at[distance * CUTS + cut], recv_sem=br_sem.at[distance * CUTS + cut],
                device_id={"dp": peer(SPAN - distance)}, device_id_type=MESH,
            )
            copy.start()
            b_copies.append(copy)
    w_copies = []
    for block in range(shards):
        copy = pltpu.make_async_copy(w_ref.at[:, pl.ds(block * wide, wide)], w_v.at[block], w_sem.at[block])
        copy.start()
        w_copies.append(copy)
    for cut in range(CUTS):
        put(0, cut)
    copy = pltpu.make_async_copy(stage.at[0], recv_ref.at[0], own_sem.at[0])
    copy.start()
    b_copies.append(copy)

    for copy in q_copies:
        copy.wait()

    def attend(distance, carry):
        message = q_recv[distance].astype(jnp.float32)
        message = jnp.concatenate([message[:rows], message[rows:]], axis=1)
        q_rows = jnp.concatenate([message[:, h * HD:(h + 1) * HD] for h in range(heads)], axis=0).astype(jnp.bfloat16)
        fresh = message[:, wide:].astype(jnp.bfloat16)
        old_len = lens[distance * MOST]
        last_len = lens[distance * MOST + 1]
        contract = (((1,), (1,)), ((), ()))
        scale = HD ** -0.5
        scores = lax.dot_general(q_rows, stage[distance, :, :, 0:HD].reshape(MOST * context, HD), contract, preferred_element_type=jnp.float32) * scale
        fresh_scores = lax.dot_general(q_rows, fresh[:, :HD], contract, preferred_element_type=jnp.float32) * scale
        rank_at = lax.broadcasted_iota(jnp.int32, scores.shape, 0) // STEPS % MOST
        position = lax.broadcasted_iota(jnp.int32, scores.shape, 1) - rank_at * context
        limit = jnp.where(rank_at == 0, old_len, last_len)
        scores = jnp.where((position >= 0) & (position < limit), scores, -1e30)
        f_row = lax.broadcasted_iota(jnp.int32, fresh_scores.shape, 0)
        f_col = lax.broadcasted_iota(jnp.int32, fresh_scores.shape, 1)
        seen = (f_row // STEPS % MOST == f_col // STEPS) & (f_col % STEPS <= f_row % STEPS)
        fresh_scores = jnp.where(seen, fresh_scores, -1e30)
        top = jnp.maximum(jnp.max(scores, axis=1, keepdims=True), jnp.max(fresh_scores, axis=1, keepdims=True))
        exp_old = jnp.exp(scores - top)
        exp_new = jnp.exp(fresh_scores - top)
        total = jnp.sum(exp_old, axis=1, keepdims=True) + jnp.sum(exp_new, axis=1, keepdims=True)
        w_old = (exp_old / total).astype(jnp.bfloat16)
        w_new = (exp_new / total).astype(jnp.bfloat16)
        out = jnp.dot(w_old, stage[distance, :, :, HD:2 * HD].reshape(MOST * context, HD), preferred_element_type=jnp.float32)
        out += jnp.dot(w_new, fresh[:, HD:], preferred_element_type=jnp.float32)
        out = jnp.concatenate([out[h * rows:(h + 1) * rows] for h in range(heads)], axis=1)
        att[pl.ds(pl.multiple_of(distance * rows, rows), rows), :] = out
        return carry

    lax.fori_loop(0, SPAN, attend, 0)
    attended = att[...].astype(jnp.bfloat16)
    for copy in w_copies:
        copy.wait()

    def p_copy(other):
        return pltpu.make_async_remote_copy(
            src_ref=p_send.at[other], dst_ref=p_recv.at[other],
            send_sem=ps_sem.at[other], recv_sem=pr_sem.at[other],
            device_id={"tensor": lax.rem(mine + other, shards)}, device_id_type=MESH,
        )

    def project(other, carry):
        product = jnp.dot(attended, w_v[lax.rem(mine + other, shards)], preferred_element_type=jnp.float32)
        p_send[other] = product.astype(jnp.bfloat16)
        p_copy(other).start()
        return carry

    @pl.when(mine < shards - 1)
    def _():
        pl.semaphore_wait(here_sem, shards - 1 - mine)

    lax.fori_loop(1, shards, project, 0)
    own = jnp.dot(attended, w_v[mine], preferred_element_type=jnp.float32)

    def gather_sums(other, total):
        p_copy(other).wait()
        return total + p_recv[other].astype(jnp.float32)

    summed = lax.fori_loop(1, shards, gather_sums, own)
    half = wide // 2
    r_copies = []
    for distance in range(SPAN):
        part = summed[distance * rows:(distance + 1) * rows]
        r_send[distance] = jnp.concatenate([part[:, :half], part[:, half:]], axis=0).astype(jnp.bfloat16)
        if distance == 0:
            copy = pltpu.make_async_copy(r_send.at[0], proj_ref.at[0], own_sem.at[1])
        else:
            copy = pltpu.make_async_remote_copy(
                src_ref=r_send.at[distance], dst_ref=proj_ref.at[distance],
                send_sem=rs_sem.at[distance], recv_sem=rr_sem.at[distance],
                device_id={"dp": peer(SPAN - distance)}, device_id_type=MESH,
            )
        copy.start()
        r_copies.append(copy)
    for copy in r_copies:
        copy.wait()
    for copy in b_copies:
        copy.wait()


def finish_kernel(recv_ref, raw_ref, new_hbm, len_hbm, par_hbm, proj_ref, cache_ref, new_ref, len_ref, par_ref, edge, zeros, in_sem, out_sem):
    me = lax.axis_index("dp")
    pages = recv_ref.shape[1]
    operands = ((par_hbm, par_ref), (len_hbm, len_ref), (new_hbm, new_ref))
    in_copies = [pltpu.make_async_copy(source, target, in_sem.at[at]) for at, (source, target) in enumerate(operands)]
    for copy in in_copies:
        copy.start()
    zeros[...] = jnp.zeros_like(zeros)
    for copy in in_copies:
        copy.wait()
    slots, owners = slots_of_children(par_ref, me)
    fresh = jnp.concatenate([new_ref[step].astype(jnp.float32) for step in range(STEPS)], axis=0).astype(jnp.bfloat16)
    fresh_row = lax.broadcasted_iota(jnp.int32, (PAGE, STEPS * BEAMS), 1)
    for child in range(BEAMS):
        slot = slots[child]
        length = len_ref[owners[child]]
        first = length // PAGE
        last = (length + STEPS - 1) // PAGE

        def whole(index, carry, child=child, slot=slot):
            pltpu.make_async_copy(recv_ref.at[slot, index], cache_ref.at[child, index], out_sem).start()
            return carry

        def clear(index, carry, child=child):
            pltpu.make_async_copy(zeros, cache_ref.at[child, index], out_sem).start()
            return carry

        def fix(index, carry, child=child, slot=slot, length=length, first=first):
            position = index * PAGE + lax.broadcasted_iota(jnp.int32, (PAGE, 2 * HD), 0)
            behind = index * PAGE - length + lax.broadcasted_iota(jnp.int32, (PAGE, STEPS * BEAMS), 0)
            pick = jnp.where((fresh_row // BEAMS == behind) & (fresh_row % BEAMS == child), 1.0, 0.0).astype(jnp.bfloat16)
            added = jnp.dot(pick, fresh, preferred_element_type=jnp.float32)
            page = jnp.where(position < length, recv_ref[slot, index].astype(jnp.float32), added)
            at = child * 2 + index - first
            edge[at] = page.astype(jnp.bfloat16)
            pltpu.make_async_copy(edge.at[at], cache_ref.at[child, index], out_sem).start()
            return carry

        lax.fori_loop(0, first, whole, 0)
        lax.fori_loop(last + 1, pages, clear, 0)
        lax.fori_loop(first, last + 1, fix, 0)

    rows = MOST * STEPS
    raw = []
    for distance in range(SPAN):
        part = raw_ref[distance].astype(jnp.float32)
        raw.append(jnp.concatenate([part[:rows], part[rows:]], axis=1))
    raw = jnp.concatenate(raw, axis=0).astype(jnp.bfloat16)
    row = lax.broadcasted_iota(jnp.int32, (BEAMS, SPAN * rows), 0)
    col = lax.broadcasted_iota(jnp.int32, (BEAMS, SPAN * rows), 1)
    slot_at = jnp.zeros_like(col)
    for child in range(BEAMS):
        slot_at = jnp.where(row == child, slots[child], slot_at)
    for step in range(STEPS):
        pick = jnp.where(col == slot_at * STEPS + step, 1.0, 0.0).astype(jnp.bfloat16)
        proj_ref[step] = jnp.dot(pick, raw, preferred_element_type=jnp.float32).astype(jnp.bfloat16)
    pltpu.make_async_copy(recv_ref, cache_ref, out_sem).wait()


def local(shards, queries, new_kv, kv_pool, page_tables, lengths, parents, out_weight):
    wide = queries.shape[2]
    channels = kv_pool.shape[2]
    pages = page_tables.shape[1]
    rows = MOST * STEPS
    vmem = pl.BlockSpec(memory_space=pltpu.VMEM)
    hbm = pl.BlockSpec(memory_space=pltpu.HBM)
    free = pl.BlockSpec(memory_space=pl.ANY)
    dma = pltpu.SemaphoreType.DMA
    bf16 = jnp.bfloat16
    with jax.named_scope("exchange"):
        recv, raw = pl.pallas_call(
            exchange_kernel,
            out_shape=(
                jax.ShapeDtypeStruct((SPAN, MOST * pages, PAGE, channels), bf16),
                jax.ShapeDtypeStruct((SPAN, 2 * rows, wide // 2), bf16),
            ),
            in_specs=[hbm] * 7,
            out_specs=(free, free),
            scratch_shapes=[
                pltpu.VMEM(queries.shape, bf16),
                pltpu.VMEM(new_kv.shape, bf16),
                pltpu.SMEM(page_tables.shape, jnp.int32),
                pltpu.SMEM(lengths.shape, jnp.int32),
                pltpu.SMEM(parents.shape, jnp.int32),
                *[pltpu.VMEM((kv_pool.shape[0], CUT, channels), bf16) for _ in range(CUTS)],
                pltpu.VMEM((shards, out_weight.shape[0], wide), bf16),
                pltpu.VMEM((SPAN, MOST * pages, PAGE, channels), bf16),
                pltpu.VMEM((SPAN, 2 * rows, (wide + channels) // 2), bf16),
                pltpu.VMEM((SPAN, 2 * rows, (wide + channels) // 2), bf16),
                pltpu.VMEM((SPAN * rows, wide), jnp.float32),
                pltpu.VMEM((shards, SPAN * rows, wide), bf16),
                pltpu.VMEM((shards, SPAN * rows, wide), bf16),
                pltpu.VMEM((SPAN, 2 * rows, wide // 2), bf16),
                pltpu.SMEM((SPAN * MOST,), jnp.int32),
                pltpu.SMEM((SPAN * MOST,), jnp.int32),
                dma((5,)), dma((CUTS,)), dma((shards,)), dma((2,)),
                dma((SPAN,)), dma((SPAN,)),
                dma((SPAN * CUTS,)), dma((SPAN * CUTS,)),
                dma((shards,)), dma((shards,)),
                dma((SPAN,)), dma((SPAN,)),
                pltpu.SemaphoreType.REGULAR,
            ],
            compiler_params=pltpu.CompilerParams(
                collective_id=0, has_side_effects=True, vmem_limit_bytes=48 * 1024 * 1024
            ),
            name="exchange",
        )(*(
            pltpu.with_memory_space_constraint(operand, pltpu.HBM)
            for operand in (queries, new_kv, kv_pool, page_tables, lengths, parents, out_weight)
        ))
    with jax.named_scope("finish"):
        projected, cache = pl.pallas_call(
            finish_kernel,
            out_shape=(
                jax.ShapeDtypeStruct(queries.shape, bf16),
                jax.ShapeDtypeStruct((BEAMS, pages, PAGE, channels), bf16),
            ),
            in_specs=[vmem, vmem, hbm, hbm, hbm],
            out_specs=(vmem, hbm),
            scratch_shapes=[
                pltpu.VMEM(new_kv.shape, bf16),
                pltpu.SMEM(lengths.shape, jnp.int32),
                pltpu.SMEM(parents.shape, jnp.int32),
                pltpu.VMEM((2 * BEAMS, PAGE, channels), bf16),
                pltpu.VMEM((PAGE, channels), bf16),
                dma((3,)), dma,
            ],
            compiler_params=pltpu.CompilerParams(vmem_limit_bytes=24 * 1024 * 1024),
            name="finish",
        )(recv.reshape(BEAMS, pages, PAGE, channels), raw, new_kv, lengths, parents)
        return projected, cache.reshape(BEAMS, pages * PAGE, channels)


def solution(mesh):
    in_specs = (
        P(None, "dp", "tensor"),
        P(None, "dp", "tensor"),
        P("dp", None, "tensor"),
        P("dp", None),
        P(),
        P(),
        P("tensor", None),
    )
    out_specs = (P(None, "dp", "tensor"), P("dp", None, "tensor"))
    body = functools.partial(local, mesh.shape["tensor"])
    return jax.shard_map(body, mesh=mesh, in_specs=in_specs, out_specs=out_specs, check_vma=False)
```

```python
import functools

import jax
import jax.numpy as jnp
from jax import lax
from jax.experimental import pallas as pl
from jax.experimental.pallas import tpu as pltpu
from jax.sharding import PartitionSpec as P

HD = 128
SPAN = 4
MOST = 2
BEAMS = 8
STEPS = 4
PAGE = 128
MESH = pl.DeviceIdType.MESH


def slots_of_children(parents, me):
    taken = [jnp.int32(0) for _ in range(SPAN)]
    slots, owners = [], []
    for child in range(BEAMS):
        parent = parents[me * BEAMS + child]
        apart = jnp.bitwise_and(parent // BEAMS - me, SPAN - 1)
        slot = jnp.int32(0)
        for distance in range(SPAN):
            hit = apart == distance
            slot = jnp.where(hit, distance * MOST + taken[distance], slot)
            taken[distance] = taken[distance] + hit.astype(jnp.int32)
        slots.append(slot)
        owners.append(parent)
    return slots, owners


def served_beams(parents, me, target):
    count = jnp.int32(0)
    beams = [jnp.int32(0) for _ in range(MOST)]
    for child in range(BEAMS):
        parent = parents[target * BEAMS + child]
        hit = parent // BEAMS == me
        for rank in range(MOST):
            beams[rank] = jnp.where(hit & (count == rank), parent % BEAMS, beams[rank])
        count = count + hit.astype(jnp.int32)
    return beams


def exchange_kernel(
    q_hbm, new_hbm, pool_ref, table_hbm, len_hbm, par_hbm, w_ref,
    recv_ref, proj_ref,
    q_ref, new_ref, table_ref, len_ref, par_ref,
    pool_v, w_v, stage, q_send, q_recv, att, p_send, p_recv, r_send, lens,
    in_sem, pool_sem, w_sem, own_sem, qs_sem, qr_sem, bs_sem, br_sem, ps_sem, pr_sem, rs_sem, rr_sem, here_sem,
):
    me = lax.axis_index("dp")
    mine = lax.axis_index("tensor")
    shards = lax.axis_size("tensor")
    y = lax.rem(me, SPAN)
    base = me - y
    context = stage.shape[1] // MOST
    wide = q_hbm.shape[2]
    heads = wide // HD
    rows = MOST * STEPS

    def peer(distance):
        return base + lax.rem(y + distance, SPAN)

    barrier = pltpu.get_barrier_semaphore()
    for distance in range(1, SPAN):
        pl.semaphore_signal(barrier, inc=1, device_id={"dp": peer(distance)}, device_id_type=MESH)
    for other in range(1, shards):
        @pl.when(mine + other < shards)
        def _(other=other):
            pl.semaphore_signal(barrier, inc=1, device_id={"tensor": mine + other}, device_id_type=MESH)
    in_copies = []
    operands = ((par_hbm, par_ref), (q_hbm, q_ref), (new_hbm, new_ref), (table_hbm, table_ref), (len_hbm, len_ref))
    for at, (source, target) in enumerate(operands):
        copy = pltpu.make_async_copy(source, target, in_sem.at[at])
        copy.start()
        in_copies.append(copy)
    pool_copy = pltpu.make_async_copy(pool_ref, pool_v, pool_sem)
    pool_copy.start()
    for copy in in_copies:
        copy.wait()

    slots, _ = slots_of_children(par_ref, me)
    row = lax.broadcasted_iota(jnp.int32, (SPAN * rows, BEAMS), 0)
    col = lax.broadcasted_iota(jnp.int32, (SPAN * rows, BEAMS), 1)
    slot_at = jnp.zeros_like(col)
    for child in range(BEAMS):
        slot_at = jnp.where(col == child, slots[child], slot_at)
    q_sorted = jnp.zeros((SPAN * rows, wide), jnp.float32)
    new_sorted = jnp.zeros((SPAN * rows, 2 * HD), jnp.float32)
    for step in range(STEPS):
        pick = jnp.where((row // STEPS == slot_at) & (row % STEPS == step), 1.0, 0.0).astype(jnp.bfloat16)
        q_sorted += jnp.dot(pick, q_ref[step], preferred_element_type=jnp.float32)
        new_sorted += jnp.dot(pick, new_ref[step], preferred_element_type=jnp.float32)
    both = jnp.concatenate([q_sorted, new_sorted], axis=1)
    half = both.shape[1] // 2
    for distance in range(SPAN):
        part = both[distance * rows:(distance + 1) * rows]
        part = jnp.concatenate([part[:, :half], part[:, half:]], axis=0).astype(jnp.bfloat16)
        if distance == 0:
            q_recv[0] = part
        else:
            q_send[distance] = part

    pl.semaphore_wait(barrier, SPAN - 1 + mine)
    for other in range(1, shards):
        @pl.when(mine >= other)
        def _(other=other):
            pl.semaphore_signal(here_sem, inc=1, device_id={"tensor": mine - other}, device_id_type=MESH)

    q_copies = []
    for distance in range(1, SPAN):
        copy = pltpu.make_async_remote_copy(
            src_ref=q_send.at[distance], dst_ref=q_recv.at[distance],
            send_sem=qs_sem.at[distance], recv_sem=qr_sem.at[distance],
            device_id={"dp": peer(distance)}, device_id_type=MESH,
        )
        copy.start()
        q_copies.append(copy)

    pool_copy.wait()
    w_copies = []
    for block in range(shards):
        copy = pltpu.make_async_copy(w_ref.at[:, pl.ds(block * wide, wide)], w_v.at[block], w_sem.at[block])
        copy.start()
        w_copies.append(copy)
    served = {}
    for distance in range(SPAN):
        served[distance] = served_beams(par_ref, me, peer(SPAN - distance))
        for rank in range(MOST):
            lens[distance * MOST + rank] = len_ref[me * BEAMS + served[distance][rank]]

    b_copies, late = [], []
    half = context // 2
    for rank in range(MOST):
        for distance in (2, 1, 3, 0):
            beam = served[distance][rank]

            def put(index, carry, distance=distance, rank=rank, beam=beam):
                at = pl.multiple_of(rank * context + index * PAGE, PAGE)
                stage[distance, pl.ds(at, PAGE), :] = pool_v[table_ref[beam, index]]
                return carry

            lax.fori_loop(0, context // PAGE, put, 0)
            for part in range(2):
                span = pl.ds(rank * context + part * half, half)
                at = (distance * MOST + rank) * 2 + part
                if distance == 0:
                    copy = pltpu.make_async_copy(stage.at[0, span], recv_ref.at[0, span], bs_sem.at[at])
                else:
                    copy = pltpu.make_async_remote_copy(
                        src_ref=stage.at[distance, span], dst_ref=recv_ref.at[distance, span],
                        send_sem=bs_sem.at[at], recv_sem=br_sem.at[at],
                        device_id={"dp": peer(SPAN - distance)}, device_id_type=MESH,
                    )
                b_copies.append(copy)
                if distance > 0 and rank == MOST - 1 and part == 1:
                    late.append(copy)
                else:
                    copy.start()

    for copy in q_copies:
        copy.wait()

    def attend(distance, carry):
        message = q_recv[distance].astype(jnp.float32)
        message = jnp.concatenate([message[:rows], message[rows:]], axis=1)
        q_rows = jnp.concatenate([message[:, h * HD:(h + 1) * HD] for h in range(heads)], axis=0).astype(jnp.bfloat16)
        fresh = message[:, wide:].astype(jnp.bfloat16)
        old_len = lens[distance * MOST]
        last_len = lens[distance * MOST + 1]
        contract = (((1,), (1,)), ((), ()))
        scale = HD ** -0.5
        scores = lax.dot_general(q_rows, stage[distance, :, 0:HD], contract, preferred_element_type=jnp.float32) * scale
        fresh_scores = lax.dot_general(q_rows, fresh[:, :HD], contract, preferred_element_type=jnp.float32) * scale
        rank_at = lax.broadcasted_iota(jnp.int32, scores.shape, 0) // STEPS % MOST
        position = lax.broadcasted_iota(jnp.int32, scores.shape, 1) - rank_at * context
        limit = jnp.where(rank_at == 0, old_len, last_len)
        scores = jnp.where((position >= 0) & (position < limit), scores, -1e30)
        f_row = lax.broadcasted_iota(jnp.int32, fresh_scores.shape, 0)
        f_col = lax.broadcasted_iota(jnp.int32, fresh_scores.shape, 1)
        seen = (f_row // STEPS % MOST == f_col // STEPS) & (f_col % STEPS <= f_row % STEPS)
        fresh_scores = jnp.where(seen, fresh_scores, -1e30)
        top = jnp.maximum(jnp.max(scores, axis=1, keepdims=True), jnp.max(fresh_scores, axis=1, keepdims=True))
        exp_old = jnp.exp(scores - top)
        exp_new = jnp.exp(fresh_scores - top)
        total = jnp.sum(exp_old, axis=1, keepdims=True) + jnp.sum(exp_new, axis=1, keepdims=True)
        w_old = (exp_old / total).astype(jnp.bfloat16)
        w_new = (exp_new / total).astype(jnp.bfloat16)
        out = jnp.dot(w_old, stage[distance, :, HD:2 * HD], preferred_element_type=jnp.float32)
        out += jnp.dot(w_new, fresh[:, HD:], preferred_element_type=jnp.float32)
        out = jnp.concatenate([out[h * rows:(h + 1) * rows] for h in range(heads)], axis=1)
        att[pl.ds(pl.multiple_of(distance * rows, rows), rows), :] = out
        return carry

    lax.fori_loop(0, SPAN, attend, 0)
    attended = att[...].astype(jnp.bfloat16)
    for copy in w_copies:
        copy.wait()

    def p_copy(other):
        return pltpu.make_async_remote_copy(
            src_ref=p_send.at[other], dst_ref=p_recv.at[other],
            send_sem=ps_sem.at[other], recv_sem=pr_sem.at[other],
            device_id={"tensor": lax.rem(mine + other, shards)}, device_id_type=MESH,
        )

    def project(other, carry):
        product = jnp.dot(attended, w_v[lax.rem(mine + other, shards)], preferred_element_type=jnp.float32)
        p_send[other] = product.astype(jnp.bfloat16)
        p_copy(other).start()
        return carry

    @pl.when(mine < shards - 1)
    def _():
        pl.semaphore_wait(here_sem, shards - 1 - mine)

    lax.fori_loop(1, shards, project, 0)
    own = jnp.dot(attended, w_v[mine], preferred_element_type=jnp.float32)

    def gather_sums(other, total):
        p_copy(other).wait()
        return total + p_recv[other].astype(jnp.float32)

    summed = lax.fori_loop(1, shards, gather_sums, own)
    half = wide // 2
    r_copies = []
    for distance in range(SPAN):
        part = summed[distance * rows:(distance + 1) * rows]
        r_send[distance] = jnp.concatenate([part[:, :half], part[:, half:]], axis=0).astype(jnp.bfloat16)
        if distance == 0:
            copy = pltpu.make_async_copy(r_send.at[0], proj_ref.at[0], own_sem)
        else:
            copy = pltpu.make_async_remote_copy(
                src_ref=r_send.at[distance], dst_ref=proj_ref.at[distance],
                send_sem=rs_sem.at[distance], recv_sem=rr_sem.at[distance],
                device_id={"dp": peer(SPAN - distance)}, device_id_type=MESH,
            )
        copy.start()
        r_copies.append(copy)
    for copy in late:
        copy.start()
    for copy in r_copies:
        copy.wait()
    for copy in b_copies:
        copy.wait()


def finish_kernel(recv_ref, raw_ref, new_hbm, len_hbm, par_hbm, proj_ref, cache_ref, new_ref, len_ref, par_ref, edge, zeros, in_sem, out_sem):
    me = lax.axis_index("dp")
    pages = recv_ref.shape[1] // PAGE
    operands = ((par_hbm, par_ref), (len_hbm, len_ref), (new_hbm, new_ref))
    in_copies = [pltpu.make_async_copy(source, target, in_sem.at[at]) for at, (source, target) in enumerate(operands)]
    for copy in in_copies:
        copy.start()
    zeros[...] = jnp.zeros_like(zeros)
    for copy in in_copies:
        copy.wait()
    slots, owners = slots_of_children(par_ref, me)
    fresh = [new_ref[step].astype(jnp.float32) for step in range(STEPS)]
    for child in range(BEAMS):
        slot = slots[child]
        length = len_ref[owners[child]]
        first = length // PAGE
        last = (length + STEPS - 1) // PAGE

        def whole(index, carry, child=child, slot=slot):
            span = pl.ds(pl.multiple_of(index * PAGE, PAGE), PAGE)
            pltpu.make_async_copy(recv_ref.at[slot, span], cache_ref.at[child, span], out_sem).start()
            return carry

        def clear(index, carry, child=child):
            span = pl.ds(pl.multiple_of(index * PAGE, PAGE), PAGE)
            pltpu.make_async_copy(zeros, cache_ref.at[child, span], out_sem).start()
            return carry

        def fix(index, carry, child=child, slot=slot, length=length, first=first):
            at = pl.multiple_of(index * PAGE, PAGE)
            position = at + lax.broadcasted_iota(jnp.int32, (PAGE, 2 * HD), 0)
            page = recv_ref[slot, pl.ds(at, PAGE), :].astype(jnp.float32)
            page = jnp.where(position < length, page, 0.0)
            for step in range(STEPS):
                page = jnp.where(position == length + step, fresh[step][child:child + 1], page)
            edge[child * 2 + index - first] = page.astype(jnp.bfloat16)
            pltpu.make_async_copy(edge.at[child * 2 + index - first], cache_ref.at[child, pl.ds(at, PAGE)], out_sem).start()
            return carry

        lax.fori_loop(0, first, whole, 0)
        lax.fori_loop(last + 1, pages, clear, 0)
        lax.fori_loop(first, last + 1, fix, 0)

    rows = MOST * STEPS
    raw = []
    for distance in range(SPAN):
        part = raw_ref[distance].astype(jnp.float32)
        raw.append(jnp.concatenate([part[:rows], part[rows:]], axis=1))
    raw = jnp.concatenate(raw, axis=0).astype(jnp.bfloat16)
    row = lax.broadcasted_iota(jnp.int32, (BEAMS, SPAN * rows), 0)
    col = lax.broadcasted_iota(jnp.int32, (BEAMS, SPAN * rows), 1)
    slot_at = jnp.zeros_like(col)
    for child in range(BEAMS):
        slot_at = jnp.where(row == child, slots[child], slot_at)
    for step in range(STEPS):
        pick = jnp.where(col == slot_at * STEPS + step, 1.0, 0.0).astype(jnp.bfloat16)
        proj_ref[step] = jnp.dot(pick, raw, preferred_element_type=jnp.float32).astype(jnp.bfloat16)
    pltpu.make_async_copy(recv_ref, cache_ref, out_sem).wait()


def local(shards, queries, new_kv, kv_pool, page_tables, lengths, parents, out_weight):
    wide = queries.shape[2]
    channels = kv_pool.shape[2]
    context = page_tables.shape[1] * kv_pool.shape[1]
    rows = MOST * STEPS
    vmem = pl.BlockSpec(memory_space=pltpu.VMEM)
    hbm = pl.BlockSpec(memory_space=pltpu.HBM)
    free = pl.BlockSpec(memory_space=pl.ANY)
    dma = pltpu.SemaphoreType.DMA
    bf16 = jnp.bfloat16
    with jax.named_scope("exchange"):
        recv, raw = pl.pallas_call(
            exchange_kernel,
            out_shape=(
                jax.ShapeDtypeStruct((SPAN, MOST * context, channels), bf16),
                jax.ShapeDtypeStruct((SPAN, 2 * rows, wide // 2), bf16),
            ),
            in_specs=[hbm] * 7,
            out_specs=(free, free),
            scratch_shapes=[
                pltpu.VMEM(queries.shape, bf16),
                pltpu.VMEM(new_kv.shape, bf16),
                pltpu.SMEM(page_tables.shape, jnp.int32),
                pltpu.SMEM(lengths.shape, jnp.int32),
                pltpu.SMEM(parents.shape, jnp.int32),
                pltpu.VMEM(kv_pool.shape, bf16),
                pltpu.VMEM((shards, out_weight.shape[0], wide), bf16),
                pltpu.VMEM((SPAN, MOST * context, channels), bf16),
                pltpu.VMEM((SPAN, 2 * rows, (wide + channels) // 2), bf16),
                pltpu.VMEM((SPAN, 2 * rows, (wide + channels) // 2), bf16),
                pltpu.VMEM((SPAN * rows, wide), jnp.float32),
                pltpu.VMEM((shards, SPAN * rows, wide), bf16),
                pltpu.VMEM((shards, SPAN * rows, wide), bf16),
                pltpu.VMEM((SPAN, 2 * rows, wide // 2), bf16),
                pltpu.SMEM((SPAN * MOST,), jnp.int32),
                dma((5,)), dma, dma((shards,)), dma,
                dma((SPAN,)), dma((SPAN,)),
                dma((SPAN * MOST * 2,)), dma((SPAN * MOST * 2,)),
                dma((shards,)), dma((shards,)),
                dma((SPAN,)), dma((SPAN,)),
                pltpu.SemaphoreType.REGULAR,
            ],
            compiler_params=pltpu.CompilerParams(
                collective_id=0, has_side_effects=True, vmem_limit_bytes=48 * 1024 * 1024
            ),
            name="exchange",
        )(*(
            pltpu.with_memory_space_constraint(operand, pltpu.HBM)
            for operand in (queries, new_kv, kv_pool, page_tables, lengths, parents, out_weight)
        ))
    with jax.named_scope("finish"):
        return pl.pallas_call(
            finish_kernel,
            out_shape=(
                jax.ShapeDtypeStruct(queries.shape, bf16),
                jax.ShapeDtypeStruct((BEAMS, context, channels), bf16),
            ),
            in_specs=[vmem, vmem, hbm, hbm, hbm],
            out_specs=(vmem, hbm),
            scratch_shapes=[
                pltpu.VMEM(new_kv.shape, bf16),
                pltpu.SMEM(lengths.shape, jnp.int32),
                pltpu.SMEM(parents.shape, jnp.int32),
                pltpu.VMEM((2 * BEAMS, PAGE, channels), bf16),
                pltpu.VMEM((PAGE, channels), bf16),
                dma((3,)), dma,
            ],
            compiler_params=pltpu.CompilerParams(vmem_limit_bytes=24 * 1024 * 1024),
            name="finish",
        )(recv.reshape(BEAMS, context, channels), raw, new_kv, lengths, parents)


def solution(mesh):
    in_specs = (
        P(None, "dp", "tensor"),
        P(None, "dp", "tensor"),
        P("dp", None, "tensor"),
        P("dp", None),
        P(),
        P(),
        P("tensor", None),
    )
    out_specs = (P(None, "dp", "tensor"), P("dp", None, "tensor"))
    body = functools.partial(local, mesh.shape["tensor"])
    return jax.shard_map(body, mesh=mesh, in_specs=in_specs, out_specs=out_specs, check_vma=False)
```

```python
import functools

import jax
import jax.numpy as jnp
from jax import lax
from jax.experimental import pallas as pl
from jax.experimental.pallas import tpu as pltpu
from jax.sharding import PartitionSpec as P

HD = 128
SPAN = 4
MOST = 2
BEAMS = 8
STEPS = 4
PAGE = 128
GRAIN = 64
PER_CHILD = 16
VIA = 20
MORE = 8
REST = 25
FIRST = VIA + MORE
LINK = FIRST + REST
MESH = pl.DeviceIdType.MESH


def grains(length):
    return (length + (GRAIN - 1)) >> 6


def choose(values, index):
    out = values[0]
    for at in range(1, len(values)):
        out = jnp.where(index == at, values[at], out)
    return out


def ring_plan(parents, lengths, ring):
    flows = [[jnp.int32(0)] * SPAN for _ in range(SPAN)]
    for target in range(SPAN):
        seen = []
        for child in range(BEAMS):
            parent = parents[(ring * SPAN + target) * BEAMS + child]
            count = grains(lengths[parent])
            for other in seen:
                count = jnp.where(parent == other, 0, count)
            seen.append(parent)
            source = (parent >> 3) & (SPAN - 1)
            for at in range(SPAN):
                if at != target:
                    ahead = (target - at) % SPAN
                    flows[at][ahead] = flows[at][ahead] + jnp.where(source == at, count, 0)
    up = [flow[1] for flow in flows]
    far = [flow[2] for flow in flows]
    down = [flow[3] for flow in flows]
    via_up = [jnp.minimum(count >> 1, VIA) for count in far]
    for at in range(SPAN):
        via_down = [far[i] - via_up[i] for i in range(SPAN)]
        nxt, prv = (at + 1) % SPAN, (at - 1) % SPAN
        load_up = jnp.maximum(up[at] + via_up[prv], up[nxt] + via_up[nxt])
        load_down = jnp.maximum(down[at] + via_down[nxt], down[prv] + via_down[prv])
        best = (load_down + far[at] - load_up) >> 1
        via_up[at] = jnp.minimum(jnp.maximum(best, jnp.maximum(far[at] - VIA, 0)), jnp.minimum(far[at], VIA))
    via_down = [far[i] - via_up[i] for i in range(SPAN)]
    return up, down, via_up, via_down


def overfull(plan):
    up, down, via_up, via_down = plan
    out = jnp.int32(0)
    for at in range(SPAN):
        load_up = up[at] + via_up[at] + via_up[(at - 1) % SPAN]
        load_down = down[at] + via_down[at] + via_down[(at + 1) % SPAN]
        out = jnp.maximum(out, jnp.where(jnp.maximum(load_up, load_down) > LINK, 1, 0))
    return out


def slots_of_children(parents, me):
    taken = [jnp.int32(0) for _ in range(SPAN)]
    slots, owners = [], []
    for child in range(BEAMS):
        parent = parents[me * BEAMS + child]
        apart = jnp.bitwise_and(parent // BEAMS - me, SPAN - 1)
        slot = jnp.int32(0)
        for distance in range(SPAN):
            hit = apart == distance
            slot = jnp.where(hit, distance * MOST + taken[distance], slot)
            taken[distance] = taken[distance] + hit.astype(jnp.int32)
        slots.append(slot)
        owners.append(parent)
    return slots, owners


def served_beams(parents, me, target):
    count = jnp.int32(0)
    beams = [jnp.int32(0) for _ in range(MOST)]
    for child in range(BEAMS):
        parent = parents[target * BEAMS + child]
        hit = parent // BEAMS == me
        for rank in range(MOST):
            beams[rank] = jnp.where(hit & (count == rank), parent % BEAMS, beams[rank])
        count = count + hit.astype(jnp.int32)
    return beams


def exchange_kernel(
    q_hbm, new_hbm, pool_ref, table_hbm, len_hbm, par_hbm, w_ref,
    recv_ref, proj_ref, meta_ref, over_ref,
    q_ref, new_ref, table_ref, len_ref, par_ref,
    pool_v, w_v, stage, first_send, first_recv, rest_send, q_send, q_recv, att, p_send, p_recv, r_send, lens, beams,
    in_sem, pool_sem, w_sem, own_sem, land_sem, qs_sem, qr_sem, bs_sem, br_sem, ps_sem, pr_sem, rs_sem, rr_sem, here_sem,
):
    me = lax.axis_index("dp")
    mine = lax.axis_index("tensor")
    shards = lax.axis_size("tensor")
    y = lax.rem(me, SPAN)
    base = me - y
    context = stage.shape[1] * GRAIN // MOST
    rings = lax.axis_size("dp") // SPAN
    wide = q_hbm.shape[2]
    heads = wide // HD
    rows = MOST * STEPS

    def peer(distance):
        return base + lax.rem(y + distance, SPAN)

    barrier = pltpu.get_barrier_semaphore()
    for distance in range(1, SPAN):
        pl.semaphore_signal(barrier, inc=1, device_id={"dp": peer(distance)}, device_id_type=MESH)
    for other in range(1, shards):
        @pl.when(mine + other < shards)
        def _(other=other):
            pl.semaphore_signal(barrier, inc=1, device_id={"tensor": mine + other}, device_id_type=MESH)
    in_copies = []
    operands = ((par_hbm, par_ref), (q_hbm, q_ref), (new_hbm, new_ref), (table_hbm, table_ref), (len_hbm, len_ref))
    for at, (source, target) in enumerate(operands):
        copy = pltpu.make_async_copy(source, target, in_sem.at[at])
        copy.start()
        in_copies.append(copy)
    pool_copy = pltpu.make_async_copy(pool_ref, pool_v, pool_sem)
    pool_copy.start()
    for copy in in_copies:
        copy.wait()

    slots, owners = slots_of_children(par_ref, me)
    plan = ring_plan(par_ref, len_ref, me >> 2)
    up, down, via_up, via_down = plan
    row = lax.broadcasted_iota(jnp.int32, (SPAN * rows, BEAMS), 0)
    col = lax.broadcasted_iota(jnp.int32, (SPAN * rows, BEAMS), 1)
    slot_at = jnp.zeros_like(col)
    for child in range(BEAMS):
        slot_at = jnp.where(col == child, slots[child], slot_at)
    q_sorted = jnp.zeros((SPAN * rows, wide), jnp.float32)
    new_sorted = jnp.zeros((SPAN * rows, 2 * HD), jnp.float32)
    for step in range(STEPS):
        pick = jnp.where((row // STEPS == slot_at) & (row % STEPS == step), 1.0, 0.0).astype(jnp.bfloat16)
        q_sorted += jnp.dot(pick, q_ref[step], preferred_element_type=jnp.float32)
        new_sorted += jnp.dot(pick, new_ref[step], preferred_element_type=jnp.float32)
    both = jnp.concatenate([q_sorted, new_sorted], axis=1)
    half = both.shape[1] // 2
    for distance in range(SPAN):
        part = both[distance * rows:(distance + 1) * rows]
        part = jnp.concatenate([part[:, :half], part[:, half:]], axis=0).astype(jnp.bfloat16)
        if distance == 0:
            q_recv[0] = part
        else:
            q_send[distance] = part

    pl.semaphore_wait(barrier, SPAN - 1 + mine)
    for other in range(1, shards):
        @pl.when(mine >= other)
        def _(other=other):
            pl.semaphore_signal(here_sem, inc=1, device_id={"tensor": mine - other}, device_id_type=MESH)

    q_copies = []
    for distance in range(1, SPAN):
        copy = pltpu.make_async_remote_copy(
            src_ref=q_send.at[distance], dst_ref=q_recv.at[distance],
            send_sem=qs_sem.at[distance], recv_sem=qr_sem.at[distance],
            device_id={"dp": peer(distance)}, device_id_type=MESH,
        )
        copy.start()
        q_copies.append(copy)

    flows = {}
    for ahead in range(SPAN):
        served = served_beams(par_ref, me, peer(ahead))
        distance = (SPAN - ahead) % SPAN
        held = [len_ref[me * BEAMS + served[rank]] for rank in range(MOST)]
        for rank in range(MOST):
            beams[distance * MOST + rank] = served[rank]
            lens[distance * MOST + rank] = held[rank]
        flows[ahead] = (served[0], served[1], grains(held[0]))

    def grain_at(flow, number):
        first, second, cut = flow
        later = number >= cut
        number = jnp.where(later, number - cut, number)
        number = jnp.minimum(jnp.maximum(number, 0), PER_CHILD - 1)
        return table_ref[jnp.where(later, second, first), number >> 1] * 2 + (number & 1)

    sides = (
        (flows[1], choose(via_up, y), jnp.int32(0), choose(via_up, (y - 1) & 3), peer(1)),
        (flows[3], choose(via_down, y), choose(via_up, y), choose(via_down, (y + 1) & 3), peer(3)),
    )
    pool_copy.wait()
    b_copies = []
    cuts = (0, VIA // 2, VIA, FIRST)
    for part in range(3):
        for side, (flow, mine_via, skip, _, target) in enumerate(sides):
            def put(at, carry, side=side, flow=flow, mine_via=mine_via, skip=skip):
                far = at < mine_via
                chosen = tuple(jnp.where(far, one, two) for one, two in zip(flows[2], flow))
                number = jnp.where(far, skip + at, at - mine_via)
                first_send[side, at] = pool_v[grain_at(chosen, number)]
                return carry

            lax.fori_loop(cuts[part], cuts[part + 1], put, 0)
            span = pl.ds(cuts[part], cuts[part + 1] - cuts[part])
            copy = pltpu.make_async_remote_copy(
                src_ref=first_send.at[side, span], dst_ref=first_recv.at[side, span],
                send_sem=bs_sem.at[side * 4 + part], recv_sem=br_sem.at[side * 4 + part],
                device_id={"dp": target}, device_id_type=MESH,
            )
            copy.start()
            b_copies.append(copy)
    w_copies = []
    for block in range(shards):
        copy = pltpu.make_async_copy(w_ref.at[:, pl.ds(block * wide, wide)], w_v.at[block], w_sem.at[block])
        copy.start()
        w_copies.append(copy)

    def put_all(index, carry):
        slot = index >> 4
        number = index & (PER_CHILD - 1)
        grain = table_ref[beams[slot], number >> 1] * 2 + (number & 1)
        stage[index >> 5, index & (MOST * PER_CHILD - 1)] = pool_v[grain]
        return carry

    lax.fori_loop(0, SPAN * MOST * PER_CHILD, put_all, 0)
    own_copy = pltpu.make_async_copy(stage.at[0], recv_ref.at[pl.ds(2 * LINK, MOST * PER_CHILD)], own_sem.at[0])
    own_copy.start()

    for copy in q_copies:
        copy.wait()

    def attend(distance, carry):
        message = q_recv[distance].astype(jnp.float32)
        message = jnp.concatenate([message[:rows], message[rows:]], axis=1)
        q_rows = jnp.concatenate([message[:, h * HD:(h + 1) * HD] for h in range(heads)], axis=0).astype(jnp.bfloat16)
        fresh = message[:, wide:].astype(jnp.bfloat16)
        old_len = lens[distance * MOST]
        last_len = lens[distance * MOST + 1]
        contract = (((1,), (1,)), ((), ()))
        scale = HD ** -0.5
        scores = lax.dot_general(q_rows, stage[distance, :, :, 0:HD].reshape(MOST * context, HD), contract, preferred_element_type=jnp.float32) * scale
        fresh_scores = lax.dot_general(q_rows, fresh[:, :HD], contract, preferred_element_type=jnp.float32) * scale
        rank_at = lax.broadcasted_iota(jnp.int32, scores.shape, 0) // STEPS % MOST
        position = lax.broadcasted_iota(jnp.int32, scores.shape, 1) - rank_at * context
        limit = jnp.where(rank_at == 0, old_len, last_len)
        scores = jnp.where((position >= 0) & (position < limit), scores, -1e30)
        f_row = lax.broadcasted_iota(jnp.int32, fresh_scores.shape, 0)
        f_col = lax.broadcasted_iota(jnp.int32, fresh_scores.shape, 1)
        seen = (f_row // STEPS % MOST == f_col // STEPS) & (f_col % STEPS <= f_row % STEPS)
        fresh_scores = jnp.where(seen, fresh_scores, -1e30)
        top = jnp.maximum(jnp.max(scores, axis=1, keepdims=True), jnp.max(fresh_scores, axis=1, keepdims=True))
        exp_old = jnp.exp(scores - top)
        exp_new = jnp.exp(fresh_scores - top)
        total = jnp.sum(exp_old, axis=1, keepdims=True) + jnp.sum(exp_new, axis=1, keepdims=True)
        w_old = (exp_old / total).astype(jnp.bfloat16)
        w_new = (exp_new / total).astype(jnp.bfloat16)
        out = jnp.dot(w_old, stage[distance, :, :, HD:2 * HD].reshape(MOST * context, HD), preferred_element_type=jnp.float32)
        out += jnp.dot(w_new, fresh[:, HD:], preferred_element_type=jnp.float32)
        out = jnp.concatenate([out[h * rows:(h + 1) * rows] for h in range(heads)], axis=1)
        att[pl.ds(pl.multiple_of(distance * rows, rows), rows), :] = out
        return carry

    lax.fori_loop(0, SPAN, attend, 0)
    for copy in b_copies:
        copy.wait()
    b_copies = []
    for side, (flow, mine_via, _, passed, target) in enumerate(sides):
        copy = pltpu.make_async_copy(first_recv.at[side], recv_ref.at[pl.ds(side * LINK, FIRST)], land_sem.at[side])
        copy.start()
        b_copies.append(copy)

        def put_rest(at, carry, side=side, flow=flow, mine_via=mine_via, passed=passed):
            number = FIRST - mine_via + at - passed
            here = pool_v[grain_at(flow, number)]
            rest_send[side, at] = jnp.where(at < passed, first_recv[side, jnp.minimum(at, VIA - 1)], here)
            return carry

        lax.fori_loop(0, REST, put_rest, 0)
        copy = pltpu.make_async_remote_copy(
            src_ref=rest_send.at[side], dst_ref=recv_ref.at[pl.ds(side * LINK + FIRST, REST)],
            send_sem=bs_sem.at[side * 4 + 3], recv_sem=br_sem.at[side * 4 + 3],
            device_id={"dp": target}, device_id_type=MESH,
        )
        copy.start()
        b_copies.append(copy)
    attended = att[...].astype(jnp.bfloat16)
    for copy in w_copies:
        copy.wait()

    def p_copy(other):
        return pltpu.make_async_remote_copy(
            src_ref=p_send.at[other], dst_ref=p_recv.at[other],
            send_sem=ps_sem.at[other], recv_sem=pr_sem.at[other],
            device_id={"tensor": lax.rem(mine + other, shards)}, device_id_type=MESH,
        )

    def project(other, carry):
        product = jnp.dot(attended, w_v[lax.rem(mine + other, shards)], preferred_element_type=jnp.float32)
        p_send[other] = product.astype(jnp.bfloat16)
        p_copy(other).start()
        return carry

    @pl.when(mine < shards - 1)
    def _():
        pl.semaphore_wait(here_sem, shards - 1 - mine)

    lax.fori_loop(1, shards, project, 0)
    own = jnp.dot(attended, w_v[mine], preferred_element_type=jnp.float32)

    def gather_sums(other, total):
        p_copy(other).wait()
        return total + p_recv[other].astype(jnp.float32)

    summed = lax.fori_loop(1, shards, gather_sums, own)
    half = wide // 2
    r_copies = []
    for distance in range(SPAN):
        part = summed[distance * rows:(distance + 1) * rows]
        r_send[distance] = jnp.concatenate([part[:, :half], part[:, half:]], axis=0).astype(jnp.bfloat16)
        if distance == 0:
            copy = pltpu.make_async_copy(r_send.at[0], proj_ref.at[0], own_sem.at[1])
        else:
            copy = pltpu.make_async_remote_copy(
                src_ref=r_send.at[distance], dst_ref=proj_ref.at[distance],
                send_sem=rs_sem.at[distance], recv_sem=rr_sem.at[distance],
                device_id={"dp": peer(SPAN - distance)}, device_id_type=MESH,
            )
        copy.start()
        r_copies.append(copy)

    over_ref[0] = lax.fori_loop(
        0, rings, lambda ring, over: jnp.maximum(over, overfull(ring_plan(par_ref, len_ref, ring))), jnp.int32(0)
    )
    for child in range(BEAMS):
        slot = slots[child]
        distance = slot >> 1
        length = len_ref[owners[child]]
        count = grains(length)
        before = jnp.int32(0)
        for other in range(BEAMS):
            if other != child:
                mate = (slots[other] >> 1 == distance) & (slots[other] < slot)
                differs = owners[other] != owners[child]
                before = jnp.where(mate & differs, grains(len_ref[owners[other]]), before)
        from_up = choose(via_up, (y - 1) & 3), choose(via_up, (y + 2) & 3)
        from_down = choose(via_down, (y + 1) & 3), choose(via_down, (y + 2) & 3)
        near_via = jnp.where(distance == 3, from_up[0], from_down[0])
        near_pass = jnp.where(distance == 3, from_up[1], from_down[1])
        near_base = jnp.where(distance == 3, 0, LINK)
        split = jnp.where(distance == 2, from_up[1], FIRST - near_via) - before
        split = jnp.minimum(jnp.maximum(split, 0), PER_CHILD)
        start = jnp.where(distance == 2, FIRST + before, near_base + near_via + before)
        again = jnp.where(distance == 2, LINK + FIRST + before + split - from_up[1], start + split + near_pass)
        own = distance == 0
        meta_ref[child * 4] = length
        meta_ref[child * 4 + 1] = jnp.where(own, 2 * LINK + (slot & 1) * PER_CHILD, start)
        meta_ref[child * 4 + 2] = jnp.where(own, PER_CHILD, split)
        meta_ref[child * 4 + 3] = jnp.where(own, 0, again)
        meta_ref[BEAMS * 4 + child] = slot
    for copy in r_copies:
        copy.wait()
    for copy in b_copies:
        copy.wait()
    own_copy.wait()


def full_kernel(
    pool_ref, table_hbm, par_hbm, recv_ref,
    table_ref, par_ref, pool_v, stage,
    in_sem, pool_sem, own_sem, bs_sem, br_sem,
):
    me = lax.axis_index("dp")
    y = lax.rem(me, SPAN)
    base = me - y
    context = stage.shape[1] // MOST

    def peer(distance):
        return base + lax.rem(y + distance, SPAN)

    barrier = pltpu.get_barrier_semaphore()
    for distance in range(1, SPAN):
        pl.semaphore_signal(barrier, inc=1, device_id={"dp": peer(distance)}, device_id_type=MESH)
    in_copies = []
    for at, (source, target) in enumerate(((par_hbm, par_ref), (table_hbm, table_ref))):
        copy = pltpu.make_async_copy(source, target, in_sem.at[at])
        copy.start()
        in_copies.append(copy)
    pool_copy = pltpu.make_async_copy(pool_ref, pool_v, pool_sem)
    pool_copy.start()
    for copy in in_copies:
        copy.wait()
    pl.semaphore_wait(barrier, SPAN - 1)
    pool_copy.wait()
    copies = []
    for distance in (2, 1, 3, 0):
        served = served_beams(par_ref, me, peer(SPAN - distance))
        for rank in range(MOST):
            beam = served[rank]

            def put(index, carry, distance=distance, rank=rank, beam=beam):
                at = pl.multiple_of(rank * context + index * PAGE, PAGE)
                stage[distance, pl.ds(at, PAGE), :] = pool_v[table_ref[beam, index]]
                return carry

            lax.fori_loop(0, context // PAGE, put, 0)
            span = pl.ds(rank * context, context)
            if distance == 0:
                copy = pltpu.make_async_copy(stage.at[0, span], recv_ref.at[0, span], own_sem.at[rank])
            else:
                copy = pltpu.make_async_remote_copy(
                    src_ref=stage.at[distance, span], dst_ref=recv_ref.at[distance, span],
                    send_sem=bs_sem.at[distance * MOST + rank], recv_sem=br_sem.at[distance * MOST + rank],
                    device_id={"dp": peer(SPAN - distance)}, device_id_type=MESH,
                )
            copy.start()
            copies.append(copy)
    for copy in copies:
        copy.wait()


def finish_kernel(recv_ref, raw_ref, new_hbm, len_hbm, par_hbm, proj_ref, cache_ref, new_ref, len_ref, par_ref, edge, zeros, in_sem, out_sem):
    me = lax.axis_index("dp")
    pages = recv_ref.shape[1] // PAGE
    operands = ((par_hbm, par_ref), (len_hbm, len_ref), (new_hbm, new_ref))
    in_copies = [pltpu.make_async_copy(source, target, in_sem.at[at]) for at, (source, target) in enumerate(operands)]
    for copy in in_copies:
        copy.start()
    zeros[...] = jnp.zeros_like(zeros)
    for copy in in_copies:
        copy.wait()
    slots, owners = slots_of_children(par_ref, me)
    fresh = [new_ref[step].astype(jnp.float32) for step in range(STEPS)]
    for child in range(BEAMS):
        slot = slots[child]
        length = len_ref[owners[child]]
        first = length // PAGE
        last = (length + STEPS - 1) // PAGE

        def whole(index, carry, child=child, slot=slot):
            span = pl.ds(pl.multiple_of(index * PAGE, PAGE), PAGE)
            pltpu.make_async_copy(recv_ref.at[slot, span], cache_ref.at[child, span], out_sem).start()
            return carry

        def clear(index, carry, child=child):
            span = pl.ds(pl.multiple_of(index * PAGE, PAGE), PAGE)
            pltpu.make_async_copy(zeros, cache_ref.at[child, span], out_sem).start()
            return carry

        def fix(index, carry, child=child, slot=slot, length=length, first=first):
            at = pl.multiple_of(index * PAGE, PAGE)
            position = at + lax.broadcasted_iota(jnp.int32, (PAGE, 2 * HD), 0)
            page = recv_ref[slot, pl.ds(at, PAGE), :].astype(jnp.float32)
            page = jnp.where(position < length, page, 0.0)
            for step in range(STEPS):
                page = jnp.where(position == length + step, fresh[step][child:child + 1], page)
            edge[child * 2 + index - first] = page.astype(jnp.bfloat16)
            pltpu.make_async_copy(edge.at[child * 2 + index - first], cache_ref.at[child, pl.ds(at, PAGE)], out_sem).start()
            return carry

        lax.fori_loop(0, first, whole, 0)
        lax.fori_loop(last + 1, pages, clear, 0)
        lax.fori_loop(first, last + 1, fix, 0)

    rows = MOST * STEPS
    raw = []
    for distance in range(SPAN):
        part = raw_ref[distance].astype(jnp.float32)
        raw.append(jnp.concatenate([part[:rows], part[rows:]], axis=1))
    raw = jnp.concatenate(raw, axis=0).astype(jnp.bfloat16)
    row = lax.broadcasted_iota(jnp.int32, (BEAMS, SPAN * rows), 0)
    col = lax.broadcasted_iota(jnp.int32, (BEAMS, SPAN * rows), 1)
    slot_at = jnp.zeros_like(col)
    for child in range(BEAMS):
        slot_at = jnp.where(row == child, slots[child], slot_at)
    for step in range(STEPS):
        pick = jnp.where(col == slot_at * STEPS + step, 1.0, 0.0).astype(jnp.bfloat16)
        proj_ref[step] = jnp.dot(pick, raw, preferred_element_type=jnp.float32).astype(jnp.bfloat16)
    pltpu.make_async_copy(recv_ref, cache_ref, out_sem).wait()


def place_kernel(recv_ref, raw_ref, new_ref, meta_ref, proj_ref, cache_ref, edge, zeros, out_sem):
    total = recv_ref.shape[0]
    zeros[...] = jnp.zeros_like(zeros)
    fresh = [new_ref[step].astype(jnp.float32) for step in range(STEPS)]
    slots = [meta_ref[BEAMS * 4 + child] for child in range(BEAMS)]
    for child in range(BEAMS):
        length, start, split, again = (meta_ref[child * 4 + at] for at in range(4))
        first = length >> 6
        last = (length + STEPS - 1) >> 6
        split = jnp.minimum(split, first)

        def move(source, source_at, at, count, child=child):
            @pl.when(count > 0)
            def _():
                pltpu.make_async_copy(
                    source.at[pl.ds(source_at, count)], cache_ref.at[child, pl.ds(at, count)], out_sem
                ).start()

        move(recv_ref, start, 0, split)
        move(recv_ref, again, split, first - split)
        move(zeros, 0, last + 1, PER_CHILD - 1 - last)

        def fix(index, carry, child=child, length=length, first=first, start=start, again=again, whole=meta_ref[child * 4 + 2]):
            position = index * GRAIN + lax.broadcasted_iota(jnp.int32, (GRAIN, 2 * HD), 0)
            at = jnp.minimum(jnp.where(index < whole, start + index, again + index - whole), total - 1)
            page = jnp.where(position < length, recv_ref[at].astype(jnp.float32), 0.0)
            for step in range(STEPS):
                page = jnp.where(position == length + step, fresh[step][child:child + 1], page)
            edge[child * 2 + index - first] = page.astype(jnp.bfloat16)
            pltpu.make_async_copy(edge.at[child * 2 + index - first], cache_ref.at[child, index], out_sem).start()
            return carry

        lax.fori_loop(first, last + 1, fix, 0)

    rows = MOST * STEPS
    raw = []
    for distance in range(SPAN):
        part = raw_ref[distance].astype(jnp.float32)
        raw.append(jnp.concatenate([part[:rows], part[rows:]], axis=1))
    raw = jnp.concatenate(raw, axis=0).astype(jnp.bfloat16)
    row = lax.broadcasted_iota(jnp.int32, (BEAMS, SPAN * rows), 0)
    col = lax.broadcasted_iota(jnp.int32, (BEAMS, SPAN * rows), 1)
    slot_at = jnp.zeros_like(col)
    for child in range(BEAMS):
        slot_at = jnp.where(row == child, slots[child], slot_at)
    for step in range(STEPS):
        pick = jnp.where(col == slot_at * STEPS + step, 1.0, 0.0).astype(jnp.bfloat16)
        proj_ref[step] = jnp.dot(pick, raw, preferred_element_type=jnp.float32).astype(jnp.bfloat16)
    pltpu.make_async_copy(cache_ref, cache_ref, out_sem).wait()


def local(shards, queries, new_kv, kv_pool, page_tables, lengths, parents, out_weight):
    wide = queries.shape[2]
    channels = kv_pool.shape[2]
    context = page_tables.shape[1] * kv_pool.shape[1]
    rows = MOST * STEPS
    vmem = pl.BlockSpec(memory_space=pltpu.VMEM)
    smem = pl.BlockSpec(memory_space=pltpu.SMEM)
    hbm = pl.BlockSpec(memory_space=pltpu.HBM)
    free = pl.BlockSpec(memory_space=pl.ANY)
    dma = pltpu.SemaphoreType.DMA
    bf16 = jnp.bfloat16

    def pinned(*operands):
        return [pltpu.with_memory_space_constraint(operand, pltpu.HBM) for operand in operands]

    grain_pool = kv_pool.reshape(-1, GRAIN, channels)
    with jax.named_scope("exchange"):
        recv, raw, meta, over = pl.pallas_call(
            exchange_kernel,
            out_shape=(
                jax.ShapeDtypeStruct((2 * LINK + MOST * PER_CHILD, GRAIN, channels), bf16),
                jax.ShapeDtypeStruct((SPAN, 2 * rows, wide // 2), bf16),
                jax.ShapeDtypeStruct((BEAMS * 5,), jnp.int32),
                jax.ShapeDtypeStruct((1,), jnp.int32),
            ),
            in_specs=[hbm] * 7,
            out_specs=(free, free, smem, smem),
            scratch_shapes=[
                pltpu.VMEM(queries.shape, bf16),
                pltpu.VMEM(new_kv.shape, bf16),
                pltpu.SMEM(page_tables.shape, jnp.int32),
                pltpu.SMEM(lengths.shape, jnp.int32),
                pltpu.SMEM(parents.shape, jnp.int32),
                pltpu.VMEM(grain_pool.shape, bf16),
                pltpu.VMEM((shards, out_weight.shape[0], wide), bf16),
                pltpu.VMEM((SPAN, MOST * PER_CHILD, GRAIN, channels), bf16),
                pltpu.VMEM((2, FIRST, GRAIN, channels), bf16),
                pltpu.VMEM((2, FIRST, GRAIN, channels), bf16),
                pltpu.VMEM((2, REST, GRAIN, channels), bf16),
                pltpu.VMEM((SPAN, 2 * rows, (wide + channels) // 2), bf16),
                pltpu.VMEM((SPAN, 2 * rows, (wide + channels) // 2), bf16),
                pltpu.VMEM((SPAN * rows, wide), jnp.float32),
                pltpu.VMEM((shards, SPAN * rows, wide), bf16),
                pltpu.VMEM((shards, SPAN * rows, wide), bf16),
                pltpu.VMEM((SPAN, 2 * rows, wide // 2), bf16),
                pltpu.SMEM((SPAN * MOST,), jnp.int32),
                pltpu.SMEM((SPAN * MOST,), jnp.int32),
                dma((5,)), dma, dma((shards,)), dma((2,)), dma((2,)),
                dma((SPAN,)), dma((SPAN,)),
                dma((8,)), dma((8,)),
                dma((shards,)), dma((shards,)),
                dma((SPAN,)), dma((SPAN,)),
                pltpu.SemaphoreType.REGULAR,
            ],
            compiler_params=pltpu.CompilerParams(
                collective_id=0, has_side_effects=True, vmem_limit_bytes=48 * 1024 * 1024
            ),
            name="exchange",
        )(*pinned(queries, new_kv, grain_pool, page_tables, lengths, parents, out_weight))

    def placed():
        with jax.named_scope("place"):
            projected, cache = pl.pallas_call(
                place_kernel,
                out_shape=(
                    jax.ShapeDtypeStruct(queries.shape, bf16),
                    jax.ShapeDtypeStruct((BEAMS, PER_CHILD, GRAIN, channels), bf16),
                ),
                in_specs=[vmem, vmem, vmem, smem],
                out_specs=(vmem, free),
                scratch_shapes=[
                    pltpu.VMEM((2 * BEAMS, GRAIN, channels), bf16),
                    pltpu.VMEM((PER_CHILD, GRAIN, channels), bf16),
                    dma,
                ],
                compiler_params=pltpu.CompilerParams(vmem_limit_bytes=24 * 1024 * 1024),
                name="place",
            )(recv, raw, new_kv, meta)
            return projected, cache.reshape(BEAMS, context, channels)

    def resent():
        with jax.named_scope("full"):
            whole = pl.pallas_call(
                full_kernel,
                out_shape=jax.ShapeDtypeStruct((SPAN, MOST * context, channels), bf16),
                in_specs=[hbm] * 3,
                out_specs=free,
                scratch_shapes=[
                    pltpu.SMEM(page_tables.shape, jnp.int32),
                    pltpu.SMEM(parents.shape, jnp.int32),
                    pltpu.VMEM(kv_pool.shape, bf16),
                    pltpu.VMEM((SPAN, MOST * context, channels), bf16),
                    dma((2,)), dma, dma((MOST,)),
                    dma((SPAN * MOST,)), dma((SPAN * MOST,)),
                ],
                compiler_params=pltpu.CompilerParams(
                    collective_id=1, has_side_effects=True, vmem_limit_bytes=24 * 1024 * 1024
                ),
                name="full",
            )(*pinned(kv_pool, page_tables, parents))
        with jax.named_scope("finish"):
            return pl.pallas_call(
                finish_kernel,
                out_shape=(
                    jax.ShapeDtypeStruct(queries.shape, bf16),
                    jax.ShapeDtypeStruct((BEAMS, context, channels), bf16),
                ),
                in_specs=[vmem, vmem, hbm, hbm, hbm],
                out_specs=(vmem, hbm),
                scratch_shapes=[
                    pltpu.VMEM(new_kv.shape, bf16),
                    pltpu.SMEM(lengths.shape, jnp.int32),
                    pltpu.SMEM(parents.shape, jnp.int32),
                    pltpu.VMEM((2 * BEAMS, PAGE, channels), bf16),
                    pltpu.VMEM((PAGE, channels), bf16),
                    dma((3,)), dma,
                ],
                compiler_params=pltpu.CompilerParams(vmem_limit_bytes=24 * 1024 * 1024),
                name="finish",
            )(whole.reshape(BEAMS, context, channels), raw, new_kv, lengths, parents)

    return lax.cond(over[0] > 0, resent, placed)


def solution(mesh):
    in_specs = (
        P(None, "dp", "tensor"),
        P(None, "dp", "tensor"),
        P("dp", None, "tensor"),
        P("dp", None),
        P(),
        P(),
        P("tensor", None),
    )
    out_specs = (P(None, "dp", "tensor"), P("dp", None, "tensor"))
    body = functools.partial(local, mesh.shape["tensor"])
    return jax.shard_map(body, mesh=mesh, in_specs=in_specs, out_specs=out_specs, check_vma=False)
```

```python
import functools

import jax
import jax.numpy as jnp
from jax import lax
from jax.experimental import pallas as pl
from jax.experimental.pallas import tpu as pltpu
from jax.sharding import PartitionSpec as P

HD = 128
SPAN = 4
MOST = 2
BEAMS = 8
STEPS = 4
PAGE = 128
GRAIN = 64
PER_CHILD = 16
VIA = 20
MORE = 8
REST = 25
FIRST = VIA + MORE
LINK = FIRST + REST
MESH = pl.DeviceIdType.MESH


def grains(length):
    return (length + (GRAIN - 1)) >> 6


def choose(values, index):
    out = values[0]
    for at in range(1, len(values)):
        out = jnp.where(index == at, values[at], out)
    return out


def ring_plan(parents, lengths, ring):
    flows = [[jnp.int32(0)] * SPAN for _ in range(SPAN)]
    for target in range(SPAN):
        seen = []
        for child in range(BEAMS):
            parent = parents[(ring * SPAN + target) * BEAMS + child]
            count = grains(lengths[parent])
            for other in seen:
                count = jnp.where(parent == other, 0, count)
            seen.append(parent)
            source = (parent >> 3) & (SPAN - 1)
            for at in range(SPAN):
                if at != target:
                    ahead = (target - at) % SPAN
                    flows[at][ahead] = flows[at][ahead] + jnp.where(source == at, count, 0)
    up = [flow[1] for flow in flows]
    far = [flow[2] for flow in flows]
    down = [flow[3] for flow in flows]
    via_up = [jnp.minimum(count >> 1, VIA) for count in far]
    for at in range(SPAN):
        via_down = [far[i] - via_up[i] for i in range(SPAN)]
        nxt, prv = (at + 1) % SPAN, (at - 1) % SPAN
        load_up = jnp.maximum(up[at] + via_up[prv], up[nxt] + via_up[nxt])
        load_down = jnp.maximum(down[at] + via_down[nxt], down[prv] + via_down[prv])
        best = (load_down + far[at] - load_up) >> 1
        via_up[at] = jnp.minimum(jnp.maximum(best, jnp.maximum(far[at] - VIA, 0)), jnp.minimum(far[at], VIA))
    via_down = [far[i] - via_up[i] for i in range(SPAN)]
    return up, down, via_up, via_down


def overfull(plan):
    up, down, via_up, via_down = plan
    out = jnp.int32(0)
    for at in range(SPAN):
        load_up = up[at] + via_up[at] + via_up[(at - 1) % SPAN]
        load_down = down[at] + via_down[at] + via_down[(at + 1) % SPAN]
        out = jnp.maximum(out, jnp.where(jnp.maximum(load_up, load_down) > LINK, 1, 0))
    return out


def slots_of_children(parents, me):
    taken = [jnp.int32(0) for _ in range(SPAN)]
    slots, owners = [], []
    for child in range(BEAMS):
        parent = parents[me * BEAMS + child]
        apart = jnp.bitwise_and(parent // BEAMS - me, SPAN - 1)
        slot = jnp.int32(0)
        for distance in range(SPAN):
            hit = apart == distance
            slot = jnp.where(hit, distance * MOST + taken[distance], slot)
            taken[distance] = taken[distance] + hit.astype(jnp.int32)
        slots.append(slot)
        owners.append(parent)
    return slots, owners


def served_beams(parents, me, target):
    count = jnp.int32(0)
    beams = [jnp.int32(0) for _ in range(MOST)]
    for child in range(BEAMS):
        parent = parents[target * BEAMS + child]
        hit = parent // BEAMS == me
        for rank in range(MOST):
            beams[rank] = jnp.where(hit & (count == rank), parent % BEAMS, beams[rank])
        count = count + hit.astype(jnp.int32)
    return beams


def exchange_kernel(
    q_hbm, new_hbm, pool_ref, table_hbm, len_hbm, par_hbm, w_ref,
    recv_ref, proj_ref, meta_ref, over_ref,
    q_ref, new_ref, table_ref, len_ref, par_ref,
    pool_v, w_v, stage, first_send, first_recv, rest_send, q_send, q_recv, att, p_send, p_recv, r_send, lens, beams,
    in_sem, pool_sem, w_sem, own_sem, land_sem, qs_sem, qr_sem, bs_sem, br_sem, ps_sem, pr_sem, rs_sem, rr_sem, here_sem,
):
    me = lax.axis_index("dp")
    mine = lax.axis_index("tensor")
    shards = lax.axis_size("tensor")
    y = lax.rem(me, SPAN)
    base = me - y
    context = stage.shape[1] * GRAIN // MOST
    rings = lax.axis_size("dp") // SPAN
    wide = q_hbm.shape[2]
    heads = wide // HD
    rows = MOST * STEPS

    def peer(distance):
        return base + lax.rem(y + distance, SPAN)

    barrier = pltpu.get_barrier_semaphore()
    for distance in range(1, SPAN):
        pl.semaphore_signal(barrier, inc=1, device_id={"dp": peer(distance)}, device_id_type=MESH)
    for other in range(1, shards):
        @pl.when(mine + other < shards)
        def _(other=other):
            pl.semaphore_signal(barrier, inc=1, device_id={"tensor": mine + other}, device_id_type=MESH)
    in_copies = []
    operands = ((par_hbm, par_ref), (q_hbm, q_ref), (new_hbm, new_ref), (table_hbm, table_ref), (len_hbm, len_ref))
    for at, (source, target) in enumerate(operands):
        copy = pltpu.make_async_copy(source, target, in_sem.at[at])
        copy.start()
        in_copies.append(copy)
    pool_copy = pltpu.make_async_copy(pool_ref, pool_v, pool_sem)
    pool_copy.start()
    for copy in in_copies:
        copy.wait()

    slots, owners = slots_of_children(par_ref, me)
    plan = ring_plan(par_ref, len_ref, me >> 2)
    up, down, via_up, via_down = plan
    row = lax.broadcasted_iota(jnp.int32, (SPAN * rows, BEAMS), 0)
    col = lax.broadcasted_iota(jnp.int32, (SPAN * rows, BEAMS), 1)
    slot_at = jnp.zeros_like(col)
    for child in range(BEAMS):
        slot_at = jnp.where(col == child, slots[child], slot_at)
    q_sorted = jnp.zeros((SPAN * rows, wide), jnp.float32)
    new_sorted = jnp.zeros((SPAN * rows, 2 * HD), jnp.float32)
    for step in range(STEPS):
        pick = jnp.where((row // STEPS == slot_at) & (row % STEPS == step), 1.0, 0.0).astype(jnp.bfloat16)
        q_sorted += jnp.dot(pick, q_ref[step], preferred_element_type=jnp.float32)
        new_sorted += jnp.dot(pick, new_ref[step], preferred_element_type=jnp.float32)
    both = jnp.concatenate([q_sorted, new_sorted], axis=1)
    half = both.shape[1] // 2
    for distance in range(SPAN):
        part = both[distance * rows:(distance + 1) * rows]
        part = jnp.concatenate([part[:, :half], part[:, half:]], axis=0).astype(jnp.bfloat16)
        if distance == 0:
            q_recv[0] = part
        else:
            q_send[distance] = part

    pl.semaphore_wait(barrier, SPAN - 1 + mine)
    for other in range(1, shards):
        @pl.when(mine >= other)
        def _(other=other):
            pl.semaphore_signal(here_sem, inc=1, device_id={"tensor": mine - other}, device_id_type=MESH)

    q_copies = []
    for distance in range(1, SPAN):
        copy = pltpu.make_async_remote_copy(
            src_ref=q_send.at[distance], dst_ref=q_recv.at[distance],
            send_sem=qs_sem.at[distance], recv_sem=qr_sem.at[distance],
            device_id={"dp": peer(distance)}, device_id_type=MESH,
        )
        copy.start()
        q_copies.append(copy)

    flows = {}
    for ahead in range(SPAN):
        served = served_beams(par_ref, me, peer(ahead))
        distance = (SPAN - ahead) % SPAN
        held = [len_ref[me * BEAMS + served[rank]] for rank in range(MOST)]
        for rank in range(MOST):
            beams[distance * MOST + rank] = served[rank]
            lens[distance * MOST + rank] = held[rank]
        flows[ahead] = (served[0], served[1], grains(held[0]))

    def grain_at(flow, number):
        first, second, cut = flow
        later = number >= cut
        number = jnp.where(later, number - cut, number)
        number = jnp.minimum(jnp.maximum(number, 0), PER_CHILD - 1)
        return table_ref[jnp.where(later, second, first), number >> 1] * 2 + (number & 1)

    sides = (
        (flows[1], choose(via_up, y), jnp.int32(0), choose(via_up, (y - 1) & 3), peer(1)),
        (flows[3], choose(via_down, y), choose(via_up, y), choose(via_down, (y + 1) & 3), peer(3)),
    )
    pool_copy.wait()
    b_copies = []
    cuts = (0, VIA // 2, VIA, FIRST)
    for part in range(3):
        for side, (flow, mine_via, skip, _, target) in enumerate(sides):
            def put(at, carry, side=side, flow=flow, mine_via=mine_via, skip=skip):
                far = at < mine_via
                chosen = tuple(jnp.where(far, one, two) for one, two in zip(flows[2], flow))
                number = jnp.where(far, skip + at, at - mine_via)
                first_send[side, at] = pool_v[grain_at(chosen, number)]
                return carry

            lax.fori_loop(cuts[part], cuts[part + 1], put, 0)
            span = pl.ds(cuts[part], cuts[part + 1] - cuts[part])
            copy = pltpu.make_async_remote_copy(
                src_ref=first_send.at[side, span], dst_ref=first_recv.at[side, span],
                send_sem=bs_sem.at[side * 4 + part], recv_sem=br_sem.at[side * 4 + part],
                device_id={"dp": target}, device_id_type=MESH,
            )
            copy.start()
            b_copies.append(copy)
    w_copies = []
    for block in range(shards):
        copy = pltpu.make_async_copy(w_ref.at[:, pl.ds(block * wide, wide)], w_v.at[block], w_sem.at[block])
        copy.start()
        w_copies.append(copy)

    def put_all(index, carry):
        slot = index >> 4
        number = index & (PER_CHILD - 1)
        grain = table_ref[beams[slot], number >> 1] * 2 + (number & 1)
        stage[index >> 5, index & (MOST * PER_CHILD - 1)] = pool_v[grain]
        return carry

    lax.fori_loop(0, SPAN * MOST * PER_CHILD, put_all, 0)
    own_copy = pltpu.make_async_copy(stage.at[0], recv_ref.at[pl.ds(2 * LINK, MOST * PER_CHILD)], own_sem.at[0])
    own_copy.start()

    for copy in q_copies:
        copy.wait()

    def attend(distance, carry):
        message = q_recv[distance].astype(jnp.float32)
        message = jnp.concatenate([message[:rows], message[rows:]], axis=1)
        q_rows = jnp.concatenate([message[:, h * HD:(h + 1) * HD] for h in range(heads)], axis=0).astype(jnp.bfloat16)
        fresh = message[:, wide:].astype(jnp.bfloat16)
        old_len = lens[distance * MOST]
        last_len = lens[distance * MOST + 1]
        contract = (((1,), (1,)), ((), ()))
        scale = HD ** -0.5
        scores = lax.dot_general(q_rows, stage[distance, :, :, 0:HD].reshape(MOST * context, HD), contract, preferred_element_type=jnp.float32) * scale
        fresh_scores = lax.dot_general(q_rows, fresh[:, :HD], contract, preferred_element_type=jnp.float32) * scale
        rank_at = lax.broadcasted_iota(jnp.int32, scores.shape, 0) // STEPS % MOST
        position = lax.broadcasted_iota(jnp.int32, scores.shape, 1) - rank_at * context
        limit = jnp.where(rank_at == 0, old_len, last_len)
        scores = jnp.where((position >= 0) & (position < limit), scores, -1e30)
        f_row = lax.broadcasted_iota(jnp.int32, fresh_scores.shape, 0)
        f_col = lax.broadcasted_iota(jnp.int32, fresh_scores.shape, 1)
        seen = (f_row // STEPS % MOST == f_col // STEPS) & (f_col % STEPS <= f_row % STEPS)
        fresh_scores = jnp.where(seen, fresh_scores, -1e30)
        top = jnp.maximum(jnp.max(scores, axis=1, keepdims=True), jnp.max(fresh_scores, axis=1, keepdims=True))
        exp_old = jnp.exp(scores - top)
        exp_new = jnp.exp(fresh_scores - top)
        total = jnp.sum(exp_old, axis=1, keepdims=True) + jnp.sum(exp_new, axis=1, keepdims=True)
        w_old = (exp_old / total).astype(jnp.bfloat16)
        w_new = (exp_new / total).astype(jnp.bfloat16)
        out = jnp.dot(w_old, stage[distance, :, :, HD:2 * HD].reshape(MOST * context, HD), preferred_element_type=jnp.float32)
        out += jnp.dot(w_new, fresh[:, HD:], preferred_element_type=jnp.float32)
        out = jnp.concatenate([out[h * rows:(h + 1) * rows] for h in range(heads)], axis=1)
        att[pl.ds(pl.multiple_of(distance * rows, rows), rows), :] = out
        return carry

    lax.fori_loop(0, SPAN, attend, 0)
    for copy in b_copies[:4]:
        copy.wait()
    more_copies = b_copies[4:]
    b_copies = []
    for side, (flow, mine_via, _, passed, target) in enumerate(sides):
        def put_passed(at, carry, side=side, flow=flow, mine_via=mine_via, passed=passed):
            here = pool_v[grain_at(flow, FIRST - mine_via + at - passed)]
            rest_send[side, at] = jnp.where(at < passed, first_recv[side, at], here)
            return carry

        def put_rest(at, carry, side=side, flow=flow, mine_via=mine_via, passed=passed):
            rest_send[side, at] = pool_v[grain_at(flow, FIRST - mine_via + at - passed)]
            return carry

        lax.fori_loop(0, VIA, put_passed, 0)
        lax.fori_loop(VIA, REST, put_rest, 0)
        copy = pltpu.make_async_remote_copy(
            src_ref=rest_send.at[side], dst_ref=recv_ref.at[pl.ds(side * LINK + FIRST, REST)],
            send_sem=bs_sem.at[side * 4 + 3], recv_sem=br_sem.at[side * 4 + 3],
            device_id={"dp": target}, device_id_type=MESH,
        )
        copy.start()
        b_copies.append(copy)
    attended = att[...].astype(jnp.bfloat16)
    for copy in w_copies:
        copy.wait()

    def p_copy(other):
        return pltpu.make_async_remote_copy(
            src_ref=p_send.at[other], dst_ref=p_recv.at[other],
            send_sem=ps_sem.at[other], recv_sem=pr_sem.at[other],
            device_id={"tensor": lax.rem(mine + other, shards)}, device_id_type=MESH,
        )

    def project(other, carry):
        product = jnp.dot(attended, w_v[lax.rem(mine + other, shards)], preferred_element_type=jnp.float32)
        p_send[other] = product.astype(jnp.bfloat16)
        p_copy(other).start()
        return carry

    @pl.when(mine < shards - 1)
    def _():
        pl.semaphore_wait(here_sem, shards - 1 - mine)

    lax.fori_loop(1, shards, project, 0)
    own = jnp.dot(attended, w_v[mine], preferred_element_type=jnp.float32)

    over_ref[0] = lax.fori_loop(
        0, rings, lambda ring, over: jnp.maximum(over, overfull(ring_plan(par_ref, len_ref, ring))), jnp.int32(0)
    )
    for child in range(BEAMS):
        slot = slots[child]
        distance = slot >> 1
        length = len_ref[owners[child]]
        before = jnp.int32(0)
        for other in range(BEAMS):
            if other != child:
                mate = (slots[other] >> 1 == distance) & (slots[other] < slot)
                differs = owners[other] != owners[child]
                before = jnp.where(mate & differs, grains(len_ref[owners[other]]), before)
        from_up = choose(via_up, (y - 1) & 3), choose(via_up, (y + 2) & 3)
        from_down = choose(via_down, (y + 1) & 3), choose(via_down, (y + 2) & 3)
        near_via = jnp.where(distance == 3, from_up[0], from_down[0])
        near_pass = jnp.where(distance == 3, from_up[1], from_down[1])
        near_base = jnp.where(distance == 3, 0, LINK)
        split = jnp.where(distance == 2, from_up[1], FIRST - near_via) - before
        split = jnp.minimum(jnp.maximum(split, 0), PER_CHILD)
        start = jnp.where(distance == 2, FIRST + before, near_base + near_via + before)
        again = jnp.where(distance == 2, LINK + FIRST + before + split - from_up[1], start + split + near_pass)
        stays = distance == 0
        meta_ref[child * 4] = length
        meta_ref[child * 4 + 1] = jnp.where(stays, 2 * LINK + (slot & 1) * PER_CHILD, start)
        meta_ref[child * 4 + 2] = jnp.where(stays, PER_CHILD, split)
        meta_ref[child * 4 + 3] = jnp.where(stays, 0, again)
        meta_ref[BEAMS * 4 + child] = slot
    for copy in more_copies:
        copy.wait()
    for side in range(2):
        copy = pltpu.make_async_copy(first_recv.at[side], recv_ref.at[pl.ds(side * LINK, FIRST)], land_sem.at[side])
        copy.start()
        b_copies.append(copy)

    def gather_sums(other, total):
        p_copy(other).wait()
        return total + p_recv[other].astype(jnp.float32)

    summed = lax.fori_loop(1, shards, gather_sums, own)
    half = wide // 2
    r_copies = []
    for distance in range(SPAN):
        part = summed[distance * rows:(distance + 1) * rows]
        r_send[distance] = jnp.concatenate([part[:, :half], part[:, half:]], axis=0).astype(jnp.bfloat16)
        if distance == 0:
            copy = pltpu.make_async_copy(r_send.at[0], proj_ref.at[0], own_sem.at[1])
        else:
            copy = pltpu.make_async_remote_copy(
                src_ref=r_send.at[distance], dst_ref=proj_ref.at[distance],
                send_sem=rs_sem.at[distance], recv_sem=rr_sem.at[distance],
                device_id={"dp": peer(SPAN - distance)}, device_id_type=MESH,
            )
        copy.start()
        r_copies.append(copy)
    for copy in r_copies:
        copy.wait()
    for copy in b_copies:
        copy.wait()
    own_copy.wait()


def full_kernel(
    pool_ref, table_hbm, par_hbm, recv_ref,
    table_ref, par_ref, pool_v, stage,
    in_sem, pool_sem, own_sem, bs_sem, br_sem,
):
    me = lax.axis_index("dp")
    y = lax.rem(me, SPAN)
    base = me - y
    context = stage.shape[1] // MOST

    def peer(distance):
        return base + lax.rem(y + distance, SPAN)

    barrier = pltpu.get_barrier_semaphore()
    for distance in range(1, SPAN):
        pl.semaphore_signal(barrier, inc=1, device_id={"dp": peer(distance)}, device_id_type=MESH)
    in_copies = []
    for at, (source, target) in enumerate(((par_hbm, par_ref), (table_hbm, table_ref))):
        copy = pltpu.make_async_copy(source, target, in_sem.at[at])
        copy.start()
        in_copies.append(copy)
    pool_copy = pltpu.make_async_copy(pool_ref, pool_v, pool_sem)
    pool_copy.start()
    for copy in in_copies:
        copy.wait()
    pl.semaphore_wait(barrier, SPAN - 1)
    pool_copy.wait()
    copies = []
    for distance in (2, 1, 3, 0):
        served = served_beams(par_ref, me, peer(SPAN - distance))
        for rank in range(MOST):
            beam = served[rank]

            def put(index, carry, distance=distance, rank=rank, beam=beam):
                at = pl.multiple_of(rank * context + index * PAGE, PAGE)
                stage[distance, pl.ds(at, PAGE), :] = pool_v[table_ref[beam, index]]
                return carry

            lax.fori_loop(0, context // PAGE, put, 0)
            span = pl.ds(rank * context, context)
            if distance == 0:
                copy = pltpu.make_async_copy(stage.at[0, span], recv_ref.at[0, span], own_sem.at[rank])
            else:
                copy = pltpu.make_async_remote_copy(
                    src_ref=stage.at[distance, span], dst_ref=recv_ref.at[distance, span],
                    send_sem=bs_sem.at[distance * MOST + rank], recv_sem=br_sem.at[distance * MOST + rank],
                    device_id={"dp": peer(SPAN - distance)}, device_id_type=MESH,
                )
            copy.start()
            copies.append(copy)
    for copy in copies:
        copy.wait()


def finish_kernel(recv_ref, raw_ref, new_hbm, len_hbm, par_hbm, proj_ref, cache_ref, new_ref, len_ref, par_ref, edge, zeros, in_sem, out_sem):
    me = lax.axis_index("dp")
    pages = recv_ref.shape[1] // PAGE
    operands = ((par_hbm, par_ref), (len_hbm, len_ref), (new_hbm, new_ref))
    in_copies = [pltpu.make_async_copy(source, target, in_sem.at[at]) for at, (source, target) in enumerate(operands)]
    for copy in in_copies:
        copy.start()
    zeros[...] = jnp.zeros_like(zeros)
    for copy in in_copies:
        copy.wait()
    slots, owners = slots_of_children(par_ref, me)
    fresh = [new_ref[step].astype(jnp.float32) for step in range(STEPS)]
    for child in range(BEAMS):
        slot = slots[child]
        length = len_ref[owners[child]]
        first = length // PAGE
        last = (length + STEPS - 1) // PAGE

        def whole(index, carry, child=child, slot=slot):
            span = pl.ds(pl.multiple_of(index * PAGE, PAGE), PAGE)
            pltpu.make_async_copy(recv_ref.at[slot, span], cache_ref.at[child, span], out_sem).start()
            return carry

        def clear(index, carry, child=child):
            span = pl.ds(pl.multiple_of(index * PAGE, PAGE), PAGE)
            pltpu.make_async_copy(zeros, cache_ref.at[child, span], out_sem).start()
            return carry

        def fix(index, carry, child=child, slot=slot, length=length, first=first):
            at = pl.multiple_of(index * PAGE, PAGE)
            position = at + lax.broadcasted_iota(jnp.int32, (PAGE, 2 * HD), 0)
            page = recv_ref[slot, pl.ds(at, PAGE), :].astype(jnp.float32)
            page = jnp.where(position < length, page, 0.0)
            for step in range(STEPS):
                page = jnp.where(position == length + step, fresh[step][child:child + 1], page)
            edge[child * 2 + index - first] = page.astype(jnp.bfloat16)
            pltpu.make_async_copy(edge.at[child * 2 + index - first], cache_ref.at[child, pl.ds(at, PAGE)], out_sem).start()
            return carry

        lax.fori_loop(0, first, whole, 0)
        lax.fori_loop(last + 1, pages, clear, 0)
        lax.fori_loop(first, last + 1, fix, 0)

    rows = MOST * STEPS
    raw = []
    for distance in range(SPAN):
        part = raw_ref[distance].astype(jnp.float32)
        raw.append(jnp.concatenate([part[:rows], part[rows:]], axis=1))
    raw = jnp.concatenate(raw, axis=0).astype(jnp.bfloat16)
    row = lax.broadcasted_iota(jnp.int32, (BEAMS, SPAN * rows), 0)
    col = lax.broadcasted_iota(jnp.int32, (BEAMS, SPAN * rows), 1)
    slot_at = jnp.zeros_like(col)
    for child in range(BEAMS):
        slot_at = jnp.where(row == child, slots[child], slot_at)
    for step in range(STEPS):
        pick = jnp.where(col == slot_at * STEPS + step, 1.0, 0.0).astype(jnp.bfloat16)
        proj_ref[step] = jnp.dot(pick, raw, preferred_element_type=jnp.float32).astype(jnp.bfloat16)
    pltpu.make_async_copy(recv_ref, cache_ref, out_sem).wait()


def place_kernel(recv_ref, raw_ref, new_ref, meta_ref, proj_ref, cache_ref, edge, zeros, out_sem):
    total = recv_ref.shape[0]
    zeros[...] = jnp.zeros_like(zeros)
    fresh = [new_ref[step].astype(jnp.float32) for step in range(STEPS)]
    slots = [meta_ref[BEAMS * 4 + child] for child in range(BEAMS)]
    for child in range(BEAMS):
        length, start, split, again = (meta_ref[child * 4 + at] for at in range(4))
        first = length >> 6
        last = (length + STEPS - 1) >> 6
        split = jnp.minimum(split, first)

        def move(source, source_at, at, count, child=child):
            @pl.when(count > 0)
            def _():
                pltpu.make_async_copy(
                    source.at[pl.ds(source_at, count)], cache_ref.at[child, pl.ds(at, count)], out_sem
                ).start()

        move(recv_ref, start, 0, split)
        move(recv_ref, again, split, first - split)
        move(zeros, 0, last + 1, PER_CHILD - 1 - last)

        def fix(index, carry, child=child, length=length, first=first, start=start, again=again, whole=meta_ref[child * 4 + 2]):
            position = index * GRAIN + lax.broadcasted_iota(jnp.int32, (GRAIN, 2 * HD), 0)
            at = jnp.minimum(jnp.where(index < whole, start + index, again + index - whole), total - 1)
            page = jnp.where(position < length, recv_ref[at].astype(jnp.float32), 0.0)
            for step in range(STEPS):
                page = jnp.where(position == length + step, fresh[step][child:child + 1], page)
            edge[child * 2 + index - first] = page.astype(jnp.bfloat16)
            pltpu.make_async_copy(edge.at[child * 2 + index - first], cache_ref.at[child, index], out_sem).start()
            return carry

        lax.fori_loop(first, last + 1, fix, 0)

    rows = MOST * STEPS
    raw = []
    for distance in range(SPAN):
        part = raw_ref[distance].astype(jnp.float32)
        raw.append(jnp.concatenate([part[:rows], part[rows:]], axis=1))
    raw = jnp.concatenate(raw, axis=0).astype(jnp.bfloat16)
    row = lax.broadcasted_iota(jnp.int32, (BEAMS, SPAN * rows), 0)
    col = lax.broadcasted_iota(jnp.int32, (BEAMS, SPAN * rows), 1)
    slot_at = jnp.zeros_like(col)
    for child in range(BEAMS):
        slot_at = jnp.where(row == child, slots[child], slot_at)
    for step in range(STEPS):
        pick = jnp.where(col == slot_at * STEPS + step, 1.0, 0.0).astype(jnp.bfloat16)
        proj_ref[step] = jnp.dot(pick, raw, preferred_element_type=jnp.float32).astype(jnp.bfloat16)
    pltpu.make_async_copy(cache_ref, cache_ref, out_sem).wait()


def local(shards, queries, new_kv, kv_pool, page_tables, lengths, parents, out_weight):
    wide = queries.shape[2]
    channels = kv_pool.shape[2]
    context = page_tables.shape[1] * kv_pool.shape[1]
    rows = MOST * STEPS
    vmem = pl.BlockSpec(memory_space=pltpu.VMEM)
    smem = pl.BlockSpec(memory_space=pltpu.SMEM)
    hbm = pl.BlockSpec(memory_space=pltpu.HBM)
    free = pl.BlockSpec(memory_space=pl.ANY)
    dma = pltpu.SemaphoreType.DMA
    bf16 = jnp.bfloat16

    def pinned(*operands):
        return [pltpu.with_memory_space_constraint(operand, pltpu.HBM) for operand in operands]

    grain_pool = kv_pool.reshape(-1, GRAIN, channels)
    with jax.named_scope("exchange"):
        recv, raw, meta, over = pl.pallas_call(
            exchange_kernel,
            out_shape=(
                jax.ShapeDtypeStruct((2 * LINK + MOST * PER_CHILD, GRAIN, channels), bf16),
                jax.ShapeDtypeStruct((SPAN, 2 * rows, wide // 2), bf16),
                jax.ShapeDtypeStruct((BEAMS * 5,), jnp.int32),
                jax.ShapeDtypeStruct((1,), jnp.int32),
            ),
            in_specs=[hbm] * 7,
            out_specs=(free, free, smem, smem),
            scratch_shapes=[
                pltpu.VMEM(queries.shape, bf16),
                pltpu.VMEM(new_kv.shape, bf16),
                pltpu.SMEM(page_tables.shape, jnp.int32),
                pltpu.SMEM(lengths.shape, jnp.int32),
                pltpu.SMEM(parents.shape, jnp.int32),
                pltpu.VMEM(grain_pool.shape, bf16),
                pltpu.VMEM((shards, out_weight.shape[0], wide), bf16),
                pltpu.VMEM((SPAN, MOST * PER_CHILD, GRAIN, channels), bf16),
                pltpu.VMEM((2, FIRST, GRAIN, channels), bf16),
                pltpu.VMEM((2, FIRST, GRAIN, channels), bf16),
                pltpu.VMEM((2, REST, GRAIN, channels), bf16),
                pltpu.VMEM((SPAN, 2 * rows, (wide + channels) // 2), bf16),
                pltpu.VMEM((SPAN, 2 * rows, (wide + channels) // 2), bf16),
                pltpu.VMEM((SPAN * rows, wide), jnp.float32),
                pltpu.VMEM((shards, SPAN * rows, wide), bf16),
                pltpu.VMEM((shards, SPAN * rows, wide), bf16),
                pltpu.VMEM((SPAN, 2 * rows, wide // 2), bf16),
                pltpu.SMEM((SPAN * MOST,), jnp.int32),
                pltpu.SMEM((SPAN * MOST,), jnp.int32),
                dma((5,)), dma, dma((shards,)), dma((2,)), dma((2,)),
                dma((SPAN,)), dma((SPAN,)),
                dma((8,)), dma((8,)),
                dma((shards,)), dma((shards,)),
                dma((SPAN,)), dma((SPAN,)),
                pltpu.SemaphoreType.REGULAR,
            ],
            compiler_params=pltpu.CompilerParams(
                collective_id=0, has_side_effects=True, vmem_limit_bytes=48 * 1024 * 1024
            ),
            name="exchange",
        )(*pinned(queries, new_kv, grain_pool, page_tables, lengths, parents, out_weight))

    def placed():
        with jax.named_scope("place"):
            projected, cache = pl.pallas_call(
                place_kernel,
                out_shape=(
                    jax.ShapeDtypeStruct(queries.shape, bf16),
                    jax.ShapeDtypeStruct((BEAMS, PER_CHILD, GRAIN, channels), bf16),
                ),
                in_specs=[vmem, vmem, vmem, smem],
                out_specs=(vmem, free),
                scratch_shapes=[
                    pltpu.VMEM((2 * BEAMS, GRAIN, channels), bf16),
                    pltpu.VMEM((PER_CHILD, GRAIN, channels), bf16),
                    dma,
                ],
                compiler_params=pltpu.CompilerParams(vmem_limit_bytes=24 * 1024 * 1024),
                name="place",
            )(recv, raw, new_kv, meta)
            return projected, cache.reshape(BEAMS, context, channels)

    def resent():
        with jax.named_scope("full"):
            whole = pl.pallas_call(
                full_kernel,
                out_shape=jax.ShapeDtypeStruct((SPAN, MOST * context, channels), bf16),
                in_specs=[hbm] * 3,
                out_specs=free,
                scratch_shapes=[
                    pltpu.SMEM(page_tables.shape, jnp.int32),
                    pltpu.SMEM(parents.shape, jnp.int32),
                    pltpu.VMEM(kv_pool.shape, bf16),
                    pltpu.VMEM((SPAN, MOST * context, channels), bf16),
                    dma((2,)), dma, dma((MOST,)),
                    dma((SPAN * MOST,)), dma((SPAN * MOST,)),
                ],
                compiler_params=pltpu.CompilerParams(
                    collective_id=1, has_side_effects=True, vmem_limit_bytes=24 * 1024 * 1024
                ),
                name="full",
            )(*pinned(kv_pool, page_tables, parents))
        with jax.named_scope("finish"):
            return pl.pallas_call(
                finish_kernel,
                out_shape=(
                    jax.ShapeDtypeStruct(queries.shape, bf16),
                    jax.ShapeDtypeStruct((BEAMS, context, channels), bf16),
                ),
                in_specs=[vmem, vmem, hbm, hbm, hbm],
                out_specs=(vmem, hbm),
                scratch_shapes=[
                    pltpu.VMEM(new_kv.shape, bf16),
                    pltpu.SMEM(lengths.shape, jnp.int32),
                    pltpu.SMEM(parents.shape, jnp.int32),
                    pltpu.VMEM((2 * BEAMS, PAGE, channels), bf16),
                    pltpu.VMEM((PAGE, channels), bf16),
                    dma((3,)), dma,
                ],
                compiler_params=pltpu.CompilerParams(vmem_limit_bytes=24 * 1024 * 1024),
                name="finish",
            )(whole.reshape(BEAMS, context, channels), raw, new_kv, lengths, parents)

    return lax.cond(over[0] > 0, resent, placed)


def solution(mesh):
    in_specs = (
        P(None, "dp", "tensor"),
        P(None, "dp", "tensor"),
        P("dp", None, "tensor"),
        P("dp", None),
        P(),
        P(),
        P("tensor", None),
    )
    out_specs = (P(None, "dp", "tensor"), P("dp", None, "tensor"))
    body = functools.partial(local, mesh.shape["tensor"])
    return jax.shard_map(body, mesh=mesh, in_specs=in_specs, out_specs=out_specs, check_vma=False)
```

```python
import functools

import jax
import jax.numpy as jnp
from jax import lax
from jax.experimental import pallas as pl
from jax.experimental.pallas import tpu as pltpu
from jax.sharding import PartitionSpec as P

HD = 128
SPAN = 4
MOST = 2
BEAMS = 8
STEPS = 4
PAGE = 128
PAGES = 8
GRAIN = 32
PER_CHILD = 32
PER_PAGE = PAGE // GRAIN
TILE = 16
VIA = 40
MORE = 16
REST = 46
FIRST = VIA + MORE
LINK = FIRST + REST
MESH = pl.DeviceIdType.MESH


def grains(length):
    return (length + (GRAIN - 1)) // GRAIN


def choose(values, index):
    out = values[0]
    for at in range(1, len(values)):
        out = jnp.where(index == at, values[at], out)
    return out


def ring_plan(parents, lengths, ring):
    flows = [[jnp.int32(0)] * SPAN for _ in range(SPAN)]
    for target in range(SPAN):
        seen = []
        for child in range(BEAMS):
            parent = parents[(ring * SPAN + target) * BEAMS + child]
            count = grains(lengths[parent])
            for other in seen:
                count = jnp.where(parent == other, 0, count)
            seen.append(parent)
            source = (parent >> 3) & (SPAN - 1)
            for at in range(SPAN):
                if at != target:
                    ahead = (target - at) % SPAN
                    flows[at][ahead] = flows[at][ahead] + jnp.where(source == at, count, 0)
    up = [flow[1] for flow in flows]
    far = [flow[2] for flow in flows]
    down = [flow[3] for flow in flows]
    via_up = [jnp.minimum(count >> 1, VIA) for count in far]
    for at in range(SPAN):
        via_down = [far[i] - via_up[i] for i in range(SPAN)]
        nxt, prv = (at + 1) % SPAN, (at - 1) % SPAN
        load_up = jnp.maximum(up[at] + via_up[prv], up[nxt] + via_up[nxt])
        load_down = jnp.maximum(down[at] + via_down[nxt], down[prv] + via_down[prv])
        best = (load_down + far[at] - load_up) >> 1
        via_up[at] = jnp.minimum(jnp.maximum(best, jnp.maximum(far[at] - VIA, 0)), jnp.minimum(far[at], VIA))
    via_down = [far[i] - via_up[i] for i in range(SPAN)]
    return up, down, via_up, via_down


def overfull(plan):
    up, down, via_up, via_down = plan
    out = jnp.int32(0)
    for at in range(SPAN):
        load_up = up[at] + via_up[at] + via_up[(at - 1) % SPAN]
        load_down = down[at] + via_down[at] + via_down[(at + 1) % SPAN]
        out = jnp.maximum(out, jnp.where(jnp.maximum(load_up, load_down) > LINK, 1, 0))
    return out


def slots_of_children(parents, me):
    taken = [jnp.int32(0) for _ in range(SPAN)]
    slots, owners = [], []
    for child in range(BEAMS):
        parent = parents[me * BEAMS + child]
        apart = jnp.bitwise_and(parent // BEAMS - me, SPAN - 1)
        slot = jnp.int32(0)
        for distance in range(SPAN):
            hit = apart == distance
            slot = jnp.where(hit, distance * MOST + taken[distance], slot)
            taken[distance] = taken[distance] + hit.astype(jnp.int32)
        slots.append(slot)
        owners.append(parent)
    return slots, owners


def served_beams(parents, me, target):
    count = jnp.int32(0)
    beams = [jnp.int32(0) for _ in range(MOST)]
    for child in range(BEAMS):
        parent = parents[target * BEAMS + child]
        hit = parent // BEAMS == me
        for rank in range(MOST):
            beams[rank] = jnp.where(hit & (count == rank), parent % BEAMS, beams[rank])
        count = count + hit.astype(jnp.int32)
    return beams


def exchange_kernel(
    q_hbm, new_hbm, pool_ref, table_hbm, len_hbm, par_hbm, w_ref,
    recv_ref, proj_ref, meta_ref, over_ref,
    q_ref, new_ref, table_ref, len_ref, par_ref,
    pool_v, w_v, stage, first_send, first_recv, rest_send, q_send, q_recv, att, p_send, p_recv, r_send, lens, beams,
    in_sem, pool_sem, w_sem, own_sem, land_sem, qs_sem, qr_sem, bs_sem, br_sem, ps_sem, pr_sem, rs_sem, rr_sem, here_sem,
):
    me = lax.axis_index("dp")
    mine = lax.axis_index("tensor")
    shards = lax.axis_size("tensor")
    y = lax.rem(me, SPAN)
    base = me - y
    context = stage.shape[1] * GRAIN // MOST
    rings = lax.axis_size("dp") // SPAN
    wide = q_hbm.shape[2]
    heads = wide // HD
    rows = MOST * STEPS

    def peer(distance):
        return base + lax.rem(y + distance, SPAN)

    barrier = pltpu.get_barrier_semaphore()
    for distance in range(1, SPAN):
        pl.semaphore_signal(barrier, inc=1, device_id={"dp": peer(distance)}, device_id_type=MESH)
    for other in range(1, shards):
        @pl.when(mine + other < shards)
        def _(other=other):
            pl.semaphore_signal(barrier, inc=1, device_id={"tensor": mine + other}, device_id_type=MESH)
    in_copies = []
    operands = ((par_hbm, par_ref), (q_hbm, q_ref), (new_hbm, new_ref), (table_hbm, table_ref), (len_hbm, len_ref))
    for at, (source, target) in enumerate(operands):
        copy = pltpu.make_async_copy(source, target, in_sem.at[at])
        copy.start()
        in_copies.append(copy)
    pool_copy = pltpu.make_async_copy(pool_ref, pool_v, pool_sem)
    pool_copy.start()
    for copy in in_copies:
        copy.wait()

    slots, owners = slots_of_children(par_ref, me)
    plan = ring_plan(par_ref, len_ref, me >> 2)
    up, down, via_up, via_down = plan
    row = lax.broadcasted_iota(jnp.int32, (SPAN * rows, BEAMS), 0)
    col = lax.broadcasted_iota(jnp.int32, (SPAN * rows, BEAMS), 1)
    slot_at = jnp.zeros_like(col)
    for child in range(BEAMS):
        slot_at = jnp.where(col == child, slots[child], slot_at)
    q_sorted = jnp.zeros((SPAN * rows, wide), jnp.float32)
    new_sorted = jnp.zeros((SPAN * rows, 2 * HD), jnp.float32)
    for step in range(STEPS):
        pick = jnp.where((row // STEPS == slot_at) & (row % STEPS == step), 1.0, 0.0).astype(jnp.bfloat16)
        q_sorted += jnp.dot(pick, q_ref[step], preferred_element_type=jnp.float32)
        new_sorted += jnp.dot(pick, new_ref[step], preferred_element_type=jnp.float32)
    both = jnp.concatenate([q_sorted, new_sorted], axis=1)
    half = both.shape[1] // 2
    for distance in range(SPAN):
        part = both[distance * rows:(distance + 1) * rows]
        part = jnp.concatenate([part[:, :half], part[:, half:]], axis=0).astype(jnp.bfloat16)
        if distance == 0:
            q_recv[0] = part
        else:
            q_send[distance] = part

    pl.semaphore_wait(barrier, SPAN - 1 + mine)
    for other in range(1, shards):
        @pl.when(mine >= other)
        def _(other=other):
            pl.semaphore_signal(here_sem, inc=1, device_id={"tensor": mine - other}, device_id_type=MESH)

    q_copies = []
    for distance in range(1, SPAN):
        copy = pltpu.make_async_remote_copy(
            src_ref=q_send.at[distance], dst_ref=q_recv.at[distance],
            send_sem=qs_sem.at[distance], recv_sem=qr_sem.at[distance],
            device_id={"dp": peer(distance)}, device_id_type=MESH,
        )
        copy.start()
        q_copies.append(copy)

    flows = {}
    for ahead in range(SPAN):
        served = served_beams(par_ref, me, peer(ahead))
        distance = (SPAN - ahead) % SPAN
        held = [len_ref[me * BEAMS + served[rank]] for rank in range(MOST)]
        for rank in range(MOST):
            beams[distance * MOST + rank] = served[rank]
            lens[distance * MOST + rank] = held[rank]
        flows[ahead] = (served[0], served[1], grains(held[0]))

    def grain_at(flow, number):
        first, second, cut = flow
        later = number >= cut
        number = jnp.where(later, number - cut, number)
        number = jnp.minimum(jnp.maximum(number, 0), PER_CHILD - 1)
        return table_ref[jnp.where(later, second, first), number >> 2] * PER_PAGE + (number & (PER_PAGE - 1))

    sides = (
        (flows[1], choose(via_up, y), jnp.int32(0), choose(via_up, (y - 1) & 3), peer(1)),
        (flows[3], choose(via_down, y), choose(via_up, y), choose(via_down, (y + 1) & 3), peer(3)),
    )
    pool_copy.wait()
    b_copies = []
    cuts = (0, 8, VIA, FIRST)
    for part in range(3):
        for side, (flow, mine_via, skip, _, target) in enumerate(sides):
            def put(at, carry, side=side, flow=flow, mine_via=mine_via, skip=skip):
                for at in (2 * at, 2 * at + 1):
                    far = at < mine_via
                    chosen = tuple(jnp.where(far, one, two) for one, two in zip(flows[2], flow))
                    number = jnp.where(far, skip + at, at - mine_via)
                    first_send[side, at] = pool_v[grain_at(chosen, number)]
                return carry

            lax.fori_loop(cuts[part] // 2, cuts[part + 1] // 2, put, 0)
            span = pl.ds(cuts[part], cuts[part + 1] - cuts[part])
            copy = pltpu.make_async_remote_copy(
                src_ref=first_send.at[side, span], dst_ref=first_recv.at[side, span],
                send_sem=bs_sem.at[side * 4 + part], recv_sem=br_sem.at[side * 4 + part],
                device_id={"dp": target}, device_id_type=MESH,
            )
            copy.start()
            b_copies.append(copy)
    w_copies = []
    for block in range(shards):
        copy = pltpu.make_async_copy(w_ref.at[:, pl.ds(block * wide, wide)], w_v.at[block], w_sem.at[block])
        copy.start()
        w_copies.append(copy)

    def put_all(index, carry):
        slot = index // PAGES
        page = table_ref[beams[slot], index % PAGES]
        at = (index % (MOST * PAGES)) * PER_PAGE
        stage[index // (MOST * PAGES), pl.ds(at, PER_PAGE)] = pool_v[pl.ds(page * PER_PAGE, PER_PAGE)]
        return carry

    lax.fori_loop(0, SPAN * MOST * PAGES, put_all, 0)
    own_copy = pltpu.make_async_copy(stage.at[0], recv_ref.at[pl.ds(2 * LINK, MOST * PER_CHILD)], own_sem.at[0])
    own_copy.start()

    for copy in q_copies:
        copy.wait()

    def attend(distance, carry):
        message = q_recv[distance].astype(jnp.float32)
        message = jnp.concatenate([message[:rows], message[rows:]], axis=1)
        q_rows = jnp.concatenate([message[:, h * HD:(h + 1) * HD] for h in range(heads)], axis=0).astype(jnp.bfloat16)
        fresh = message[:, wide:].astype(jnp.bfloat16)
        old_len = lens[distance * MOST]
        last_len = lens[distance * MOST + 1]
        contract = (((1,), (1,)), ((), ()))
        scale = HD ** -0.5
        scores = lax.dot_general(q_rows, stage[distance, :, :, 0:HD].reshape(MOST * context, HD), contract, preferred_element_type=jnp.float32) * scale
        fresh_scores = lax.dot_general(q_rows, fresh[:, :HD], contract, preferred_element_type=jnp.float32) * scale
        rank_at = lax.broadcasted_iota(jnp.int32, scores.shape, 0) // STEPS % MOST
        position = lax.broadcasted_iota(jnp.int32, scores.shape, 1) - rank_at * context
        limit = jnp.where(rank_at == 0, old_len, last_len)
        scores = jnp.where((position >= 0) & (position < limit), scores, -1e30)
        f_row = lax.broadcasted_iota(jnp.int32, fresh_scores.shape, 0)
        f_col = lax.broadcasted_iota(jnp.int32, fresh_scores.shape, 1)
        seen = (f_row // STEPS % MOST == f_col // STEPS) & (f_col % STEPS <= f_row % STEPS)
        fresh_scores = jnp.where(seen, fresh_scores, -1e30)
        top = jnp.maximum(jnp.max(scores, axis=1, keepdims=True), jnp.max(fresh_scores, axis=1, keepdims=True))
        exp_old = jnp.exp(scores - top)
        exp_new = jnp.exp(fresh_scores - top)
        total = jnp.sum(exp_old, axis=1, keepdims=True) + jnp.sum(exp_new, axis=1, keepdims=True)
        w_old = (exp_old / total).astype(jnp.bfloat16)
        w_new = (exp_new / total).astype(jnp.bfloat16)
        out = jnp.dot(w_old, stage[distance, :, :, HD:2 * HD].reshape(MOST * context, HD), preferred_element_type=jnp.float32)
        out += jnp.dot(w_new, fresh[:, HD:], preferred_element_type=jnp.float32)
        out = jnp.concatenate([out[h * rows:(h + 1) * rows] for h in range(heads)], axis=1)
        att[pl.ds(pl.multiple_of(distance * rows, rows), rows), :] = out
        return carry

    lax.fori_loop(0, SPAN, attend, 0)
    for copy in b_copies[:4]:
        copy.wait()
    more_copies = b_copies[4:]
    b_copies = []
    for side, (flow, mine_via, _, passed, target) in enumerate(sides):
        def put_passed(at, carry, side=side, flow=flow, mine_via=mine_via, passed=passed):
            for at in (2 * at, 2 * at + 1):
                here = pool_v[grain_at(flow, FIRST - mine_via + at - passed)]
                rest_send[side, at] = jnp.where(at < passed, first_recv[side, at], here)
            return carry

        def put_rest(at, carry, side=side, flow=flow, mine_via=mine_via, passed=passed):
            for at in (2 * at, 2 * at + 1):
                rest_send[side, at] = pool_v[grain_at(flow, FIRST - mine_via + at - passed)]
            return carry

        lax.fori_loop(0, VIA // 2, put_passed, 0)
        lax.fori_loop(VIA // 2, REST // 2, put_rest, 0)
        copy = pltpu.make_async_remote_copy(
            src_ref=rest_send.at[side], dst_ref=recv_ref.at[pl.ds(side * LINK + FIRST, REST)],
            send_sem=bs_sem.at[side * 4 + 3], recv_sem=br_sem.at[side * 4 + 3],
            device_id={"dp": target}, device_id_type=MESH,
        )
        copy.start()
        b_copies.append(copy)
    attended = att[...].astype(jnp.bfloat16)
    for copy in w_copies:
        copy.wait()

    def p_copy(other):
        return pltpu.make_async_remote_copy(
            src_ref=p_send.at[other], dst_ref=p_recv.at[other],
            send_sem=ps_sem.at[other], recv_sem=pr_sem.at[other],
            device_id={"tensor": lax.rem(mine + other, shards)}, device_id_type=MESH,
        )

    def project(other, carry):
        product = jnp.dot(attended, w_v[lax.rem(mine + other, shards)], preferred_element_type=jnp.float32)
        p_send[other] = product.astype(jnp.bfloat16)
        p_copy(other).start()
        return carry

    @pl.when(mine < shards - 1)
    def _():
        pl.semaphore_wait(here_sem, shards - 1 - mine)

    lax.fori_loop(1, shards, project, 0)
    own = jnp.dot(attended, w_v[mine], preferred_element_type=jnp.float32)

    over_ref[0] = lax.fori_loop(
        0, rings, lambda ring, over: jnp.maximum(over, overfull(ring_plan(par_ref, len_ref, ring))), jnp.int32(0)
    )
    for child in range(BEAMS):
        slot = slots[child]
        distance = slot >> 1
        length = len_ref[owners[child]]
        before = jnp.int32(0)
        for other in range(BEAMS):
            if other != child:
                mate = (slots[other] >> 1 == distance) & (slots[other] < slot)
                differs = owners[other] != owners[child]
                before = jnp.where(mate & differs, grains(len_ref[owners[other]]), before)
        from_up = choose(via_up, (y - 1) & 3), choose(via_up, (y + 2) & 3)
        from_down = choose(via_down, (y + 1) & 3), choose(via_down, (y + 2) & 3)
        near_via = jnp.where(distance == 3, from_up[0], from_down[0])
        near_pass = jnp.where(distance == 3, from_up[1], from_down[1])
        near_base = jnp.where(distance == 3, 0, LINK)
        split = jnp.where(distance == 2, from_up[1], FIRST - near_via) - before
        split = jnp.minimum(jnp.maximum(split, 0), PER_CHILD)
        start = jnp.where(distance == 2, FIRST + before, near_base + near_via + before)
        again = jnp.where(distance == 2, LINK + FIRST + before + split - from_up[1], start + split + near_pass)
        stays = distance == 0
        meta_ref[child * 4] = length
        meta_ref[child * 4 + 1] = jnp.where(stays, 2 * LINK + (slot & 1) * PER_CHILD, start)
        meta_ref[child * 4 + 2] = jnp.where(stays, PER_CHILD, split)
        meta_ref[child * 4 + 3] = jnp.where(stays, 0, again)
        meta_ref[BEAMS * 4 + child] = slot
    for copy in more_copies:
        copy.wait()
    for side in range(2):
        copy = pltpu.make_async_copy(first_recv.at[side], recv_ref.at[pl.ds(side * LINK, FIRST)], land_sem.at[side])
        copy.start()
        b_copies.append(copy)

    def gather_sums(other, total):
        p_copy(other).wait()
        return total + p_recv[other].astype(jnp.float32)

    summed = lax.fori_loop(1, shards, gather_sums, own)
    half = wide // 2
    r_copies = []
    for distance in range(SPAN):
        part = summed[distance * rows:(distance + 1) * rows]
        r_send[distance] = jnp.concatenate([part[:, :half], part[:, half:]], axis=0).astype(jnp.bfloat16)
        if distance == 0:
            copy = pltpu.make_async_copy(r_send.at[0], proj_ref.at[0], own_sem.at[1])
        else:
            copy = pltpu.make_async_remote_copy(
                src_ref=r_send.at[distance], dst_ref=proj_ref.at[distance],
                send_sem=rs_sem.at[distance], recv_sem=rr_sem.at[distance],
                device_id={"dp": peer(SPAN - distance)}, device_id_type=MESH,
            )
        copy.start()
        r_copies.append(copy)
    for copy in r_copies:
        copy.wait()
    for copy in b_copies:
        copy.wait()
    own_copy.wait()


def full_kernel(
    pool_ref, table_hbm, par_hbm, recv_ref,
    table_ref, par_ref, pool_v, stage,
    in_sem, pool_sem, own_sem, bs_sem, br_sem,
):
    me = lax.axis_index("dp")
    y = lax.rem(me, SPAN)
    base = me - y
    context = stage.shape[1] // MOST

    def peer(distance):
        return base + lax.rem(y + distance, SPAN)

    barrier = pltpu.get_barrier_semaphore()
    for distance in range(1, SPAN):
        pl.semaphore_signal(barrier, inc=1, device_id={"dp": peer(distance)}, device_id_type=MESH)
    in_copies = []
    for at, (source, target) in enumerate(((par_hbm, par_ref), (table_hbm, table_ref))):
        copy = pltpu.make_async_copy(source, target, in_sem.at[at])
        copy.start()
        in_copies.append(copy)
    pool_copy = pltpu.make_async_copy(pool_ref, pool_v, pool_sem)
    pool_copy.start()
    for copy in in_copies:
        copy.wait()
    pl.semaphore_wait(barrier, SPAN - 1)
    pool_copy.wait()
    copies = []
    for distance in (2, 1, 3, 0):
        served = served_beams(par_ref, me, peer(SPAN - distance))
        for rank in range(MOST):
            beam = served[rank]

            def put(index, carry, distance=distance, rank=rank, beam=beam):
                at = pl.multiple_of(rank * context + index * PAGE, PAGE)
                stage[distance, pl.ds(at, PAGE), :] = pool_v[table_ref[beam, index]]
                return carry

            lax.fori_loop(0, context // PAGE, put, 0)
            span = pl.ds(rank * context, context)
            if distance == 0:
                copy = pltpu.make_async_copy(stage.at[0, span], recv_ref.at[0, span], own_sem.at[rank])
            else:
                copy = pltpu.make_async_remote_copy(
                    src_ref=stage.at[distance, span], dst_ref=recv_ref.at[distance, span],
                    send_sem=bs_sem.at[distance * MOST + rank], recv_sem=br_sem.at[distance * MOST + rank],
                    device_id={"dp": peer(SPAN - distance)}, device_id_type=MESH,
                )
            copy.start()
            copies.append(copy)
    for copy in copies:
        copy.wait()


def finish_kernel(recv_ref, raw_ref, new_hbm, len_hbm, par_hbm, proj_ref, cache_ref, new_ref, len_ref, par_ref, edge, zeros, in_sem, out_sem):
    me = lax.axis_index("dp")
    pages = recv_ref.shape[1] // PAGE
    operands = ((par_hbm, par_ref), (len_hbm, len_ref), (new_hbm, new_ref))
    in_copies = [pltpu.make_async_copy(source, target, in_sem.at[at]) for at, (source, target) in enumerate(operands)]
    for copy in in_copies:
        copy.start()
    zeros[...] = jnp.zeros_like(zeros)
    for copy in in_copies:
        copy.wait()
    slots, owners = slots_of_children(par_ref, me)
    fresh = [new_ref[step].astype(jnp.float32) for step in range(STEPS)]
    for child in range(BEAMS):
        slot = slots[child]
        length = len_ref[owners[child]]
        first = length // PAGE
        last = (length + STEPS - 1) // PAGE

        def whole(index, carry, child=child, slot=slot):
            span = pl.ds(pl.multiple_of(index * PAGE, PAGE), PAGE)
            pltpu.make_async_copy(recv_ref.at[slot, span], cache_ref.at[child, span], out_sem).start()
            return carry

        def clear(index, carry, child=child):
            span = pl.ds(pl.multiple_of(index * PAGE, PAGE), PAGE)
            pltpu.make_async_copy(zeros, cache_ref.at[child, span], out_sem).start()
            return carry

        def fix(index, carry, child=child, slot=slot, length=length, first=first):
            at = pl.multiple_of(index * PAGE, PAGE)
            position = at + lax.broadcasted_iota(jnp.int32, (PAGE, 2 * HD), 0)
            page = recv_ref[slot, pl.ds(at, PAGE), :].astype(jnp.float32)
            page = jnp.where(position < length, page, 0.0)
            for step in range(STEPS):
                page = jnp.where(position == length + step, fresh[step][child:child + 1], page)
            edge[child * 2 + index - first] = page.astype(jnp.bfloat16)
            pltpu.make_async_copy(edge.at[child * 2 + index - first], cache_ref.at[child, pl.ds(at, PAGE)], out_sem).start()
            return carry

        lax.fori_loop(0, first, whole, 0)
        lax.fori_loop(last + 1, pages, clear, 0)
        lax.fori_loop(first, last + 1, fix, 0)

    rows = MOST * STEPS
    raw = []
    for distance in range(SPAN):
        part = raw_ref[distance].astype(jnp.float32)
        raw.append(jnp.concatenate([part[:rows], part[rows:]], axis=1))
    raw = jnp.concatenate(raw, axis=0).astype(jnp.bfloat16)
    row = lax.broadcasted_iota(jnp.int32, (BEAMS, SPAN * rows), 0)
    col = lax.broadcasted_iota(jnp.int32, (BEAMS, SPAN * rows), 1)
    slot_at = jnp.zeros_like(col)
    for child in range(BEAMS):
        slot_at = jnp.where(row == child, slots[child], slot_at)
    for step in range(STEPS):
        pick = jnp.where(col == slot_at * STEPS + step, 1.0, 0.0).astype(jnp.bfloat16)
        proj_ref[step] = jnp.dot(pick, raw, preferred_element_type=jnp.float32).astype(jnp.bfloat16)
    pltpu.make_async_copy(recv_ref, cache_ref, out_sem).wait()


def place_kernel(recv_ref, raw_ref, new_ref, meta_ref, proj_ref, cache_ref, edge, zeros, out_sem):
    total = recv_ref.shape[0]
    zeros[...] = jnp.zeros_like(zeros)
    fresh = [new_ref[step].astype(jnp.float32) for step in range(STEPS)]
    slots = [meta_ref[BEAMS * 4 + child] for child in range(BEAMS)]
    per_child = cache_ref.shape[1]
    scale = GRAIN // TILE
    for child in range(BEAMS):
        length, start, split, again = (meta_ref[child * 4 + at] for at in range(4))
        first = length // TILE
        last = (length + STEPS - 1) // TILE
        split = jnp.minimum(split * scale, first)

        def move(source, source_at, at, count, child=child):
            @pl.when(count > 0)
            def _():
                pltpu.make_async_copy(
                    source.at[pl.ds(source_at, count)], cache_ref.at[child, pl.ds(at, count)], out_sem
                ).start()

        move(recv_ref, start * scale, 0, split)
        move(recv_ref, again * scale, split, first - split)
        move(zeros, 0, last + 1, per_child - 1 - last)
    for child in range(BEAMS):
        length, start, split, again = (meta_ref[child * 4 + at] for at in range(4))
        first = length // TILE
        last = (length + STEPS - 1) // TILE

        def fix(index, carry, child=child, length=length, first=first, start=start * scale, split=split * scale, again=again * scale):
            position = index * TILE + lax.broadcasted_iota(jnp.int32, (TILE, 2 * HD), 0)
            at = jnp.minimum(jnp.where(index < split, start + index, again + index - split), total - 1)
            part = jnp.where(position < length, recv_ref[at].astype(jnp.float32), 0.0)
            for step in range(STEPS):
                part = jnp.where(position == length + step, fresh[step][child:child + 1], part)
            edge[child * 2 + index - first] = part.astype(jnp.bfloat16)
            pltpu.make_async_copy(edge.at[child * 2 + index - first], cache_ref.at[child, index], out_sem).start()
            return carry

        lax.fori_loop(first, last + 1, fix, 0)

    rows = MOST * STEPS
    raw = []
    for distance in range(SPAN):
        part = raw_ref[distance].astype(jnp.float32)
        raw.append(jnp.concatenate([part[:rows], part[rows:]], axis=1))
    raw = jnp.concatenate(raw, axis=0).astype(jnp.bfloat16)
    row = lax.broadcasted_iota(jnp.int32, (BEAMS, SPAN * rows), 0)
    col = lax.broadcasted_iota(jnp.int32, (BEAMS, SPAN * rows), 1)
    slot_at = jnp.zeros_like(col)
    for child in range(BEAMS):
        slot_at = jnp.where(row == child, slots[child], slot_at)
    for step in range(STEPS):
        pick = jnp.where(col == slot_at * STEPS + step, 1.0, 0.0).astype(jnp.bfloat16)
        proj_ref[step] = jnp.dot(pick, raw, preferred_element_type=jnp.float32).astype(jnp.bfloat16)
    pltpu.make_async_copy(cache_ref, cache_ref, out_sem).wait()


def local(shards, queries, new_kv, kv_pool, page_tables, lengths, parents, out_weight):
    wide = queries.shape[2]
    channels = kv_pool.shape[2]
    context = page_tables.shape[1] * kv_pool.shape[1]
    rows = MOST * STEPS
    vmem = pl.BlockSpec(memory_space=pltpu.VMEM)
    smem = pl.BlockSpec(memory_space=pltpu.SMEM)
    hbm = pl.BlockSpec(memory_space=pltpu.HBM)
    free = pl.BlockSpec(memory_space=pl.ANY)
    dma = pltpu.SemaphoreType.DMA
    bf16 = jnp.bfloat16

    def pinned(*operands):
        return [pltpu.with_memory_space_constraint(operand, pltpu.HBM) for operand in operands]

    grain_pool = kv_pool.reshape(-1, GRAIN, channels)
    with jax.named_scope("exchange"):
        recv, raw, meta, over = pl.pallas_call(
            exchange_kernel,
            out_shape=(
                jax.ShapeDtypeStruct((2 * LINK + MOST * PER_CHILD, GRAIN, channels), bf16),
                jax.ShapeDtypeStruct((SPAN, 2 * rows, wide // 2), bf16),
                jax.ShapeDtypeStruct((BEAMS * 5,), jnp.int32),
                jax.ShapeDtypeStruct((1,), jnp.int32),
            ),
            in_specs=[hbm] * 7,
            out_specs=(free, free, smem, smem),
            scratch_shapes=[
                pltpu.VMEM(queries.shape, bf16),
                pltpu.VMEM(new_kv.shape, bf16),
                pltpu.SMEM(page_tables.shape, jnp.int32),
                pltpu.SMEM(lengths.shape, jnp.int32),
                pltpu.SMEM(parents.shape, jnp.int32),
                pltpu.VMEM(grain_pool.shape, bf16),
                pltpu.VMEM((shards, out_weight.shape[0], wide), bf16),
                pltpu.VMEM((SPAN, MOST * PER_CHILD, GRAIN, channels), bf16),
                pltpu.VMEM((2, FIRST, GRAIN, channels), bf16),
                pltpu.VMEM((2, FIRST, GRAIN, channels), bf16),
                pltpu.VMEM((2, REST, GRAIN, channels), bf16),
                pltpu.VMEM((SPAN, 2 * rows, (wide + channels) // 2), bf16),
                pltpu.VMEM((SPAN, 2 * rows, (wide + channels) // 2), bf16),
                pltpu.VMEM((SPAN * rows, wide), jnp.float32),
                pltpu.VMEM((shards, SPAN * rows, wide), bf16),
                pltpu.VMEM((shards, SPAN * rows, wide), bf16),
                pltpu.VMEM((SPAN, 2 * rows, wide // 2), bf16),
                pltpu.SMEM((SPAN * MOST,), jnp.int32),
                pltpu.SMEM((SPAN * MOST,), jnp.int32),
                dma((5,)), dma, dma((shards,)), dma((2,)), dma((2,)),
                dma((SPAN,)), dma((SPAN,)),
                dma((8,)), dma((8,)),
                dma((shards,)), dma((shards,)),
                dma((SPAN,)), dma((SPAN,)),
                pltpu.SemaphoreType.REGULAR,
            ],
            compiler_params=pltpu.CompilerParams(
                collective_id=0, has_side_effects=True, vmem_limit_bytes=48 * 1024 * 1024
            ),
            name="exchange",
        )(*pinned(queries, new_kv, grain_pool, page_tables, lengths, parents, out_weight))

    def placed():
        with jax.named_scope("place"):
            projected, cache = pl.pallas_call(
                place_kernel,
                out_shape=(
                    jax.ShapeDtypeStruct(queries.shape, bf16),
                    jax.ShapeDtypeStruct((BEAMS, context // TILE, TILE, channels), bf16),
                ),
                in_specs=[vmem, vmem, vmem, smem],
                out_specs=(vmem, free),
                scratch_shapes=[
                    pltpu.VMEM((2 * BEAMS, TILE, channels), bf16),
                    pltpu.VMEM((context // TILE, TILE, channels), bf16),
                    dma,
                ],
                compiler_params=pltpu.CompilerParams(vmem_limit_bytes=24 * 1024 * 1024),
                name="place",
            )(recv.reshape(-1, TILE, channels), raw, new_kv, meta)
            return projected, cache.reshape(BEAMS, context, channels)

    def resent():
        with jax.named_scope("full"):
            whole = pl.pallas_call(
                full_kernel,
                out_shape=jax.ShapeDtypeStruct((SPAN, MOST * context, channels), bf16),
                in_specs=[hbm] * 3,
                out_specs=free,
                scratch_shapes=[
                    pltpu.SMEM(page_tables.shape, jnp.int32),
                    pltpu.SMEM(parents.shape, jnp.int32),
                    pltpu.VMEM(kv_pool.shape, bf16),
                    pltpu.VMEM((SPAN, MOST * context, channels), bf16),
                    dma((2,)), dma, dma((MOST,)),
                    dma((SPAN * MOST,)), dma((SPAN * MOST,)),
                ],
                compiler_params=pltpu.CompilerParams(
                    collective_id=1, has_side_effects=True, vmem_limit_bytes=24 * 1024 * 1024
                ),
                name="full",
            )(*pinned(kv_pool, page_tables, parents))
        with jax.named_scope("finish"):
            return pl.pallas_call(
                finish_kernel,
                out_shape=(
                    jax.ShapeDtypeStruct(queries.shape, bf16),
                    jax.ShapeDtypeStruct((BEAMS, context, channels), bf16),
                ),
                in_specs=[vmem, vmem, hbm, hbm, hbm],
                out_specs=(vmem, hbm),
                scratch_shapes=[
                    pltpu.VMEM(new_kv.shape, bf16),
                    pltpu.SMEM(lengths.shape, jnp.int32),
                    pltpu.SMEM(parents.shape, jnp.int32),
                    pltpu.VMEM((2 * BEAMS, PAGE, channels), bf16),
                    pltpu.VMEM((PAGE, channels), bf16),
                    dma((3,)), dma,
                ],
                compiler_params=pltpu.CompilerParams(vmem_limit_bytes=24 * 1024 * 1024),
                name="finish",
            )(whole.reshape(BEAMS, context, channels), raw, new_kv, lengths, parents)

    return lax.switch(over[0], (placed, resent))


def solution(mesh):
    in_specs = (
        P(None, "dp", "tensor"),
        P(None, "dp", "tensor"),
        P("dp", None, "tensor"),
        P("dp", None),
        P(),
        P(),
        P("tensor", None),
    )
    out_specs = (P(None, "dp", "tensor"), P("dp", None, "tensor"))
    body = functools.partial(local, mesh.shape["tensor"])
    return jax.shard_map(body, mesh=mesh, in_specs=in_specs, out_specs=out_specs, check_vma=False)
```

```python
import functools

import jax
import jax.numpy as jnp
from jax import lax
from jax.experimental import pallas as pl
from jax.experimental.pallas import tpu as pltpu
from jax.sharding import PartitionSpec as P

HD = 128
SPAN = 4
MOST = 2
BEAMS = 8
STEPS = 4
PAGE = 128
PAGES = 8
GRAIN = 32
PER_CHILD = 32
PER_PAGE = PAGE // GRAIN
TILE = 16
VIA = 36
MORE = 18
REST = 40
LEFT = 12
FIRST = VIA + MORE
LINK = FIRST + REST
META = 7
MESH = pl.DeviceIdType.MESH


def grains(length):
    return (length + (GRAIN - 1)) // GRAIN


def choose(values, index):
    out = values[0]
    for at in range(1, len(values)):
        out = jnp.where(index == at, values[at], out)
    return out


def ring_plan(parents, lengths, ring):
    flows = [[jnp.int32(0)] * SPAN for _ in range(SPAN)]
    for target in range(SPAN):
        seen = []
        for child in range(BEAMS):
            parent = parents[(ring * SPAN + target) * BEAMS + child]
            count = grains(lengths[parent])
            for other in seen:
                count = jnp.where(parent == other, 0, count)
            seen.append(parent)
            source = (parent >> 3) & (SPAN - 1)
            for at in range(SPAN):
                if at != target:
                    ahead = (target - at) % SPAN
                    flows[at][ahead] = flows[at][ahead] + jnp.where(source == at, count, 0)
    up = [flow[1] for flow in flows]
    far = [flow[2] for flow in flows]
    down = [flow[3] for flow in flows]
    via_up = [jnp.minimum(count >> 1, VIA) for count in far]
    for at in range(SPAN):
        via_down = [far[i] - via_up[i] for i in range(SPAN)]
        nxt, prv = (at + 1) % SPAN, (at - 1) % SPAN
        load_up = jnp.maximum(up[at] + via_up[prv], up[nxt] + via_up[nxt])
        load_down = jnp.maximum(down[at] + via_down[nxt], down[prv] + via_down[prv])
        best = (load_down + far[at] - load_up) >> 1
        via_up[at] = jnp.minimum(jnp.maximum(best, jnp.maximum(far[at] - VIA, 0)), jnp.minimum(far[at], VIA))
    via_down = [far[i] - via_up[i] for i in range(SPAN)]
    return up, down, via_up, via_down


def heaviest(plan):
    up, down, via_up, via_down = plan
    out = jnp.int32(0)
    for at in range(SPAN):
        load_up = up[at] + via_up[at] + via_up[(at - 1) % SPAN]
        load_down = down[at] + via_down[at] + via_down[(at + 1) % SPAN]
        out = jnp.maximum(out, jnp.maximum(load_up, load_down))
    return out


def slots_of_children(parents, me):
    taken = [jnp.int32(0) for _ in range(SPAN)]
    slots, owners = [], []
    for child in range(BEAMS):
        parent = parents[me * BEAMS + child]
        apart = jnp.bitwise_and(parent // BEAMS - me, SPAN - 1)
        slot = jnp.int32(0)
        for distance in range(SPAN):
            hit = apart == distance
            slot = jnp.where(hit, distance * MOST + taken[distance], slot)
            taken[distance] = taken[distance] + hit.astype(jnp.int32)
        slots.append(slot)
        owners.append(parent)
    return slots, owners


def served_beams(parents, me, target):
    count = jnp.int32(0)
    beams = [jnp.int32(0) for _ in range(MOST)]
    for child in range(BEAMS):
        parent = parents[target * BEAMS + child]
        hit = parent // BEAMS == me
        for rank in range(MOST):
            beams[rank] = jnp.where(hit & (count == rank), parent % BEAMS, beams[rank])
        count = count + hit.astype(jnp.int32)
    return beams


def exchange_kernel(
    q_hbm, new_hbm, pool_ref, table_hbm, len_hbm, par_hbm, w_ref,
    recv_ref, proj_ref, left_ref, meta_ref, over_ref,
    q_ref, new_ref, table_ref, len_ref, par_ref,
    pool_v, w_v, stage, first_send, first_recv, rest_send, left_send, q_send, q_recv, att, p_send, p_recv, r_send, lens, beams,
    in_sem, pool_sem, w_sem, own_sem, land_sem, qs_sem, qr_sem, bs_sem, br_sem, ps_sem, pr_sem, rs_sem, rr_sem, here_sem,
):
    me = lax.axis_index("dp")
    mine = lax.axis_index("tensor")
    shards = lax.axis_size("tensor")
    y = lax.rem(me, SPAN)
    base = me - y
    context = stage.shape[1] * GRAIN // MOST
    rings = lax.axis_size("dp") // SPAN
    wide = q_hbm.shape[2]
    heads = wide // HD
    rows = MOST * STEPS

    def peer(distance):
        return base + lax.rem(y + distance, SPAN)

    barrier = pltpu.get_barrier_semaphore()
    for distance in range(1, SPAN):
        pl.semaphore_signal(barrier, inc=1, device_id={"dp": peer(distance)}, device_id_type=MESH)
    for other in range(1, shards):
        @pl.when(mine + other < shards)
        def _(other=other):
            pl.semaphore_signal(barrier, inc=1, device_id={"tensor": mine + other}, device_id_type=MESH)
    in_copies = []
    operands = ((par_hbm, par_ref), (q_hbm, q_ref), (new_hbm, new_ref), (table_hbm, table_ref), (len_hbm, len_ref))
    for at, (source, target) in enumerate(operands):
        copy = pltpu.make_async_copy(source, target, in_sem.at[at])
        copy.start()
        in_copies.append(copy)
    quarter = pool_v.shape[0] // 4
    pool_copies = []
    for at in range(4):
        span = pl.ds(at * quarter, quarter)
        copy = pltpu.make_async_copy(pool_ref.at[span], pool_v.at[span], pool_sem.at[at])
        copy.start()
        pool_copies.append(copy)
    for copy in in_copies:
        copy.wait()

    slots, owners = slots_of_children(par_ref, me)
    plan = ring_plan(par_ref, len_ref, me >> 2)
    up, down, via_up, via_down = plan
    row = lax.broadcasted_iota(jnp.int32, (SPAN * rows, BEAMS), 0)
    col = lax.broadcasted_iota(jnp.int32, (SPAN * rows, BEAMS), 1)
    slot_at = jnp.zeros_like(col)
    for child in range(BEAMS):
        slot_at = jnp.where(col == child, slots[child], slot_at)
    q_sorted = jnp.zeros((SPAN * rows, wide), jnp.float32)
    new_sorted = jnp.zeros((SPAN * rows, 2 * HD), jnp.float32)
    for step in range(STEPS):
        pick = jnp.where((row // STEPS == slot_at) & (row % STEPS == step), 1.0, 0.0).astype(jnp.bfloat16)
        q_sorted += jnp.dot(pick, q_ref[step], preferred_element_type=jnp.float32)
        new_sorted += jnp.dot(pick, new_ref[step], preferred_element_type=jnp.float32)
    both = jnp.concatenate([q_sorted, new_sorted], axis=1)
    half = both.shape[1] // 2
    for distance in range(SPAN):
        part = both[distance * rows:(distance + 1) * rows]
        part = jnp.concatenate([part[:, :half], part[:, half:]], axis=0).astype(jnp.bfloat16)
        if distance == 0:
            q_recv[0] = part
        else:
            q_send[distance] = part

    pl.semaphore_wait(barrier, SPAN - 1 + mine)
    for other in range(1, shards):
        @pl.when(mine >= other)
        def _(other=other):
            pl.semaphore_signal(here_sem, inc=1, device_id={"tensor": mine - other}, device_id_type=MESH)

    q_copies = []
    for distance in range(1, SPAN):
        copy = pltpu.make_async_remote_copy(
            src_ref=q_send.at[distance], dst_ref=q_recv.at[distance],
            send_sem=qs_sem.at[distance], recv_sem=qr_sem.at[distance],
            device_id={"dp": peer(distance)}, device_id_type=MESH,
        )
        copy.start()
        q_copies.append(copy)

    flows = {}
    for ahead in range(SPAN):
        served = served_beams(par_ref, me, peer(ahead))
        distance = (SPAN - ahead) % SPAN
        held = [len_ref[me * BEAMS + served[rank]] for rank in range(MOST)]
        for rank in range(MOST):
            beams[distance * MOST + rank] = served[rank]
            lens[distance * MOST + rank] = held[rank]
        flows[ahead] = (served[0], served[1], grains(held[0]))

    def grain_at(flow, number):
        first, second, cut = flow
        later = number >= cut
        number = jnp.where(later, number - cut, number)
        number = jnp.minimum(jnp.maximum(number, 0), PER_CHILD - 1)
        return table_ref[jnp.where(later, second, first), number >> 2] * PER_PAGE + (number & (PER_PAGE - 1))

    sides = (
        (flows[1], choose(via_up, y), jnp.int32(0), choose(via_up, (y - 1) & 3), peer(1)),
        (flows[3], choose(via_down, y), choose(via_up, y), choose(via_down, (y + 1) & 3), peer(3)),
    )
    for copy in pool_copies:
        copy.wait()
    b_copies = []
    cuts = (0, 8, VIA, FIRST)
    for part in range(3):
        for side, (flow, mine_via, skip, _, target) in enumerate(sides):
            def put(at, carry, side=side, flow=flow, mine_via=mine_via, skip=skip):
                for at in (2 * at, 2 * at + 1):
                    far = at < mine_via
                    chosen = tuple(jnp.where(far, one, two) for one, two in zip(flows[2], flow))
                    number = jnp.where(far, skip + at, at - mine_via)
                    first_send[side, at] = pool_v[grain_at(chosen, number)]
                return carry

            lax.fori_loop(cuts[part] // 2, cuts[part + 1] // 2, put, 0)
            span = pl.ds(cuts[part], cuts[part + 1] - cuts[part])
            copy = pltpu.make_async_remote_copy(
                src_ref=first_send.at[side, span], dst_ref=first_recv.at[side, span],
                send_sem=bs_sem.at[side * 4 + part], recv_sem=br_sem.at[side * 4 + part],
                device_id={"dp": target}, device_id_type=MESH,
            )
            copy.start()
            b_copies.append(copy)
    w_copies = []
    for block in range(shards):
        copy = pltpu.make_async_copy(w_ref.at[:, pl.ds(block * wide, wide)], w_v.at[block], w_sem.at[block])
        copy.start()
        w_copies.append(copy)

    def put_all(index, carry):
        slot = index // PAGES
        page = table_ref[beams[slot], index % PAGES]
        at = (index % (MOST * PAGES)) * PER_PAGE
        stage[index // (MOST * PAGES), pl.ds(at, PER_PAGE)] = pool_v[pl.ds(page * PER_PAGE, PER_PAGE)]
        return carry

    lax.fori_loop(0, SPAN * MOST * PAGES, put_all, 0)
    own_copy = pltpu.make_async_copy(stage.at[0], recv_ref.at[pl.ds(2 * LINK, MOST * PER_CHILD)], own_sem.at[0])
    own_copy.start()

    for copy in q_copies:
        copy.wait()

    def attend(distance, carry):
        message = q_recv[distance].astype(jnp.float32)
        message = jnp.concatenate([message[:rows], message[rows:]], axis=1)
        q_rows = jnp.concatenate([message[:, h * HD:(h + 1) * HD] for h in range(heads)], axis=0).astype(jnp.bfloat16)
        fresh = message[:, wide:].astype(jnp.bfloat16)
        old_len = lens[distance * MOST]
        last_len = lens[distance * MOST + 1]
        contract = (((1,), (1,)), ((), ()))
        scale = HD ** -0.5
        half = MOST * PER_CHILD // 2
        keys = [stage[distance, pl.ds(rank * half, half), :, 0:HD].reshape(context, HD) for rank in range(MOST)]
        scores = [lax.dot_general(q_rows, key, contract, preferred_element_type=jnp.float32) for key in keys]
        rank_at = lax.broadcasted_iota(jnp.int32, scores[0].shape, 0) // STEPS % MOST
        scores = jnp.where(rank_at == 0, scores[0], scores[1]) * scale
        fresh_scores = lax.dot_general(q_rows, fresh[:, :HD], contract, preferred_element_type=jnp.float32) * scale
        position = lax.broadcasted_iota(jnp.int32, scores.shape, 1)
        limit = jnp.where(rank_at == 0, old_len, last_len)
        scores = jnp.where(position < limit, scores, -1e30)
        f_row = lax.broadcasted_iota(jnp.int32, fresh_scores.shape, 0)
        f_col = lax.broadcasted_iota(jnp.int32, fresh_scores.shape, 1)
        seen = (f_row // STEPS % MOST == f_col // STEPS) & (f_col % STEPS <= f_row % STEPS)
        fresh_scores = jnp.where(seen, fresh_scores, -1e30)
        top = jnp.maximum(jnp.max(scores, axis=1, keepdims=True), jnp.max(fresh_scores, axis=1, keepdims=True))
        exp_old = jnp.exp(scores - top)
        exp_new = jnp.exp(fresh_scores - top)
        total = jnp.sum(exp_old, axis=1, keepdims=True) + jnp.sum(exp_new, axis=1, keepdims=True)
        share = 1.0 / total
        w_old = (exp_old * share).astype(jnp.bfloat16)
        w_new = (exp_new * share).astype(jnp.bfloat16)
        values = [stage[distance, pl.ds(rank * half, half), :, HD:2 * HD].reshape(context, HD) for rank in range(MOST)]
        out = [jnp.dot(w_old, value, preferred_element_type=jnp.float32) for value in values]
        out = jnp.where(rank_at[:, :HD] == 0, out[0], out[1])
        out += jnp.dot(w_new, fresh[:, HD:], preferred_element_type=jnp.float32)
        out = jnp.concatenate([out[h * rows:(h + 1) * rows] for h in range(heads)], axis=1)
        att[pl.ds(pl.multiple_of(distance * rows, rows), rows), :] = out
        return carry

    lax.fori_loop(0, SPAN, attend, 0)
    for copy in b_copies[:4]:
        copy.wait()
    more_copies = b_copies[4:]
    b_copies = []
    for side, (flow, mine_via, _, passed, target) in enumerate(sides):
        def put_passed(at, carry, side=side, flow=flow, mine_via=mine_via, passed=passed):
            for at in (2 * at, 2 * at + 1):
                here = pool_v[grain_at(flow, FIRST - mine_via + at - passed)]
                rest_send[side, at] = jnp.where(at < passed, first_recv[side, at], here)
            return carry

        def put_rest(at, carry, side=side, flow=flow, mine_via=mine_via, passed=passed):
            for at in (2 * at, 2 * at + 1):
                rest_send[side, at] = pool_v[grain_at(flow, FIRST - mine_via + at - passed)]
            return carry

        lax.fori_loop(0, VIA // 2, put_passed, 0)
        lax.fori_loop(VIA // 2, REST // 2, put_rest, 0)
        copy = pltpu.make_async_remote_copy(
            src_ref=rest_send.at[side], dst_ref=recv_ref.at[pl.ds(side * LINK + FIRST, REST)],
            send_sem=bs_sem.at[side * 4 + 3], recv_sem=br_sem.at[side * 4 + 3],
            device_id={"dp": target}, device_id_type=MESH,
        )
        copy.start()
        b_copies.append(copy)
    attended = att[...].astype(jnp.bfloat16)
    for copy in w_copies:
        copy.wait()

    def p_copy(other):
        return pltpu.make_async_remote_copy(
            src_ref=p_send.at[other], dst_ref=p_recv.at[other],
            send_sem=ps_sem.at[other], recv_sem=pr_sem.at[other],
            device_id={"tensor": lax.rem(mine + other, shards)}, device_id_type=MESH,
        )

    def project(other, carry):
        product = jnp.dot(attended, w_v[lax.rem(mine + other, shards)], preferred_element_type=jnp.float32)
        p_send[other] = product.astype(jnp.bfloat16)
        p_copy(other).start()
        return carry

    @pl.when(mine < shards - 1)
    def _():
        pl.semaphore_wait(here_sem, shards - 1 - mine)

    lax.fori_loop(1, shards, project, 0)
    own = jnp.dot(attended, w_v[mine], preferred_element_type=jnp.float32)

    load = lax.fori_loop(
        0, rings, lambda ring, load: jnp.maximum(load, heaviest(ring_plan(par_ref, len_ref, ring))), jnp.int32(0)
    )
    over_ref[0] = jnp.where(load > LINK, 1, 0) + jnp.where(load > LINK + LEFT, 1, 0)
    for side, (flow, mine_via, _, passed, _) in enumerate(sides):
        def put_left(at, carry, side=side, flow=flow, mine_via=mine_via, passed=passed):
            left_send[side, at] = pool_v[grain_at(flow, LINK - mine_via - passed + at)]
            return carry

        lax.fori_loop(0, LEFT, put_left, 0)
    copy = pltpu.make_async_copy(left_send, left_ref, land_sem.at[2])
    copy.start()
    b_copies.append(copy)
    for child in range(BEAMS):
        slot = slots[child]
        distance = slot >> 1
        length = len_ref[owners[child]]
        before = jnp.int32(0)
        for other in range(BEAMS):
            if other != child:
                mate = (slots[other] >> 1 == distance) & (slots[other] < slot)
                differs = owners[other] != owners[child]
                before = jnp.where(mate & differs, grains(len_ref[owners[other]]), before)
        from_up = choose(via_up, (y - 1) & 3), choose(via_up, (y + 2) & 3)
        from_down = choose(via_down, (y + 1) & 3), choose(via_down, (y + 2) & 3)
        near_via = jnp.where(distance == 3, from_up[0], from_down[0])
        near_pass = jnp.where(distance == 3, from_up[1], from_down[1])
        near_base = jnp.where(distance == 3, 0, LINK)
        split = jnp.where(distance == 2, from_up[1], FIRST - near_via) - before
        split = jnp.minimum(jnp.maximum(split, 0), PER_CHILD)
        start = jnp.where(distance == 2, FIRST + before, near_base + near_via + before)
        again = jnp.where(distance == 2, LINK + FIRST + before + split - from_up[1], start + split + near_pass)
        near = jnp.where(distance == 2, False, distance != 0)
        until = LINK - near_via - near_pass - before
        until = jnp.where(near, jnp.minimum(jnp.maximum(until, 0), PER_CHILD), PER_CHILD)
        third = jnp.where(distance == 3, 0, LEFT) + near_via + near_pass + before + until - LINK
        stays = distance == 0
        meta_ref[child * META] = length
        meta_ref[child * META + 1] = jnp.where(stays, 2 * LINK + (slot & 1) * PER_CHILD, start)
        meta_ref[child * META + 2] = jnp.where(stays, PER_CHILD, split)
        meta_ref[child * META + 3] = jnp.where(stays, 0, again)
        meta_ref[child * META + 4] = until
        meta_ref[child * META + 5] = jnp.where(near, third, 0)
        meta_ref[child * META + 6] = slot
    for copy in more_copies:
        copy.wait()
    for side in range(2):
        copy = pltpu.make_async_copy(first_recv.at[side], recv_ref.at[pl.ds(side * LINK, FIRST)], land_sem.at[side])
        copy.start()
        b_copies.append(copy)

    def gather_sums(other, total):
        p_copy(other).wait()
        return total + p_recv[other].astype(jnp.float32)

    summed = lax.fori_loop(1, shards, gather_sums, own)
    half = wide // 2
    r_copies = []
    for distance in range(SPAN):
        part = summed[distance * rows:(distance + 1) * rows]
        r_send[distance] = jnp.concatenate([part[:, :half], part[:, half:]], axis=0).astype(jnp.bfloat16)
        if distance == 0:
            copy = pltpu.make_async_copy(r_send.at[0], proj_ref.at[0], own_sem.at[1])
        else:
            copy = pltpu.make_async_remote_copy(
                src_ref=r_send.at[distance], dst_ref=proj_ref.at[distance],
                send_sem=rs_sem.at[distance], recv_sem=rr_sem.at[distance],
                device_id={"dp": peer(SPAN - distance)}, device_id_type=MESH,
            )
        copy.start()
        r_copies.append(copy)
    for copy in r_copies:
        copy.wait()
    for copy in b_copies:
        copy.wait()
    own_copy.wait()


def full_kernel(
    pool_ref, table_hbm, par_hbm, recv_ref,
    table_ref, par_ref, pool_v, stage,
    in_sem, pool_sem, own_sem, bs_sem, br_sem,
):
    me = lax.axis_index("dp")
    y = lax.rem(me, SPAN)
    base = me - y
    context = stage.shape[1] // MOST

    def peer(distance):
        return base + lax.rem(y + distance, SPAN)

    barrier = pltpu.get_barrier_semaphore()
    for distance in range(1, SPAN):
        pl.semaphore_signal(barrier, inc=1, device_id={"dp": peer(distance)}, device_id_type=MESH)
    in_copies = []
    for at, (source, target) in enumerate(((par_hbm, par_ref), (table_hbm, table_ref))):
        copy = pltpu.make_async_copy(source, target, in_sem.at[at])
        copy.start()
        in_copies.append(copy)
    pool_copy = pltpu.make_async_copy(pool_ref, pool_v, pool_sem)
    pool_copy.start()
    for copy in in_copies:
        copy.wait()
    pl.semaphore_wait(barrier, SPAN - 1)
    pool_copy.wait()
    copies = []
    for distance in (2, 1, 3, 0):
        served = served_beams(par_ref, me, peer(SPAN - distance))
        for rank in range(MOST):
            beam = served[rank]

            def put(index, carry, distance=distance, rank=rank, beam=beam):
                at = pl.multiple_of(rank * context + index * PAGE, PAGE)
                stage[distance, pl.ds(at, PAGE), :] = pool_v[table_ref[beam, index]]
                return carry

            lax.fori_loop(0, context // PAGE, put, 0)
            span = pl.ds(rank * context, context)
            if distance == 0:
                copy = pltpu.make_async_copy(stage.at[0, span], recv_ref.at[0, span], own_sem.at[rank])
            else:
                copy = pltpu.make_async_remote_copy(
                    src_ref=stage.at[distance, span], dst_ref=recv_ref.at[distance, span],
                    send_sem=bs_sem.at[distance * MOST + rank], recv_sem=br_sem.at[distance * MOST + rank],
                    device_id={"dp": peer(SPAN - distance)}, device_id_type=MESH,
                )
            copy.start()
            copies.append(copy)
    for copy in copies:
        copy.wait()


def finish_kernel(recv_ref, raw_ref, new_hbm, len_hbm, par_hbm, proj_ref, cache_ref, new_ref, len_ref, par_ref, edge, zeros, in_sem, out_sem):
    me = lax.axis_index("dp")
    pages = recv_ref.shape[1] // PAGE
    operands = ((par_hbm, par_ref), (len_hbm, len_ref), (new_hbm, new_ref))
    in_copies = [pltpu.make_async_copy(source, target, in_sem.at[at]) for at, (source, target) in enumerate(operands)]
    for copy in in_copies:
        copy.start()
    zeros[...] = jnp.zeros_like(zeros)
    for copy in in_copies:
        copy.wait()
    slots, owners = slots_of_children(par_ref, me)
    fresh = [new_ref[step].astype(jnp.float32) for step in range(STEPS)]
    for child in range(BEAMS):
        slot = slots[child]
        length = len_ref[owners[child]]
        first = length // PAGE
        last = (length + STEPS - 1) // PAGE

        def whole(index, carry, child=child, slot=slot):
            span = pl.ds(pl.multiple_of(index * PAGE, PAGE), PAGE)
            pltpu.make_async_copy(recv_ref.at[slot, span], cache_ref.at[child, span], out_sem).start()
            return carry

        def clear(index, carry, child=child):
            span = pl.ds(pl.multiple_of(index * PAGE, PAGE), PAGE)
            pltpu.make_async_copy(zeros, cache_ref.at[child, span], out_sem).start()
            return carry

        def fix(index, carry, child=child, slot=slot, length=length, first=first):
            at = pl.multiple_of(index * PAGE, PAGE)
            position = at + lax.broadcasted_iota(jnp.int32, (PAGE, 2 * HD), 0)
            page = recv_ref[slot, pl.ds(at, PAGE), :].astype(jnp.float32)
            page = jnp.where(position < length, page, 0.0)
            for step in range(STEPS):
                page = jnp.where(position == length + step, fresh[step][child:child + 1], page)
            edge[child * 2 + index - first] = page.astype(jnp.bfloat16)
            pltpu.make_async_copy(edge.at[child * 2 + index - first], cache_ref.at[child, pl.ds(at, PAGE)], out_sem).start()
            return carry

        lax.fori_loop(0, first, whole, 0)
        lax.fori_loop(last + 1, pages, clear, 0)
        lax.fori_loop(first, last + 1, fix, 0)

    rows = MOST * STEPS
    raw = []
    for distance in range(SPAN):
        part = raw_ref[distance].astype(jnp.float32)
        raw.append(jnp.concatenate([part[:rows], part[rows:]], axis=1))
    raw = jnp.concatenate(raw, axis=0).astype(jnp.bfloat16)
    row = lax.broadcasted_iota(jnp.int32, (BEAMS, SPAN * rows), 0)
    col = lax.broadcasted_iota(jnp.int32, (BEAMS, SPAN * rows), 1)
    slot_at = jnp.zeros_like(col)
    for child in range(BEAMS):
        slot_at = jnp.where(row == child, slots[child], slot_at)
    for step in range(STEPS):
        pick = jnp.where(col == slot_at * STEPS + step, 1.0, 0.0).astype(jnp.bfloat16)
        proj_ref[step] = jnp.dot(pick, raw, preferred_element_type=jnp.float32).astype(jnp.bfloat16)
    pltpu.make_async_copy(recv_ref, cache_ref, out_sem).wait()


def left_kernel(left_ref, got_ref, send_sem, recv_sem):
    me = lax.axis_index("dp")
    y = lax.rem(me, SPAN)
    targets = [me - y + lax.rem(y + ahead, SPAN) for ahead in (1, SPAN - 1)]
    barrier = pltpu.get_barrier_semaphore()
    for target in targets:
        pl.semaphore_signal(barrier, inc=1, device_id={"dp": target}, device_id_type=MESH)
    pl.semaphore_wait(barrier, 2)
    copies = []
    for side, target in enumerate(targets):
        copy = pltpu.make_async_remote_copy(
            src_ref=left_ref.at[side], dst_ref=got_ref.at[side],
            send_sem=send_sem.at[side], recv_sem=recv_sem.at[side],
            device_id={"dp": target}, device_id_type=MESH,
        )
        copy.start()
        copies.append(copy)
    for copy in copies:
        copy.wait()


def place_kernel(with_left, recv_ref, raw_ref, new_ref, meta_ref, *refs):
    left_ref = refs[0] if with_left else None
    proj_ref, cache_ref, edge, zeros, out_sem = refs[-5:]
    total = recv_ref.shape[0]
    zeros[...] = jnp.zeros_like(zeros)
    fresh = [new_ref[step].astype(jnp.float32) for step in range(STEPS)]
    slots = [meta_ref[child * META + 6] for child in range(BEAMS)]
    per_child = cache_ref.shape[1]
    scale = GRAIN // TILE
    for child in range(BEAMS):
        length, start, split, again, until, third = (meta_ref[child * META + at] for at in range(6))
        first = length // TILE
        last = (length + STEPS - 1) // TILE
        until = jnp.minimum(until * scale, first) if with_left else first
        split = jnp.minimum(split * scale, until)

        def move(source, source_at, at, count, child=child):
            @pl.when(count > 0)
            def _():
                pltpu.make_async_copy(
                    source.at[pl.ds(source_at, count)], cache_ref.at[child, pl.ds(at, count)], out_sem
                ).start()

        move(recv_ref, start * scale, 0, split)
        move(recv_ref, again * scale, split, until - split)
        if with_left:
            move(left_ref, third * scale, until, first - until)
        move(zeros, 0, last + 1, per_child - 1 - last)
    for child in range(BEAMS):
        length, start, split, again, until, third = (meta_ref[child * META + at] for at in range(6))
        first = length // TILE
        last = (length + STEPS - 1) // TILE

        def fix(
            index, carry, child=child, length=length, first=first, start=start * scale, split=split * scale,
            again=again * scale, until=until * scale, third=third * scale,
        ):
            position = index * TILE + lax.broadcasted_iota(jnp.int32, (TILE, 2 * HD), 0)
            at = jnp.minimum(jnp.where(index < split, start + index, again + index - split), total - 1)
            part = recv_ref[at].astype(jnp.float32)
            if with_left:
                at = jnp.minimum(jnp.maximum(third + index - until, 0), left_ref.shape[0] - 1)
                part = jnp.where(index < until, part, left_ref[at].astype(jnp.float32))
            part = jnp.where(position < length, part, 0.0)
            for step in range(STEPS):
                part = jnp.where(position == length + step, fresh[step][child:child + 1], part)
            edge[child * 2 + index - first] = part.astype(jnp.bfloat16)
            pltpu.make_async_copy(edge.at[child * 2 + index - first], cache_ref.at[child, index], out_sem).start()
            return carry

        lax.fori_loop(first, last + 1, fix, 0)

    rows = MOST * STEPS
    raw = []
    for distance in range(SPAN):
        part = raw_ref[distance].astype(jnp.float32)
        raw.append(jnp.concatenate([part[:rows], part[rows:]], axis=1))
    raw = jnp.concatenate(raw, axis=0).astype(jnp.bfloat16)
    row = lax.broadcasted_iota(jnp.int32, (BEAMS, SPAN * rows), 0)
    col = lax.broadcasted_iota(jnp.int32, (BEAMS, SPAN * rows), 1)
    slot_at = jnp.zeros_like(col)
    for child in range(BEAMS):
        slot_at = jnp.where(row == child, slots[child], slot_at)
    for step in range(STEPS):
        pick = jnp.where(col == slot_at * STEPS + step, 1.0, 0.0).astype(jnp.bfloat16)
        proj_ref[step] = jnp.dot(pick, raw, preferred_element_type=jnp.float32).astype(jnp.bfloat16)
    pltpu.make_async_copy(cache_ref, cache_ref, out_sem).wait()


def local(shards, queries, new_kv, kv_pool, page_tables, lengths, parents, out_weight):
    wide = queries.shape[2]
    channels = kv_pool.shape[2]
    context = page_tables.shape[1] * kv_pool.shape[1]
    rows = MOST * STEPS
    vmem = pl.BlockSpec(memory_space=pltpu.VMEM)
    smem = pl.BlockSpec(memory_space=pltpu.SMEM)
    hbm = pl.BlockSpec(memory_space=pltpu.HBM)
    free = pl.BlockSpec(memory_space=pl.ANY)
    dma = pltpu.SemaphoreType.DMA
    bf16 = jnp.bfloat16

    def pinned(*operands):
        return [pltpu.with_memory_space_constraint(operand, pltpu.HBM) for operand in operands]

    grain_pool = kv_pool.reshape(-1, GRAIN, channels)
    with jax.named_scope("exchange"):
        recv, raw, left, meta, over = pl.pallas_call(
            exchange_kernel,
            out_shape=(
                jax.ShapeDtypeStruct((2 * LINK + MOST * PER_CHILD, GRAIN, channels), bf16),
                jax.ShapeDtypeStruct((SPAN, 2 * rows, wide // 2), bf16),
                jax.ShapeDtypeStruct((2, LEFT, GRAIN, channels), bf16),
                jax.ShapeDtypeStruct((BEAMS * META,), jnp.int32),
                jax.ShapeDtypeStruct((1,), jnp.int32),
            ),
            in_specs=[hbm] * 7,
            out_specs=(free, free, free, smem, smem),
            scratch_shapes=[
                pltpu.VMEM(queries.shape, bf16),
                pltpu.VMEM(new_kv.shape, bf16),
                pltpu.SMEM(page_tables.shape, jnp.int32),
                pltpu.SMEM(lengths.shape, jnp.int32),
                pltpu.SMEM(parents.shape, jnp.int32),
                pltpu.VMEM(grain_pool.shape, bf16),
                pltpu.VMEM((shards, out_weight.shape[0], wide), bf16),
                pltpu.VMEM((SPAN, MOST * PER_CHILD, GRAIN, channels), bf16),
                pltpu.VMEM((2, FIRST, GRAIN, channels), bf16),
                pltpu.VMEM((2, FIRST, GRAIN, channels), bf16),
                pltpu.VMEM((2, REST, GRAIN, channels), bf16),
                pltpu.VMEM((2, LEFT, GRAIN, channels), bf16),
                pltpu.VMEM((SPAN, 2 * rows, (wide + channels) // 2), bf16),
                pltpu.VMEM((SPAN, 2 * rows, (wide + channels) // 2), bf16),
                pltpu.VMEM((SPAN * rows, wide), jnp.float32),
                pltpu.VMEM((shards, SPAN * rows, wide), bf16),
                pltpu.VMEM((shards, SPAN * rows, wide), bf16),
                pltpu.VMEM((SPAN, 2 * rows, wide // 2), bf16),
                pltpu.SMEM((SPAN * MOST,), jnp.int32),
                pltpu.SMEM((SPAN * MOST,), jnp.int32),
                dma((5,)), dma((4,)), dma((shards,)), dma((2,)), dma((3,)),
                dma((SPAN,)), dma((SPAN,)),
                dma((8,)), dma((8,)),
                dma((shards,)), dma((shards,)),
                dma((SPAN,)), dma((SPAN,)),
                pltpu.SemaphoreType.REGULAR,
            ],
            compiler_params=pltpu.CompilerParams(
                collective_id=0, has_side_effects=True, vmem_limit_bytes=48 * 1024 * 1024
            ),
            name="exchange",
        )(*pinned(queries, new_kv, grain_pool, page_tables, lengths, parents, out_weight))

    def place(*got):
        with jax.named_scope("place"):
            projected, cache = pl.pallas_call(
                functools.partial(place_kernel, len(got) > 0),
                out_shape=(
                    jax.ShapeDtypeStruct(queries.shape, bf16),
                    jax.ShapeDtypeStruct((BEAMS, context // TILE, TILE, channels), bf16),
                ),
                in_specs=[vmem, vmem, vmem, smem] + [vmem] * len(got),
                out_specs=(vmem, free),
                scratch_shapes=[
                    pltpu.VMEM((2 * BEAMS, TILE, channels), bf16),
                    pltpu.VMEM((context // TILE, TILE, channels), bf16),
                    dma,
                ],
                compiler_params=pltpu.CompilerParams(vmem_limit_bytes=24 * 1024 * 1024),
                name="place_left" if got else "place",
            )(recv.reshape(-1, TILE, channels), raw, new_kv, meta, *got)
            return projected, cache.reshape(BEAMS, context, channels)

    def placed():
        return place()

    def topped():
        with jax.named_scope("left"):
            got = pl.pallas_call(
                left_kernel,
                out_shape=jax.ShapeDtypeStruct(left.shape, bf16),
                in_specs=[free],
                out_specs=free,
                scratch_shapes=[dma((2,)), dma((2,))],
                compiler_params=pltpu.CompilerParams(
                    collective_id=2, has_side_effects=True, vmem_limit_bytes=4 * 1024 * 1024
                ),
                name="left",
            )(left)
        return place(got.reshape(-1, TILE, channels))

    def resent():
        with jax.named_scope("full"):
            whole = pl.pallas_call(
                full_kernel,
                out_shape=jax.ShapeDtypeStruct((SPAN, MOST * context, channels), bf16),
                in_specs=[hbm] * 3,
                out_specs=free,
                scratch_shapes=[
                    pltpu.SMEM(page_tables.shape, jnp.int32),
                    pltpu.SMEM(parents.shape, jnp.int32),
                    pltpu.VMEM(kv_pool.shape, bf16),
                    pltpu.VMEM((SPAN, MOST * context, channels), bf16),
                    dma((2,)), dma, dma((MOST,)),
                    dma((SPAN * MOST,)), dma((SPAN * MOST,)),
                ],
                compiler_params=pltpu.CompilerParams(
                    collective_id=1, has_side_effects=True, vmem_limit_bytes=24 * 1024 * 1024
                ),
                name="full",
            )(*pinned(kv_pool, page_tables, parents))
        with jax.named_scope("finish"):
            return pl.pallas_call(
                finish_kernel,
                out_shape=(
                    jax.ShapeDtypeStruct(queries.shape, bf16),
                    jax.ShapeDtypeStruct((BEAMS, context, channels), bf16),
                ),
                in_specs=[vmem, vmem, hbm, hbm, hbm],
                out_specs=(vmem, hbm),
                scratch_shapes=[
                    pltpu.VMEM(new_kv.shape, bf16),
                    pltpu.SMEM(lengths.shape, jnp.int32),
                    pltpu.SMEM(parents.shape, jnp.int32),
                    pltpu.VMEM((2 * BEAMS, PAGE, channels), bf16),
                    pltpu.VMEM((PAGE, channels), bf16),
                    dma((3,)), dma,
                ],
                compiler_params=pltpu.CompilerParams(vmem_limit_bytes=24 * 1024 * 1024),
                name="finish",
            )(whole.reshape(BEAMS, context, channels), raw, new_kv, lengths, parents)

    return lax.switch(over[0], (placed, topped, resent))


def solution(mesh):
    in_specs = (
        P(None, "dp", "tensor"),
        P(None, "dp", "tensor"),
        P("dp", None, "tensor"),
        P("dp", None),
        P(),
        P(),
        P("tensor", None),
    )
    out_specs = (P(None, "dp", "tensor"), P("dp", None, "tensor"))
    body = functools.partial(local, mesh.shape["tensor"])
    return jax.shard_map(body, mesh=mesh, in_specs=in_specs, out_specs=out_specs, check_vma=False)
```

```python
import functools

import jax
import jax.numpy as jnp
from jax import lax
from jax.experimental import pallas as pl
from jax.experimental.pallas import tpu as pltpu
from jax.sharding import PartitionSpec as P

HD = 128
SPAN = 4
MOST = 2
BEAMS = 8
STEPS = 4
PAGE = 128
PAGES = 8
GRAIN = 32
PER_CHILD = 32
PER_PAGE = PAGE // GRAIN
TILE = 16
VIA = 36
MORE = 18
REST = 46
LEFT = 12
FIRST = VIA + MORE
LINK = FIRST + REST
META = 7
MESH = pl.DeviceIdType.MESH


def grains(length):
    return (length + (GRAIN - 1)) // GRAIN


def choose(values, index):
    out = values[0]
    for at in range(1, len(values)):
        out = jnp.where(index == at, values[at], out)
    return out


def ring_plan(parents, lengths, ring):
    flows = [[jnp.int32(0)] * SPAN for _ in range(SPAN)]
    for target in range(SPAN):
        seen = []
        for child in range(BEAMS):
            parent = parents[(ring * SPAN + target) * BEAMS + child]
            count = grains(lengths[parent])
            for other in seen:
                count = jnp.where(parent == other, 0, count)
            seen.append(parent)
            source = (parent >> 3) & (SPAN - 1)
            for at in range(SPAN):
                if at != target:
                    ahead = (target - at) % SPAN
                    flows[at][ahead] = flows[at][ahead] + jnp.where(source == at, count, 0)
    up = [flow[1] for flow in flows]
    far = [flow[2] for flow in flows]
    down = [flow[3] for flow in flows]
    via_up = [jnp.minimum(count >> 1, VIA) for count in far]
    for at in range(SPAN):
        via_down = [far[i] - via_up[i] for i in range(SPAN)]
        nxt, prv = (at + 1) % SPAN, (at - 1) % SPAN
        load_up = jnp.maximum(up[at] + via_up[prv], up[nxt] + via_up[nxt])
        load_down = jnp.maximum(down[at] + via_down[nxt], down[prv] + via_down[prv])
        best = (load_down + far[at] - load_up) >> 1
        via_up[at] = jnp.minimum(jnp.maximum(best, jnp.maximum(far[at] - VIA, 0)), jnp.minimum(far[at], VIA))
    via_down = [far[i] - via_up[i] for i in range(SPAN)]
    return up, down, via_up, via_down


def heaviest(plan):
    up, down, via_up, via_down = plan
    out = jnp.int32(0)
    for at in range(SPAN):
        load_up = up[at] + via_up[at] + via_up[(at - 1) % SPAN]
        load_down = down[at] + via_down[at] + via_down[(at + 1) % SPAN]
        out = jnp.maximum(out, jnp.maximum(load_up, load_down))
    return out


def slots_of_children(parents, me):
    taken = [jnp.int32(0) for _ in range(SPAN)]
    slots, owners = [], []
    for child in range(BEAMS):
        parent = parents[me * BEAMS + child]
        apart = jnp.bitwise_and(parent // BEAMS - me, SPAN - 1)
        slot = jnp.int32(0)
        for distance in range(SPAN):
            hit = apart == distance
            slot = jnp.where(hit, distance * MOST + taken[distance], slot)
            taken[distance] = taken[distance] + hit.astype(jnp.int32)
        slots.append(slot)
        owners.append(parent)
    return slots, owners


def served_beams(parents, me, target):
    count = jnp.int32(0)
    beams = [jnp.int32(0) for _ in range(MOST)]
    for child in range(BEAMS):
        parent = parents[target * BEAMS + child]
        hit = parent // BEAMS == me
        for rank in range(MOST):
            beams[rank] = jnp.where(hit & (count == rank), parent % BEAMS, beams[rank])
        count = count + hit.astype(jnp.int32)
    return beams


def exchange_kernel(
    q_hbm, new_hbm, pool_ref, table_hbm, len_hbm, par_hbm, w_ref,
    recv_ref, proj_ref, left_ref, meta_ref, over_ref,
    q_ref, new_ref, table_ref, len_ref, par_ref,
    pool_v, w_v, stage, first_send, first_recv, rest_send, left_send, q_send, q_recv, att, p_send, p_recv, r_send, lens, beams,
    in_sem, pool_sem, w_sem, own_sem, land_sem, qs_sem, qr_sem, bs_sem, br_sem, ps_sem, pr_sem, rs_sem, rr_sem, here_sem,
):
    me = lax.axis_index("dp")
    mine = lax.axis_index("tensor")
    shards = lax.axis_size("tensor")
    y = lax.rem(me, SPAN)
    base = me - y
    context = stage.shape[1] * GRAIN // MOST
    rings = lax.axis_size("dp") // SPAN
    wide = q_hbm.shape[2]
    heads = wide // HD
    rows = MOST * STEPS

    def peer(distance):
        return base + lax.rem(y + distance, SPAN)

    barrier = pltpu.get_barrier_semaphore()
    for distance in range(1, SPAN):
        pl.semaphore_signal(barrier, inc=1, device_id={"dp": peer(distance)}, device_id_type=MESH)
    for other in range(1, shards):
        @pl.when(mine + other < shards)
        def _(other=other):
            pl.semaphore_signal(barrier, inc=1, device_id={"tensor": mine + other}, device_id_type=MESH)
    in_copies = []
    operands = ((par_hbm, par_ref), (q_hbm, q_ref), (new_hbm, new_ref), (table_hbm, table_ref), (len_hbm, len_ref))
    for at, (source, target) in enumerate(operands):
        copy = pltpu.make_async_copy(source, target, in_sem.at[at])
        copy.start()
        in_copies.append(copy)
    quarter = pool_v.shape[0] // 4
    pool_copies = []
    for at in range(4):
        span = pl.ds(at * quarter, quarter)
        copy = pltpu.make_async_copy(pool_ref.at[span], pool_v.at[span], pool_sem.at[at])
        copy.start()
        pool_copies.append(copy)
    for copy in in_copies:
        copy.wait()

    slots, owners = slots_of_children(par_ref, me)
    plan = ring_plan(par_ref, len_ref, me >> 2)
    up, down, via_up, via_down = plan
    flows = {}
    for ahead in range(SPAN):
        served = served_beams(par_ref, me, peer(ahead))
        distance = (SPAN - ahead) % SPAN
        held = [len_ref[me * BEAMS + served[rank]] for rank in range(MOST)]
        for rank in range(MOST):
            beams[distance * MOST + rank] = served[rank]
            lens[distance * MOST + rank] = held[rank]
        flows[ahead] = (served[0], served[1], grains(held[0]))

    def grain_at(flow, number):
        first, second, cut = flow
        later = number >= cut
        number = jnp.where(later, number - cut, number)
        number = jnp.minimum(jnp.maximum(number, 0), PER_CHILD - 1)
        return table_ref[jnp.where(later, second, first), number >> 2] * PER_PAGE + (number & (PER_PAGE - 1))

    sides = (
        (flows[1], choose(via_up, y), jnp.int32(0), choose(via_up, (y - 1) & 3), peer(1)),
        (flows[3], choose(via_down, y), choose(via_up, y), choose(via_down, (y + 1) & 3), peer(3)),
    )
    pl.semaphore_wait(barrier, SPAN - 1 + mine)
    for other in range(1, shards):
        @pl.when(mine >= other)
        def _(other=other):
            pl.semaphore_signal(here_sem, inc=1, device_id={"tensor": mine - other}, device_id_type=MESH)
    for copy in pool_copies:
        copy.wait()
    b_copies = []
    cuts = (0, 8, VIA, FIRST)

    def send_part(part):
        for side, (flow, mine_via, skip, _, target) in enumerate(sides):
            def put(at, carry, side=side, flow=flow, mine_via=mine_via, skip=skip):
                for at in (2 * at, 2 * at + 1):
                    far = at < mine_via
                    chosen = tuple(jnp.where(far, one, two) for one, two in zip(flows[2], flow))
                    number = jnp.where(far, skip + at, at - mine_via)
                    first_send[side, at] = pool_v[grain_at(chosen, number)]
                return carry

            lax.fori_loop(cuts[part] // 2, cuts[part + 1] // 2, put, 0)
            span = pl.ds(cuts[part], cuts[part + 1] - cuts[part])
            copy = pltpu.make_async_remote_copy(
                src_ref=first_send.at[side, span], dst_ref=first_recv.at[side, span],
                send_sem=bs_sem.at[side * 4 + part], recv_sem=br_sem.at[side * 4 + part],
                device_id={"dp": target}, device_id_type=MESH,
            )
            copy.start()
            b_copies.append(copy)

    send_part(0)

    row = lax.broadcasted_iota(jnp.int32, (SPAN * rows, BEAMS), 0)
    col = lax.broadcasted_iota(jnp.int32, (SPAN * rows, BEAMS), 1)
    slot_at = jnp.zeros_like(col)
    for child in range(BEAMS):
        slot_at = jnp.where(col == child, slots[child], slot_at)
    q_sorted = jnp.zeros((SPAN * rows, wide), jnp.float32)
    new_sorted = jnp.zeros((SPAN * rows, 2 * HD), jnp.float32)
    for step in range(STEPS):
        pick = jnp.where((row // STEPS == slot_at) & (row % STEPS == step), 1.0, 0.0).astype(jnp.bfloat16)
        q_sorted += jnp.dot(pick, q_ref[step], preferred_element_type=jnp.float32)
        new_sorted += jnp.dot(pick, new_ref[step], preferred_element_type=jnp.float32)
    both = jnp.concatenate([q_sorted, new_sorted], axis=1)
    half = both.shape[1] // 2
    for distance in range(SPAN):
        part = both[distance * rows:(distance + 1) * rows]
        part = jnp.concatenate([part[:, :half], part[:, half:]], axis=0).astype(jnp.bfloat16)
        if distance == 0:
            q_recv[0] = part
        else:
            q_send[distance] = part
    q_copies = []
    for distance in range(1, SPAN):
        copy = pltpu.make_async_remote_copy(
            src_ref=q_send.at[distance], dst_ref=q_recv.at[distance],
            send_sem=qs_sem.at[distance], recv_sem=qr_sem.at[distance],
            device_id={"dp": peer(distance)}, device_id_type=MESH,
        )
        copy.start()
        q_copies.append(copy)
    send_part(1)
    send_part(2)
    w_copies = []
    for block in range(shards):
        copy = pltpu.make_async_copy(w_ref.at[:, pl.ds(block * wide, wide)], w_v.at[block], w_sem.at[block])
        copy.start()
        w_copies.append(copy)

    def put_all(index, carry):
        slot = index // PAGES
        page = table_ref[beams[slot], index % PAGES]
        at = (index % (MOST * PAGES)) * PER_PAGE
        stage[index // (MOST * PAGES), pl.ds(at, PER_PAGE)] = pool_v[pl.ds(page * PER_PAGE, PER_PAGE)]
        return carry

    lax.fori_loop(0, SPAN * MOST * PAGES, put_all, 0)
    own_copy = pltpu.make_async_copy(stage.at[0], recv_ref.at[pl.ds(2 * LINK, MOST * PER_CHILD)], own_sem.at[0])
    own_copy.start()

    for copy in q_copies:
        copy.wait()

    def attend(distance, carry):
        message = q_recv[distance].astype(jnp.float32)
        message = jnp.concatenate([message[:rows], message[rows:]], axis=1)
        q_rows = jnp.concatenate([message[:, h * HD:(h + 1) * HD] for h in range(heads)], axis=0).astype(jnp.bfloat16)
        fresh = message[:, wide:].astype(jnp.bfloat16)
        old_len = lens[distance * MOST]
        last_len = lens[distance * MOST + 1]
        contract = (((1,), (1,)), ((), ()))
        scale = HD ** -0.5
        half = MOST * PER_CHILD // 2
        keys = [stage[distance, pl.ds(rank * half, half), :, 0:HD].reshape(context, HD) for rank in range(MOST)]
        scores = [lax.dot_general(q_rows, key, contract, preferred_element_type=jnp.float32) for key in keys]
        rank_at = lax.broadcasted_iota(jnp.int32, scores[0].shape, 0) // STEPS % MOST
        scores = jnp.where(rank_at == 0, scores[0], scores[1]) * scale
        fresh_scores = lax.dot_general(q_rows, fresh[:, :HD], contract, preferred_element_type=jnp.float32) * scale
        position = lax.broadcasted_iota(jnp.int32, scores.shape, 1)
        limit = jnp.where(rank_at == 0, old_len, last_len)
        scores = jnp.where(position < limit, scores, -1e30)
        f_row = lax.broadcasted_iota(jnp.int32, fresh_scores.shape, 0)
        f_col = lax.broadcasted_iota(jnp.int32, fresh_scores.shape, 1)
        seen = (f_row // STEPS % MOST == f_col // STEPS) & (f_col % STEPS <= f_row % STEPS)
        fresh_scores = jnp.where(seen, fresh_scores, -1e30)
        top = jnp.maximum(jnp.max(scores, axis=1, keepdims=True), jnp.max(fresh_scores, axis=1, keepdims=True))
        exp_old = jnp.exp(scores - top)
        exp_new = jnp.exp(fresh_scores - top)
        total = jnp.sum(exp_old, axis=1, keepdims=True) + jnp.sum(exp_new, axis=1, keepdims=True)
        share = 1.0 / total
        w_old = (exp_old * share).astype(jnp.bfloat16)
        w_new = (exp_new * share).astype(jnp.bfloat16)
        values = [stage[distance, pl.ds(rank * half, half), :, HD:2 * HD].reshape(context, HD) for rank in range(MOST)]
        out = [jnp.dot(w_old, value, preferred_element_type=jnp.float32) for value in values]
        out = jnp.where(rank_at[:, :HD] == 0, out[0], out[1])
        out += jnp.dot(w_new, fresh[:, HD:], preferred_element_type=jnp.float32)
        out = jnp.concatenate([out[h * rows:(h + 1) * rows] for h in range(heads)], axis=1)
        att[pl.ds(pl.multiple_of(distance * rows, rows), rows), :] = out
        return carry

    lax.fori_loop(0, SPAN, attend, 0)
    load = lax.fori_loop(
        0, rings, lambda ring, load: jnp.maximum(load, heaviest(ring_plan(par_ref, len_ref, ring))), jnp.int32(0)
    )
    over_ref[0] = jnp.where(load > LINK, 1, 0) + jnp.where(load > LINK + LEFT, 1, 0)
    for side, (flow, mine_via, _, passed, _) in enumerate(sides):
        def put_left(at, carry, side=side, flow=flow, mine_via=mine_via, passed=passed):
            left_send[side, at] = pool_v[grain_at(flow, LINK - mine_via - passed + at)]
            return carry

        lax.fori_loop(0, LEFT, put_left, 0)
    left_copy = pltpu.make_async_copy(left_send, left_ref, land_sem.at[2])
    left_copy.start()
    for child in range(BEAMS):
        slot = slots[child]
        distance = slot >> 1
        length = len_ref[owners[child]]
        before = jnp.int32(0)
        for other in range(BEAMS):
            if other != child:
                mate = (slots[other] >> 1 == distance) & (slots[other] < slot)
                differs = owners[other] != owners[child]
                before = jnp.where(mate & differs, grains(len_ref[owners[other]]), before)
        from_up = choose(via_up, (y - 1) & 3), choose(via_up, (y + 2) & 3)
        from_down = choose(via_down, (y + 1) & 3), choose(via_down, (y + 2) & 3)
        near_via = jnp.where(distance == 3, from_up[0], from_down[0])
        near_pass = jnp.where(distance == 3, from_up[1], from_down[1])
        near_base = jnp.where(distance == 3, 0, LINK)
        split = jnp.where(distance == 2, from_up[1], FIRST - near_via) - before
        split = jnp.minimum(jnp.maximum(split, 0), PER_CHILD)
        start = jnp.where(distance == 2, FIRST + before, near_base + near_via + before)
        again = jnp.where(distance == 2, LINK + FIRST + before + split - from_up[1], start + split + near_pass)
        near = jnp.where(distance == 2, False, distance != 0)
        until = LINK - near_via - near_pass - before
        until = jnp.where(near, jnp.minimum(jnp.maximum(until, 0), PER_CHILD), PER_CHILD)
        third = jnp.where(distance == 3, 0, LEFT) + near_via + near_pass + before + until - LINK
        stays = distance == 0
        meta_ref[child * META] = length
        meta_ref[child * META + 1] = jnp.where(stays, 2 * LINK + (slot & 1) * PER_CHILD, start)
        meta_ref[child * META + 2] = jnp.where(stays, PER_CHILD, split)
        meta_ref[child * META + 3] = jnp.where(stays, 0, again)
        meta_ref[child * META + 4] = until
        meta_ref[child * META + 5] = jnp.where(near, third, 0)
        meta_ref[child * META + 6] = slot
    for copy in b_copies[:4]:
        copy.wait()
    more_copies = b_copies[4:]
    b_copies = []
    for side, (flow, mine_via, _, passed, target) in enumerate(sides):
        def put_passed(at, carry, side=side, flow=flow, mine_via=mine_via, passed=passed):
            for at in (2 * at, 2 * at + 1):
                here = pool_v[grain_at(flow, FIRST - mine_via + at - passed)]
                rest_send[side, at] = jnp.where(at < passed, first_recv[side, at], here)
            return carry

        def put_rest(at, carry, side=side, flow=flow, mine_via=mine_via, passed=passed):
            for at in (2 * at, 2 * at + 1):
                rest_send[side, at] = pool_v[grain_at(flow, FIRST - mine_via + at - passed)]
            return carry

        lax.fori_loop(0, VIA // 2, put_passed, 0)
        lax.fori_loop(VIA // 2, REST // 2, put_rest, 0)
        copy = pltpu.make_async_remote_copy(
            src_ref=rest_send.at[side], dst_ref=recv_ref.at[pl.ds(side * LINK + FIRST, REST)],
            send_sem=bs_sem.at[side * 4 + 3], recv_sem=br_sem.at[side * 4 + 3],
            device_id={"dp": target}, device_id_type=MESH,
        )
        copy.start()
        b_copies.append(copy)
    attended = att[...].astype(jnp.bfloat16)
    for copy in w_copies:
        copy.wait()

    def p_copy(other):
        return pltpu.make_async_remote_copy(
            src_ref=p_send.at[other], dst_ref=p_recv.at[other],
            send_sem=ps_sem.at[other], recv_sem=pr_sem.at[other],
            device_id={"tensor": lax.rem(mine + other, shards)}, device_id_type=MESH,
        )

    def project(other, carry):
        product = jnp.dot(attended, w_v[lax.rem(mine + other, shards)], preferred_element_type=jnp.float32)
        p_send[other] = product.astype(jnp.bfloat16)
        p_copy(other).start()
        return carry

    @pl.when(mine < shards - 1)
    def _():
        pl.semaphore_wait(here_sem, shards - 1 - mine)

    lax.fori_loop(1, shards, project, 0)
    own = jnp.dot(attended, w_v[mine], preferred_element_type=jnp.float32)

    for copy in more_copies:
        copy.wait()
    for side in range(2):
        copy = pltpu.make_async_copy(first_recv.at[side], recv_ref.at[pl.ds(side * LINK, FIRST)], land_sem.at[side])
        copy.start()
        b_copies.append(copy)

    def gather_sums(other, total):
        p_copy(other).wait()
        return total + p_recv[other].astype(jnp.float32)

    summed = lax.fori_loop(1, shards, gather_sums, own)
    half = wide // 2
    r_copies = []
    for distance in range(SPAN):
        part = summed[distance * rows:(distance + 1) * rows]
        r_send[distance] = jnp.concatenate([part[:, :half], part[:, half:]], axis=0).astype(jnp.bfloat16)
        if distance == 0:
            copy = pltpu.make_async_copy(r_send.at[0], proj_ref.at[0], own_sem.at[1])
        else:
            copy = pltpu.make_async_remote_copy(
                src_ref=r_send.at[distance], dst_ref=proj_ref.at[distance],
                send_sem=rs_sem.at[distance], recv_sem=rr_sem.at[distance],
                device_id={"dp": peer(SPAN - distance)}, device_id_type=MESH,
            )
        copy.start()
        r_copies.append(copy)
    for copy in r_copies:
        copy.wait()
    for copy in b_copies:
        copy.wait()
    own_copy.wait()
    left_copy.wait()


def full_kernel(
    pool_ref, table_hbm, par_hbm, recv_ref,
    table_ref, par_ref, pool_v, stage,
    in_sem, pool_sem, own_sem, bs_sem, br_sem,
):
    me = lax.axis_index("dp")
    y = lax.rem(me, SPAN)
    base = me - y
    context = stage.shape[1] // MOST

    def peer(distance):
        return base + lax.rem(y + distance, SPAN)

    barrier = pltpu.get_barrier_semaphore()
    for distance in range(1, SPAN):
        pl.semaphore_signal(barrier, inc=1, device_id={"dp": peer(distance)}, device_id_type=MESH)
    in_copies = []
    for at, (source, target) in enumerate(((par_hbm, par_ref), (table_hbm, table_ref))):
        copy = pltpu.make_async_copy(source, target, in_sem.at[at])
        copy.start()
        in_copies.append(copy)
    pool_copy = pltpu.make_async_copy(pool_ref, pool_v, pool_sem)
    pool_copy.start()
    for copy in in_copies:
        copy.wait()
    pl.semaphore_wait(barrier, SPAN - 1)
    pool_copy.wait()
    copies = []
    for distance in (2, 1, 3, 0):
        served = served_beams(par_ref, me, peer(SPAN - distance))
        for rank in range(MOST):
            beam = served[rank]

            def put(index, carry, distance=distance, rank=rank, beam=beam):
                at = pl.multiple_of(rank * context + index * PAGE, PAGE)
                stage[distance, pl.ds(at, PAGE), :] = pool_v[table_ref[beam, index]]
                return carry

            lax.fori_loop(0, context // PAGE, put, 0)
            span = pl.ds(rank * context, context)
            if distance == 0:
                copy = pltpu.make_async_copy(stage.at[0, span], recv_ref.at[0, span], own_sem.at[rank])
            else:
                copy = pltpu.make_async_remote_copy(
                    src_ref=stage.at[distance, span], dst_ref=recv_ref.at[distance, span],
                    send_sem=bs_sem.at[distance * MOST + rank], recv_sem=br_sem.at[distance * MOST + rank],
                    device_id={"dp": peer(SPAN - distance)}, device_id_type=MESH,
                )
            copy.start()
            copies.append(copy)
    for copy in copies:
        copy.wait()


def finish_kernel(recv_ref, raw_ref, new_hbm, len_hbm, par_hbm, proj_ref, cache_ref, new_ref, len_ref, par_ref, edge, zeros, in_sem, out_sem):
    me = lax.axis_index("dp")
    pages = recv_ref.shape[1] // PAGE
    operands = ((par_hbm, par_ref), (len_hbm, len_ref), (new_hbm, new_ref))
    in_copies = [pltpu.make_async_copy(source, target, in_sem.at[at]) for at, (source, target) in enumerate(operands)]
    for copy in in_copies:
        copy.start()
    zeros[...] = jnp.zeros_like(zeros)
    for copy in in_copies:
        copy.wait()
    slots, owners = slots_of_children(par_ref, me)
    fresh = [new_ref[step].astype(jnp.float32) for step in range(STEPS)]
    for child in range(BEAMS):
        slot = slots[child]
        length = len_ref[owners[child]]
        first = length // PAGE
        last = (length + STEPS - 1) // PAGE

        def whole(index, carry, child=child, slot=slot):
            span = pl.ds(pl.multiple_of(index * PAGE, PAGE), PAGE)
            pltpu.make_async_copy(recv_ref.at[slot, span], cache_ref.at[child, span], out_sem).start()
            return carry

        def clear(index, carry, child=child):
            span = pl.ds(pl.multiple_of(index * PAGE, PAGE), PAGE)
            pltpu.make_async_copy(zeros, cache_ref.at[child, span], out_sem).start()
            return carry

        def fix(index, carry, child=child, slot=slot, length=length, first=first):
            at = pl.multiple_of(index * PAGE, PAGE)
            position = at + lax.broadcasted_iota(jnp.int32, (PAGE, 2 * HD), 0)
            page = recv_ref[slot, pl.ds(at, PAGE), :].astype(jnp.float32)
            page = jnp.where(position < length, page, 0.0)
            for step in range(STEPS):
                page = jnp.where(position == length + step, fresh[step][child:child + 1], page)
            edge[child * 2 + index - first] = page.astype(jnp.bfloat16)
            pltpu.make_async_copy(edge.at[child * 2 + index - first], cache_ref.at[child, pl.ds(at, PAGE)], out_sem).start()
            return carry

        lax.fori_loop(0, first, whole, 0)
        lax.fori_loop(last + 1, pages, clear, 0)
        lax.fori_loop(first, last + 1, fix, 0)

    rows = MOST * STEPS
    raw = []
    for distance in range(SPAN):
        part = raw_ref[distance].astype(jnp.float32)
        raw.append(jnp.concatenate([part[:rows], part[rows:]], axis=1))
    raw = jnp.concatenate(raw, axis=0).astype(jnp.bfloat16)
    row = lax.broadcasted_iota(jnp.int32, (BEAMS, SPAN * rows), 0)
    col = lax.broadcasted_iota(jnp.int32, (BEAMS, SPAN * rows), 1)
    slot_at = jnp.zeros_like(col)
    for child in range(BEAMS):
        slot_at = jnp.where(row == child, slots[child], slot_at)
    for step in range(STEPS):
        pick = jnp.where(col == slot_at * STEPS + step, 1.0, 0.0).astype(jnp.bfloat16)
        proj_ref[step] = jnp.dot(pick, raw, preferred_element_type=jnp.float32).astype(jnp.bfloat16)
    pltpu.make_async_copy(recv_ref, cache_ref, out_sem).wait()


def left_kernel(left_ref, got_ref, send_sem, recv_sem):
    me = lax.axis_index("dp")
    y = lax.rem(me, SPAN)
    targets = [me - y + lax.rem(y + ahead, SPAN) for ahead in (1, SPAN - 1)]
    barrier = pltpu.get_barrier_semaphore()
    for target in targets:
        pl.semaphore_signal(barrier, inc=1, device_id={"dp": target}, device_id_type=MESH)
    pl.semaphore_wait(barrier, 2)
    copies = []
    for side, target in enumerate(targets):
        copy = pltpu.make_async_remote_copy(
            src_ref=left_ref.at[side], dst_ref=got_ref.at[side],
            send_sem=send_sem.at[side], recv_sem=recv_sem.at[side],
            device_id={"dp": target}, device_id_type=MESH,
        )
        copy.start()
        copies.append(copy)
    for copy in copies:
        copy.wait()


def place_kernel(with_left, recv_ref, raw_ref, new_ref, meta_ref, *refs):
    left_ref = refs[0] if with_left else None
    proj_hbm, cache_ref, edge, zeros, proj_ref, out_sem, proj_sem = refs[-7:]
    total = recv_ref.shape[0]
    zeros[...] = jnp.zeros_like(zeros)
    fresh = [new_ref[step].astype(jnp.float32) for step in range(STEPS)]
    slots = [meta_ref[child * META + 6] for child in range(BEAMS)]
    per_child = cache_ref.shape[1]
    scale = GRAIN // TILE
    for child in range(BEAMS):
        length, start, split, again, until, third = (meta_ref[child * META + at] for at in range(6))
        first = length // TILE
        last = (length + STEPS - 1) // TILE
        until = jnp.minimum(until * scale, first) if with_left else first
        split = jnp.minimum(split * scale, until)

        def move(source, source_at, at, count, child=child):
            @pl.when(count > 0)
            def _():
                pltpu.make_async_copy(
                    source.at[pl.ds(source_at, count)], cache_ref.at[child, pl.ds(at, count)], out_sem
                ).start()

        move(recv_ref, start * scale, 0, split)
        move(recv_ref, again * scale, split, until - split)
        if with_left:
            move(left_ref, third * scale, until, first - until)
        move(zeros, 0, last + 1, per_child - 1 - last)
    for child in range(BEAMS):
        length, start, split, again, until, third = (meta_ref[child * META + at] for at in range(6))
        first = length // TILE
        last = (length + STEPS - 1) // TILE

        def fix(
            index, carry, child=child, length=length, first=first, start=start * scale, split=split * scale,
            again=again * scale, until=until * scale, third=third * scale,
        ):
            position = index * TILE + lax.broadcasted_iota(jnp.int32, (TILE, 2 * HD), 0)
            at = jnp.minimum(jnp.where(index < split, start + index, again + index - split), total - 1)
            part = recv_ref[at].astype(jnp.float32)
            if with_left:
                at = jnp.minimum(jnp.maximum(third + index - until, 0), left_ref.shape[0] - 1)
                part = jnp.where(index < until, part, left_ref[at].astype(jnp.float32))
            part = jnp.where(position < length, part, 0.0)
            for step in range(STEPS):
                part = jnp.where(position == length + step, fresh[step][child:child + 1], part)
            edge[child * 2 + index - first] = part.astype(jnp.bfloat16)
            pltpu.make_async_copy(edge.at[child * 2 + index - first], cache_ref.at[child, index], out_sem).start()
            return carry

        lax.fori_loop(first, last + 1, fix, 0)

    rows = MOST * STEPS
    raw = []
    for distance in range(SPAN):
        part = raw_ref[distance].astype(jnp.float32)
        raw.append(jnp.concatenate([part[:rows], part[rows:]], axis=1))
    raw = jnp.concatenate(raw, axis=0).astype(jnp.bfloat16)
    row = lax.broadcasted_iota(jnp.int32, (BEAMS, SPAN * rows), 0)
    col = lax.broadcasted_iota(jnp.int32, (BEAMS, SPAN * rows), 1)
    slot_at = jnp.zeros_like(col)
    for child in range(BEAMS):
        slot_at = jnp.where(row == child, slots[child], slot_at)
    for step in range(STEPS):
        pick = jnp.where(col == slot_at * STEPS + step, 1.0, 0.0).astype(jnp.bfloat16)
        proj_ref[step] = jnp.dot(pick, raw, preferred_element_type=jnp.float32).astype(jnp.bfloat16)
    proj_copy = pltpu.make_async_copy(proj_ref, proj_hbm, proj_sem)
    proj_copy.start()
    pltpu.make_async_copy(cache_ref, cache_ref, out_sem).wait()
    proj_copy.wait()


def local(shards, queries, new_kv, kv_pool, page_tables, lengths, parents, out_weight):
    wide = queries.shape[2]
    channels = kv_pool.shape[2]
    context = page_tables.shape[1] * kv_pool.shape[1]
    rows = MOST * STEPS
    vmem = pl.BlockSpec(memory_space=pltpu.VMEM)
    smem = pl.BlockSpec(memory_space=pltpu.SMEM)
    hbm = pl.BlockSpec(memory_space=pltpu.HBM)
    free = pl.BlockSpec(memory_space=pl.ANY)
    dma = pltpu.SemaphoreType.DMA
    bf16 = jnp.bfloat16

    def pinned(*operands):
        return [pltpu.with_memory_space_constraint(operand, pltpu.HBM) for operand in operands]

    grain_pool = kv_pool.reshape(-1, GRAIN, channels)
    with jax.named_scope("exchange"):
        recv, raw, left, meta, over = pl.pallas_call(
            exchange_kernel,
            out_shape=(
                jax.ShapeDtypeStruct((2 * LINK + MOST * PER_CHILD, GRAIN, channels), bf16),
                jax.ShapeDtypeStruct((SPAN, 2 * rows, wide // 2), bf16),
                jax.ShapeDtypeStruct((2, LEFT, GRAIN, channels), bf16),
                jax.ShapeDtypeStruct((BEAMS * META,), jnp.int32),
                jax.ShapeDtypeStruct((1,), jnp.int32),
            ),
            in_specs=[hbm] * 7,
            out_specs=(free, free, free, smem, smem),
            scratch_shapes=[
                pltpu.VMEM(queries.shape, bf16),
                pltpu.VMEM(new_kv.shape, bf16),
                pltpu.SMEM(page_tables.shape, jnp.int32),
                pltpu.SMEM(lengths.shape, jnp.int32),
                pltpu.SMEM(parents.shape, jnp.int32),
                pltpu.VMEM(grain_pool.shape, bf16),
                pltpu.VMEM((shards, out_weight.shape[0], wide), bf16),
                pltpu.VMEM((SPAN, MOST * PER_CHILD, GRAIN, channels), bf16),
                pltpu.VMEM((2, FIRST, GRAIN, channels), bf16),
                pltpu.VMEM((2, FIRST, GRAIN, channels), bf16),
                pltpu.VMEM((2, REST, GRAIN, channels), bf16),
                pltpu.VMEM((2, LEFT, GRAIN, channels), bf16),
                pltpu.VMEM((SPAN, 2 * rows, (wide + channels) // 2), bf16),
                pltpu.VMEM((SPAN, 2 * rows, (wide + channels) // 2), bf16),
                pltpu.VMEM((SPAN * rows, wide), jnp.float32),
                pltpu.VMEM((shards, SPAN * rows, wide), bf16),
                pltpu.VMEM((shards, SPAN * rows, wide), bf16),
                pltpu.VMEM((SPAN, 2 * rows, wide // 2), bf16),
                pltpu.SMEM((SPAN * MOST,), jnp.int32),
                pltpu.SMEM((SPAN * MOST,), jnp.int32),
                dma((5,)), dma((4,)), dma((shards,)), dma((2,)), dma((3,)),
                dma((SPAN,)), dma((SPAN,)),
                dma((8,)), dma((8,)),
                dma((shards,)), dma((shards,)),
                dma((SPAN,)), dma((SPAN,)),
                pltpu.SemaphoreType.REGULAR,
            ],
            compiler_params=pltpu.CompilerParams(
                collective_id=0, has_side_effects=True, vmem_limit_bytes=48 * 1024 * 1024
            ),
            name="exchange",
        )(*pinned(queries, new_kv, grain_pool, page_tables, lengths, parents, out_weight))

    def place(*got):
        with jax.named_scope("place"):
            projected, cache = pl.pallas_call(
                functools.partial(place_kernel, len(got) > 0),
                out_shape=(
                    jax.ShapeDtypeStruct(queries.shape, bf16),
                    jax.ShapeDtypeStruct((BEAMS, context // TILE, TILE, channels), bf16),
                ),
                in_specs=[vmem, vmem, vmem, smem] + [vmem] * len(got),
                out_specs=(free, free),
                scratch_shapes=[
                    pltpu.VMEM((2 * BEAMS, TILE, channels), bf16),
                    pltpu.VMEM((context // TILE, TILE, channels), bf16),
                    pltpu.VMEM(queries.shape, bf16),
                    dma, dma,
                ],
                compiler_params=pltpu.CompilerParams(vmem_limit_bytes=24 * 1024 * 1024),
                name="place_left" if got else "place",
            )(recv.reshape(-1, TILE, channels), raw, new_kv, meta, *got)
            return projected, cache.reshape(BEAMS, context, channels)

    def placed():
        return place()

    def topped():
        with jax.named_scope("left"):
            got = pl.pallas_call(
                left_kernel,
                out_shape=jax.ShapeDtypeStruct(left.shape, bf16),
                in_specs=[free],
                out_specs=free,
                scratch_shapes=[dma((2,)), dma((2,))],
                compiler_params=pltpu.CompilerParams(
                    collective_id=2, has_side_effects=True, vmem_limit_bytes=4 * 1024 * 1024
                ),
                name="left",
            )(left)
        return place(got.reshape(-1, TILE, channels))

    def resent():
        with jax.named_scope("full"):
            whole = pl.pallas_call(
                full_kernel,
                out_shape=jax.ShapeDtypeStruct((SPAN, MOST * context, channels), bf16),
                in_specs=[hbm] * 3,
                out_specs=free,
                scratch_shapes=[
                    pltpu.SMEM(page_tables.shape, jnp.int32),
                    pltpu.SMEM(parents.shape, jnp.int32),
                    pltpu.VMEM(kv_pool.shape, bf16),
                    pltpu.VMEM((SPAN, MOST * context, channels), bf16),
                    dma((2,)), dma, dma((MOST,)),
                    dma((SPAN * MOST,)), dma((SPAN * MOST,)),
                ],
                compiler_params=pltpu.CompilerParams(
                    collective_id=1, has_side_effects=True, vmem_limit_bytes=24 * 1024 * 1024
                ),
                name="full",
            )(*pinned(kv_pool, page_tables, parents))
        with jax.named_scope("finish"):
            return pl.pallas_call(
                finish_kernel,
                out_shape=(
                    jax.ShapeDtypeStruct(queries.shape, bf16),
                    jax.ShapeDtypeStruct((BEAMS, context, channels), bf16),
                ),
                in_specs=[vmem, vmem, hbm, hbm, hbm],
                out_specs=(vmem, hbm),
                scratch_shapes=[
                    pltpu.VMEM(new_kv.shape, bf16),
                    pltpu.SMEM(lengths.shape, jnp.int32),
                    pltpu.SMEM(parents.shape, jnp.int32),
                    pltpu.VMEM((2 * BEAMS, PAGE, channels), bf16),
                    pltpu.VMEM((PAGE, channels), bf16),
                    dma((3,)), dma,
                ],
                compiler_params=pltpu.CompilerParams(vmem_limit_bytes=24 * 1024 * 1024),
                name="finish",
            )(whole.reshape(BEAMS, context, channels), raw, new_kv, lengths, parents)

    return lax.switch(over[0], (placed, topped, resent))


def solution(mesh):
    in_specs = (
        P(None, "dp", "tensor"),
        P(None, "dp", "tensor"),
        P("dp", None, "tensor"),
        P("dp", None),
        P(),
        P(),
        P("tensor", None),
    )
    out_specs = (P(None, "dp", "tensor"), P("dp", None, "tensor"))
    body = functools.partial(local, mesh.shape["tensor"])
    return jax.shard_map(body, mesh=mesh, in_specs=in_specs, out_specs=out_specs, check_vma=False)
```

```python
import functools

import jax
import jax.numpy as jnp
from jax import lax
from jax.experimental import pallas as pl
from jax.experimental.pallas import tpu as pltpu
from jax.sharding import PartitionSpec as P

HD = 128
SPAN = 4
MOST = 2
BEAMS = 8
STEPS = 4
PAGE = 128
PAGES = 8
GRAIN = 32
PER_CHILD = 32
PER_PAGE = PAGE // GRAIN
TILE = 16
VIA = 36
MORE = 28
REST = 36
LEFT = 12
FIRST = VIA + MORE
LINK = FIRST + REST
META = 7
MESH = pl.DeviceIdType.MESH


def grains(length):
    return (length + (GRAIN - 1)) // GRAIN


def choose(values, index):
    out = values[0]
    for at in range(1, len(values)):
        out = jnp.where(index == at, values[at], out)
    return out


def ring_plan(parents, lengths, ring):
    flows = [[jnp.int32(0)] * SPAN for _ in range(SPAN)]
    for target in range(SPAN):
        seen = []
        for child in range(BEAMS):
            parent = parents[(ring * SPAN + target) * BEAMS + child]
            count = grains(lengths[parent])
            for other in seen:
                count = jnp.where(parent == other, 0, count)
            seen.append(parent)
            source = (parent >> 3) & (SPAN - 1)
            for at in range(SPAN):
                if at != target:
                    ahead = (target - at) % SPAN
                    flows[at][ahead] = flows[at][ahead] + jnp.where(source == at, count, 0)
    up = [flow[1] for flow in flows]
    far = [flow[2] for flow in flows]
    down = [flow[3] for flow in flows]
    via_up = [jnp.minimum(count >> 1, VIA) for count in far]
    for at in range(SPAN):
        via_down = [far[i] - via_up[i] for i in range(SPAN)]
        nxt, prv = (at + 1) % SPAN, (at - 1) % SPAN
        load_up = jnp.maximum(up[at] + via_up[prv], up[nxt] + via_up[nxt])
        load_down = jnp.maximum(down[at] + via_down[nxt], down[prv] + via_down[prv])
        best = (load_down + far[at] - load_up) >> 1
        via_up[at] = jnp.minimum(jnp.maximum(best, jnp.maximum(far[at] - VIA, 0)), jnp.minimum(far[at], VIA))
    via_down = [far[i] - via_up[i] for i in range(SPAN)]
    return up, down, via_up, via_down


def heaviest(plan):
    up, down, via_up, via_down = plan
    out = jnp.int32(0)
    for at in range(SPAN):
        load_up = up[at] + via_up[at] + via_up[(at - 1) % SPAN]
        load_down = down[at] + via_down[at] + via_down[(at + 1) % SPAN]
        out = jnp.maximum(out, jnp.maximum(load_up, load_down))
    return out


def slots_of_children(parents, me):
    taken = [jnp.int32(0) for _ in range(SPAN)]
    slots, owners = [], []
    for child in range(BEAMS):
        parent = parents[me * BEAMS + child]
        apart = jnp.bitwise_and(parent // BEAMS - me, SPAN - 1)
        slot = jnp.int32(0)
        for distance in range(SPAN):
            hit = apart == distance
            slot = jnp.where(hit, distance * MOST + taken[distance], slot)
            taken[distance] = taken[distance] + hit.astype(jnp.int32)
        slots.append(slot)
        owners.append(parent)
    return slots, owners


def served_beams(parents, me, target):
    count = jnp.int32(0)
    beams = [jnp.int32(0) for _ in range(MOST)]
    for child in range(BEAMS):
        parent = parents[target * BEAMS + child]
        hit = parent // BEAMS == me
        for rank in range(MOST):
            beams[rank] = jnp.where(hit & (count == rank), parent % BEAMS, beams[rank])
        count = count + hit.astype(jnp.int32)
    return beams


def exchange_kernel(
    q_hbm, new_hbm, pool_ref, table_hbm, len_hbm, par_hbm, w_ref,
    recv_ref, proj_ref, left_ref, meta_ref, over_ref,
    q_ref, new_ref, table_ref, len_ref, par_ref,
    pool_v, w_v, stage, first_send, first_recv, rest_send, left_send, q_send, q_recv, att, p_send, p_recv, r_send, lens, beams,
    in_sem, pool_sem, w_sem, own_sem, land_sem, qs_sem, qr_sem, bs_sem, br_sem, ps_sem, pr_sem, rs_sem, rr_sem, here_sem,
):
    me = lax.axis_index("dp")
    mine = lax.axis_index("tensor")
    shards = lax.axis_size("tensor")
    y = lax.rem(me, SPAN)
    base = me - y
    context = stage.shape[1] * GRAIN // MOST
    rings = lax.axis_size("dp") // SPAN
    wide = q_hbm.shape[2]
    heads = wide // HD
    rows = MOST * STEPS

    def peer(distance):
        return base + lax.rem(y + distance, SPAN)

    barrier = pltpu.get_barrier_semaphore()
    for distance in range(1, SPAN):
        pl.semaphore_signal(barrier, inc=1, device_id={"dp": peer(distance)}, device_id_type=MESH)
    for other in range(1, shards):
        @pl.when(mine + other < shards)
        def _(other=other):
            pl.semaphore_signal(barrier, inc=1, device_id={"tensor": mine + other}, device_id_type=MESH)
    in_copies = []
    operands = ((par_hbm, par_ref), (q_hbm, q_ref), (new_hbm, new_ref), (table_hbm, table_ref), (len_hbm, len_ref))
    for at, (source, target) in enumerate(operands):
        copy = pltpu.make_async_copy(source, target, in_sem.at[at])
        copy.start()
        in_copies.append(copy)
    quarter = pool_v.shape[0] // 4
    pool_copies = []
    for at in range(4):
        span = pl.ds(at * quarter, quarter)
        copy = pltpu.make_async_copy(pool_ref.at[span], pool_v.at[span], pool_sem.at[at])
        copy.start()
        pool_copies.append(copy)
    for copy in in_copies:
        copy.wait()

    slots, owners = slots_of_children(par_ref, me)
    plan = ring_plan(par_ref, len_ref, me >> 2)
    up, down, via_up, via_down = plan
    flows = {}
    for ahead in range(SPAN):
        served = served_beams(par_ref, me, peer(ahead))
        distance = (SPAN - ahead) % SPAN
        held = [len_ref[me * BEAMS + served[rank]] for rank in range(MOST)]
        for rank in range(MOST):
            beams[distance * MOST + rank] = served[rank]
            lens[distance * MOST + rank] = held[rank]
        flows[ahead] = (served[0], served[1], grains(held[0]))

    def grain_at(flow, number):
        first, second, cut = flow
        later = number >= cut
        number = jnp.where(later, number - cut, number)
        number = jnp.minimum(jnp.maximum(number, 0), PER_CHILD - 1)
        return table_ref[jnp.where(later, second, first), number >> 2] * PER_PAGE + (number & (PER_PAGE - 1))

    sides = (
        (flows[1], choose(via_up, y), jnp.int32(0), choose(via_up, (y - 1) & 3), peer(1)),
        (flows[3], choose(via_down, y), choose(via_up, y), choose(via_down, (y + 1) & 3), peer(3)),
    )
    pl.semaphore_wait(barrier, SPAN - 1 + mine)
    for other in range(1, shards):
        @pl.when(mine >= other)
        def _(other=other):
            pl.semaphore_signal(here_sem, inc=1, device_id={"tensor": mine - other}, device_id_type=MESH)
    for copy in pool_copies:
        copy.wait()
    b_copies = []
    cuts = (0, 8, VIA, FIRST)

    def send_part(part):
        for side, (flow, mine_via, skip, _, target) in enumerate(sides):
            def put(at, carry, side=side, flow=flow, mine_via=mine_via, skip=skip):
                for at in (2 * at, 2 * at + 1):
                    far = at < mine_via
                    chosen = tuple(jnp.where(far, one, two) for one, two in zip(flows[2], flow))
                    number = jnp.where(far, skip + at, at - mine_via)
                    first_send[side, at] = pool_v[grain_at(chosen, number)]
                return carry

            lax.fori_loop(cuts[part] // 2, cuts[part + 1] // 2, put, 0)
            span = pl.ds(cuts[part], cuts[part + 1] - cuts[part])
            copy = pltpu.make_async_remote_copy(
                src_ref=first_send.at[side, span], dst_ref=first_recv.at[side, span],
                send_sem=bs_sem.at[side * 4 + part], recv_sem=br_sem.at[side * 4 + part],
                device_id={"dp": target}, device_id_type=MESH,
            )
            copy.start()
            b_copies.append(copy)

    send_part(0)

    row = lax.broadcasted_iota(jnp.int32, (SPAN * rows, BEAMS), 0)
    col = lax.broadcasted_iota(jnp.int32, (SPAN * rows, BEAMS), 1)
    slot_at = jnp.zeros_like(col)
    for child in range(BEAMS):
        slot_at = jnp.where(col == child, slots[child], slot_at)
    q_sorted = jnp.zeros((SPAN * rows, wide), jnp.float32)
    new_sorted = jnp.zeros((SPAN * rows, 2 * HD), jnp.float32)
    for step in range(STEPS):
        pick = jnp.where((row // STEPS == slot_at) & (row % STEPS == step), 1.0, 0.0).astype(jnp.bfloat16)
        q_sorted += jnp.dot(pick, q_ref[step], preferred_element_type=jnp.float32)
        new_sorted += jnp.dot(pick, new_ref[step], preferred_element_type=jnp.float32)
    both = jnp.concatenate([q_sorted, new_sorted], axis=1)
    half = both.shape[1] // 2
    for distance in range(SPAN):
        part = both[distance * rows:(distance + 1) * rows]
        part = jnp.concatenate([part[:, :half], part[:, half:]], axis=0).astype(jnp.bfloat16)
        if distance == 0:
            q_recv[0] = part
        else:
            q_send[distance] = part
    q_copies = []
    for distance in range(1, SPAN):
        copy = pltpu.make_async_remote_copy(
            src_ref=q_send.at[distance], dst_ref=q_recv.at[distance],
            send_sem=qs_sem.at[distance], recv_sem=qr_sem.at[distance],
            device_id={"dp": peer(distance)}, device_id_type=MESH,
        )
        copy.start()
        q_copies.append(copy)
    send_part(1)
    send_part(2)
    w_copies = []
    for block in range(shards):
        copy = pltpu.make_async_copy(w_ref.at[:, pl.ds(block * wide, wide)], w_v.at[block], w_sem.at[block])
        copy.start()
        w_copies.append(copy)

    def put_all(index, carry):
        slot = index // PAGES
        page = table_ref[beams[slot], index % PAGES]
        at = (index % (MOST * PAGES)) * PER_PAGE
        stage[index // (MOST * PAGES), pl.ds(at, PER_PAGE)] = pool_v[pl.ds(page * PER_PAGE, PER_PAGE)]
        return carry

    lax.fori_loop(0, SPAN * MOST * PAGES, put_all, 0)
    own_copy = pltpu.make_async_copy(stage.at[0], recv_ref.at[pl.ds(2 * LINK, MOST * PER_CHILD)], own_sem.at[0])
    own_copy.start()

    for copy in q_copies:
        copy.wait()

    def attend(distance, carry):
        message = q_recv[distance].astype(jnp.float32)
        message = jnp.concatenate([message[:rows], message[rows:]], axis=1)
        q_rows = jnp.concatenate([message[:, h * HD:(h + 1) * HD] for h in range(heads)], axis=0).astype(jnp.bfloat16)
        fresh = message[:, wide:].astype(jnp.bfloat16)
        old_len = lens[distance * MOST]
        last_len = lens[distance * MOST + 1]
        contract = (((1,), (1,)), ((), ()))
        scale = HD ** -0.5
        half = MOST * PER_CHILD // 2
        keys = [stage[distance, pl.ds(rank * half, half), :, 0:HD].reshape(context, HD) for rank in range(MOST)]
        scores = [lax.dot_general(q_rows, key, contract, preferred_element_type=jnp.float32) for key in keys]
        rank_at = lax.broadcasted_iota(jnp.int32, scores[0].shape, 0) // STEPS % MOST
        scores = jnp.where(rank_at == 0, scores[0], scores[1]) * scale
        fresh_scores = lax.dot_general(q_rows, fresh[:, :HD], contract, preferred_element_type=jnp.float32) * scale
        position = lax.broadcasted_iota(jnp.int32, scores.shape, 1)
        limit = jnp.where(rank_at == 0, old_len, last_len)
        scores = jnp.where(position < limit, scores, -1e30)
        f_row = lax.broadcasted_iota(jnp.int32, fresh_scores.shape, 0)
        f_col = lax.broadcasted_iota(jnp.int32, fresh_scores.shape, 1)
        seen = (f_row // STEPS % MOST == f_col // STEPS) & (f_col % STEPS <= f_row % STEPS)
        fresh_scores = jnp.where(seen, fresh_scores, -1e30)
        top = jnp.maximum(jnp.max(scores, axis=1, keepdims=True), jnp.max(fresh_scores, axis=1, keepdims=True))
        exp_old = jnp.exp(scores - top)
        exp_new = jnp.exp(fresh_scores - top)
        total = jnp.sum(exp_old, axis=1, keepdims=True) + jnp.sum(exp_new, axis=1, keepdims=True)
        share = 1.0 / total
        w_old = (exp_old * share).astype(jnp.bfloat16)
        w_new = (exp_new * share).astype(jnp.bfloat16)
        values = [stage[distance, pl.ds(rank * half, half), :, HD:2 * HD].reshape(context, HD) for rank in range(MOST)]
        out = [jnp.dot(w_old, value, preferred_element_type=jnp.float32) for value in values]
        out = jnp.where(rank_at[:, :HD] == 0, out[0], out[1])
        out += jnp.dot(w_new, fresh[:, HD:], preferred_element_type=jnp.float32)
        out = jnp.concatenate([out[h * rows:(h + 1) * rows] for h in range(heads)], axis=1)
        att[pl.ds(pl.multiple_of(distance * rows, rows), rows), :] = out
        return carry

    lax.fori_loop(0, SPAN, attend, 0)
    for copy in b_copies[:4]:
        copy.wait()
    more_copies = b_copies[4:]
    b_copies = []
    for side, (flow, mine_via, _, passed, target) in enumerate(sides):
        def put_passed(at, carry, side=side, flow=flow, mine_via=mine_via, passed=passed):
            for at in (2 * at, 2 * at + 1):
                here = pool_v[grain_at(flow, FIRST - mine_via + at - passed)]
                rest_send[side, at] = jnp.where(at < passed, first_recv[side, at], here)
            return carry

        lax.fori_loop(0, REST // 2, put_passed, 0)
        copy = pltpu.make_async_remote_copy(
            src_ref=rest_send.at[side], dst_ref=recv_ref.at[pl.ds(side * LINK + FIRST, REST)],
            send_sem=bs_sem.at[side * 4 + 3], recv_sem=br_sem.at[side * 4 + 3],
            device_id={"dp": target}, device_id_type=MESH,
        )
        copy.start()
        b_copies.append(copy)
    attended = att[...].astype(jnp.bfloat16)
    for copy in w_copies:
        copy.wait()

    def p_copy(other):
        return pltpu.make_async_remote_copy(
            src_ref=p_send.at[other], dst_ref=p_recv.at[other],
            send_sem=ps_sem.at[other], recv_sem=pr_sem.at[other],
            device_id={"tensor": lax.rem(mine + other, shards)}, device_id_type=MESH,
        )

    def project(other, carry):
        product = jnp.dot(attended, w_v[lax.rem(mine + other, shards)], preferred_element_type=jnp.float32)
        p_send[other] = product.astype(jnp.bfloat16)
        p_copy(other).start()
        return carry

    @pl.when(mine < shards - 1)
    def _():
        pl.semaphore_wait(here_sem, shards - 1 - mine)

    lax.fori_loop(1, shards, project, 0)
    own = jnp.dot(attended, w_v[mine], preferred_element_type=jnp.float32)

    for copy in more_copies:
        copy.wait()
    for side in range(2):
        copy = pltpu.make_async_copy(first_recv.at[side], recv_ref.at[pl.ds(side * LINK, FIRST)], land_sem.at[side])
        copy.start()
        b_copies.append(copy)

    def gather_sums(other, total):
        p_copy(other).wait()
        return total + p_recv[other].astype(jnp.float32)

    summed = lax.fori_loop(1, shards, gather_sums, own)
    half = wide // 2
    r_copies = []
    for distance in range(SPAN):
        part = summed[distance * rows:(distance + 1) * rows]
        r_send[distance] = jnp.concatenate([part[:, :half], part[:, half:]], axis=0).astype(jnp.bfloat16)
        if distance == 0:
            copy = pltpu.make_async_copy(r_send.at[0], proj_ref.at[0], own_sem.at[1])
        else:
            copy = pltpu.make_async_remote_copy(
                src_ref=r_send.at[distance], dst_ref=proj_ref.at[distance],
                send_sem=rs_sem.at[distance], recv_sem=rr_sem.at[distance],
                device_id={"dp": peer(SPAN - distance)}, device_id_type=MESH,
            )
        copy.start()
        r_copies.append(copy)
    load = lax.fori_loop(
        0, rings, lambda ring, load: jnp.maximum(load, heaviest(ring_plan(par_ref, len_ref, ring))), jnp.int32(0)
    )
    over_ref[0] = jnp.where(load > LINK, 1, 0) + jnp.where(load > LINK + LEFT, 1, 0)
    for side, (flow, mine_via, _, passed, _) in enumerate(sides):
        def put_left(at, carry, side=side, flow=flow, mine_via=mine_via, passed=passed):
            left_send[side, at] = pool_v[grain_at(flow, LINK - mine_via - passed + at)]
            return carry

        lax.fori_loop(0, LEFT, put_left, 0)
    left_copy = pltpu.make_async_copy(left_send, left_ref, land_sem.at[2])
    left_copy.start()
    for child in range(BEAMS):
        slot = slots[child]
        distance = slot >> 1
        length = len_ref[owners[child]]
        before = jnp.int32(0)
        for other in range(BEAMS):
            if other != child:
                mate = (slots[other] >> 1 == distance) & (slots[other] < slot)
                differs = owners[other] != owners[child]
                before = jnp.where(mate & differs, grains(len_ref[owners[other]]), before)
        from_up = choose(via_up, (y - 1) & 3), choose(via_up, (y + 2) & 3)
        from_down = choose(via_down, (y + 1) & 3), choose(via_down, (y + 2) & 3)
        near_via = jnp.where(distance == 3, from_up[0], from_down[0])
        near_pass = jnp.where(distance == 3, from_up[1], from_down[1])
        near_base = jnp.where(distance == 3, 0, LINK)
        split = jnp.where(distance == 2, from_up[1], FIRST - near_via) - before
        split = jnp.minimum(jnp.maximum(split, 0), PER_CHILD)
        start = jnp.where(distance == 2, FIRST + before, near_base + near_via + before)
        again = jnp.where(distance == 2, LINK + FIRST + before + split - from_up[1], start + split + near_pass)
        near = jnp.where(distance == 2, False, distance != 0)
        until = LINK - near_via - near_pass - before
        until = jnp.where(near, jnp.minimum(jnp.maximum(until, 0), PER_CHILD), PER_CHILD)
        third = jnp.where(distance == 3, 0, LEFT) + near_via + near_pass + before + until - LINK
        stays = distance == 0
        meta_ref[child * META] = length
        meta_ref[child * META + 1] = jnp.where(stays, 2 * LINK + (slot & 1) * PER_CHILD, start)
        meta_ref[child * META + 2] = jnp.where(stays, PER_CHILD, split)
        meta_ref[child * META + 3] = jnp.where(stays, 0, again)
        meta_ref[child * META + 4] = until
        meta_ref[child * META + 5] = jnp.where(near, third, 0)
        meta_ref[child * META + 6] = slot
    for copy in r_copies:
        copy.wait()
    for copy in b_copies:
        copy.wait()
    own_copy.wait()
    left_copy.wait()


def full_kernel(
    pool_ref, table_hbm, par_hbm, recv_ref,
    table_ref, par_ref, pool_v, stage,
    in_sem, pool_sem, own_sem, bs_sem, br_sem,
):
    me = lax.axis_index("dp")
    y = lax.rem(me, SPAN)
    base = me - y
    context = stage.shape[1] // MOST

    def peer(distance):
        return base + lax.rem(y + distance, SPAN)

    barrier = pltpu.get_barrier_semaphore()
    for distance in range(1, SPAN):
        pl.semaphore_signal(barrier, inc=1, device_id={"dp": peer(distance)}, device_id_type=MESH)
    in_copies = []
    for at, (source, target) in enumerate(((par_hbm, par_ref), (table_hbm, table_ref))):
        copy = pltpu.make_async_copy(source, target, in_sem.at[at])
        copy.start()
        in_copies.append(copy)
    pool_copy = pltpu.make_async_copy(pool_ref, pool_v, pool_sem)
    pool_copy.start()
    for copy in in_copies:
        copy.wait()
    pl.semaphore_wait(barrier, SPAN - 1)
    pool_copy.wait()
    copies = []
    for distance in (2, 1, 3, 0):
        served = served_beams(par_ref, me, peer(SPAN - distance))
        for rank in range(MOST):
            beam = served[rank]

            def put(index, carry, distance=distance, rank=rank, beam=beam):
                at = pl.multiple_of(rank * context + index * PAGE, PAGE)
                stage[distance, pl.ds(at, PAGE), :] = pool_v[table_ref[beam, index]]
                return carry

            lax.fori_loop(0, context // PAGE, put, 0)
            span = pl.ds(rank * context, context)
            if distance == 0:
                copy = pltpu.make_async_copy(stage.at[0, span], recv_ref.at[0, span], own_sem.at[rank])
            else:
                copy = pltpu.make_async_remote_copy(
                    src_ref=stage.at[distance, span], dst_ref=recv_ref.at[distance, span],
                    send_sem=bs_sem.at[distance * MOST + rank], recv_sem=br_sem.at[distance * MOST + rank],
                    device_id={"dp": peer(SPAN - distance)}, device_id_type=MESH,
                )
            copy.start()
            copies.append(copy)
    for copy in copies:
        copy.wait()


def finish_kernel(recv_ref, raw_ref, new_hbm, len_hbm, par_hbm, proj_ref, cache_ref, new_ref, len_ref, par_ref, edge, zeros, in_sem, out_sem):
    me = lax.axis_index("dp")
    pages = recv_ref.shape[1] // PAGE
    operands = ((par_hbm, par_ref), (len_hbm, len_ref), (new_hbm, new_ref))
    in_copies = [pltpu.make_async_copy(source, target, in_sem.at[at]) for at, (source, target) in enumerate(operands)]
    for copy in in_copies:
        copy.start()
    zeros[...] = jnp.zeros_like(zeros)
    for copy in in_copies:
        copy.wait()
    slots, owners = slots_of_children(par_ref, me)
    fresh = [new_ref[step].astype(jnp.float32) for step in range(STEPS)]
    for child in range(BEAMS):
        slot = slots[child]
        length = len_ref[owners[child]]
        first = length // PAGE
        last = (length + STEPS - 1) // PAGE

        def whole(index, carry, child=child, slot=slot):
            span = pl.ds(pl.multiple_of(index * PAGE, PAGE), PAGE)
            pltpu.make_async_copy(recv_ref.at[slot, span], cache_ref.at[child, span], out_sem).start()
            return carry

        def clear(index, carry, child=child):
            span = pl.ds(pl.multiple_of(index * PAGE, PAGE), PAGE)
            pltpu.make_async_copy(zeros, cache_ref.at[child, span], out_sem).start()
            return carry

        def fix(index, carry, child=child, slot=slot, length=length, first=first):
            at = pl.multiple_of(index * PAGE, PAGE)
            position = at + lax.broadcasted_iota(jnp.int32, (PAGE, 2 * HD), 0)
            page = recv_ref[slot, pl.ds(at, PAGE), :].astype(jnp.float32)
            page = jnp.where(position < length, page, 0.0)
            for step in range(STEPS):
                page = jnp.where(position == length + step, fresh[step][child:child + 1], page)
            edge[child * 2 + index - first] = page.astype(jnp.bfloat16)
            pltpu.make_async_copy(edge.at[child * 2 + index - first], cache_ref.at[child, pl.ds(at, PAGE)], out_sem).start()
            return carry

        lax.fori_loop(0, first, whole, 0)
        lax.fori_loop(last + 1, pages, clear, 0)
        lax.fori_loop(first, last + 1, fix, 0)

    rows = MOST * STEPS
    raw = []
    for distance in range(SPAN):
        part = raw_ref[distance].astype(jnp.float32)
        raw.append(jnp.concatenate([part[:rows], part[rows:]], axis=1))
    raw = jnp.concatenate(raw, axis=0).astype(jnp.bfloat16)
    row = lax.broadcasted_iota(jnp.int32, (BEAMS, SPAN * rows), 0)
    col = lax.broadcasted_iota(jnp.int32, (BEAMS, SPAN * rows), 1)
    slot_at = jnp.zeros_like(col)
    for child in range(BEAMS):
        slot_at = jnp.where(row == child, slots[child], slot_at)
    for step in range(STEPS):
        pick = jnp.where(col == slot_at * STEPS + step, 1.0, 0.0).astype(jnp.bfloat16)
        proj_ref[step] = jnp.dot(pick, raw, preferred_element_type=jnp.float32).astype(jnp.bfloat16)
    pltpu.make_async_copy(recv_ref, cache_ref, out_sem).wait()


def left_kernel(left_ref, got_ref, send_sem, recv_sem):
    me = lax.axis_index("dp")
    y = lax.rem(me, SPAN)
    targets = [me - y + lax.rem(y + ahead, SPAN) for ahead in (1, SPAN - 1)]
    barrier = pltpu.get_barrier_semaphore()
    for target in targets:
        pl.semaphore_signal(barrier, inc=1, device_id={"dp": target}, device_id_type=MESH)
    pl.semaphore_wait(barrier, 2)
    copies = []
    for side, target in enumerate(targets):
        copy = pltpu.make_async_remote_copy(
            src_ref=left_ref.at[side], dst_ref=got_ref.at[side],
            send_sem=send_sem.at[side], recv_sem=recv_sem.at[side],
            device_id={"dp": target}, device_id_type=MESH,
        )
        copy.start()
        copies.append(copy)
    for copy in copies:
        copy.wait()


def place_kernel(with_left, recv_ref, raw_ref, new_ref, meta_ref, *refs):
    left_ref = refs[0] if with_left else None
    proj_hbm, cache_ref, edge, zeros, proj_ref, out_sem, proj_sem = refs[-7:]
    total = recv_ref.shape[0]
    zeros[...] = jnp.zeros_like(zeros)
    fresh = [new_ref[step].astype(jnp.float32) for step in range(STEPS)]
    slots = [meta_ref[child * META + 6] for child in range(BEAMS)]
    per_child = cache_ref.shape[1]
    scale = GRAIN // TILE
    for child in range(BEAMS):
        length, start, split, again, until, third = (meta_ref[child * META + at] for at in range(6))
        first = length // TILE
        last = (length + STEPS - 1) // TILE
        until = jnp.minimum(until * scale, first) if with_left else first
        split = jnp.minimum(split * scale, until)

        def move(source, source_at, at, count, child=child):
            @pl.when(count > 0)
            def _():
                pltpu.make_async_copy(
                    source.at[pl.ds(source_at, count)], cache_ref.at[child, pl.ds(at, count)], out_sem
                ).start()

        move(recv_ref, start * scale, 0, split)
        move(recv_ref, again * scale, split, until - split)
        if with_left:
            move(left_ref, third * scale, until, first - until)
        move(zeros, 0, last + 1, per_child - 1 - last)
    for child in range(BEAMS):
        length, start, split, again, until, third = (meta_ref[child * META + at] for at in range(6))
        first = length // TILE
        last = (length + STEPS - 1) // TILE

        def fix(
            index, carry, child=child, length=length, first=first, start=start * scale, split=split * scale,
            again=again * scale, until=until * scale, third=third * scale,
        ):
            position = index * TILE + lax.broadcasted_iota(jnp.int32, (TILE, 2 * HD), 0)
            at = jnp.minimum(jnp.where(index < split, start + index, again + index - split), total - 1)
            part = recv_ref[at].astype(jnp.float32)
            if with_left:
                at = jnp.minimum(jnp.maximum(third + index - until, 0), left_ref.shape[0] - 1)
                part = jnp.where(index < until, part, left_ref[at].astype(jnp.float32))
            part = jnp.where(position < length, part, 0.0)
            for step in range(STEPS):
                part = jnp.where(position == length + step, fresh[step][child:child + 1], part)
            edge[child * 2 + index - first] = part.astype(jnp.bfloat16)
            pltpu.make_async_copy(edge.at[child * 2 + index - first], cache_ref.at[child, index], out_sem).start()
            return carry

        lax.fori_loop(first, last + 1, fix, 0)

    rows = MOST * STEPS
    raw = []
    for distance in range(SPAN):
        part = raw_ref[distance].astype(jnp.float32)
        raw.append(jnp.concatenate([part[:rows], part[rows:]], axis=1))
    raw = jnp.concatenate(raw, axis=0).astype(jnp.bfloat16)
    row = lax.broadcasted_iota(jnp.int32, (BEAMS, SPAN * rows), 0)
    col = lax.broadcasted_iota(jnp.int32, (BEAMS, SPAN * rows), 1)
    slot_at = jnp.zeros_like(col)
    for child in range(BEAMS):
        slot_at = jnp.where(row == child, slots[child], slot_at)
    for step in range(STEPS):
        pick = jnp.where(col == slot_at * STEPS + step, 1.0, 0.0).astype(jnp.bfloat16)
        proj_ref[step] = jnp.dot(pick, raw, preferred_element_type=jnp.float32).astype(jnp.bfloat16)
    proj_copy = pltpu.make_async_copy(proj_ref, proj_hbm, proj_sem)
    proj_copy.start()
    pltpu.make_async_copy(cache_ref, cache_ref, out_sem).wait()
    proj_copy.wait()


def local(shards, queries, new_kv, kv_pool, page_tables, lengths, parents, out_weight):
    wide = queries.shape[2]
    channels = kv_pool.shape[2]
    context = page_tables.shape[1] * kv_pool.shape[1]
    rows = MOST * STEPS
    vmem = pl.BlockSpec(memory_space=pltpu.VMEM)
    smem = pl.BlockSpec(memory_space=pltpu.SMEM)
    hbm = pl.BlockSpec(memory_space=pltpu.HBM)
    free = pl.BlockSpec(memory_space=pl.ANY)
    dma = pltpu.SemaphoreType.DMA
    bf16 = jnp.bfloat16

    def pinned(*operands):
        return [pltpu.with_memory_space_constraint(operand, pltpu.HBM) for operand in operands]

    grain_pool = kv_pool.reshape(-1, GRAIN, channels)
    with jax.named_scope("exchange"):
        recv, raw, left, meta, over = pl.pallas_call(
            exchange_kernel,
            out_shape=(
                jax.ShapeDtypeStruct((2 * LINK + MOST * PER_CHILD, GRAIN, channels), bf16),
                jax.ShapeDtypeStruct((SPAN, 2 * rows, wide // 2), bf16),
                jax.ShapeDtypeStruct((2, LEFT, GRAIN, channels), bf16),
                jax.ShapeDtypeStruct((BEAMS * META,), jnp.int32),
                jax.ShapeDtypeStruct((1,), jnp.int32),
            ),
            in_specs=[hbm] * 7,
            out_specs=(free, free, free, smem, smem),
            scratch_shapes=[
                pltpu.VMEM(queries.shape, bf16),
                pltpu.VMEM(new_kv.shape, bf16),
                pltpu.SMEM(page_tables.shape, jnp.int32),
                pltpu.SMEM(lengths.shape, jnp.int32),
                pltpu.SMEM(parents.shape, jnp.int32),
                pltpu.VMEM(grain_pool.shape, bf16),
                pltpu.VMEM((shards, out_weight.shape[0], wide), bf16),
                pltpu.VMEM((SPAN, MOST * PER_CHILD, GRAIN, channels), bf16),
                pltpu.VMEM((2, FIRST, GRAIN, channels), bf16),
                pltpu.VMEM((2, FIRST, GRAIN, channels), bf16),
                pltpu.VMEM((2, REST, GRAIN, channels), bf16),
                pltpu.VMEM((2, LEFT, GRAIN, channels), bf16),
                pltpu.VMEM((SPAN, 2 * rows, (wide + channels) // 2), bf16),
                pltpu.VMEM((SPAN, 2 * rows, (wide + channels) // 2), bf16),
                pltpu.VMEM((SPAN * rows, wide), jnp.float32),
                pltpu.VMEM((shards, SPAN * rows, wide), bf16),
                pltpu.VMEM((shards, SPAN * rows, wide), bf16),
                pltpu.VMEM((SPAN, 2 * rows, wide // 2), bf16),
                pltpu.SMEM((SPAN * MOST,), jnp.int32),
                pltpu.SMEM((SPAN * MOST,), jnp.int32),
                dma((5,)), dma((4,)), dma((shards,)), dma((2,)), dma((3,)),
                dma((SPAN,)), dma((SPAN,)),
                dma((8,)), dma((8,)),
                dma((shards,)), dma((shards,)),
                dma((SPAN,)), dma((SPAN,)),
                pltpu.SemaphoreType.REGULAR,
            ],
            compiler_params=pltpu.CompilerParams(
                collective_id=0, has_side_effects=True, vmem_limit_bytes=48 * 1024 * 1024
            ),
            name="exchange",
        )(*pinned(queries, new_kv, grain_pool, page_tables, lengths, parents, out_weight))

    def place(*got):
        with jax.named_scope("place"):
            projected, cache = pl.pallas_call(
                functools.partial(place_kernel, len(got) > 0),
                out_shape=(
                    jax.ShapeDtypeStruct(queries.shape, bf16),
                    jax.ShapeDtypeStruct((BEAMS, context // TILE, TILE, channels), bf16),
                ),
                in_specs=[vmem, vmem, vmem, smem] + [vmem] * len(got),
                out_specs=(free, free),
                scratch_shapes=[
                    pltpu.VMEM((2 * BEAMS, TILE, channels), bf16),
                    pltpu.VMEM((context // TILE, TILE, channels), bf16),
                    pltpu.VMEM(queries.shape, bf16),
                    dma, dma,
                ],
                compiler_params=pltpu.CompilerParams(vmem_limit_bytes=24 * 1024 * 1024),
                name="place_left" if got else "place",
            )(recv.reshape(-1, TILE, channels), raw, new_kv, meta, *got)
            return projected, cache.reshape(BEAMS, context, channels)

    def placed():
        return place()

    def topped():
        with jax.named_scope("left"):
            got = pl.pallas_call(
                left_kernel,
                out_shape=jax.ShapeDtypeStruct(left.shape, bf16),
                in_specs=[free],
                out_specs=free,
                scratch_shapes=[dma((2,)), dma((2,))],
                compiler_params=pltpu.CompilerParams(
                    collective_id=2, has_side_effects=True, vmem_limit_bytes=4 * 1024 * 1024
                ),
                name="left",
            )(left)
        return place(got.reshape(-1, TILE, channels))

    def resent():
        with jax.named_scope("full"):
            whole = pl.pallas_call(
                full_kernel,
                out_shape=jax.ShapeDtypeStruct((SPAN, MOST * context, channels), bf16),
                in_specs=[hbm] * 3,
                out_specs=free,
                scratch_shapes=[
                    pltpu.SMEM(page_tables.shape, jnp.int32),
                    pltpu.SMEM(parents.shape, jnp.int32),
                    pltpu.VMEM(kv_pool.shape, bf16),
                    pltpu.VMEM((SPAN, MOST * context, channels), bf16),
                    dma((2,)), dma, dma((MOST,)),
                    dma((SPAN * MOST,)), dma((SPAN * MOST,)),
                ],
                compiler_params=pltpu.CompilerParams(
                    collective_id=1, has_side_effects=True, vmem_limit_bytes=24 * 1024 * 1024
                ),
                name="full",
            )(*pinned(kv_pool, page_tables, parents))
        with jax.named_scope("finish"):
            return pl.pallas_call(
                finish_kernel,
                out_shape=(
                    jax.ShapeDtypeStruct(queries.shape, bf16),
                    jax.ShapeDtypeStruct((BEAMS, context, channels), bf16),
                ),
                in_specs=[vmem, vmem, hbm, hbm, hbm],
                out_specs=(vmem, hbm),
                scratch_shapes=[
                    pltpu.VMEM(new_kv.shape, bf16),
                    pltpu.SMEM(lengths.shape, jnp.int32),
                    pltpu.SMEM(parents.shape, jnp.int32),
                    pltpu.VMEM((2 * BEAMS, PAGE, channels), bf16),
                    pltpu.VMEM((PAGE, channels), bf16),
                    dma((3,)), dma,
                ],
                compiler_params=pltpu.CompilerParams(vmem_limit_bytes=24 * 1024 * 1024),
                name="finish",
            )(whole.reshape(BEAMS, context, channels), raw, new_kv, lengths, parents)

    return lax.switch(over[0], (placed, topped, resent))


def solution(mesh):
    in_specs = (
        P(None, "dp", "tensor"),
        P(None, "dp", "tensor"),
        P("dp", None, "tensor"),
        P("dp", None),
        P(),
        P(),
        P("tensor", None),
    )
    out_specs = (P(None, "dp", "tensor"), P("dp", None, "tensor"))
    body = functools.partial(local, mesh.shape["tensor"])
    return jax.shard_map(body, mesh=mesh, in_specs=in_specs, out_specs=out_specs, check_vma=False)
```

```python
import functools

import jax
import jax.numpy as jnp
from jax import lax
from jax.experimental import pallas as pl
from jax.experimental.pallas import tpu as pltpu
from jax.sharding import PartitionSpec as P

HD = 128
SPAN = 4
MOST = 2
BEAMS = 8
STEPS = 4
PAGE = 128
PAGES = 8
GRAIN = 32
PER_CHILD = 32
PER_PAGE = PAGE // GRAIN
TILE = 16
VIA = 36
MORE = 28
REST = 36
LEFT = 12
FIRST = VIA + MORE
LINK = FIRST + REST
META = 7
MESH = pl.DeviceIdType.MESH


def grains(length):
    return (length + (GRAIN - 1)) // GRAIN


def choose(values, index):
    out = values[0]
    for at in range(1, len(values)):
        out = jnp.where(index == at, values[at], out)
    return out


def balanced(up, far, down):
    via_up = [jnp.minimum(count >> 1, VIA) for count in far]
    for at in range(SPAN):
        via_down = [far[i] - via_up[i] for i in range(SPAN)]
        nxt, prv = (at + 1) % SPAN, (at - 1) % SPAN
        load_up = jnp.maximum(up[at] + via_up[prv], up[nxt] + via_up[nxt])
        load_down = jnp.maximum(down[at] + via_down[nxt], down[prv] + via_down[prv])
        best = (load_down + far[at] - load_up) >> 1
        via_up[at] = jnp.minimum(jnp.maximum(best, jnp.maximum(far[at] - VIA, 0)), jnp.minimum(far[at], VIA))
    via_down = [far[i] - via_up[i] for i in range(SPAN)]
    return via_up, via_down


def ring_plan(parents, lengths, ring):
    flows = [[jnp.int32(0)] * SPAN for _ in range(SPAN)]
    for target in range(SPAN):
        seen = []
        for child in range(BEAMS):
            parent = parents[(ring * SPAN + target) * BEAMS + child]
            count = grains(lengths[parent])
            for other in seen:
                count = jnp.where(parent == other, 0, count)
            seen.append(parent)
            source = (parent >> 3) & (SPAN - 1)
            for at in range(SPAN):
                if at != target:
                    ahead = (target - at) % SPAN
                    flows[at][ahead] = flows[at][ahead] + jnp.where(source == at, count, 0)
    up = [flow[1] for flow in flows]
    far = [flow[2] for flow in flows]
    down = [flow[3] for flow in flows]
    via_up, via_down = balanced(up, far, down)
    return up, down, via_up, via_down


def heaviest(parents, lengths, rings):
    beams = rings * SPAN * BEAMS
    counts = grains(lengths).astype(jnp.float32).astype(jnp.bfloat16)
    beam = lax.broadcasted_iota(jnp.int32, (beams, beams), 0)
    chosen = jnp.where(beam == parents, 1.0, 0.0).astype(jnp.bfloat16)
    counts = jnp.dot(jnp.broadcast_to(counts, (16, beams)), chosen, preferred_element_type=jnp.float32)[:1]
    lane = lax.broadcasted_iota(jnp.int32, (1, beams), 1)
    for back in range(1, BEAMS):
        same = (pltpu.roll(parents, back, 1) == parents) & (lane % BEAMS >= back)
        counts = jnp.where(same, 0.0, counts)
    source = (parents // BEAMS) % SPAN
    rows = jnp.concatenate([jnp.where(source == at, counts, 0.0) for at in range(SPAN)] * 4, axis=0).astype(jnp.bfloat16)
    child = lax.broadcasted_iota(jnp.int32, (beams, 128), 0)
    ring = lax.broadcasted_iota(jnp.int32, (beams, 128), 1)
    flows = []
    for target in range(SPAN):
        member = (child // BEAMS % SPAN == target) & (child // (BEAMS * SPAN) == ring)
        flows.append(jnp.dot(rows, jnp.where(member, 1.0, 0.0).astype(jnp.bfloat16), preferred_element_type=jnp.float32))

    def flow(at, ahead):
        return flows[(at + ahead) % SPAN][at:at + 1].astype(jnp.int32)

    up, far, down = ([flow(at, ahead) for at in range(SPAN)] for ahead in (1, 2, 3))
    via_up, via_down = balanced(up, far, down)
    out = jnp.zeros_like(up[0])
    for at in range(SPAN):
        load_up = up[at] + via_up[at] + via_up[(at - 1) % SPAN]
        load_down = down[at] + via_down[at] + via_down[(at + 1) % SPAN]
        out = jnp.maximum(out, jnp.maximum(load_up, load_down))
    return jnp.max(out)


def slots_of_children(parents, me):
    taken = [jnp.int32(0) for _ in range(SPAN)]
    slots, owners = [], []
    for child in range(BEAMS):
        parent = parents[me * BEAMS + child]
        apart = jnp.bitwise_and(parent // BEAMS - me, SPAN - 1)
        slot = jnp.int32(0)
        for distance in range(SPAN):
            hit = apart == distance
            slot = jnp.where(hit, distance * MOST + taken[distance], slot)
            taken[distance] = taken[distance] + hit.astype(jnp.int32)
        slots.append(slot)
        owners.append(parent)
    return slots, owners


def served_beams(parents, me, target):
    count = jnp.int32(0)
    beams = [jnp.int32(0) for _ in range(MOST)]
    for child in range(BEAMS):
        parent = parents[target * BEAMS + child]
        hit = parent // BEAMS == me
        for rank in range(MOST):
            beams[rank] = jnp.where(hit & (count == rank), parent % BEAMS, beams[rank])
        count = count + hit.astype(jnp.int32)
    return beams


def exchange_kernel(
    q_hbm, new_hbm, pool_ref, table_hbm, len_hbm, par_hbm, w_ref,
    recv_ref, proj_ref, left_ref, meta_ref, over_ref,
    q_ref, new_ref, table_ref, len_ref, par_ref, len_row, par_row,
    pool_v, w_v, stage, first_send, first_recv, rest_send, left_send, q_send, q_recv, att, p_send, p_recv, r_send, lens, beams,
    in_sem, pool_sem, w_sem, own_sem, land_sem, qs_sem, qr_sem, bs_sem, br_sem, ps_sem, pr_sem, rs_sem, rr_sem, here_sem,
):
    me = lax.axis_index("dp")
    mine = lax.axis_index("tensor")
    shards = lax.axis_size("tensor")
    y = lax.rem(me, SPAN)
    base = me - y
    context = stage.shape[1] * GRAIN // MOST
    rings = lax.axis_size("dp") // SPAN
    wide = q_hbm.shape[2]
    heads = wide // HD
    rows = MOST * STEPS

    def peer(distance):
        return base + lax.rem(y + distance, SPAN)

    barrier = pltpu.get_barrier_semaphore()
    for distance in range(1, SPAN):
        pl.semaphore_signal(barrier, inc=1, device_id={"dp": peer(distance)}, device_id_type=MESH)
    for other in range(1, shards):
        @pl.when(mine + other < shards)
        def _(other=other):
            pl.semaphore_signal(barrier, inc=1, device_id={"tensor": mine + other}, device_id_type=MESH)
    in_copies = []
    operands = ((par_hbm, par_ref), (q_hbm, q_ref), (new_hbm, new_ref), (table_hbm, table_ref), (len_hbm, len_ref))
    rows_in = ((par_hbm, par_row.at[0]), (len_hbm, len_row.at[0]))
    for at, (source, target) in enumerate(operands):
        copy = pltpu.make_async_copy(source, target, in_sem.at[at])
        copy.start()
        in_copies.append(copy)
    row_copies = []
    for at, (source, target) in enumerate(rows_in):
        copy = pltpu.make_async_copy(source, target, in_sem.at[5 + at])
        copy.start()
        row_copies.append(copy)
    quarter = pool_v.shape[0] // 4
    pool_copies = []
    for at in range(4):
        span = pl.ds(at * quarter, quarter)
        copy = pltpu.make_async_copy(pool_ref.at[span], pool_v.at[span], pool_sem.at[at])
        copy.start()
        pool_copies.append(copy)
    for copy in in_copies:
        copy.wait()

    slots, owners = slots_of_children(par_ref, me)
    plan = ring_plan(par_ref, len_ref, me >> 2)
    up, down, via_up, via_down = plan
    flows = {}
    for ahead in range(SPAN):
        served = served_beams(par_ref, me, peer(ahead))
        distance = (SPAN - ahead) % SPAN
        held = [len_ref[me * BEAMS + served[rank]] for rank in range(MOST)]
        for rank in range(MOST):
            beams[distance * MOST + rank] = served[rank]
            lens[distance * MOST + rank] = held[rank]
        flows[ahead] = (served[0], served[1], grains(held[0]))

    def grain_at(flow, number):
        first, second, cut = flow
        later = number >= cut
        number = jnp.where(later, number - cut, number)
        number = jnp.minimum(jnp.maximum(number, 0), PER_CHILD - 1)
        return table_ref[jnp.where(later, second, first), number >> 2] * PER_PAGE + (number & (PER_PAGE - 1))

    sides = (
        (flows[1], choose(via_up, y), jnp.int32(0), choose(via_up, (y - 1) & 3), peer(1)),
        (flows[3], choose(via_down, y), choose(via_up, y), choose(via_down, (y + 1) & 3), peer(3)),
    )
    pl.semaphore_wait(barrier, SPAN - 1 + mine)
    for other in range(1, shards):
        @pl.when(mine >= other)
        def _(other=other):
            pl.semaphore_signal(here_sem, inc=1, device_id={"tensor": mine - other}, device_id_type=MESH)
    for copy in pool_copies:
        copy.wait()
    b_copies = []
    cuts = (0, 8, VIA, FIRST)

    def send_part(part):
        for side, (flow, mine_via, skip, _, target) in enumerate(sides):
            def put(at, carry, side=side, flow=flow, mine_via=mine_via, skip=skip):
                for at in [4 * at + more for more in range(4)]:
                    far = at < mine_via
                    chosen = tuple(jnp.where(far, one, two) for one, two in zip(flows[2], flow))
                    number = jnp.where(far, skip + at, at - mine_via)
                    first_send[side, at] = pool_v[grain_at(chosen, number)]
                return carry

            lax.fori_loop(cuts[part] // 4, cuts[part + 1] // 4, put, 0)
            span = pl.ds(cuts[part], cuts[part + 1] - cuts[part])
            copy = pltpu.make_async_remote_copy(
                src_ref=first_send.at[side, span], dst_ref=first_recv.at[side, span],
                send_sem=bs_sem.at[side * 4 + part], recv_sem=br_sem.at[side * 4 + part],
                device_id={"dp": target}, device_id_type=MESH,
            )
            copy.start()
            b_copies.append(copy)

    send_part(0)

    row = lax.broadcasted_iota(jnp.int32, (SPAN * rows, BEAMS), 0)
    col = lax.broadcasted_iota(jnp.int32, (SPAN * rows, BEAMS), 1)
    slot_at = jnp.zeros_like(col)
    for child in range(BEAMS):
        slot_at = jnp.where(col == child, slots[child], slot_at)
    q_sorted = jnp.zeros((SPAN * rows, wide), jnp.float32)
    new_sorted = jnp.zeros((SPAN * rows, 2 * HD), jnp.float32)
    for step in range(STEPS):
        pick = jnp.where((row // STEPS == slot_at) & (row % STEPS == step), 1.0, 0.0).astype(jnp.bfloat16)
        q_sorted += jnp.dot(pick, q_ref[step], preferred_element_type=jnp.float32)
        new_sorted += jnp.dot(pick, new_ref[step], preferred_element_type=jnp.float32)
    both = jnp.concatenate([q_sorted, new_sorted], axis=1)
    half = both.shape[1] // 2
    for distance in range(SPAN):
        part = both[distance * rows:(distance + 1) * rows]
        part = jnp.concatenate([part[:, :half], part[:, half:]], axis=0).astype(jnp.bfloat16)
        if distance == 0:
            q_recv[0] = part
        else:
            q_send[distance] = part
    q_copies = []
    for distance in range(1, SPAN):
        copy = pltpu.make_async_remote_copy(
            src_ref=q_send.at[distance], dst_ref=q_recv.at[distance],
            send_sem=qs_sem.at[distance], recv_sem=qr_sem.at[distance],
            device_id={"dp": peer(distance)}, device_id_type=MESH,
        )
        copy.start()
        q_copies.append(copy)
    send_part(1)
    send_part(2)
    w_copies = []
    for block in range(shards):
        copy = pltpu.make_async_copy(w_ref.at[:, pl.ds(block * wide, wide)], w_v.at[block], w_sem.at[block])
        copy.start()
        w_copies.append(copy)

    def put_all(index, carry):
        slot = index // PAGES
        page = table_ref[beams[slot], index % PAGES]
        at = (index % (MOST * PAGES)) * PER_PAGE
        stage[index // (MOST * PAGES), pl.ds(at, PER_PAGE)] = pool_v[pl.ds(page * PER_PAGE, PER_PAGE)]
        return carry

    lax.fori_loop(0, SPAN * MOST * PAGES, put_all, 0)
    own_copy = pltpu.make_async_copy(stage.at[0], recv_ref.at[pl.ds(2 * LINK, MOST * PER_CHILD)], own_sem.at[0])
    own_copy.start()

    for copy in q_copies:
        copy.wait()

    def attend(distance):
        message = q_recv[distance].astype(jnp.float32)
        message = jnp.concatenate([message[:rows], message[rows:]], axis=1)
        q_rows = jnp.concatenate([message[:, h * HD:(h + 1) * HD] for h in range(heads)], axis=0).astype(jnp.bfloat16)
        fresh = message[:, wide:].astype(jnp.bfloat16)
        old_len = lens[distance * MOST]
        last_len = lens[distance * MOST + 1]
        contract = (((1,), (1,)), ((), ()))
        scale = HD ** -0.5
        half = MOST * PER_CHILD // 2
        keys = [stage[distance, pl.ds(rank * half, half), :, 0:HD].reshape(context, HD) for rank in range(MOST)]
        scores = [lax.dot_general(q_rows, key, contract, preferred_element_type=jnp.float32) for key in keys]
        rank_at = lax.broadcasted_iota(jnp.int32, scores[0].shape, 0) // STEPS % MOST
        scores = jnp.where(rank_at == 0, scores[0], scores[1]) * scale
        fresh_scores = lax.dot_general(q_rows, fresh[:, :HD], contract, preferred_element_type=jnp.float32) * scale
        position = lax.broadcasted_iota(jnp.int32, scores.shape, 1)
        limit = jnp.where(rank_at == 0, old_len, last_len)
        scores = jnp.where(position < limit, scores, -1e30)
        f_row = lax.broadcasted_iota(jnp.int32, fresh_scores.shape, 0)
        f_col = lax.broadcasted_iota(jnp.int32, fresh_scores.shape, 1)
        seen = (f_row // STEPS % MOST == f_col // STEPS) & (f_col % STEPS <= f_row % STEPS)
        fresh_scores = jnp.where(seen, fresh_scores, -1e30)
        top = jnp.maximum(jnp.max(scores, axis=1, keepdims=True), jnp.max(fresh_scores, axis=1, keepdims=True))
        exp_old = jnp.exp(scores - top)
        exp_new = jnp.exp(fresh_scores - top)
        total = jnp.sum(exp_old, axis=1, keepdims=True) + jnp.sum(exp_new, axis=1, keepdims=True)
        share = 1.0 / total
        w_old = (exp_old * share).astype(jnp.bfloat16)
        w_new = (exp_new * share).astype(jnp.bfloat16)
        values = [stage[distance, pl.ds(rank * half, half), :, HD:2 * HD].reshape(context, HD) for rank in range(MOST)]
        out = [jnp.dot(w_old, value, preferred_element_type=jnp.float32) for value in values]
        out = jnp.where(rank_at[:, :HD] == 0, out[0], out[1])
        out += jnp.dot(w_new, fresh[:, HD:], preferred_element_type=jnp.float32)
        out = jnp.concatenate([out[h * rows:(h + 1) * rows] for h in range(heads)], axis=1)
        att[pl.ds(pl.multiple_of(distance * rows, rows), rows), :] = out

    def attend_two(at, carry):
        attend(2 * at)
        attend(2 * at + 1)
        return carry

    lax.fori_loop(0, SPAN // 2, attend_two, 0)
    for copy in b_copies[:4]:
        copy.wait()
    more_copies = b_copies[4:]
    b_copies = []
    for side, (flow, mine_via, _, passed, target) in enumerate(sides):
        def put_passed(at, carry, side=side, flow=flow, mine_via=mine_via, passed=passed):
            for at in [4 * at + more for more in range(4)]:
                here = pool_v[grain_at(flow, FIRST - mine_via + at - passed)]
                rest_send[side, at] = jnp.where(at < passed, first_recv[side, at], here)
            return carry

        lax.fori_loop(0, REST // 4, put_passed, 0)
        copy = pltpu.make_async_remote_copy(
            src_ref=rest_send.at[side], dst_ref=recv_ref.at[pl.ds(side * LINK + FIRST, REST)],
            send_sem=bs_sem.at[side * 4 + 3], recv_sem=br_sem.at[side * 4 + 3],
            device_id={"dp": target}, device_id_type=MESH,
        )
        copy.start()
        b_copies.append(copy)
    attended = att[...].astype(jnp.bfloat16)
    for copy in w_copies:
        copy.wait()

    def p_copy(other):
        return pltpu.make_async_remote_copy(
            src_ref=p_send.at[other], dst_ref=p_recv.at[other],
            send_sem=ps_sem.at[other], recv_sem=pr_sem.at[other],
            device_id={"tensor": lax.rem(mine + other, shards)}, device_id_type=MESH,
        )

    def project(other, carry):
        product = jnp.dot(attended, w_v[lax.rem(mine + other, shards)], preferred_element_type=jnp.float32)
        p_send[other] = product.astype(jnp.bfloat16)
        p_copy(other).start()
        return carry

    @pl.when(mine < shards - 1)
    def _():
        pl.semaphore_wait(here_sem, shards - 1 - mine)

    lax.fori_loop(1, shards, project, 0)
    own = jnp.dot(attended, w_v[mine], preferred_element_type=jnp.float32)

    for copy in more_copies:
        copy.wait()
    for side in range(2):
        copy = pltpu.make_async_copy(first_recv.at[side], recv_ref.at[pl.ds(side * LINK, FIRST)], land_sem.at[side])
        copy.start()
        b_copies.append(copy)

    def gather_sums(other, total):
        p_copy(other).wait()
        return total + p_recv[other].astype(jnp.float32)

    summed = lax.fori_loop(1, shards, gather_sums, own)
    half = wide // 2
    r_copies = []
    for distance in range(SPAN):
        part = summed[distance * rows:(distance + 1) * rows]
        r_send[distance] = jnp.concatenate([part[:, :half], part[:, half:]], axis=0).astype(jnp.bfloat16)
        if distance == 0:
            copy = pltpu.make_async_copy(r_send.at[0], proj_ref.at[0], own_sem.at[1])
        else:
            copy = pltpu.make_async_remote_copy(
                src_ref=r_send.at[distance], dst_ref=proj_ref.at[distance],
                send_sem=rs_sem.at[distance], recv_sem=rr_sem.at[distance],
                device_id={"dp": peer(SPAN - distance)}, device_id_type=MESH,
            )
        copy.start()
        r_copies.append(copy)
    for copy in row_copies:
        copy.wait()
    load = heaviest(par_row[...], len_row[...], rings)
    over_ref[0] = jnp.where(load > LINK, 1, 0) + jnp.where(load > LINK + LEFT, 1, 0)
    for side, (flow, mine_via, _, passed, _) in enumerate(sides):
        def put_left(at, carry, side=side, flow=flow, mine_via=mine_via, passed=passed):
            for at in [4 * at + more for more in range(4)]:
                left_send[side, at] = pool_v[grain_at(flow, LINK - mine_via - passed + at)]
            return carry

        lax.fori_loop(0, LEFT // 4, put_left, 0)
    left_copy = pltpu.make_async_copy(left_send, left_ref, land_sem.at[2])
    left_copy.start()
    for child in range(BEAMS):
        slot = slots[child]
        distance = slot >> 1
        length = len_ref[owners[child]]
        before = jnp.int32(0)
        for other in range(BEAMS):
            if other != child:
                mate = (slots[other] >> 1 == distance) & (slots[other] < slot)
                differs = owners[other] != owners[child]
                before = jnp.where(mate & differs, grains(len_ref[owners[other]]), before)
        from_up = choose(via_up, (y - 1) & 3), choose(via_up, (y + 2) & 3)
        from_down = choose(via_down, (y + 1) & 3), choose(via_down, (y + 2) & 3)
        near_via = jnp.where(distance == 3, from_up[0], from_down[0])
        near_pass = jnp.where(distance == 3, from_up[1], from_down[1])
        near_base = jnp.where(distance == 3, 0, LINK)
        split = jnp.where(distance == 2, from_up[1], FIRST - near_via) - before
        split = jnp.minimum(jnp.maximum(split, 0), PER_CHILD)
        start = jnp.where(distance == 2, FIRST + before, near_base + near_via + before)
        again = jnp.where(distance == 2, LINK + FIRST + before + split - from_up[1], start + split + near_pass)
        near = jnp.where(distance == 2, False, distance != 0)
        until = LINK - near_via - near_pass - before
        until = jnp.where(near, jnp.minimum(jnp.maximum(until, 0), PER_CHILD), PER_CHILD)
        third = jnp.where(distance == 3, 0, LEFT) + near_via + near_pass + before + until - LINK
        stays = distance == 0
        meta_ref[child * META] = length
        meta_ref[child * META + 1] = jnp.where(stays, 2 * LINK + (slot & 1) * PER_CHILD, start)
        meta_ref[child * META + 2] = jnp.where(stays, PER_CHILD, split)
        meta_ref[child * META + 3] = jnp.where(stays, 0, again)
        meta_ref[child * META + 4] = until
        meta_ref[child * META + 5] = jnp.where(near, third, 0)
        meta_ref[child * META + 6] = slot
    for copy in r_copies:
        copy.wait()
    for copy in b_copies:
        copy.wait()
    own_copy.wait()
    left_copy.wait()


def full_kernel(
    pool_ref, table_hbm, par_hbm, recv_ref,
    table_ref, par_ref, pool_v, stage,
    in_sem, pool_sem, own_sem, bs_sem, br_sem,
):
    me = lax.axis_index("dp")
    y = lax.rem(me, SPAN)
    base = me - y
    context = stage.shape[1] // MOST

    def peer(distance):
        return base + lax.rem(y + distance, SPAN)

    barrier = pltpu.get_barrier_semaphore()
    for distance in range(1, SPAN):
        pl.semaphore_signal(barrier, inc=1, device_id={"dp": peer(distance)}, device_id_type=MESH)
    in_copies = []
    for at, (source, target) in enumerate(((par_hbm, par_ref), (table_hbm, table_ref))):
        copy = pltpu.make_async_copy(source, target, in_sem.at[at])
        copy.start()
        in_copies.append(copy)
    pool_copy = pltpu.make_async_copy(pool_ref, pool_v, pool_sem)
    pool_copy.start()
    for copy in in_copies:
        copy.wait()
    pl.semaphore_wait(barrier, SPAN - 1)
    pool_copy.wait()
    copies = []
    for distance in (2, 1, 3, 0):
        served = served_beams(par_ref, me, peer(SPAN - distance))
        for rank in range(MOST):
            beam = served[rank]

            def put(index, carry, distance=distance, rank=rank, beam=beam):
                at = pl.multiple_of(rank * context + index * PAGE, PAGE)
                stage[distance, pl.ds(at, PAGE), :] = pool_v[table_ref[beam, index]]
                return carry

            lax.fori_loop(0, context // PAGE, put, 0)
            span = pl.ds(rank * context, context)
            if distance == 0:
                copy = pltpu.make_async_copy(stage.at[0, span], recv_ref.at[0, span], own_sem.at[rank])
            else:
                copy = pltpu.make_async_remote_copy(
                    src_ref=stage.at[distance, span], dst_ref=recv_ref.at[distance, span],
                    send_sem=bs_sem.at[distance * MOST + rank], recv_sem=br_sem.at[distance * MOST + rank],
                    device_id={"dp": peer(SPAN - distance)}, device_id_type=MESH,
                )
            copy.start()
            copies.append(copy)
    for copy in copies:
        copy.wait()


def finish_kernel(recv_ref, raw_ref, new_hbm, len_hbm, par_hbm, proj_ref, cache_ref, new_ref, len_ref, par_ref, edge, zeros, in_sem, out_sem):
    me = lax.axis_index("dp")
    pages = recv_ref.shape[1] // PAGE
    operands = ((par_hbm, par_ref), (len_hbm, len_ref), (new_hbm, new_ref))
    in_copies = [pltpu.make_async_copy(source, target, in_sem.at[at]) for at, (source, target) in enumerate(operands)]
    for copy in in_copies:
        copy.start()
    zeros[...] = jnp.zeros_like(zeros)
    for copy in in_copies:
        copy.wait()
    slots, owners = slots_of_children(par_ref, me)
    fresh = [new_ref[step].astype(jnp.float32) for step in range(STEPS)]
    for child in range(BEAMS):
        slot = slots[child]
        length = len_ref[owners[child]]
        first = length // PAGE
        last = (length + STEPS - 1) // PAGE

        def whole(index, carry, child=child, slot=slot):
            span = pl.ds(pl.multiple_of(index * PAGE, PAGE), PAGE)
            pltpu.make_async_copy(recv_ref.at[slot, span], cache_ref.at[child, span], out_sem).start()
            return carry

        def clear(index, carry, child=child):
            span = pl.ds(pl.multiple_of(index * PAGE, PAGE), PAGE)
            pltpu.make_async_copy(zeros, cache_ref.at[child, span], out_sem).start()
            return carry

        def fix(index, carry, child=child, slot=slot, length=length, first=first):
            at = pl.multiple_of(index * PAGE, PAGE)
            position = at + lax.broadcasted_iota(jnp.int32, (PAGE, 2 * HD), 0)
            page = recv_ref[slot, pl.ds(at, PAGE), :].astype(jnp.float32)
            page = jnp.where(position < length, page, 0.0)
            for step in range(STEPS):
                page = jnp.where(position == length + step, fresh[step][child:child + 1], page)
            edge[child * 2 + index - first] = page.astype(jnp.bfloat16)
            pltpu.make_async_copy(edge.at[child * 2 + index - first], cache_ref.at[child, pl.ds(at, PAGE)], out_sem).start()
            return carry

        lax.fori_loop(0, first, whole, 0)
        lax.fori_loop(last + 1, pages, clear, 0)
        lax.fori_loop(first, last + 1, fix, 0)

    rows = MOST * STEPS
    raw = []
    for distance in range(SPAN):
        part = raw_ref[distance].astype(jnp.float32)
        raw.append(jnp.concatenate([part[:rows], part[rows:]], axis=1))
    raw = jnp.concatenate(raw, axis=0).astype(jnp.bfloat16)
    row = lax.broadcasted_iota(jnp.int32, (BEAMS, SPAN * rows), 0)
    col = lax.broadcasted_iota(jnp.int32, (BEAMS, SPAN * rows), 1)
    slot_at = jnp.zeros_like(col)
    for child in range(BEAMS):
        slot_at = jnp.where(row == child, slots[child], slot_at)
    for step in range(STEPS):
        pick = jnp.where(col == slot_at * STEPS + step, 1.0, 0.0).astype(jnp.bfloat16)
        proj_ref[step] = jnp.dot(pick, raw, preferred_element_type=jnp.float32).astype(jnp.bfloat16)
    pltpu.make_async_copy(recv_ref, cache_ref, out_sem).wait()


def left_kernel(left_ref, got_ref, send_sem, recv_sem):
    me = lax.axis_index("dp")
    y = lax.rem(me, SPAN)
    targets = [me - y + lax.rem(y + ahead, SPAN) for ahead in (1, SPAN - 1)]
    barrier = pltpu.get_barrier_semaphore()
    for target in targets:
        pl.semaphore_signal(barrier, inc=1, device_id={"dp": target}, device_id_type=MESH)
    pl.semaphore_wait(barrier, 2)
    copies = []
    for side, target in enumerate(targets):
        copy = pltpu.make_async_remote_copy(
            src_ref=left_ref.at[side], dst_ref=got_ref.at[side],
            send_sem=send_sem.at[side], recv_sem=recv_sem.at[side],
            device_id={"dp": target}, device_id_type=MESH,
        )
        copy.start()
        copies.append(copy)
    for copy in copies:
        copy.wait()


def place_kernel(with_left, recv_ref, raw_ref, new_ref, meta_ref, *refs):
    left_ref = refs[0] if with_left else None
    proj_hbm, cache_ref, edge, zeros, proj_ref, out_sem, proj_sem = refs[-7:]
    total = recv_ref.shape[0]
    zeros[...] = jnp.zeros_like(zeros)
    fresh = [new_ref[step].astype(jnp.float32) for step in range(STEPS)]
    slots = [meta_ref[child * META + 6] for child in range(BEAMS)]
    per_child = cache_ref.shape[1]
    scale = GRAIN // TILE
    for child in range(BEAMS):
        length, start, split, again, until, third = (meta_ref[child * META + at] for at in range(6))
        first = length // TILE
        last = (length + STEPS - 1) // TILE
        until = jnp.minimum(until * scale, first) if with_left else first
        split = jnp.minimum(split * scale, until)

        def move(source, source_at, at, count, child=child):
            @pl.when(count > 0)
            def _():
                pltpu.make_async_copy(
                    source.at[pl.ds(source_at, count)], cache_ref.at[child, pl.ds(at, count)], out_sem
                ).start()

        move(recv_ref, start * scale, 0, split)
        move(recv_ref, again * scale, split, until - split)
        if with_left:
            move(left_ref, third * scale, until, first - until)
        move(zeros, 0, last + 1, per_child - 1 - last)
    for child in range(BEAMS):
        length, start, split, again, until, third = (meta_ref[child * META + at] for at in range(6))
        first = length // TILE
        last = (length + STEPS - 1) // TILE

        def fix(
            index, carry, child=child, length=length, first=first, start=start * scale, split=split * scale,
            again=again * scale, until=until * scale, third=third * scale,
        ):
            position = index * TILE + lax.broadcasted_iota(jnp.int32, (TILE, 2 * HD), 0)
            at = jnp.minimum(jnp.where(index < split, start + index, again + index - split), total - 1)
            part = recv_ref[at].astype(jnp.float32)
            if with_left:
                at = jnp.minimum(jnp.maximum(third + index - until, 0), left_ref.shape[0] - 1)
                part = jnp.where(index < until, part, left_ref[at].astype(jnp.float32))
            part = jnp.where(position < length, part, 0.0)
            for step in range(STEPS):
                part = jnp.where(position == length + step, fresh[step][child:child + 1], part)
            edge[child * 2 + index - first] = part.astype(jnp.bfloat16)
            pltpu.make_async_copy(edge.at[child * 2 + index - first], cache_ref.at[child, index], out_sem).start()
            return carry

        lax.fori_loop(first, last + 1, fix, 0)

    rows = MOST * STEPS
    raw = []
    for distance in range(SPAN):
        part = raw_ref[distance].astype(jnp.float32)
        raw.append(jnp.concatenate([part[:rows], part[rows:]], axis=1))
    raw = jnp.concatenate(raw, axis=0).astype(jnp.bfloat16)
    row = lax.broadcasted_iota(jnp.int32, (BEAMS, SPAN * rows), 0)
    col = lax.broadcasted_iota(jnp.int32, (BEAMS, SPAN * rows), 1)
    slot_at = jnp.zeros_like(col)
    for child in range(BEAMS):
        slot_at = jnp.where(row == child, slots[child], slot_at)
    for step in range(STEPS):
        pick = jnp.where(col == slot_at * STEPS + step, 1.0, 0.0).astype(jnp.bfloat16)
        proj_ref[step] = jnp.dot(pick, raw, preferred_element_type=jnp.float32).astype(jnp.bfloat16)
    proj_copy = pltpu.make_async_copy(proj_ref, proj_hbm, proj_sem)
    proj_copy.start()
    pltpu.make_async_copy(cache_ref, cache_ref, out_sem).wait()
    proj_copy.wait()


def local(shards, queries, new_kv, kv_pool, page_tables, lengths, parents, out_weight):
    wide = queries.shape[2]
    channels = kv_pool.shape[2]
    context = page_tables.shape[1] * kv_pool.shape[1]
    rows = MOST * STEPS
    vmem = pl.BlockSpec(memory_space=pltpu.VMEM)
    smem = pl.BlockSpec(memory_space=pltpu.SMEM)
    hbm = pl.BlockSpec(memory_space=pltpu.HBM)
    free = pl.BlockSpec(memory_space=pl.ANY)
    dma = pltpu.SemaphoreType.DMA
    bf16 = jnp.bfloat16

    def pinned(*operands):
        return [pltpu.with_memory_space_constraint(operand, pltpu.HBM) for operand in operands]

    grain_pool = kv_pool.reshape(-1, GRAIN, channels)
    with jax.named_scope("exchange"):
        recv, raw, left, meta, over = pl.pallas_call(
            exchange_kernel,
            out_shape=(
                jax.ShapeDtypeStruct((2 * LINK + MOST * PER_CHILD, GRAIN, channels), bf16),
                jax.ShapeDtypeStruct((SPAN, 2 * rows, wide // 2), bf16),
                jax.ShapeDtypeStruct((2, LEFT, GRAIN, channels), bf16),
                jax.ShapeDtypeStruct((BEAMS * META,), jnp.int32),
                jax.ShapeDtypeStruct((1,), jnp.int32),
            ),
            in_specs=[hbm] * 7,
            out_specs=(free, free, free, smem, smem),
            scratch_shapes=[
                pltpu.VMEM(queries.shape, bf16),
                pltpu.VMEM(new_kv.shape, bf16),
                pltpu.SMEM(page_tables.shape, jnp.int32),
                pltpu.SMEM(lengths.shape, jnp.int32),
                pltpu.SMEM(parents.shape, jnp.int32),
                pltpu.VMEM((1, *lengths.shape), jnp.int32),
                pltpu.VMEM((1, *parents.shape), jnp.int32),
                pltpu.VMEM(grain_pool.shape, bf16),
                pltpu.VMEM((shards, out_weight.shape[0], wide), bf16),
                pltpu.VMEM((SPAN, MOST * PER_CHILD, GRAIN, channels), bf16),
                pltpu.VMEM((2, FIRST, GRAIN, channels), bf16),
                pltpu.VMEM((2, FIRST, GRAIN, channels), bf16),
                pltpu.VMEM((2, REST, GRAIN, channels), bf16),
                pltpu.VMEM((2, LEFT, GRAIN, channels), bf16),
                pltpu.VMEM((SPAN, 2 * rows, (wide + channels) // 2), bf16),
                pltpu.VMEM((SPAN, 2 * rows, (wide + channels) // 2), bf16),
                pltpu.VMEM((SPAN * rows, wide), jnp.float32),
                pltpu.VMEM((shards, SPAN * rows, wide), bf16),
                pltpu.VMEM((shards, SPAN * rows, wide), bf16),
                pltpu.VMEM((SPAN, 2 * rows, wide // 2), bf16),
                pltpu.SMEM((SPAN * MOST,), jnp.int32),
                pltpu.SMEM((SPAN * MOST,), jnp.int32),
                dma((7,)), dma((4,)), dma((shards,)), dma((2,)), dma((3,)),
                dma((SPAN,)), dma((SPAN,)),
                dma((8,)), dma((8,)),
                dma((shards,)), dma((shards,)),
                dma((SPAN,)), dma((SPAN,)),
                pltpu.SemaphoreType.REGULAR,
            ],
            compiler_params=pltpu.CompilerParams(
                collective_id=0, has_side_effects=True, vmem_limit_bytes=48 * 1024 * 1024
            ),
            name="exchange",
        )(*pinned(queries, new_kv, grain_pool, page_tables, lengths, parents, out_weight))

    def place(*got):
        with jax.named_scope("place"):
            projected, cache = pl.pallas_call(
                functools.partial(place_kernel, len(got) > 0),
                out_shape=(
                    jax.ShapeDtypeStruct(queries.shape, bf16),
                    jax.ShapeDtypeStruct((BEAMS, context // TILE, TILE, channels), bf16),
                ),
                in_specs=[vmem, vmem, vmem, smem] + [vmem] * len(got),
                out_specs=(free, free),
                scratch_shapes=[
                    pltpu.VMEM((2 * BEAMS, TILE, channels), bf16),
                    pltpu.VMEM((context // TILE, TILE, channels), bf16),
                    pltpu.VMEM(queries.shape, bf16),
                    dma, dma,
                ],
                compiler_params=pltpu.CompilerParams(vmem_limit_bytes=24 * 1024 * 1024),
                name="place_left" if got else "place",
            )(recv.reshape(-1, TILE, channels), raw, new_kv, meta, *got)
            return projected, cache.reshape(BEAMS, context, channels)

    def placed():
        return place()

    def topped():
        with jax.named_scope("left"):
            got = pl.pallas_call(
                left_kernel,
                out_shape=jax.ShapeDtypeStruct(left.shape, bf16),
                in_specs=[free],
                out_specs=free,
                scratch_shapes=[dma((2,)), dma((2,))],
                compiler_params=pltpu.CompilerParams(
                    collective_id=2, has_side_effects=True, vmem_limit_bytes=4 * 1024 * 1024
                ),
                name="left",
            )(left)
        return place(got.reshape(-1, TILE, channels))

    def resent():
        with jax.named_scope("full"):
            whole = pl.pallas_call(
                full_kernel,
                out_shape=jax.ShapeDtypeStruct((SPAN, MOST * context, channels), bf16),
                in_specs=[hbm] * 3,
                out_specs=free,
                scratch_shapes=[
                    pltpu.SMEM(page_tables.shape, jnp.int32),
                    pltpu.SMEM(parents.shape, jnp.int32),
                    pltpu.VMEM(kv_pool.shape, bf16),
                    pltpu.VMEM((SPAN, MOST * context, channels), bf16),
                    dma((2,)), dma, dma((MOST,)),
                    dma((SPAN * MOST,)), dma((SPAN * MOST,)),
                ],
                compiler_params=pltpu.CompilerParams(
                    collective_id=1, has_side_effects=True, vmem_limit_bytes=24 * 1024 * 1024
                ),
                name="full",
            )(*pinned(kv_pool, page_tables, parents))
        with jax.named_scope("finish"):
            return pl.pallas_call(
                finish_kernel,
                out_shape=(
                    jax.ShapeDtypeStruct(queries.shape, bf16),
                    jax.ShapeDtypeStruct((BEAMS, context, channels), bf16),
                ),
                in_specs=[vmem, vmem, hbm, hbm, hbm],
                out_specs=(vmem, hbm),
                scratch_shapes=[
                    pltpu.VMEM(new_kv.shape, bf16),
                    pltpu.SMEM(lengths.shape, jnp.int32),
                    pltpu.SMEM(parents.shape, jnp.int32),
                    pltpu.VMEM((2 * BEAMS, PAGE, channels), bf16),
                    pltpu.VMEM((PAGE, channels), bf16),
                    dma((3,)), dma,
                ],
                compiler_params=pltpu.CompilerParams(vmem_limit_bytes=24 * 1024 * 1024),
                name="finish",
            )(whole.reshape(BEAMS, context, channels), raw, new_kv, lengths, parents)

    return lax.switch(over[0], (placed, topped, resent))


def solution(mesh):
    in_specs = (
        P(None, "dp", "tensor"),
        P(None, "dp", "tensor"),
        P("dp", None, "tensor"),
        P("dp", None),
        P(),
        P(),
        P("tensor", None),
    )
    out_specs = (P(None, "dp", "tensor"), P("dp", None, "tensor"))
    body = functools.partial(local, mesh.shape["tensor"])
    return jax.shard_map(body, mesh=mesh, in_specs=in_specs, out_specs=out_specs, check_vma=False)
```

```python
import functools

import jax
import jax.numpy as jnp
from jax import lax
from jax.experimental import pallas as pl
from jax.experimental.pallas import tpu as pltpu
from jax.sharding import PartitionSpec as P

HD = 128
SPAN = 4
MOST = 2
BEAMS = 8
STEPS = 4
PAGE = 128
PAGES = 8
GRAIN = 32
PER_CHILD = 32
PER_PAGE = PAGE // GRAIN
TILE = 16
VIA = 36
MORE = 24
REST = 36
LEFT = 12
FIRST = VIA + MORE
LINK = FIRST + REST
META = 7
MESH = pl.DeviceIdType.MESH


def grains(length):
    return (length + (GRAIN - 1)) // GRAIN


def choose(values, index):
    out = values[0]
    for at in range(1, len(values)):
        out = jnp.where(index == at, values[at], out)
    return out


def balanced(up, far, down, keep_up, keep_down):
    least = [jnp.maximum(keep_up[i], far[i] - VIA) for i in range(SPAN)]
    most = [jnp.minimum(far[i] - keep_down[i], VIA) for i in range(SPAN)]
    via_up = [jnp.minimum(jnp.maximum(far[i] >> 1, least[i]), most[i]) for i in range(SPAN)]
    for at in range(SPAN):
        via_down = [far[i] - via_up[i] for i in range(SPAN)]
        nxt, prv = (at + 1) % SPAN, (at - 1) % SPAN
        load_up = jnp.maximum(up[at] + via_up[prv], up[nxt] + via_up[nxt])
        load_down = jnp.maximum(down[at] + via_down[nxt], down[prv] + via_down[prv])
        best = (load_down + far[at] - load_up) >> 1
        via_up[at] = jnp.minimum(jnp.maximum(best, least[at]), most[at])
    via_down = [far[i] - via_up[i] for i in range(SPAN)]
    return via_up, via_down


def planned(flows):
    names = ("up", "down", "far", "first", "second", "cut", "up_id", "down_id", "keep_up", "keep_down")
    plan = {name: [] for name in names}
    for at in range(SPAN):
        u0, u1, gu0, gu1 = flows[at][1]
        f0, f1, gf0, gf1 = flows[at][2]
        d0, d1, gd0, gd1 = flows[at][3]
        gu1 = jnp.where(u0 == u1, 0, gu1)
        gf1 = jnp.where(f0 == f1, 0, gf1)
        gd1 = jnp.where(d0 == d1, 0, gd1)

        def shared(parent, count, one, two):
            return jnp.where((parent == one) | (parent == two), count, 0)

        straight = shared(f0, gf0, u0, u1) + shared(f1, gf1, d0, d1)
        crossed = shared(f1, gf1, u0, u1) + shared(f0, gf0, d0, d1)
        swap = crossed > straight
        first, second = jnp.where(swap, f1, f0), jnp.where(swap, f0, f1)
        cut, rest = jnp.where(swap, gf1, gf0), jnp.where(swap, gf0, gf1)
        keep_up, keep_down = shared(first, cut, u0, u1), shared(second, rest, d0, d1)
        values = (
            gu0 + gu1 - keep_up, gd0 + gd1 - keep_down, gf0 + gf1, first, second, cut,
            jnp.where(keep_up > 0, first, -1), jnp.where(keep_down > 0, second, -1), keep_up, keep_down,
        )
        for name, value in zip(names, values):
            plan[name].append(value)
    plan["via_up"], plan["via_down"] = balanced(
        plan["up"], plan["far"], plan["down"], plan["keep_up"], plan["keep_down"]
    )
    return plan


def ring_plan(parents, lengths, ring):
    flows = [[None] * SPAN for _ in range(SPAN)]
    for target in range(SPAN):
        owners = [parents[(ring * SPAN + target) * BEAMS + child] for child in range(BEAMS)]
        sources = [(owner >> 3) & (SPAN - 1) for owner in owners]
        for at in range(SPAN):
            if at != target:
                one, two = owners[0], owners[0]
                for child in range(1, BEAMS):
                    two = jnp.where(sources[child] == at, owners[child], two)
                one = owners[BEAMS - 1]
                for child in range(BEAMS - 2, -1, -1):
                    one = jnp.where(sources[child] == at, owners[child], one)
                flows[at][(target - at) % SPAN] = (one, two, grains(lengths[one]), grains(lengths[two]))
    return planned(flows)


def heaviest(parents, lengths, rings):
    beams = rings * SPAN * BEAMS
    counts = grains(lengths).astype(jnp.float32).astype(jnp.bfloat16)
    beam = lax.broadcasted_iota(jnp.int32, (beams, beams), 0)
    chosen = jnp.where(beam == parents, 1.0, 0.0).astype(jnp.bfloat16)
    counts = jnp.dot(jnp.broadcast_to(counts, (16, beams)), chosen, preferred_element_type=jnp.float32)[:1]
    lane = lax.broadcasted_iota(jnp.int32, (1, beams), 1)
    source = (parents // BEAMS) % SPAN
    rank = jnp.zeros_like(lane)
    for back in range(1, BEAMS):
        rank = rank + jnp.where((pltpu.roll(source, back, 1) == source) & (lane % BEAMS >= back), 1, 0)
    names = (parents % (SPAN * BEAMS)).astype(jnp.float32)
    rows = [
        jnp.where((source == at) & (rank == order), value, 0.0)
        for value in (names, counts) for at in range(SPAN) for order in range(MOST)
    ]
    rows = jnp.concatenate(rows, axis=0).astype(jnp.bfloat16)
    child = lax.broadcasted_iota(jnp.int32, (beams, 128), 0)
    ring = lax.broadcasted_iota(jnp.int32, (beams, 128), 1)
    flows = [[None] * SPAN for _ in range(SPAN)]
    for target in range(SPAN):
        member = (child // BEAMS % SPAN == target) & (child // (BEAMS * SPAN) == ring)
        member = jnp.where(member, 1.0, 0.0).astype(jnp.bfloat16)
        found = jnp.dot(rows, member, preferred_element_type=jnp.float32).astype(jnp.int32)
        for at in range(SPAN):
            wanted = (at * MOST, at * MOST + 1, (SPAN + at) * MOST, (SPAN + at) * MOST + 1)
            flows[at][(target - at) % SPAN] = tuple(found[one:one + 1] for one in wanted)
    plan = planned(flows)
    out = jnp.zeros_like(plan["far"][0])
    for at in range(SPAN):
        load_up = plan["up"][at] + plan["via_up"][at] + plan["via_up"][(at - 1) % SPAN]
        load_down = plan["down"][at] + plan["via_down"][at] + plan["via_down"][(at + 1) % SPAN]
        out = jnp.maximum(out, jnp.maximum(load_up, load_down))
    return jnp.max(out)


def slots_of_children(parents, me):
    taken = [jnp.int32(0) for _ in range(SPAN)]
    slots, owners = [], []
    for child in range(BEAMS):
        parent = parents[me * BEAMS + child]
        apart = jnp.bitwise_and(parent // BEAMS - me, SPAN - 1)
        slot = jnp.int32(0)
        for distance in range(SPAN):
            hit = apart == distance
            slot = jnp.where(hit, distance * MOST + taken[distance], slot)
            taken[distance] = taken[distance] + hit.astype(jnp.int32)
        slots.append(slot)
        owners.append(parent)
    return slots, owners


def served_beams(parents, me, target):
    count = jnp.int32(0)
    beams = [jnp.int32(0) for _ in range(MOST)]
    for child in range(BEAMS):
        parent = parents[target * BEAMS + child]
        hit = parent // BEAMS == me
        for rank in range(MOST):
            beams[rank] = jnp.where(hit & (count == rank), parent % BEAMS, beams[rank])
        count = count + hit.astype(jnp.int32)
    return beams


def exchange_kernel(
    q_hbm, new_hbm, pool_ref, table_hbm, len_hbm, par_hbm, w_ref,
    recv_ref, proj_ref, left_ref, meta_ref, over_ref,
    q_ref, new_ref, table_ref, len_ref, par_ref, len_row, par_row,
    pool_v, w_v, stage, first_send, first_recv, rest_send, left_send, q_send, q_recv, att, p_send, p_recv, r_send, lens, beams,
    in_sem, pool_sem, w_sem, own_sem, land_sem, qs_sem, qr_sem, bs_sem, br_sem, ps_sem, pr_sem, rs_sem, rr_sem, here_sem,
):
    me = lax.axis_index("dp")
    mine = lax.axis_index("tensor")
    shards = lax.axis_size("tensor")
    y = lax.rem(me, SPAN)
    base = me - y
    context = stage.shape[1] * GRAIN // MOST
    rings = lax.axis_size("dp") // SPAN
    wide = q_hbm.shape[2]
    heads = wide // HD
    rows = MOST * STEPS

    def peer(distance):
        return base + lax.rem(y + distance, SPAN)

    barrier = pltpu.get_barrier_semaphore()
    for distance in range(1, SPAN):
        pl.semaphore_signal(barrier, inc=1, device_id={"dp": peer(distance)}, device_id_type=MESH)
    for other in range(1, shards):
        @pl.when(mine + other < shards)
        def _(other=other):
            pl.semaphore_signal(barrier, inc=1, device_id={"tensor": mine + other}, device_id_type=MESH)
    in_copies = []
    operands = ((par_hbm, par_ref), (q_hbm, q_ref), (new_hbm, new_ref), (table_hbm, table_ref), (len_hbm, len_ref))
    rows_in = ((par_hbm, par_row.at[0]), (len_hbm, len_row.at[0]))
    for at, (source, target) in enumerate(operands):
        copy = pltpu.make_async_copy(source, target, in_sem.at[at])
        copy.start()
        in_copies.append(copy)
    row_copies = []
    for at, (source, target) in enumerate(rows_in):
        copy = pltpu.make_async_copy(source, target, in_sem.at[5 + at])
        copy.start()
        row_copies.append(copy)
    quarter = pool_v.shape[0] // 4
    pool_copies = []
    for at in range(4):
        span = pl.ds(at * quarter, quarter)
        copy = pltpu.make_async_copy(pool_ref.at[span], pool_v.at[span], pool_sem.at[at])
        copy.start()
        pool_copies.append(copy)
    for copy in in_copies:
        copy.wait()

    slots, owners = slots_of_children(par_ref, me)
    plan = ring_plan(par_ref, len_ref, me >> 2)
    via_up, via_down = plan["via_up"], plan["via_down"]
    flows = {}
    for ahead in range(SPAN):
        served = served_beams(par_ref, me, peer(ahead))
        distance = (SPAN - ahead) % SPAN
        held = [len_ref[me * BEAMS + served[rank]] for rank in range(MOST)]
        for rank in range(MOST):
            beams[distance * MOST + rank] = served[rank]
            lens[distance * MOST + rank] = held[rank]
        flows[ahead] = (served[0], served[1], grains(held[0]))

    for ahead, kept in ((1, "up_id"), (3, "down_id")):
        first, second, cut = flows[ahead]
        flows[ahead] = (first, second, jnp.where(me * BEAMS + first == choose(plan[kept], y), 0, cut))
    flows[2] = (choose(plan["first"], y) & 7, choose(plan["second"], y) & 7, choose(plan["cut"], y))

    def grain_at(flow, number):
        first, second, cut = flow
        later = number >= cut
        number = jnp.where(later, number - cut, number)
        number = jnp.minimum(jnp.maximum(number, 0), PER_CHILD - 1)
        return table_ref[jnp.where(later, second, first), number >> 2] * PER_PAGE + (number & (PER_PAGE - 1))

    sides = (
        (flows[1], choose(via_up, y), jnp.int32(0), choose(via_up, (y - 1) & 3), peer(1)),
        (flows[3], choose(via_down, y), choose(via_up, y), choose(via_down, (y + 1) & 3), peer(3)),
    )
    pl.semaphore_wait(barrier, SPAN - 1 + mine)
    for other in range(1, shards):
        @pl.when(mine >= other)
        def _(other=other):
            pl.semaphore_signal(here_sem, inc=1, device_id={"tensor": mine - other}, device_id_type=MESH)
    for copy in pool_copies:
        copy.wait()
    b_copies = []
    cuts = (0, 8, VIA, FIRST)

    def send_part(part):
        for side, (flow, mine_via, skip, _, target) in enumerate(sides):
            def put(at, carry, side=side, flow=flow, mine_via=mine_via, skip=skip):
                for at in [4 * at + more for more in range(4)]:
                    far = at < mine_via
                    chosen = tuple(jnp.where(far, one, two) for one, two in zip(flows[2], flow))
                    number = jnp.where(far, skip + at, at - mine_via)
                    first_send[side, at] = pool_v[grain_at(chosen, number)]
                return carry

            lax.fori_loop(cuts[part] // 4, cuts[part + 1] // 4, put, 0)
            span = pl.ds(cuts[part], cuts[part + 1] - cuts[part])
            copy = pltpu.make_async_remote_copy(
                src_ref=first_send.at[side, span], dst_ref=first_recv.at[side, span],
                send_sem=bs_sem.at[side * 4 + part], recv_sem=br_sem.at[side * 4 + part],
                device_id={"dp": target}, device_id_type=MESH,
            )
            copy.start()
            b_copies.append(copy)

    send_part(0)

    row = lax.broadcasted_iota(jnp.int32, (SPAN * rows, BEAMS), 0)
    col = lax.broadcasted_iota(jnp.int32, (SPAN * rows, BEAMS), 1)
    slot_at = jnp.zeros_like(col)
    for child in range(BEAMS):
        slot_at = jnp.where(col == child, slots[child], slot_at)
    q_sorted = jnp.zeros((SPAN * rows, wide), jnp.float32)
    new_sorted = jnp.zeros((SPAN * rows, 2 * HD), jnp.float32)
    for step in range(STEPS):
        pick = jnp.where((row // STEPS == slot_at) & (row % STEPS == step), 1.0, 0.0).astype(jnp.bfloat16)
        q_sorted += jnp.dot(pick, q_ref[step], preferred_element_type=jnp.float32)
        new_sorted += jnp.dot(pick, new_ref[step], preferred_element_type=jnp.float32)
    both = jnp.concatenate([q_sorted, new_sorted], axis=1)
    half = both.shape[1] // 2
    for distance in range(SPAN):
        part = both[distance * rows:(distance + 1) * rows]
        part = jnp.concatenate([part[:, :half], part[:, half:]], axis=0).astype(jnp.bfloat16)
        if distance == 0:
            q_recv[0] = part
        else:
            q_send[distance] = part
    q_copies = []
    for distance in range(1, SPAN):
        copy = pltpu.make_async_remote_copy(
            src_ref=q_send.at[distance], dst_ref=q_recv.at[distance],
            send_sem=qs_sem.at[distance], recv_sem=qr_sem.at[distance],
            device_id={"dp": peer(distance)}, device_id_type=MESH,
        )
        copy.start()
        q_copies.append(copy)
    send_part(1)
    send_part(2)
    w_copies = []
    for block in range(shards):
        copy = pltpu.make_async_copy(w_ref.at[:, pl.ds(block * wide, wide)], w_v.at[block], w_sem.at[block])
        copy.start()
        w_copies.append(copy)

    def put_all(index, carry):
        slot = index // PAGES
        page = table_ref[beams[slot], index % PAGES]
        at = (index % (MOST * PAGES)) * PER_PAGE
        stage[index // (MOST * PAGES), pl.ds(at, PER_PAGE)] = pool_v[pl.ds(page * PER_PAGE, PER_PAGE)]
        return carry

    lax.fori_loop(0, SPAN * MOST * PAGES, put_all, 0)
    own_copy = pltpu.make_async_copy(stage.at[0], recv_ref.at[pl.ds(2 * LINK, MOST * PER_CHILD)], own_sem.at[0])
    own_copy.start()

    for copy in q_copies:
        copy.wait()

    def attend(distance):
        message = q_recv[distance].astype(jnp.float32)
        message = jnp.concatenate([message[:rows], message[rows:]], axis=1)
        q_rows = jnp.concatenate([message[:, h * HD:(h + 1) * HD] for h in range(heads)], axis=0).astype(jnp.bfloat16)
        fresh = message[:, wide:].astype(jnp.bfloat16)
        old_len = lens[distance * MOST]
        last_len = lens[distance * MOST + 1]
        contract = (((1,), (1,)), ((), ()))
        scale = HD ** -0.5
        half = MOST * PER_CHILD // 2
        keys = [stage[distance, pl.ds(rank * half, half), :, 0:HD].reshape(context, HD) for rank in range(MOST)]
        scores = [lax.dot_general(q_rows, key, contract, preferred_element_type=jnp.float32) for key in keys]
        rank_at = lax.broadcasted_iota(jnp.int32, scores[0].shape, 0) // STEPS % MOST
        scores = jnp.where(rank_at == 0, scores[0], scores[1]) * scale
        fresh_scores = lax.dot_general(q_rows, fresh[:, :HD], contract, preferred_element_type=jnp.float32) * scale
        position = lax.broadcasted_iota(jnp.int32, scores.shape, 1)
        limit = jnp.where(rank_at == 0, old_len, last_len)
        scores = jnp.where(position < limit, scores, -1e30)
        f_row = lax.broadcasted_iota(jnp.int32, fresh_scores.shape, 0)
        f_col = lax.broadcasted_iota(jnp.int32, fresh_scores.shape, 1)
        seen = (f_row // STEPS % MOST == f_col // STEPS) & (f_col % STEPS <= f_row % STEPS)
        fresh_scores = jnp.where(seen, fresh_scores, -1e30)
        top = jnp.maximum(jnp.max(scores, axis=1, keepdims=True), jnp.max(fresh_scores, axis=1, keepdims=True))
        exp_old = jnp.exp(scores - top)
        exp_new = jnp.exp(fresh_scores - top)
        total = jnp.sum(exp_old, axis=1, keepdims=True) + jnp.sum(exp_new, axis=1, keepdims=True)
        share = 1.0 / total
        w_old = (exp_old * share).astype(jnp.bfloat16)
        w_new = (exp_new * share).astype(jnp.bfloat16)
        values = [stage[distance, pl.ds(rank * half, half), :, HD:2 * HD].reshape(context, HD) for rank in range(MOST)]
        out = [jnp.dot(w_old, value, preferred_element_type=jnp.float32) for value in values]
        out = jnp.where(rank_at[:, :HD] == 0, out[0], out[1])
        out += jnp.dot(w_new, fresh[:, HD:], preferred_element_type=jnp.float32)
        out = jnp.concatenate([out[h * rows:(h + 1) * rows] for h in range(heads)], axis=1)
        att[pl.ds(pl.multiple_of(distance * rows, rows), rows), :] = out

    def attend_two(at, carry):
        attend(2 * at)
        attend(2 * at + 1)
        return carry

    lax.fori_loop(0, SPAN // 2, attend_two, 0)
    for copy in b_copies[:4]:
        copy.wait()
    more_copies = b_copies[4:]
    b_copies = []
    for side, (flow, mine_via, _, passed, target) in enumerate(sides):
        def put_passed(at, carry, side=side, flow=flow, mine_via=mine_via, passed=passed):
            for at in [4 * at + more for more in range(4)]:
                here = pool_v[grain_at(flow, FIRST - mine_via + at - passed)]
                rest_send[side, at] = jnp.where(at < passed, first_recv[side, at], here)
            return carry

        lax.fori_loop(0, REST // 4, put_passed, 0)
        copy = pltpu.make_async_remote_copy(
            src_ref=rest_send.at[side], dst_ref=recv_ref.at[pl.ds(side * LINK + FIRST, REST)],
            send_sem=bs_sem.at[side * 4 + 3], recv_sem=br_sem.at[side * 4 + 3],
            device_id={"dp": target}, device_id_type=MESH,
        )
        copy.start()
        b_copies.append(copy)
    attended = att[...].astype(jnp.bfloat16)
    for copy in w_copies:
        copy.wait()

    def p_copy(other):
        return pltpu.make_async_remote_copy(
            src_ref=p_send.at[other], dst_ref=p_recv.at[other],
            send_sem=ps_sem.at[other], recv_sem=pr_sem.at[other],
            device_id={"tensor": lax.rem(mine + other, shards)}, device_id_type=MESH,
        )

    def project(other, carry):
        product = jnp.dot(attended, w_v[lax.rem(mine + other, shards)], preferred_element_type=jnp.float32)
        p_send[other] = product.astype(jnp.bfloat16)
        p_copy(other).start()
        return carry

    @pl.when(mine < shards - 1)
    def _():
        pl.semaphore_wait(here_sem, shards - 1 - mine)

    lax.fori_loop(1, shards, project, 0)
    own = jnp.dot(attended, w_v[mine], preferred_element_type=jnp.float32)

    for copy in more_copies:
        copy.wait()
    for side in range(2):
        copy = pltpu.make_async_copy(first_recv.at[side], recv_ref.at[pl.ds(side * LINK, FIRST)], land_sem.at[side])
        copy.start()
        b_copies.append(copy)

    def gather_sums(other, total):
        p_copy(other).wait()
        return total + p_recv[other].astype(jnp.float32)

    summed = lax.fori_loop(1, shards, gather_sums, own)
    half = wide // 2
    r_copies = []
    for distance in range(SPAN):
        part = summed[distance * rows:(distance + 1) * rows]
        r_send[distance] = jnp.concatenate([part[:, :half], part[:, half:]], axis=0).astype(jnp.bfloat16)
        if distance == 0:
            copy = pltpu.make_async_copy(r_send.at[0], proj_ref.at[0], own_sem.at[1])
        else:
            copy = pltpu.make_async_remote_copy(
                src_ref=r_send.at[distance], dst_ref=proj_ref.at[distance],
                send_sem=rs_sem.at[distance], recv_sem=rr_sem.at[distance],
                device_id={"dp": peer(SPAN - distance)}, device_id_type=MESH,
            )
        copy.start()
        r_copies.append(copy)
    for copy in row_copies:
        copy.wait()
    load = heaviest(par_row[...], len_row[...], rings)
    over_ref[0] = jnp.where(load > LINK, 1, 0) + jnp.where(load > LINK + LEFT, 1, 0)
    for side, (flow, mine_via, _, passed, _) in enumerate(sides):
        def put_left(at, carry, side=side, flow=flow, mine_via=mine_via, passed=passed):
            for at in [4 * at + more for more in range(4)]:
                left_send[side, at] = pool_v[grain_at(flow, LINK - mine_via - passed + at)]
            return carry

        lax.fori_loop(0, LEFT // 4, put_left, 0)
    left_copy = pltpu.make_async_copy(left_send, left_ref, land_sem.at[2])
    left_copy.start()
    for child in range(BEAMS):
        slot = slots[child]
        distance = slot >> 1
        length = len_ref[owners[child]]
        kept = jnp.where(distance == 3, choose(plan["up_id"], (y - 1) & 3), choose(plan["down_id"], (y + 1) & 3))
        before = jnp.int32(0)
        for other in range(BEAMS):
            if other != child:
                mate = (slots[other] >> 1 == distance) & (slots[other] < slot)
                counts = (owners[other] != owners[child]) & (owners[other] != kept)
                before = jnp.where(mate & counts, grains(len_ref[owners[other]]), before)
        far_before = jnp.where(owners[child] == choose(plan["first"], (y + 2) & 3), 0, choose(plan["cut"], (y + 2) & 3))
        before = jnp.where(distance == 2, far_before, before)
        from_up = choose(via_up, (y - 1) & 3), choose(via_up, (y + 2) & 3)
        from_down = choose(via_down, (y + 1) & 3), choose(via_down, (y + 2) & 3)
        near_via = jnp.where(distance == 3, from_up[0], from_down[0])
        near_pass = jnp.where(distance == 3, from_up[1], from_down[1])
        near_base = jnp.where(distance == 3, 0, LINK)
        split = jnp.where(distance == 2, from_up[1], FIRST - near_via) - before
        split = jnp.minimum(jnp.maximum(split, 0), PER_CHILD)
        start = jnp.where(distance == 2, FIRST + before, near_base + near_via + before)
        again = jnp.where(distance == 2, LINK + FIRST + before + split - from_up[1], start + split + near_pass)
        near = (distance == 1) | (distance == 3)
        until = LINK - near_via - near_pass - before
        until = jnp.where(near, jnp.minimum(jnp.maximum(until, 0), PER_CHILD), PER_CHILD)
        third = jnp.where(distance == 3, 0, LEFT) + near_via + near_pass + before + until - LINK
        held = near & (owners[child] == kept)
        kept_down = LINK + choose(via_down, (y + 1) & 3) - choose(plan["keep_down"], (y + 1) & 3)
        start = jnp.where(held, jnp.where(distance == 3, 0, kept_down), start)
        split = jnp.where(held, PER_CHILD, split)
        again = jnp.where(held, 0, again)
        until = jnp.where(held, PER_CHILD, until)
        third = jnp.where(held, 0, third)
        stays = distance == 0
        meta_ref[child * META] = length
        meta_ref[child * META + 1] = jnp.where(stays, 2 * LINK + (slot & 1) * PER_CHILD, start)
        meta_ref[child * META + 2] = jnp.where(stays, PER_CHILD, split)
        meta_ref[child * META + 3] = jnp.where(stays, 0, again)
        meta_ref[child * META + 4] = until
        meta_ref[child * META + 5] = jnp.where(near, third, 0)
        meta_ref[child * META + 6] = slot
    for copy in r_copies:
        copy.wait()
    for copy in b_copies:
        copy.wait()
    own_copy.wait()
    left_copy.wait()


def full_kernel(
    pool_ref, table_hbm, par_hbm, recv_ref,
    table_ref, par_ref, pool_v, stage,
    in_sem, pool_sem, own_sem, bs_sem, br_sem,
):
    me = lax.axis_index("dp")
    y = lax.rem(me, SPAN)
    base = me - y
    context = stage.shape[1] // MOST

    def peer(distance):
        return base + lax.rem(y + distance, SPAN)

    barrier = pltpu.get_barrier_semaphore()
    for distance in range(1, SPAN):
        pl.semaphore_signal(barrier, inc=1, device_id={"dp": peer(distance)}, device_id_type=MESH)
    in_copies = []
    for at, (source, target) in enumerate(((par_hbm, par_ref), (table_hbm, table_ref))):
        copy = pltpu.make_async_copy(source, target, in_sem.at[at])
        copy.start()
        in_copies.append(copy)
    pool_copy = pltpu.make_async_copy(pool_ref, pool_v, pool_sem)
    pool_copy.start()
    for copy in in_copies:
        copy.wait()
    pl.semaphore_wait(barrier, SPAN - 1)
    pool_copy.wait()
    copies = []
    for distance in (2, 1, 3, 0):
        served = served_beams(par_ref, me, peer(SPAN - distance))
        for rank in range(MOST):
            beam = served[rank]

            def put(index, carry, distance=distance, rank=rank, beam=beam):
                at = pl.multiple_of(rank * context + index * PAGE, PAGE)
                stage[distance, pl.ds(at, PAGE), :] = pool_v[table_ref[beam, index]]
                return carry

            lax.fori_loop(0, context // PAGE, put, 0)
            span = pl.ds(rank * context, context)
            if distance == 0:
                copy = pltpu.make_async_copy(stage.at[0, span], recv_ref.at[0, span], own_sem.at[rank])
            else:
                copy = pltpu.make_async_remote_copy(
                    src_ref=stage.at[distance, span], dst_ref=recv_ref.at[distance, span],
                    send_sem=bs_sem.at[distance * MOST + rank], recv_sem=br_sem.at[distance * MOST + rank],
                    device_id={"dp": peer(SPAN - distance)}, device_id_type=MESH,
                )
            copy.start()
            copies.append(copy)
    for copy in copies:
        copy.wait()


def finish_kernel(recv_ref, raw_ref, new_hbm, len_hbm, par_hbm, proj_ref, cache_ref, new_ref, len_ref, par_ref, edge, zeros, in_sem, out_sem):
    me = lax.axis_index("dp")
    pages = recv_ref.shape[1] // PAGE
    operands = ((par_hbm, par_ref), (len_hbm, len_ref), (new_hbm, new_ref))
    in_copies = [pltpu.make_async_copy(source, target, in_sem.at[at]) for at, (source, target) in enumerate(operands)]
    for copy in in_copies:
        copy.start()
    zeros[...] = jnp.zeros_like(zeros)
    for copy in in_copies:
        copy.wait()
    slots, owners = slots_of_children(par_ref, me)
    fresh = [new_ref[step].astype(jnp.float32) for step in range(STEPS)]
    for child in range(BEAMS):
        slot = slots[child]
        length = len_ref[owners[child]]
        first = length // PAGE
        last = (length + STEPS - 1) // PAGE

        def whole(index, carry, child=child, slot=slot):
            span = pl.ds(pl.multiple_of(index * PAGE, PAGE), PAGE)
            pltpu.make_async_copy(recv_ref.at[slot, span], cache_ref.at[child, span], out_sem).start()
            return carry

        def clear(index, carry, child=child):
            span = pl.ds(pl.multiple_of(index * PAGE, PAGE), PAGE)
            pltpu.make_async_copy(zeros, cache_ref.at[child, span], out_sem).start()
            return carry

        def fix(index, carry, child=child, slot=slot, length=length, first=first):
            at = pl.multiple_of(index * PAGE, PAGE)
            position = at + lax.broadcasted_iota(jnp.int32, (PAGE, 2 * HD), 0)
            page = recv_ref[slot, pl.ds(at, PAGE), :].astype(jnp.float32)
            page = jnp.where(position < length, page, 0.0)
            for step in range(STEPS):
                page = jnp.where(position == length + step, fresh[step][child:child + 1], page)
            edge[child * 2 + index - first] = page.astype(jnp.bfloat16)
            pltpu.make_async_copy(edge.at[child * 2 + index - first], cache_ref.at[child, pl.ds(at, PAGE)], out_sem).start()
            return carry

        lax.fori_loop(0, first, whole, 0)
        lax.fori_loop(last + 1, pages, clear, 0)
        lax.fori_loop(first, last + 1, fix, 0)

    rows = MOST * STEPS
    raw = []
    for distance in range(SPAN):
        part = raw_ref[distance].astype(jnp.float32)
        raw.append(jnp.concatenate([part[:rows], part[rows:]], axis=1))
    raw = jnp.concatenate(raw, axis=0).astype(jnp.bfloat16)
    row = lax.broadcasted_iota(jnp.int32, (BEAMS, SPAN * rows), 0)
    col = lax.broadcasted_iota(jnp.int32, (BEAMS, SPAN * rows), 1)
    slot_at = jnp.zeros_like(col)
    for child in range(BEAMS):
        slot_at = jnp.where(row == child, slots[child], slot_at)
    for step in range(STEPS):
        pick = jnp.where(col == slot_at * STEPS + step, 1.0, 0.0).astype(jnp.bfloat16)
        proj_ref[step] = jnp.dot(pick, raw, preferred_element_type=jnp.float32).astype(jnp.bfloat16)
    pltpu.make_async_copy(recv_ref, cache_ref, out_sem).wait()


def left_kernel(left_ref, got_ref, send_sem, recv_sem):
    me = lax.axis_index("dp")
    y = lax.rem(me, SPAN)
    targets = [me - y + lax.rem(y + ahead, SPAN) for ahead in (1, SPAN - 1)]
    barrier = pltpu.get_barrier_semaphore()
    for target in targets:
        pl.semaphore_signal(barrier, inc=1, device_id={"dp": target}, device_id_type=MESH)
    pl.semaphore_wait(barrier, 2)
    copies = []
    for side, target in enumerate(targets):
        copy = pltpu.make_async_remote_copy(
            src_ref=left_ref.at[side], dst_ref=got_ref.at[side],
            send_sem=send_sem.at[side], recv_sem=recv_sem.at[side],
            device_id={"dp": target}, device_id_type=MESH,
        )
        copy.start()
        copies.append(copy)
    for copy in copies:
        copy.wait()


def place_kernel(with_left, recv_ref, raw_ref, new_ref, meta_ref, *refs):
    left_ref = refs[0] if with_left else None
    proj_hbm, cache_ref, edge, zeros, proj_ref, out_sem, proj_sem = refs[-7:]
    total = recv_ref.shape[0]
    zeros[...] = jnp.zeros_like(zeros)
    fresh = [new_ref[step].astype(jnp.float32) for step in range(STEPS)]
    slots = [meta_ref[child * META + 6] for child in range(BEAMS)]
    per_child = cache_ref.shape[1]
    scale = GRAIN // TILE
    for child in range(BEAMS):
        length, start, split, again, until, third = (meta_ref[child * META + at] for at in range(6))
        first = length // TILE
        last = (length + STEPS - 1) // TILE
        until = jnp.minimum(until * scale, first) if with_left else first
        split = jnp.minimum(split * scale, until)

        def move(source, source_at, at, count, child=child):
            @pl.when(count > 0)
            def _():
                pltpu.make_async_copy(
                    source.at[pl.ds(source_at, count)], cache_ref.at[child, pl.ds(at, count)], out_sem
                ).start()

        move(recv_ref, start * scale, 0, split)
        move(recv_ref, again * scale, split, until - split)
        if with_left:
            move(left_ref, third * scale, until, first - until)
        move(zeros, 0, last + 1, per_child - 1 - last)
    for child in range(BEAMS):
        length, start, split, again, until, third = (meta_ref[child * META + at] for at in range(6))
        first = length // TILE
        last = (length + STEPS - 1) // TILE

        def fix(
            index, carry, child=child, length=length, first=first, start=start * scale, split=split * scale,
            again=again * scale, until=until * scale, third=third * scale,
        ):
            position = index * TILE + lax.broadcasted_iota(jnp.int32, (TILE, 2 * HD), 0)
            at = jnp.minimum(jnp.where(index < split, start + index, again + index - split), total - 1)
            part = recv_ref[at].astype(jnp.float32)
            if with_left:
                at = jnp.minimum(jnp.maximum(third + index - until, 0), left_ref.shape[0] - 1)
                part = jnp.where(index < until, part, left_ref[at].astype(jnp.float32))
            part = jnp.where(position < length, part, 0.0)
            for step in range(STEPS):
                part = jnp.where(position == length + step, fresh[step][child:child + 1], part)
            edge[child * 2 + index - first] = part.astype(jnp.bfloat16)
            pltpu.make_async_copy(edge.at[child * 2 + index - first], cache_ref.at[child, index], out_sem).start()
            return carry

        lax.fori_loop(first, last + 1, fix, 0)

    rows = MOST * STEPS
    raw = []
    for distance in range(SPAN):
        part = raw_ref[distance].astype(jnp.float32)
        raw.append(jnp.concatenate([part[:rows], part[rows:]], axis=1))
    raw = jnp.concatenate(raw, axis=0).astype(jnp.bfloat16)
    row = lax.broadcasted_iota(jnp.int32, (BEAMS, SPAN * rows), 0)
    col = lax.broadcasted_iota(jnp.int32, (BEAMS, SPAN * rows), 1)
    slot_at = jnp.zeros_like(col)
    for child in range(BEAMS):
        slot_at = jnp.where(row == child, slots[child], slot_at)
    for step in range(STEPS):
        pick = jnp.where(col == slot_at * STEPS + step, 1.0, 0.0).astype(jnp.bfloat16)
        proj_ref[step] = jnp.dot(pick, raw, preferred_element_type=jnp.float32).astype(jnp.bfloat16)
    proj_copy = pltpu.make_async_copy(proj_ref, proj_hbm, proj_sem)
    proj_copy.start()
    pltpu.make_async_copy(cache_ref, cache_ref, out_sem).wait()
    proj_copy.wait()


def local(shards, queries, new_kv, kv_pool, page_tables, lengths, parents, out_weight):
    wide = queries.shape[2]
    channels = kv_pool.shape[2]
    context = page_tables.shape[1] * kv_pool.shape[1]
    rows = MOST * STEPS
    vmem = pl.BlockSpec(memory_space=pltpu.VMEM)
    smem = pl.BlockSpec(memory_space=pltpu.SMEM)
    hbm = pl.BlockSpec(memory_space=pltpu.HBM)
    free = pl.BlockSpec(memory_space=pl.ANY)
    dma = pltpu.SemaphoreType.DMA
    bf16 = jnp.bfloat16

    def pinned(*operands):
        return [pltpu.with_memory_space_constraint(operand, pltpu.HBM) for operand in operands]

    grain_pool = kv_pool.reshape(-1, GRAIN, channels)
    with jax.named_scope("exchange"):
        recv, raw, left, meta, over = pl.pallas_call(
            exchange_kernel,
            out_shape=(
                jax.ShapeDtypeStruct((2 * LINK + MOST * PER_CHILD, GRAIN, channels), bf16),
                jax.ShapeDtypeStruct((SPAN, 2 * rows, wide // 2), bf16),
                jax.ShapeDtypeStruct((2, LEFT, GRAIN, channels), bf16),
                jax.ShapeDtypeStruct((BEAMS * META,), jnp.int32),
                jax.ShapeDtypeStruct((1,), jnp.int32),
            ),
            in_specs=[hbm] * 7,
            out_specs=(free, free, free, smem, smem),
            scratch_shapes=[
                pltpu.VMEM(queries.shape, bf16),
                pltpu.VMEM(new_kv.shape, bf16),
                pltpu.SMEM(page_tables.shape, jnp.int32),
                pltpu.SMEM(lengths.shape, jnp.int32),
                pltpu.SMEM(parents.shape, jnp.int32),
                pltpu.VMEM((1, *lengths.shape), jnp.int32),
                pltpu.VMEM((1, *parents.shape), jnp.int32),
                pltpu.VMEM(grain_pool.shape, bf16),
                pltpu.VMEM((shards, out_weight.shape[0], wide), bf16),
                pltpu.VMEM((SPAN, MOST * PER_CHILD, GRAIN, channels), bf16),
                pltpu.VMEM((2, FIRST, GRAIN, channels), bf16),
                pltpu.VMEM((2, FIRST, GRAIN, channels), bf16),
                pltpu.VMEM((2, REST, GRAIN, channels), bf16),
                pltpu.VMEM((2, LEFT, GRAIN, channels), bf16),
                pltpu.VMEM((SPAN, 2 * rows, (wide + channels) // 2), bf16),
                pltpu.VMEM((SPAN, 2 * rows, (wide + channels) // 2), bf16),
                pltpu.VMEM((SPAN * rows, wide), jnp.float32),
                pltpu.VMEM((shards, SPAN * rows, wide), bf16),
                pltpu.VMEM((shards, SPAN * rows, wide), bf16),
                pltpu.VMEM((SPAN, 2 * rows, wide // 2), bf16),
                pltpu.SMEM((SPAN * MOST,), jnp.int32),
                pltpu.SMEM((SPAN * MOST,), jnp.int32),
                dma((7,)), dma((4,)), dma((shards,)), dma((2,)), dma((3,)),
                dma((SPAN,)), dma((SPAN,)),
                dma((8,)), dma((8,)),
                dma((shards,)), dma((shards,)),
                dma((SPAN,)), dma((SPAN,)),
                pltpu.SemaphoreType.REGULAR,
            ],
            compiler_params=pltpu.CompilerParams(
                collective_id=0, has_side_effects=True, vmem_limit_bytes=48 * 1024 * 1024
            ),
            name="exchange",
        )(*pinned(queries, new_kv, grain_pool, page_tables, lengths, parents, out_weight))

    def place(*got):
        with jax.named_scope("place"):
            projected, cache = pl.pallas_call(
                functools.partial(place_kernel, len(got) > 0),
                out_shape=(
                    jax.ShapeDtypeStruct(queries.shape, bf16),
                    jax.ShapeDtypeStruct((BEAMS, context // TILE, TILE, channels), bf16),
                ),
                in_specs=[vmem, vmem, vmem, smem] + [vmem] * len(got),
                out_specs=(free, free),
                scratch_shapes=[
                    pltpu.VMEM((2 * BEAMS, TILE, channels), bf16),
                    pltpu.VMEM((context // TILE, TILE, channels), bf16),
                    pltpu.VMEM(queries.shape, bf16),
                    dma, dma,
                ],
                compiler_params=pltpu.CompilerParams(vmem_limit_bytes=24 * 1024 * 1024),
                name="place_left" if got else "place",
            )(recv.reshape(-1, TILE, channels), raw, new_kv, meta, *got)
            return projected, cache.reshape(BEAMS, context, channels)

    def placed():
        return place()

    def topped():
        with jax.named_scope("left"):
            got = pl.pallas_call(
                left_kernel,
                out_shape=jax.ShapeDtypeStruct(left.shape, bf16),
                in_specs=[free],
                out_specs=free,
                scratch_shapes=[dma((2,)), dma((2,))],
                compiler_params=pltpu.CompilerParams(
                    collective_id=2, has_side_effects=True, vmem_limit_bytes=4 * 1024 * 1024
                ),
                name="left",
            )(left)
        return place(got.reshape(-1, TILE, channels))

    def resent():
        with jax.named_scope("full"):
            whole = pl.pallas_call(
                full_kernel,
                out_shape=jax.ShapeDtypeStruct((SPAN, MOST * context, channels), bf16),
                in_specs=[hbm] * 3,
                out_specs=free,
                scratch_shapes=[
                    pltpu.SMEM(page_tables.shape, jnp.int32),
                    pltpu.SMEM(parents.shape, jnp.int32),
                    pltpu.VMEM(kv_pool.shape, bf16),
                    pltpu.VMEM((SPAN, MOST * context, channels), bf16),
                    dma((2,)), dma, dma((MOST,)),
                    dma((SPAN * MOST,)), dma((SPAN * MOST,)),
                ],
                compiler_params=pltpu.CompilerParams(
                    collective_id=1, has_side_effects=True, vmem_limit_bytes=24 * 1024 * 1024
                ),
                name="full",
            )(*pinned(kv_pool, page_tables, parents))
        with jax.named_scope("finish"):
            return pl.pallas_call(
                finish_kernel,
                out_shape=(
                    jax.ShapeDtypeStruct(queries.shape, bf16),
                    jax.ShapeDtypeStruct((BEAMS, context, channels), bf16),
                ),
                in_specs=[vmem, vmem, hbm, hbm, hbm],
                out_specs=(vmem, hbm),
                scratch_shapes=[
                    pltpu.VMEM(new_kv.shape, bf16),
                    pltpu.SMEM(lengths.shape, jnp.int32),
                    pltpu.SMEM(parents.shape, jnp.int32),
                    pltpu.VMEM((2 * BEAMS, PAGE, channels), bf16),
                    pltpu.VMEM((PAGE, channels), bf16),
                    dma((3,)), dma,
                ],
                compiler_params=pltpu.CompilerParams(vmem_limit_bytes=24 * 1024 * 1024),
                name="finish",
            )(whole.reshape(BEAMS, context, channels), raw, new_kv, lengths, parents)

    return lax.switch(over[0], (placed, topped, resent))


def solution(mesh):
    in_specs = (
        P(None, "dp", "tensor"),
        P(None, "dp", "tensor"),
        P("dp", None, "tensor"),
        P("dp", None),
        P(),
        P(),
        P("tensor", None),
    )
    out_specs = (P(None, "dp", "tensor"), P("dp", None, "tensor"))
    body = functools.partial(local, mesh.shape["tensor"])
    return jax.shard_map(body, mesh=mesh, in_specs=in_specs, out_specs=out_specs, check_vma=False)
```

```python
import functools

import jax
import jax.numpy as jnp
from jax import lax
from jax.experimental import pallas as pl
from jax.experimental.pallas import tpu as pltpu
from jax.sharding import PartitionSpec as P

HD = 128
SPAN = 4
MOST = 2
BEAMS = 8
STEPS = 4
PAGE = 128
PAGES = 8
GRAIN = 32
PER_CHILD = 32
PER_PAGE = PAGE // GRAIN
TILE = 16
VIA = 32
MORE = 24
REST = 32
SOME = 6
LEFT = 20
FIRST = VIA + MORE
LINK = FIRST + REST
META = 7
MESH = pl.DeviceIdType.MESH


def grains(length):
    return (length + (GRAIN - 1)) // GRAIN


def choose(values, index):
    out = values[0]
    for at in range(1, len(values)):
        out = jnp.where(index == at, values[at], out)
    return out


def balanced(up, far, down, keep_up, keep_down):
    least = [jnp.maximum(keep_up[i], far[i] - VIA) for i in range(SPAN)]
    most = [jnp.minimum(far[i] - keep_down[i], VIA) for i in range(SPAN)]
    via_up = [jnp.minimum(jnp.maximum(far[i] >> 1, least[i]), most[i]) for i in range(SPAN)]
    for at in range(SPAN):
        via_down = [far[i] - via_up[i] for i in range(SPAN)]
        nxt, prv = (at + 1) % SPAN, (at - 1) % SPAN
        load_up = jnp.maximum(up[at] + via_up[prv], up[nxt] + via_up[nxt])
        load_down = jnp.maximum(down[at] + via_down[nxt], down[prv] + via_down[prv])
        best = (load_down + far[at] - load_up) >> 1
        via_up[at] = jnp.minimum(jnp.maximum(best, least[at]), most[at])
    via_down = [far[i] - via_up[i] for i in range(SPAN)]
    return via_up, via_down


def planned(flows):
    names = ("up", "down", "far", "first", "second", "cut", "up_id", "down_id", "keep_up", "keep_down")
    plan = {name: [] for name in names}
    for at in range(SPAN):
        u0, u1, gu0, gu1 = flows[at][1]
        f0, f1, gf0, gf1 = flows[at][2]
        d0, d1, gd0, gd1 = flows[at][3]
        gu1 = jnp.where(u0 == u1, 0, gu1)
        gf1 = jnp.where(f0 == f1, 0, gf1)
        gd1 = jnp.where(d0 == d1, 0, gd1)

        def shared(parent, count, one, two):
            return jnp.where((parent == one) | (parent == two), count, 0)

        straight = shared(f0, gf0, u0, u1) + shared(f1, gf1, d0, d1)
        crossed = shared(f1, gf1, u0, u1) + shared(f0, gf0, d0, d1)
        swap = crossed > straight
        first, second = jnp.where(swap, f1, f0), jnp.where(swap, f0, f1)
        cut, rest = jnp.where(swap, gf1, gf0), jnp.where(swap, gf0, gf1)
        keep_up, keep_down = shared(first, cut, u0, u1), shared(second, rest, d0, d1)
        values = (
            gu0 + gu1 - keep_up, gd0 + gd1 - keep_down, gf0 + gf1, first, second, cut,
            jnp.where(keep_up > 0, first, -1), jnp.where(keep_down > 0, second, -1), keep_up, keep_down,
        )
        for name, value in zip(names, values):
            plan[name].append(value)
    plan["via_up"], plan["via_down"] = balanced(
        plan["up"], plan["far"], plan["down"], plan["keep_up"], plan["keep_down"]
    )
    return plan


def ring_plan(parents, lengths, ring):
    flows = [[None] * SPAN for _ in range(SPAN)]
    for target in range(SPAN):
        owners = [parents[(ring * SPAN + target) * BEAMS + child] for child in range(BEAMS)]
        sources = [(owner >> 3) & (SPAN - 1) for owner in owners]
        for at in range(SPAN):
            if at != target:
                one, two = owners[0], owners[0]
                for child in range(1, BEAMS):
                    two = jnp.where(sources[child] == at, owners[child], two)
                one = owners[BEAMS - 1]
                for child in range(BEAMS - 2, -1, -1):
                    one = jnp.where(sources[child] == at, owners[child], one)
                flows[at][(target - at) % SPAN] = (one, two, grains(lengths[one]), grains(lengths[two]))
    return planned(flows)


def heaviest(parents, lengths, rings):
    beams = rings * SPAN * BEAMS
    counts = grains(lengths).astype(jnp.float32).astype(jnp.bfloat16)
    beam = lax.broadcasted_iota(jnp.int32, (beams, beams), 0)
    chosen = jnp.where(beam == parents, 1.0, 0.0).astype(jnp.bfloat16)
    counts = jnp.dot(jnp.broadcast_to(counts, (16, beams)), chosen, preferred_element_type=jnp.float32)[:1]
    lane = lax.broadcasted_iota(jnp.int32, (1, beams), 1)
    source = (parents // BEAMS) % SPAN
    rank = jnp.zeros_like(lane)
    for back in range(1, BEAMS):
        rank = rank + jnp.where((pltpu.roll(source, back, 1) == source) & (lane % BEAMS >= back), 1, 0)
    names = (parents % (SPAN * BEAMS)).astype(jnp.float32)
    rows = [
        jnp.where((source == at) & (rank == order), value, 0.0)
        for value in (names, counts) for at in range(SPAN) for order in range(MOST)
    ]
    rows = jnp.concatenate(rows, axis=0).astype(jnp.bfloat16)
    child = lax.broadcasted_iota(jnp.int32, (beams, 128), 0)
    ring = lax.broadcasted_iota(jnp.int32, (beams, 128), 1)
    flows = [[None] * SPAN for _ in range(SPAN)]
    for target in range(SPAN):
        member = (child // BEAMS % SPAN == target) & (child // (BEAMS * SPAN) == ring)
        member = jnp.where(member, 1.0, 0.0).astype(jnp.bfloat16)
        found = jnp.dot(rows, member, preferred_element_type=jnp.float32).astype(jnp.int32)
        for at in range(SPAN):
            wanted = (at * MOST, at * MOST + 1, (SPAN + at) * MOST, (SPAN + at) * MOST + 1)
            flows[at][(target - at) % SPAN] = tuple(found[one:one + 1] for one in wanted)
    plan = planned(flows)
    out = jnp.zeros_like(plan["far"][0])
    for at in range(SPAN):
        load_up = plan["up"][at] + plan["via_up"][at] + plan["via_up"][(at - 1) % SPAN]
        load_down = plan["down"][at] + plan["via_down"][at] + plan["via_down"][(at + 1) % SPAN]
        out = jnp.maximum(out, jnp.maximum(load_up, load_down))
    return jnp.max(out)


def slots_of_children(parents, me):
    taken = [jnp.int32(0) for _ in range(SPAN)]
    slots, owners = [], []
    for child in range(BEAMS):
        parent = parents[me * BEAMS + child]
        apart = jnp.bitwise_and(parent // BEAMS - me, SPAN - 1)
        slot = jnp.int32(0)
        for distance in range(SPAN):
            hit = apart == distance
            slot = jnp.where(hit, distance * MOST + taken[distance], slot)
            taken[distance] = taken[distance] + hit.astype(jnp.int32)
        slots.append(slot)
        owners.append(parent)
    return slots, owners


def served_beams(parents, me, target):
    count = jnp.int32(0)
    beams = [jnp.int32(0) for _ in range(MOST)]
    for child in range(BEAMS):
        parent = parents[target * BEAMS + child]
        hit = parent // BEAMS == me
        for rank in range(MOST):
            beams[rank] = jnp.where(hit & (count == rank), parent % BEAMS, beams[rank])
        count = count + hit.astype(jnp.int32)
    return beams


def exchange_kernel(
    q_hbm, new_hbm, pool_ref, table_hbm, len_hbm, par_hbm, w_ref,
    recv_ref, proj_ref, left_ref, meta_ref, over_ref,
    q_ref, new_ref, table_ref, len_ref, par_ref, len_row, par_row,
    pool_v, w_v, stage, first_send, first_recv, rest_send, left_send, q_send, q_recv, att, p_send, p_recv, r_send, lens, beams,
    in_sem, pool_sem, w_sem, own_sem, land_sem, qs_sem, qr_sem, bs_sem, br_sem, ps_sem, pr_sem, rs_sem, rr_sem, here_sem,
):
    me = lax.axis_index("dp")
    mine = lax.axis_index("tensor")
    shards = lax.axis_size("tensor")
    y = lax.rem(me, SPAN)
    base = me - y
    context = stage.shape[1] * GRAIN // MOST
    rings = lax.axis_size("dp") // SPAN
    wide = q_hbm.shape[2]
    heads = wide // HD
    rows = MOST * STEPS

    def peer(distance):
        return base + lax.rem(y + distance, SPAN)

    barrier = pltpu.get_barrier_semaphore()
    for distance in range(1, SPAN):
        pl.semaphore_signal(barrier, inc=1, device_id={"dp": peer(distance)}, device_id_type=MESH)
    for other in range(1, shards):
        @pl.when(mine + other < shards)
        def _(other=other):
            pl.semaphore_signal(barrier, inc=1, device_id={"tensor": mine + other}, device_id_type=MESH)
    in_copies = []
    operands = ((par_hbm, par_ref), (q_hbm, q_ref), (new_hbm, new_ref), (table_hbm, table_ref), (len_hbm, len_ref))
    rows_in = ((par_hbm, par_row.at[0]), (len_hbm, len_row.at[0]))
    for at, (source, target) in enumerate(operands):
        copy = pltpu.make_async_copy(source, target, in_sem.at[at])
        copy.start()
        in_copies.append(copy)
    row_copies = []
    for at, (source, target) in enumerate(rows_in):
        copy = pltpu.make_async_copy(source, target, in_sem.at[5 + at])
        copy.start()
        row_copies.append(copy)
    quarter = pool_v.shape[0] // 4
    pool_copies = []
    for at in range(4):
        span = pl.ds(at * quarter, quarter)
        copy = pltpu.make_async_copy(pool_ref.at[span], pool_v.at[span], pool_sem.at[at])
        copy.start()
        pool_copies.append(copy)
    for copy in in_copies:
        copy.wait()

    slots, owners = slots_of_children(par_ref, me)
    plan = ring_plan(par_ref, len_ref, me >> 2)
    via_up, via_down = plan["via_up"], plan["via_down"]
    flows = {}
    for ahead in range(SPAN):
        served = served_beams(par_ref, me, peer(ahead))
        distance = (SPAN - ahead) % SPAN
        held = [len_ref[me * BEAMS + served[rank]] for rank in range(MOST)]
        for rank in range(MOST):
            beams[distance * MOST + rank] = served[rank]
            lens[distance * MOST + rank] = held[rank]
        flows[ahead] = (served[0], served[1], grains(held[0]))

    for ahead, kept in ((1, "up_id"), (3, "down_id")):
        first, second, cut = flows[ahead]
        flows[ahead] = (first, second, jnp.where(me * BEAMS + first == choose(plan[kept], y), 0, cut))
    flows[2] = (choose(plan["first"], y) & 7, choose(plan["second"], y) & 7, choose(plan["cut"], y))

    def grain_at(flow, number):
        first, second, cut = flow
        later = number >= cut
        number = jnp.where(later, number - cut, number)
        number = jnp.minimum(jnp.maximum(number, 0), PER_CHILD - 1)
        return table_ref[jnp.where(later, second, first), number >> 2] * PER_PAGE + (number & (PER_PAGE - 1))

    sides = (
        (flows[1], choose(via_up, y), jnp.int32(0), choose(via_up, (y - 1) & 3), peer(1)),
        (flows[3], choose(via_down, y), choose(via_up, y), choose(via_down, (y + 1) & 3), peer(3)),
    )
    pl.semaphore_wait(barrier, SPAN - 1 + mine)
    for other in range(1, shards):
        @pl.when(mine >= other)
        def _(other=other):
            pl.semaphore_signal(here_sem, inc=1, device_id={"tensor": mine - other}, device_id_type=MESH)
    for copy in pool_copies:
        copy.wait()
    b_copies = []
    cuts = (0, 8, VIA, FIRST)

    def send_part(part):
        for side, (flow, mine_via, skip, _, target) in enumerate(sides):
            def put(at, carry, side=side, flow=flow, mine_via=mine_via, skip=skip):
                for at in [4 * at + more for more in range(4)]:
                    far = at < mine_via
                    chosen = tuple(jnp.where(far, one, two) for one, two in zip(flows[2], flow))
                    number = jnp.where(far, skip + at, at - mine_via)
                    first_send[side, at] = pool_v[grain_at(chosen, number)]
                return carry

            lax.fori_loop(cuts[part] // 4, cuts[part + 1] // 4, put, 0)
            span = pl.ds(cuts[part], cuts[part + 1] - cuts[part])
            copy = pltpu.make_async_remote_copy(
                src_ref=first_send.at[side, span], dst_ref=first_recv.at[side, span],
                send_sem=bs_sem.at[side * 4 + part], recv_sem=br_sem.at[side * 4 + part],
                device_id={"dp": target}, device_id_type=MESH,
            )
            copy.start()
            b_copies.append(copy)

    send_part(0)

    row = lax.broadcasted_iota(jnp.int32, (SPAN * rows, BEAMS), 0)
    col = lax.broadcasted_iota(jnp.int32, (SPAN * rows, BEAMS), 1)
    slot_at = jnp.zeros_like(col)
    for child in range(BEAMS):
        slot_at = jnp.where(col == child, slots[child], slot_at)
    q_sorted = jnp.zeros((SPAN * rows, wide), jnp.float32)
    new_sorted = jnp.zeros((SPAN * rows, 2 * HD), jnp.float32)
    for step in range(STEPS):
        pick = jnp.where((row // STEPS == slot_at) & (row % STEPS == step), 1.0, 0.0).astype(jnp.bfloat16)
        q_sorted += jnp.dot(pick, q_ref[step], preferred_element_type=jnp.float32)
        new_sorted += jnp.dot(pick, new_ref[step], preferred_element_type=jnp.float32)
    both = jnp.concatenate([q_sorted, new_sorted], axis=1)
    half = both.shape[1] // 2
    for distance in range(SPAN):
        part = both[distance * rows:(distance + 1) * rows]
        part = jnp.concatenate([part[:, :half], part[:, half:]], axis=0).astype(jnp.bfloat16)
        if distance == 0:
            q_recv[0] = part
        else:
            q_send[distance] = part
    q_copies = []
    for distance in range(1, SPAN):
        copy = pltpu.make_async_remote_copy(
            src_ref=q_send.at[distance], dst_ref=q_recv.at[distance],
            send_sem=qs_sem.at[distance], recv_sem=qr_sem.at[distance],
            device_id={"dp": peer(distance)}, device_id_type=MESH,
        )
        copy.start()
        q_copies.append(copy)
    send_part(1)
    send_part(2)
    w_copies = []
    for block in range(shards):
        copy = pltpu.make_async_copy(w_ref.at[:, pl.ds(block * wide, wide)], w_v.at[block], w_sem.at[block])
        copy.start()
        w_copies.append(copy)

    def put_all(index, carry):
        slot = index // PAGES
        page = table_ref[beams[slot], index % PAGES]
        at = (index % (MOST * PAGES)) * PER_PAGE
        stage[index // (MOST * PAGES), pl.ds(at, PER_PAGE)] = pool_v[pl.ds(page * PER_PAGE, PER_PAGE)]
        return carry

    lax.fori_loop(0, SPAN * MOST * PAGES, put_all, 0)
    own_copy = pltpu.make_async_copy(stage.at[0], recv_ref.at[pl.ds(2 * LINK, MOST * PER_CHILD)], own_sem.at[0])
    own_copy.start()

    for copy in q_copies:
        copy.wait()

    def attend(distance):
        message = q_recv[distance].astype(jnp.float32)
        message = jnp.concatenate([message[:rows], message[rows:]], axis=1)
        q_rows = jnp.concatenate([message[:, h * HD:(h + 1) * HD] for h in range(heads)], axis=0).astype(jnp.bfloat16)
        fresh = message[:, wide:].astype(jnp.bfloat16)
        old_len = lens[distance * MOST]
        last_len = lens[distance * MOST + 1]
        contract = (((1,), (1,)), ((), ()))
        scale = HD ** -0.5
        half = MOST * PER_CHILD // 2
        keys = [stage[distance, pl.ds(rank * half, half), :, 0:HD].reshape(context, HD) for rank in range(MOST)]
        scores = [lax.dot_general(q_rows, key, contract, preferred_element_type=jnp.float32) for key in keys]
        rank_at = lax.broadcasted_iota(jnp.int32, scores[0].shape, 0) // STEPS % MOST
        scores = jnp.where(rank_at == 0, scores[0], scores[1]) * scale
        fresh_scores = lax.dot_general(q_rows, fresh[:, :HD], contract, preferred_element_type=jnp.float32) * scale
        position = lax.broadcasted_iota(jnp.int32, scores.shape, 1)
        limit = jnp.where(rank_at == 0, old_len, last_len)
        scores = jnp.where(position < limit, scores, -1e30)
        f_row = lax.broadcasted_iota(jnp.int32, fresh_scores.shape, 0)
        f_col = lax.broadcasted_iota(jnp.int32, fresh_scores.shape, 1)
        seen = (f_row // STEPS % MOST == f_col // STEPS) & (f_col % STEPS <= f_row % STEPS)
        fresh_scores = jnp.where(seen, fresh_scores, -1e30)
        top = jnp.maximum(jnp.max(scores, axis=1, keepdims=True), jnp.max(fresh_scores, axis=1, keepdims=True))
        exp_old = jnp.exp(scores - top)
        exp_new = jnp.exp(fresh_scores - top)
        total = jnp.sum(exp_old, axis=1, keepdims=True) + jnp.sum(exp_new, axis=1, keepdims=True)
        share = 1.0 / total
        w_old = (exp_old * share).astype(jnp.bfloat16)
        w_new = (exp_new * share).astype(jnp.bfloat16)
        values = [stage[distance, pl.ds(rank * half, half), :, HD:2 * HD].reshape(context, HD) for rank in range(MOST)]
        out = [jnp.dot(w_old, value, preferred_element_type=jnp.float32) for value in values]
        out = jnp.where(rank_at[:, :HD] == 0, out[0], out[1])
        out += jnp.dot(w_new, fresh[:, HD:], preferred_element_type=jnp.float32)
        out = jnp.concatenate([out[h * rows:(h + 1) * rows] for h in range(heads)], axis=1)
        att[pl.ds(pl.multiple_of(distance * rows, rows), rows), :] = out

    def attend_two(at, carry):
        attend(2 * at)
        attend(2 * at + 1)
        return carry

    lax.fori_loop(0, SPAN // 2, attend_two, 0)
    for copy in b_copies[:4]:
        copy.wait()
    more_copies = b_copies[4:]
    b_copies = []
    for side, (flow, mine_via, _, passed, target) in enumerate(sides):
        def put_passed(at, carry, side=side, flow=flow, mine_via=mine_via, passed=passed):
            for at in [4 * at + more for more in range(4)]:
                here = pool_v[grain_at(flow, FIRST - mine_via + at - passed)]
                rest_send[side, at] = jnp.where(at < passed, first_recv[side, at], here)
            return carry

        lax.fori_loop(0, REST // 4, put_passed, 0)
        copy = pltpu.make_async_remote_copy(
            src_ref=rest_send.at[side], dst_ref=recv_ref.at[pl.ds(side * LINK + FIRST, REST)],
            send_sem=bs_sem.at[side * 4 + 3], recv_sem=br_sem.at[side * 4 + 3],
            device_id={"dp": target}, device_id_type=MESH,
        )
        copy.start()
        b_copies.append(copy)
    attended = att[...].astype(jnp.bfloat16)
    for copy in w_copies:
        copy.wait()

    def p_copy(other):
        return pltpu.make_async_remote_copy(
            src_ref=p_send.at[other], dst_ref=p_recv.at[other],
            send_sem=ps_sem.at[other], recv_sem=pr_sem.at[other],
            device_id={"tensor": lax.rem(mine + other, shards)}, device_id_type=MESH,
        )

    def project(other, carry):
        product = jnp.dot(attended, w_v[lax.rem(mine + other, shards)], preferred_element_type=jnp.float32)
        p_send[other] = product.astype(jnp.bfloat16)
        p_copy(other).start()
        return carry

    @pl.when(mine < shards - 1)
    def _():
        pl.semaphore_wait(here_sem, shards - 1 - mine)

    lax.fori_loop(1, shards, project, 0)
    own = jnp.dot(attended, w_v[mine], preferred_element_type=jnp.float32)

    for copy in more_copies:
        copy.wait()
    for side in range(2):
        copy = pltpu.make_async_copy(first_recv.at[side], recv_ref.at[pl.ds(side * LINK, FIRST)], land_sem.at[side])
        copy.start()
        b_copies.append(copy)

    def gather_sums(other, total):
        p_copy(other).wait()
        return total + p_recv[other].astype(jnp.float32)

    summed = lax.fori_loop(1, shards, gather_sums, own)
    half = wide // 2
    r_copies = []
    for distance in range(SPAN):
        part = summed[distance * rows:(distance + 1) * rows]
        r_send[distance] = jnp.concatenate([part[:, :half], part[:, half:]], axis=0).astype(jnp.bfloat16)
        if distance == 0:
            copy = pltpu.make_async_copy(r_send.at[0], proj_ref.at[0], own_sem.at[1])
        else:
            copy = pltpu.make_async_remote_copy(
                src_ref=r_send.at[distance], dst_ref=proj_ref.at[distance],
                send_sem=rs_sem.at[distance], recv_sem=rr_sem.at[distance],
                device_id={"dp": peer(SPAN - distance)}, device_id_type=MESH,
            )
        copy.start()
        r_copies.append(copy)
    for copy in row_copies:
        copy.wait()
    load = heaviest(par_row[...], len_row[...], rings)
    over_ref[0] = sum(jnp.where(load > limit, 1, 0) for limit in (LINK, LINK + SOME, LINK + LEFT))
    for side, (flow, mine_via, _, passed, _) in enumerate(sides):
        def put_left(at, carry, side=side, flow=flow, mine_via=mine_via, passed=passed):
            for at in [4 * at + more for more in range(4)]:
                left_send[side, at] = pool_v[grain_at(flow, LINK - mine_via - passed + at)]
            return carry

        lax.fori_loop(0, LEFT // 4, put_left, 0)
    left_copy = pltpu.make_async_copy(left_send, left_ref, land_sem.at[2])
    left_copy.start()
    for child in range(BEAMS):
        slot = slots[child]
        distance = slot >> 1
        length = len_ref[owners[child]]
        kept = jnp.where(distance == 3, choose(plan["up_id"], (y - 1) & 3), choose(plan["down_id"], (y + 1) & 3))
        before = jnp.int32(0)
        for other in range(BEAMS):
            if other != child:
                mate = (slots[other] >> 1 == distance) & (slots[other] < slot)
                counts = (owners[other] != owners[child]) & (owners[other] != kept)
                before = jnp.where(mate & counts, grains(len_ref[owners[other]]), before)
        far_before = jnp.where(owners[child] == choose(plan["first"], (y + 2) & 3), 0, choose(plan["cut"], (y + 2) & 3))
        before = jnp.where(distance == 2, far_before, before)
        from_up = choose(via_up, (y - 1) & 3), choose(via_up, (y + 2) & 3)
        from_down = choose(via_down, (y + 1) & 3), choose(via_down, (y + 2) & 3)
        near_via = jnp.where(distance == 3, from_up[0], from_down[0])
        near_pass = jnp.where(distance == 3, from_up[1], from_down[1])
        near_base = jnp.where(distance == 3, 0, LINK)
        split = jnp.where(distance == 2, from_up[1], FIRST - near_via) - before
        split = jnp.minimum(jnp.maximum(split, 0), PER_CHILD)
        start = jnp.where(distance == 2, FIRST + before, near_base + near_via + before)
        again = jnp.where(distance == 2, LINK + FIRST + before + split - from_up[1], start + split + near_pass)
        near = (distance == 1) | (distance == 3)
        until = LINK - near_via - near_pass - before
        until = jnp.where(near, jnp.minimum(jnp.maximum(until, 0), PER_CHILD), PER_CHILD)
        third = jnp.where(distance == 3, 0, LEFT) + near_via + near_pass + before + until - LINK
        held = near & (owners[child] == kept)
        kept_down = LINK + choose(via_down, (y + 1) & 3) - choose(plan["keep_down"], (y + 1) & 3)
        start = jnp.where(held, jnp.where(distance == 3, 0, kept_down), start)
        split = jnp.where(held, PER_CHILD, split)
        again = jnp.where(held, 0, again)
        until = jnp.where(held, PER_CHILD, until)
        third = jnp.where(held, 0, third)
        stays = distance == 0
        meta_ref[child * META] = length
        meta_ref[child * META + 1] = jnp.where(stays, 2 * LINK + (slot & 1) * PER_CHILD, start)
        meta_ref[child * META + 2] = jnp.where(stays, PER_CHILD, split)
        meta_ref[child * META + 3] = jnp.where(stays, 0, again)
        meta_ref[child * META + 4] = until
        meta_ref[child * META + 5] = jnp.where(near, third, 0)
        meta_ref[child * META + 6] = slot
    for copy in r_copies:
        copy.wait()
    for copy in b_copies:
        copy.wait()
    own_copy.wait()
    left_copy.wait()


def full_kernel(
    pool_ref, table_hbm, par_hbm, recv_ref,
    table_ref, par_ref, pool_v, stage,
    in_sem, pool_sem, own_sem, bs_sem, br_sem,
):
    me = lax.axis_index("dp")
    y = lax.rem(me, SPAN)
    base = me - y
    context = stage.shape[1] // MOST

    def peer(distance):
        return base + lax.rem(y + distance, SPAN)

    barrier = pltpu.get_barrier_semaphore()
    for distance in range(1, SPAN):
        pl.semaphore_signal(barrier, inc=1, device_id={"dp": peer(distance)}, device_id_type=MESH)
    in_copies = []
    for at, (source, target) in enumerate(((par_hbm, par_ref), (table_hbm, table_ref))):
        copy = pltpu.make_async_copy(source, target, in_sem.at[at])
        copy.start()
        in_copies.append(copy)
    pool_copy = pltpu.make_async_copy(pool_ref, pool_v, pool_sem)
    pool_copy.start()
    for copy in in_copies:
        copy.wait()
    pl.semaphore_wait(barrier, SPAN - 1)
    pool_copy.wait()
    copies = []
    for distance in (2, 1, 3, 0):
        served = served_beams(par_ref, me, peer(SPAN - distance))
        for rank in range(MOST):
            beam = served[rank]

            def put(index, carry, distance=distance, rank=rank, beam=beam):
                at = pl.multiple_of(rank * context + index * PAGE, PAGE)
                stage[distance, pl.ds(at, PAGE), :] = pool_v[table_ref[beam, index]]
                return carry

            lax.fori_loop(0, context // PAGE, put, 0)
            span = pl.ds(rank * context, context)
            if distance == 0:
                copy = pltpu.make_async_copy(stage.at[0, span], recv_ref.at[0, span], own_sem.at[rank])
            else:
                copy = pltpu.make_async_remote_copy(
                    src_ref=stage.at[distance, span], dst_ref=recv_ref.at[distance, span],
                    send_sem=bs_sem.at[distance * MOST + rank], recv_sem=br_sem.at[distance * MOST + rank],
                    device_id={"dp": peer(SPAN - distance)}, device_id_type=MESH,
                )
            copy.start()
            copies.append(copy)
    for copy in copies:
        copy.wait()


def finish_kernel(recv_ref, raw_ref, new_hbm, len_hbm, par_hbm, proj_ref, cache_ref, new_ref, len_ref, par_ref, edge, zeros, in_sem, out_sem):
    me = lax.axis_index("dp")
    pages = recv_ref.shape[1] // PAGE
    operands = ((par_hbm, par_ref), (len_hbm, len_ref), (new_hbm, new_ref))
    in_copies = [pltpu.make_async_copy(source, target, in_sem.at[at]) for at, (source, target) in enumerate(operands)]
    for copy in in_copies:
        copy.start()
    zeros[...] = jnp.zeros_like(zeros)
    for copy in in_copies:
        copy.wait()
    slots, owners = slots_of_children(par_ref, me)
    fresh = [new_ref[step].astype(jnp.float32) for step in range(STEPS)]
    for child in range(BEAMS):
        slot = slots[child]
        length = len_ref[owners[child]]
        first = length // PAGE
        last = (length + STEPS - 1) // PAGE

        def whole(index, carry, child=child, slot=slot):
            span = pl.ds(pl.multiple_of(index * PAGE, PAGE), PAGE)
            pltpu.make_async_copy(recv_ref.at[slot, span], cache_ref.at[child, span], out_sem).start()
            return carry

        def clear(index, carry, child=child):
            span = pl.ds(pl.multiple_of(index * PAGE, PAGE), PAGE)
            pltpu.make_async_copy(zeros, cache_ref.at[child, span], out_sem).start()
            return carry

        def fix(index, carry, child=child, slot=slot, length=length, first=first):
            at = pl.multiple_of(index * PAGE, PAGE)
            position = at + lax.broadcasted_iota(jnp.int32, (PAGE, 2 * HD), 0)
            page = recv_ref[slot, pl.ds(at, PAGE), :].astype(jnp.float32)
            page = jnp.where(position < length, page, 0.0)
            for step in range(STEPS):
                page = jnp.where(position == length + step, fresh[step][child:child + 1], page)
            edge[child * 2 + index - first] = page.astype(jnp.bfloat16)
            pltpu.make_async_copy(edge.at[child * 2 + index - first], cache_ref.at[child, pl.ds(at, PAGE)], out_sem).start()
            return carry

        lax.fori_loop(0, first, whole, 0)
        lax.fori_loop(last + 1, pages, clear, 0)
        lax.fori_loop(first, last + 1, fix, 0)

    rows = MOST * STEPS
    raw = []
    for distance in range(SPAN):
        part = raw_ref[distance].astype(jnp.float32)
        raw.append(jnp.concatenate([part[:rows], part[rows:]], axis=1))
    raw = jnp.concatenate(raw, axis=0).astype(jnp.bfloat16)
    row = lax.broadcasted_iota(jnp.int32, (BEAMS, SPAN * rows), 0)
    col = lax.broadcasted_iota(jnp.int32, (BEAMS, SPAN * rows), 1)
    slot_at = jnp.zeros_like(col)
    for child in range(BEAMS):
        slot_at = jnp.where(row == child, slots[child], slot_at)
    for step in range(STEPS):
        pick = jnp.where(col == slot_at * STEPS + step, 1.0, 0.0).astype(jnp.bfloat16)
        proj_ref[step] = jnp.dot(pick, raw, preferred_element_type=jnp.float32).astype(jnp.bfloat16)
    pltpu.make_async_copy(recv_ref, cache_ref, out_sem).wait()


def left_kernel(count, left_ref, got_ref, send_sem, recv_sem):
    me = lax.axis_index("dp")
    y = lax.rem(me, SPAN)
    targets = [me - y + lax.rem(y + ahead, SPAN) for ahead in (1, SPAN - 1)]
    barrier = pltpu.get_barrier_semaphore()
    for target in targets:
        pl.semaphore_signal(barrier, inc=1, device_id={"dp": target}, device_id_type=MESH)
    pl.semaphore_wait(barrier, 2)
    copies = []
    for side, target in enumerate(targets):
        copy = pltpu.make_async_remote_copy(
            src_ref=left_ref.at[side, pl.ds(0, count)], dst_ref=got_ref.at[side, pl.ds(0, count)],
            send_sem=send_sem.at[side], recv_sem=recv_sem.at[side],
            device_id={"dp": target}, device_id_type=MESH,
        )
        copy.start()
        copies.append(copy)
    for copy in copies:
        copy.wait()


def place_kernel(with_left, recv_ref, raw_ref, new_ref, meta_ref, *refs):
    left_ref = refs[0] if with_left else None
    proj_hbm, cache_ref, edge, zeros, proj_ref, out_sem, proj_sem = refs[-7:]
    total = recv_ref.shape[0]
    zeros[...] = jnp.zeros_like(zeros)
    fresh = [new_ref[step].astype(jnp.float32) for step in range(STEPS)]
    slots = [meta_ref[child * META + 6] for child in range(BEAMS)]
    per_child = cache_ref.shape[1]
    scale = GRAIN // TILE
    for child in range(BEAMS):
        length, start, split, again, until, third = (meta_ref[child * META + at] for at in range(6))
        first = length // TILE
        last = (length + STEPS - 1) // TILE
        until = jnp.minimum(until * scale, first) if with_left else first
        split = jnp.minimum(split * scale, until)

        def move(source, source_at, at, count, child=child):
            @pl.when(count > 0)
            def _():
                pltpu.make_async_copy(
                    source.at[pl.ds(source_at, count)], cache_ref.at[child, pl.ds(at, count)], out_sem
                ).start()

        move(recv_ref, start * scale, 0, split)
        move(recv_ref, again * scale, split, until - split)
        if with_left:
            move(left_ref, third * scale, until, first - until)
        move(zeros, 0, last + 1, per_child - 1 - last)
    for child in range(BEAMS):
        length, start, split, again, until, third = (meta_ref[child * META + at] for at in range(6))
        first = length // TILE
        last = (length + STEPS - 1) // TILE

        def fix(
            index, carry, child=child, length=length, first=first, start=start * scale, split=split * scale,
            again=again * scale, until=until * scale, third=third * scale,
        ):
            position = index * TILE + lax.broadcasted_iota(jnp.int32, (TILE, 2 * HD), 0)
            at = jnp.minimum(jnp.where(index < split, start + index, again + index - split), total - 1)
            part = recv_ref[at].astype(jnp.float32)
            if with_left:
                at = jnp.minimum(jnp.maximum(third + index - until, 0), left_ref.shape[0] - 1)
                part = jnp.where(index < until, part, left_ref[at].astype(jnp.float32))
            part = jnp.where(position < length, part, 0.0)
            for step in range(STEPS):
                part = jnp.where(position == length + step, fresh[step][child:child + 1], part)
            edge[child * 2 + index - first] = part.astype(jnp.bfloat16)
            pltpu.make_async_copy(edge.at[child * 2 + index - first], cache_ref.at[child, index], out_sem).start()
            return carry

        lax.fori_loop(first, last + 1, fix, 0)

    rows = MOST * STEPS
    raw = []
    for distance in range(SPAN):
        part = raw_ref[distance].astype(jnp.float32)
        raw.append(jnp.concatenate([part[:rows], part[rows:]], axis=1))
    raw = jnp.concatenate(raw, axis=0).astype(jnp.bfloat16)
    row = lax.broadcasted_iota(jnp.int32, (BEAMS, SPAN * rows), 0)
    col = lax.broadcasted_iota(jnp.int32, (BEAMS, SPAN * rows), 1)
    slot_at = jnp.zeros_like(col)
    for child in range(BEAMS):
        slot_at = jnp.where(row == child, slots[child], slot_at)
    for step in range(STEPS):
        pick = jnp.where(col == slot_at * STEPS + step, 1.0, 0.0).astype(jnp.bfloat16)
        proj_ref[step] = jnp.dot(pick, raw, preferred_element_type=jnp.float32).astype(jnp.bfloat16)
    proj_copy = pltpu.make_async_copy(proj_ref, proj_hbm, proj_sem)
    proj_copy.start()
    pltpu.make_async_copy(cache_ref, cache_ref, out_sem).wait()
    proj_copy.wait()


def local(shards, queries, new_kv, kv_pool, page_tables, lengths, parents, out_weight):
    wide = queries.shape[2]
    channels = kv_pool.shape[2]
    context = page_tables.shape[1] * kv_pool.shape[1]
    rows = MOST * STEPS
    vmem = pl.BlockSpec(memory_space=pltpu.VMEM)
    smem = pl.BlockSpec(memory_space=pltpu.SMEM)
    hbm = pl.BlockSpec(memory_space=pltpu.HBM)
    free = pl.BlockSpec(memory_space=pl.ANY)
    dma = pltpu.SemaphoreType.DMA
    bf16 = jnp.bfloat16

    def pinned(*operands):
        return [pltpu.with_memory_space_constraint(operand, pltpu.HBM) for operand in operands]

    grain_pool = kv_pool.reshape(-1, GRAIN, channels)
    with jax.named_scope("exchange"):
        recv, raw, left, meta, over = pl.pallas_call(
            exchange_kernel,
            out_shape=(
                jax.ShapeDtypeStruct((2 * LINK + MOST * PER_CHILD, GRAIN, channels), bf16),
                jax.ShapeDtypeStruct((SPAN, 2 * rows, wide // 2), bf16),
                jax.ShapeDtypeStruct((2, LEFT, GRAIN, channels), bf16),
                jax.ShapeDtypeStruct((BEAMS * META,), jnp.int32),
                jax.ShapeDtypeStruct((1,), jnp.int32),
            ),
            in_specs=[hbm] * 7,
            out_specs=(free, free, free, smem, smem),
            scratch_shapes=[
                pltpu.VMEM(queries.shape, bf16),
                pltpu.VMEM(new_kv.shape, bf16),
                pltpu.SMEM(page_tables.shape, jnp.int32),
                pltpu.SMEM(lengths.shape, jnp.int32),
                pltpu.SMEM(parents.shape, jnp.int32),
                pltpu.VMEM((1, *lengths.shape), jnp.int32),
                pltpu.VMEM((1, *parents.shape), jnp.int32),
                pltpu.VMEM(grain_pool.shape, bf16),
                pltpu.VMEM((shards, out_weight.shape[0], wide), bf16),
                pltpu.VMEM((SPAN, MOST * PER_CHILD, GRAIN, channels), bf16),
                pltpu.VMEM((2, FIRST, GRAIN, channels), bf16),
                pltpu.VMEM((2, FIRST, GRAIN, channels), bf16),
                pltpu.VMEM((2, REST, GRAIN, channels), bf16),
                pltpu.VMEM((2, LEFT, GRAIN, channels), bf16),
                pltpu.VMEM((SPAN, 2 * rows, (wide + channels) // 2), bf16),
                pltpu.VMEM((SPAN, 2 * rows, (wide + channels) // 2), bf16),
                pltpu.VMEM((SPAN * rows, wide), jnp.float32),
                pltpu.VMEM((shards, SPAN * rows, wide), bf16),
                pltpu.VMEM((shards, SPAN * rows, wide), bf16),
                pltpu.VMEM((SPAN, 2 * rows, wide // 2), bf16),
                pltpu.SMEM((SPAN * MOST,), jnp.int32),
                pltpu.SMEM((SPAN * MOST,), jnp.int32),
                dma((7,)), dma((4,)), dma((shards,)), dma((2,)), dma((3,)),
                dma((SPAN,)), dma((SPAN,)),
                dma((8,)), dma((8,)),
                dma((shards,)), dma((shards,)),
                dma((SPAN,)), dma((SPAN,)),
                pltpu.SemaphoreType.REGULAR,
            ],
            compiler_params=pltpu.CompilerParams(
                collective_id=0, has_side_effects=True, vmem_limit_bytes=48 * 1024 * 1024
            ),
            name="exchange",
        )(*pinned(queries, new_kv, grain_pool, page_tables, lengths, parents, out_weight))

    def place(*got):
        with jax.named_scope("place"):
            projected, cache = pl.pallas_call(
                functools.partial(place_kernel, len(got) > 0),
                out_shape=(
                    jax.ShapeDtypeStruct(queries.shape, bf16),
                    jax.ShapeDtypeStruct((BEAMS, context // TILE, TILE, channels), bf16),
                ),
                in_specs=[vmem, vmem, vmem, smem] + [vmem] * len(got),
                out_specs=(free, free),
                scratch_shapes=[
                    pltpu.VMEM((2 * BEAMS, TILE, channels), bf16),
                    pltpu.VMEM((context // TILE, TILE, channels), bf16),
                    pltpu.VMEM(queries.shape, bf16),
                    dma, dma,
                ],
                compiler_params=pltpu.CompilerParams(vmem_limit_bytes=24 * 1024 * 1024),
                name="place_left" if got else "place",
            )(recv.reshape(-1, TILE, channels), raw, new_kv, meta, *got)
            return projected, cache.reshape(BEAMS, context, channels)

    def placed():
        return place()

    def topped(count, number):
        with jax.named_scope("left"):
            got = pl.pallas_call(
                functools.partial(left_kernel, count),
                out_shape=jax.ShapeDtypeStruct(left.shape, bf16),
                in_specs=[free],
                out_specs=free,
                scratch_shapes=[dma((2,)), dma((2,))],
                compiler_params=pltpu.CompilerParams(
                    collective_id=number, has_side_effects=True, vmem_limit_bytes=4 * 1024 * 1024
                ),
                name="left",
            )(left)
        return place(got.reshape(-1, TILE, channels))

    def resent():
        with jax.named_scope("full"):
            whole = pl.pallas_call(
                full_kernel,
                out_shape=jax.ShapeDtypeStruct((SPAN, MOST * context, channels), bf16),
                in_specs=[hbm] * 3,
                out_specs=free,
                scratch_shapes=[
                    pltpu.SMEM(page_tables.shape, jnp.int32),
                    pltpu.SMEM(parents.shape, jnp.int32),
                    pltpu.VMEM(kv_pool.shape, bf16),
                    pltpu.VMEM((SPAN, MOST * context, channels), bf16),
                    dma((2,)), dma, dma((MOST,)),
                    dma((SPAN * MOST,)), dma((SPAN * MOST,)),
                ],
                compiler_params=pltpu.CompilerParams(
                    collective_id=1, has_side_effects=True, vmem_limit_bytes=24 * 1024 * 1024
                ),
                name="full",
            )(*pinned(kv_pool, page_tables, parents))
        with jax.named_scope("finish"):
            return pl.pallas_call(
                finish_kernel,
                out_shape=(
                    jax.ShapeDtypeStruct(queries.shape, bf16),
                    jax.ShapeDtypeStruct((BEAMS, context, channels), bf16),
                ),
                in_specs=[vmem, vmem, hbm, hbm, hbm],
                out_specs=(vmem, hbm),
                scratch_shapes=[
                    pltpu.VMEM(new_kv.shape, bf16),
                    pltpu.SMEM(lengths.shape, jnp.int32),
                    pltpu.SMEM(parents.shape, jnp.int32),
                    pltpu.VMEM((2 * BEAMS, PAGE, channels), bf16),
                    pltpu.VMEM((PAGE, channels), bf16),
                    dma((3,)), dma,
                ],
                compiler_params=pltpu.CompilerParams(vmem_limit_bytes=24 * 1024 * 1024),
                name="finish",
            )(whole.reshape(BEAMS, context, channels), raw, new_kv, lengths, parents)

    return lax.switch(over[0], (placed, functools.partial(topped, SOME, 2), functools.partial(topped, LEFT, 3), resent))


def solution(mesh):
    in_specs = (
        P(None, "dp", "tensor"),
        P(None, "dp", "tensor"),
        P("dp", None, "tensor"),
        P("dp", None),
        P(),
        P(),
        P("tensor", None),
    )
    out_specs = (P(None, "dp", "tensor"), P("dp", None, "tensor"))
    body = functools.partial(local, mesh.shape["tensor"])
    return jax.shard_map(body, mesh=mesh, in_specs=in_specs, out_specs=out_specs, check_vma=False)
```

```python
import functools

import jax
import jax.numpy as jnp
from jax import lax
from jax.experimental import pallas as pl
from jax.experimental.pallas import tpu as pltpu
from jax.sharding import PartitionSpec as P

HD = 128
SPAN = 4
MOST = 2
BEAMS = 8
STEPS = 4
PAGE = 128
PAGES = 8
GRAIN = 32
PER_CHILD = 32
PER_PAGE = PAGE // GRAIN
TILE = 16
VIA = 36
MORE = 16
REST = 36
TIERS = (4, 10, 24)
LEFT = TIERS[-1]
FIRST = VIA + MORE
LINK = FIRST + REST
META = 7
MESH = pl.DeviceIdType.MESH


def grains(length):
    return (length + (GRAIN - 1)) // GRAIN


def choose(values, index):
    out = values[0]
    for at in range(1, len(values)):
        out = jnp.where(index == at, values[at], out)
    return out


def balanced(up, far, down, keep_up, keep_down):
    least = [jnp.maximum(keep_up[i], far[i] - VIA) for i in range(SPAN)]
    most = [jnp.minimum(far[i] - keep_down[i], VIA) for i in range(SPAN)]
    via_up = [jnp.minimum(jnp.maximum(far[i] >> 1, least[i]), most[i]) for i in range(SPAN)]
    for at in range(SPAN):
        via_down = [far[i] - via_up[i] for i in range(SPAN)]
        nxt, prv = (at + 1) % SPAN, (at - 1) % SPAN
        load_up = jnp.maximum(up[at] + via_up[prv], up[nxt] + via_up[nxt])
        load_down = jnp.maximum(down[at] + via_down[nxt], down[prv] + via_down[prv])
        best = (load_down + far[at] - load_up) >> 1
        via_up[at] = jnp.minimum(jnp.maximum(best, least[at]), most[at])
    via_down = [far[i] - via_up[i] for i in range(SPAN)]
    return via_up, via_down


def planned(flows):
    names = ("up", "down", "far", "first", "second", "cut", "up_id", "down_id", "keep_up", "keep_down")
    plan = {name: [] for name in names}
    for at in range(SPAN):
        u0, u1, gu0, gu1 = flows[at][1]
        f0, f1, gf0, gf1 = flows[at][2]
        d0, d1, gd0, gd1 = flows[at][3]
        gu1 = jnp.where(u0 == u1, 0, gu1)
        gf1 = jnp.where(f0 == f1, 0, gf1)
        gd1 = jnp.where(d0 == d1, 0, gd1)

        def shared(parent, count, one, two):
            return jnp.where((parent == one) | (parent == two), count, 0)

        straight = shared(f0, gf0, u0, u1) + shared(f1, gf1, d0, d1)
        crossed = shared(f1, gf1, u0, u1) + shared(f0, gf0, d0, d1)
        swap = crossed > straight
        first, second = jnp.where(swap, f1, f0), jnp.where(swap, f0, f1)
        cut, rest = jnp.where(swap, gf1, gf0), jnp.where(swap, gf0, gf1)
        keep_up, keep_down = shared(first, cut, u0, u1), shared(second, rest, d0, d1)
        values = (
            gu0 + gu1 - keep_up, gd0 + gd1 - keep_down, gf0 + gf1, first, second, cut,
            jnp.where(keep_up > 0, first, -1), jnp.where(keep_down > 0, second, -1), keep_up, keep_down,
        )
        for name, value in zip(names, values):
            plan[name].append(value)
    plan["via_up"], plan["via_down"] = balanced(
        plan["up"], plan["far"], plan["down"], plan["keep_up"], plan["keep_down"]
    )
    return plan


def ring_plan(parents, lengths, ring):
    flows = [[None] * SPAN for _ in range(SPAN)]
    for target in range(SPAN):
        owners = [parents[(ring * SPAN + target) * BEAMS + child] for child in range(BEAMS)]
        sources = [(owner >> 3) & (SPAN - 1) for owner in owners]
        for at in range(SPAN):
            if at != target:
                one, two = owners[0], owners[0]
                for child in range(1, BEAMS):
                    two = jnp.where(sources[child] == at, owners[child], two)
                one = owners[BEAMS - 1]
                for child in range(BEAMS - 2, -1, -1):
                    one = jnp.where(sources[child] == at, owners[child], one)
                flows[at][(target - at) % SPAN] = (one, two, grains(lengths[one]), grains(lengths[two]))
    return planned(flows)


def heaviest(parents, lengths, rings):
    beams = rings * SPAN * BEAMS
    counts = grains(lengths).astype(jnp.float32).astype(jnp.bfloat16)
    beam = lax.broadcasted_iota(jnp.int32, (beams, beams), 0)
    chosen = jnp.where(beam == parents, 1.0, 0.0).astype(jnp.bfloat16)
    counts = jnp.dot(jnp.broadcast_to(counts, (16, beams)), chosen, preferred_element_type=jnp.float32)[:1]
    lane = lax.broadcasted_iota(jnp.int32, (1, beams), 1)
    source = (parents // BEAMS) % SPAN
    rank = jnp.zeros_like(lane)
    for back in range(1, BEAMS):
        rank = rank + jnp.where((pltpu.roll(source, back, 1) == source) & (lane % BEAMS >= back), 1, 0)
    names = (parents % (SPAN * BEAMS)).astype(jnp.float32)
    rows = [
        jnp.where((source == at) & (rank == order), value, 0.0)
        for value in (names, counts) for at in range(SPAN) for order in range(MOST)
    ]
    rows = jnp.concatenate(rows, axis=0).astype(jnp.bfloat16)
    child = lax.broadcasted_iota(jnp.int32, (beams, 128), 0)
    ring = lax.broadcasted_iota(jnp.int32, (beams, 128), 1)
    flows = [[None] * SPAN for _ in range(SPAN)]
    for target in range(SPAN):
        member = (child // BEAMS % SPAN == target) & (child // (BEAMS * SPAN) == ring)
        member = jnp.where(member, 1.0, 0.0).astype(jnp.bfloat16)
        found = jnp.dot(rows, member, preferred_element_type=jnp.float32).astype(jnp.int32)
        for at in range(SPAN):
            wanted = (at * MOST, at * MOST + 1, (SPAN + at) * MOST, (SPAN + at) * MOST + 1)
            flows[at][(target - at) % SPAN] = tuple(found[one:one + 1] for one in wanted)
    plan = planned(flows)
    out = jnp.zeros_like(plan["far"][0])
    for at in range(SPAN):
        load_up = plan["up"][at] + plan["via_up"][at] + plan["via_up"][(at - 1) % SPAN]
        load_down = plan["down"][at] + plan["via_down"][at] + plan["via_down"][(at + 1) % SPAN]
        out = jnp.maximum(out, jnp.maximum(load_up, load_down))
    return jnp.max(out)


def slots_of_children(parents, me):
    taken = [jnp.int32(0) for _ in range(SPAN)]
    slots, owners = [], []
    for child in range(BEAMS):
        parent = parents[me * BEAMS + child]
        apart = jnp.bitwise_and(parent // BEAMS - me, SPAN - 1)
        slot = jnp.int32(0)
        for distance in range(SPAN):
            hit = apart == distance
            slot = jnp.where(hit, distance * MOST + taken[distance], slot)
            taken[distance] = taken[distance] + hit.astype(jnp.int32)
        slots.append(slot)
        owners.append(parent)
    return slots, owners


def served_beams(parents, me, target):
    count = jnp.int32(0)
    beams = [jnp.int32(0) for _ in range(MOST)]
    for child in range(BEAMS):
        parent = parents[target * BEAMS + child]
        hit = parent // BEAMS == me
        for rank in range(MOST):
            beams[rank] = jnp.where(hit & (count == rank), parent % BEAMS, beams[rank])
        count = count + hit.astype(jnp.int32)
    return beams


def exchange_kernel(
    q_hbm, new_hbm, pool_ref, table_hbm, len_hbm, par_hbm, w_ref,
    recv_ref, proj_ref, left_ref, meta_ref, over_ref,
    q_ref, new_ref, table_ref, len_ref, par_ref, len_row, par_row,
    pool_v, w_v, stage, first_send, first_recv, rest_send, left_send, q_send, q_recv, att, p_send, p_recv, r_send, lens, beams,
    in_sem, pool_sem, w_sem, own_sem, land_sem, qs_sem, qr_sem, bs_sem, br_sem, ps_sem, pr_sem, rs_sem, rr_sem, here_sem,
):
    me = lax.axis_index("dp")
    mine = lax.axis_index("tensor")
    shards = lax.axis_size("tensor")
    y = lax.rem(me, SPAN)
    base = me - y
    context = stage.shape[1] * GRAIN // MOST
    rings = lax.axis_size("dp") // SPAN
    wide = q_hbm.shape[2]
    heads = wide // HD
    rows = MOST * STEPS

    def peer(distance):
        return base + lax.rem(y + distance, SPAN)

    barrier = pltpu.get_barrier_semaphore()
    for distance in range(1, SPAN):
        pl.semaphore_signal(barrier, inc=1, device_id={"dp": peer(distance)}, device_id_type=MESH)
    for other in range(1, shards):
        @pl.when(mine + other < shards)
        def _(other=other):
            pl.semaphore_signal(barrier, inc=1, device_id={"tensor": mine + other}, device_id_type=MESH)
    in_copies = []
    operands = ((par_hbm, par_ref), (q_hbm, q_ref), (new_hbm, new_ref), (table_hbm, table_ref), (len_hbm, len_ref))
    rows_in = ((par_hbm, par_row.at[0]), (len_hbm, len_row.at[0]))
    for at, (source, target) in enumerate(operands):
        copy = pltpu.make_async_copy(source, target, in_sem.at[at])
        copy.start()
        in_copies.append(copy)
    row_copies = []
    for at, (source, target) in enumerate(rows_in):
        copy = pltpu.make_async_copy(source, target, in_sem.at[5 + at])
        copy.start()
        row_copies.append(copy)
    pool_copy = pltpu.make_async_copy(pool_ref, pool_v, pool_sem)
    pool_copy.start()
    for copy in in_copies:
        copy.wait()

    slots, owners = slots_of_children(par_ref, me)
    plan = ring_plan(par_ref, len_ref, me >> 2)
    via_up, via_down = plan["via_up"], plan["via_down"]
    flows = {}
    for ahead in range(SPAN):
        served = served_beams(par_ref, me, peer(ahead))
        distance = (SPAN - ahead) % SPAN
        held = [len_ref[me * BEAMS + served[rank]] for rank in range(MOST)]
        for rank in range(MOST):
            beams[distance * MOST + rank] = served[rank]
            lens[distance * MOST + rank] = held[rank]
        flows[ahead] = (served[0], served[1], grains(held[0]))

    for ahead, kept in ((1, "up_id"), (3, "down_id")):
        first, second, cut = flows[ahead]
        flows[ahead] = (first, second, jnp.where(me * BEAMS + first == choose(plan[kept], y), 0, cut))
    flows[2] = (choose(plan["first"], y) & 7, choose(plan["second"], y) & 7, choose(plan["cut"], y))

    def grain_at(flow, number):
        first, second, cut = flow
        later = number >= cut
        number = jnp.where(later, number - cut, number)
        number = jnp.minimum(jnp.maximum(number, 0), PER_CHILD - 1)
        return table_ref[jnp.where(later, second, first), number >> 2] * PER_PAGE + (number & (PER_PAGE - 1))

    sides = (
        (flows[1], choose(via_up, y), jnp.int32(0), choose(via_up, (y - 1) & 3), peer(1)),
        (flows[3], choose(via_down, y), choose(via_up, y), choose(via_down, (y + 1) & 3), peer(3)),
    )
    pl.semaphore_wait(barrier, SPAN - 1 + mine)
    for other in range(1, shards):
        @pl.when(mine >= other)
        def _(other=other):
            pl.semaphore_signal(here_sem, inc=1, device_id={"tensor": mine - other}, device_id_type=MESH)
    pool_copy.wait()
    b_copies = []
    cuts = (0, 8, VIA, FIRST)

    def send_part(part):
        for side, (flow, mine_via, skip, _, target) in enumerate(sides):
            def put(at, carry, side=side, flow=flow, mine_via=mine_via, skip=skip):
                for at in [4 * at + more for more in range(4)]:
                    far = at < mine_via
                    chosen = tuple(jnp.where(far, one, two) for one, two in zip(flows[2], flow))
                    number = jnp.where(far, skip + at, at - mine_via)
                    first_send[side, at] = pool_v[grain_at(chosen, number)]
                return carry

            lax.fori_loop(cuts[part] // 4, cuts[part + 1] // 4, put, 0)
            span = pl.ds(cuts[part], cuts[part + 1] - cuts[part])
            copy = pltpu.make_async_remote_copy(
                src_ref=first_send.at[side, span], dst_ref=first_recv.at[side, span],
                send_sem=bs_sem.at[side * 4 + part], recv_sem=br_sem.at[side * 4 + part],
                device_id={"dp": target}, device_id_type=MESH,
            )
            copy.start()
            b_copies.append(copy)

    send_part(0)

    row = lax.broadcasted_iota(jnp.int32, (SPAN * rows, BEAMS), 0)
    col = lax.broadcasted_iota(jnp.int32, (SPAN * rows, BEAMS), 1)
    slot_at = jnp.zeros_like(col)
    for child in range(BEAMS):
        slot_at = jnp.where(col == child, slots[child], slot_at)
    q_sorted = jnp.zeros((SPAN * rows, wide), jnp.float32)
    new_sorted = jnp.zeros((SPAN * rows, 2 * HD), jnp.float32)
    for step in range(STEPS):
        pick = jnp.where((row // STEPS == slot_at) & (row % STEPS == step), 1.0, 0.0).astype(jnp.bfloat16)
        q_sorted += jnp.dot(pick, q_ref[step], preferred_element_type=jnp.float32)
        new_sorted += jnp.dot(pick, new_ref[step], preferred_element_type=jnp.float32)
    both = jnp.concatenate([q_sorted, new_sorted], axis=1)
    half = both.shape[1] // 2
    for distance in range(SPAN):
        part = both[distance * rows:(distance + 1) * rows]
        part = jnp.concatenate([part[:, :half], part[:, half:]], axis=0).astype(jnp.bfloat16)
        if distance == 0:
            q_recv[0] = part
        else:
            q_send[distance] = part
    q_copies = []
    for distance in range(1, SPAN):
        copy = pltpu.make_async_remote_copy(
            src_ref=q_send.at[distance], dst_ref=q_recv.at[distance],
            send_sem=qs_sem.at[distance], recv_sem=qr_sem.at[distance],
            device_id={"dp": peer(distance)}, device_id_type=MESH,
        )
        copy.start()
        q_copies.append(copy)
    send_part(1)
    send_part(2)
    w_copies = []
    for block in range(shards):
        copy = pltpu.make_async_copy(w_ref.at[:, pl.ds(block * wide, wide)], w_v.at[block], w_sem.at[block])
        copy.start()
        w_copies.append(copy)

    def put_all(index, carry):
        slot = index // PAGES
        page = table_ref[beams[slot], index % PAGES]
        at = (index % (MOST * PAGES)) * PER_PAGE
        stage[index // (MOST * PAGES), pl.ds(at, PER_PAGE)] = pool_v[pl.ds(page * PER_PAGE, PER_PAGE)]
        return carry

    lax.fori_loop(0, SPAN * MOST * PAGES, put_all, 0)
    own_copy = pltpu.make_async_copy(stage.at[0], recv_ref.at[pl.ds(2 * LINK, MOST * PER_CHILD)], own_sem.at[0])
    own_copy.start()

    for copy in q_copies:
        copy.wait()

    def attend(distance):
        message = q_recv[distance].astype(jnp.float32)
        message = jnp.concatenate([message[:rows], message[rows:]], axis=1)
        q_rows = jnp.concatenate([message[:, h * HD:(h + 1) * HD] for h in range(heads)], axis=0).astype(jnp.bfloat16)
        fresh = message[:, wide:].astype(jnp.bfloat16)
        old_len = lens[distance * MOST]
        last_len = lens[distance * MOST + 1]
        contract = (((1,), (1,)), ((), ()))
        scale = HD ** -0.5
        half = MOST * PER_CHILD // 2
        keys = [stage[distance, pl.ds(rank * half, half), :, 0:HD].reshape(context, HD) for rank in range(MOST)]
        scores = [lax.dot_general(q_rows, key, contract, preferred_element_type=jnp.float32) for key in keys]
        rank_at = lax.broadcasted_iota(jnp.int32, scores[0].shape, 0) // STEPS % MOST
        scores = jnp.where(rank_at == 0, scores[0], scores[1]) * scale
        fresh_scores = lax.dot_general(q_rows, fresh[:, :HD], contract, preferred_element_type=jnp.float32) * scale
        position = lax.broadcasted_iota(jnp.int32, scores.shape, 1)
        limit = jnp.where(rank_at == 0, old_len, last_len)
        scores = jnp.where(position < limit, scores, -1e30)
        f_row = lax.broadcasted_iota(jnp.int32, fresh_scores.shape, 0)
        f_col = lax.broadcasted_iota(jnp.int32, fresh_scores.shape, 1)
        seen = (f_row // STEPS % MOST == f_col // STEPS) & (f_col % STEPS <= f_row % STEPS)
        fresh_scores = jnp.where(seen, fresh_scores, -1e30)
        top = jnp.maximum(jnp.max(scores, axis=1, keepdims=True), jnp.max(fresh_scores, axis=1, keepdims=True))
        exp_old = jnp.exp(scores - top)
        exp_new = jnp.exp(fresh_scores - top)
        total = jnp.sum(exp_old, axis=1, keepdims=True) + jnp.sum(exp_new, axis=1, keepdims=True)
        share = 1.0 / total
        w_old = (exp_old * share).astype(jnp.bfloat16)
        w_new = (exp_new * share).astype(jnp.bfloat16)
        values = [stage[distance, pl.ds(rank * half, half), :, HD:2 * HD].reshape(context, HD) for rank in range(MOST)]
        out = [jnp.dot(w_old, value, preferred_element_type=jnp.float32) for value in values]
        out = jnp.where(rank_at[:, :HD] == 0, out[0], out[1])
        out += jnp.dot(w_new, fresh[:, HD:], preferred_element_type=jnp.float32)
        out = jnp.concatenate([out[h * rows:(h + 1) * rows] for h in range(heads)], axis=1)
        att[pl.ds(pl.multiple_of(distance * rows, rows), rows), :] = out

    def attend_two(at, carry):
        attend(2 * at)
        attend(2 * at + 1)
        return carry

    lax.fori_loop(0, SPAN // 2, attend_two, 0)
    for copy in b_copies[:4]:
        copy.wait()
    more_copies = b_copies[4:]
    b_copies = []
    for side, (flow, mine_via, _, passed, target) in enumerate(sides):
        def put_passed(at, carry, side=side, flow=flow, mine_via=mine_via, passed=passed):
            for at in [4 * at + more for more in range(4)]:
                here = pool_v[grain_at(flow, FIRST - mine_via + at - passed)]
                rest_send[side, at] = jnp.where(at < passed, first_recv[side, at], here)
            return carry

        lax.fori_loop(0, REST // 4, put_passed, 0)
        copy = pltpu.make_async_remote_copy(
            src_ref=rest_send.at[side], dst_ref=recv_ref.at[pl.ds(side * LINK + FIRST, REST)],
            send_sem=bs_sem.at[side * 4 + 3], recv_sem=br_sem.at[side * 4 + 3],
            device_id={"dp": target}, device_id_type=MESH,
        )
        copy.start()
        b_copies.append(copy)
    attended = att[...].astype(jnp.bfloat16)
    for copy in w_copies:
        copy.wait()

    def p_copy(other):
        return pltpu.make_async_remote_copy(
            src_ref=p_send.at[other], dst_ref=p_recv.at[other],
            send_sem=ps_sem.at[other], recv_sem=pr_sem.at[other],
            device_id={"tensor": lax.rem(mine + other, shards)}, device_id_type=MESH,
        )

    def project(other, carry):
        product = jnp.dot(attended, w_v[lax.rem(mine + other, shards)], preferred_element_type=jnp.float32)
        p_send[other] = product.astype(jnp.bfloat16)
        p_copy(other).start()
        return carry

    @pl.when(mine < shards - 1)
    def _():
        pl.semaphore_wait(here_sem, shards - 1 - mine)

    lax.fori_loop(1, shards, project, 0)
    own = jnp.dot(attended, w_v[mine], preferred_element_type=jnp.float32)

    for copy in more_copies:
        copy.wait()
    for side in range(2):
        copy = pltpu.make_async_copy(first_recv.at[side], recv_ref.at[pl.ds(side * LINK, FIRST)], land_sem.at[side])
        copy.start()
        b_copies.append(copy)

    def gather_sums(other, total):
        p_copy(other).wait()
        return total + p_recv[other].astype(jnp.float32)

    summed = lax.fori_loop(1, shards, gather_sums, own)
    half = wide // 2
    r_copies = []
    for distance in range(SPAN):
        part = summed[distance * rows:(distance + 1) * rows]
        r_send[distance] = jnp.concatenate([part[:, :half], part[:, half:]], axis=0).astype(jnp.bfloat16)
        if distance == 0:
            copy = pltpu.make_async_copy(r_send.at[0], proj_ref.at[0], own_sem.at[1])
        else:
            copy = pltpu.make_async_remote_copy(
                src_ref=r_send.at[distance], dst_ref=proj_ref.at[distance],
                send_sem=rs_sem.at[distance], recv_sem=rr_sem.at[distance],
                device_id={"dp": peer(SPAN - distance)}, device_id_type=MESH,
            )
        copy.start()
        r_copies.append(copy)
    for copy in row_copies:
        copy.wait()
    load = heaviest(par_row[...], len_row[...], rings)
    over_ref[0] = sum(jnp.where(load > limit, 1, 0) for limit in (LINK, *(LINK + count for count in TIERS)))
    for side, (flow, mine_via, _, passed, _) in enumerate(sides):
        def put_left(at, carry, side=side, flow=flow, mine_via=mine_via, passed=passed):
            for at in [4 * at + more for more in range(4)]:
                left_send[side, at] = pool_v[grain_at(flow, LINK - mine_via - passed + at)]
            return carry

        lax.fori_loop(0, LEFT // 4, put_left, 0)
    left_copy = pltpu.make_async_copy(left_send, left_ref, land_sem.at[2])
    left_copy.start()
    for child in range(BEAMS):
        slot = slots[child]
        distance = slot >> 1
        length = len_ref[owners[child]]
        kept = jnp.where(distance == 3, choose(plan["up_id"], (y - 1) & 3), choose(plan["down_id"], (y + 1) & 3))
        before = jnp.int32(0)
        for other in range(BEAMS):
            if other != child:
                mate = (slots[other] >> 1 == distance) & (slots[other] < slot)
                counts = (owners[other] != owners[child]) & (owners[other] != kept)
                before = jnp.where(mate & counts, grains(len_ref[owners[other]]), before)
        far_before = jnp.where(owners[child] == choose(plan["first"], (y + 2) & 3), 0, choose(plan["cut"], (y + 2) & 3))
        before = jnp.where(distance == 2, far_before, before)
        from_up = choose(via_up, (y - 1) & 3), choose(via_up, (y + 2) & 3)
        from_down = choose(via_down, (y + 1) & 3), choose(via_down, (y + 2) & 3)
        near_via = jnp.where(distance == 3, from_up[0], from_down[0])
        near_pass = jnp.where(distance == 3, from_up[1], from_down[1])
        near_base = jnp.where(distance == 3, 0, LINK)
        split = jnp.where(distance == 2, from_up[1], FIRST - near_via) - before
        split = jnp.minimum(jnp.maximum(split, 0), PER_CHILD)
        start = jnp.where(distance == 2, FIRST + before, near_base + near_via + before)
        again = jnp.where(distance == 2, LINK + FIRST + before + split - from_up[1], start + split + near_pass)
        near = (distance == 1) | (distance == 3)
        until = LINK - near_via - near_pass - before
        until = jnp.where(near, jnp.minimum(jnp.maximum(until, 0), PER_CHILD), PER_CHILD)
        third = jnp.where(distance == 3, 0, LEFT) + near_via + near_pass + before + until - LINK
        held = near & (owners[child] == kept)
        kept_down = LINK + choose(via_down, (y + 1) & 3) - choose(plan["keep_down"], (y + 1) & 3)
        start = jnp.where(held, jnp.where(distance == 3, 0, kept_down), start)
        split = jnp.where(held, PER_CHILD, split)
        again = jnp.where(held, 0, again)
        until = jnp.where(held, PER_CHILD, until)
        third = jnp.where(held, 0, third)
        stays = distance == 0
        meta_ref[child * META] = length
        meta_ref[child * META + 1] = jnp.where(stays, 2 * LINK + (slot & 1) * PER_CHILD, start)
        meta_ref[child * META + 2] = jnp.where(stays, PER_CHILD, split)
        meta_ref[child * META + 3] = jnp.where(stays, 0, again)
        meta_ref[child * META + 4] = until
        meta_ref[child * META + 5] = jnp.where(near, third, 0)
        meta_ref[child * META + 6] = slot
    for copy in r_copies:
        copy.wait()
    for copy in b_copies:
        copy.wait()
    own_copy.wait()
    left_copy.wait()


def full_kernel(
    pool_ref, table_hbm, par_hbm, recv_ref,
    table_ref, par_ref, pool_v, stage,
    in_sem, pool_sem, own_sem, bs_sem, br_sem,
):
    me = lax.axis_index("dp")
    y = lax.rem(me, SPAN)
    base = me - y
    context = stage.shape[1] // MOST

    def peer(distance):
        return base + lax.rem(y + distance, SPAN)

    barrier = pltpu.get_barrier_semaphore()
    for distance in range(1, SPAN):
        pl.semaphore_signal(barrier, inc=1, device_id={"dp": peer(distance)}, device_id_type=MESH)
    in_copies = []
    for at, (source, target) in enumerate(((par_hbm, par_ref), (table_hbm, table_ref))):
        copy = pltpu.make_async_copy(source, target, in_sem.at[at])
        copy.start()
        in_copies.append(copy)
    pool_copy = pltpu.make_async_copy(pool_ref, pool_v, pool_sem)
    pool_copy.start()
    for copy in in_copies:
        copy.wait()
    pl.semaphore_wait(barrier, SPAN - 1)
    pool_copy.wait()
    copies = []
    for distance in (2, 1, 3, 0):
        served = served_beams(par_ref, me, peer(SPAN - distance))
        for rank in range(MOST):
            beam = served[rank]

            def put(index, carry, distance=distance, rank=rank, beam=beam):
                at = pl.multiple_of(rank * context + index * PAGE, PAGE)
                stage[distance, pl.ds(at, PAGE), :] = pool_v[table_ref[beam, index]]
                return carry

            lax.fori_loop(0, context // PAGE, put, 0)
            span = pl.ds(rank * context, context)
            if distance == 0:
                copy = pltpu.make_async_copy(stage.at[0, span], recv_ref.at[0, span], own_sem.at[rank])
            else:
                copy = pltpu.make_async_remote_copy(
                    src_ref=stage.at[distance, span], dst_ref=recv_ref.at[distance, span],
                    send_sem=bs_sem.at[distance * MOST + rank], recv_sem=br_sem.at[distance * MOST + rank],
                    device_id={"dp": peer(SPAN - distance)}, device_id_type=MESH,
                )
            copy.start()
            copies.append(copy)
    for copy in copies:
        copy.wait()


def finish_kernel(recv_ref, raw_ref, new_hbm, len_hbm, par_hbm, proj_ref, cache_ref, new_ref, len_ref, par_ref, edge, zeros, in_sem, out_sem):
    me = lax.axis_index("dp")
    pages = recv_ref.shape[1] // PAGE
    operands = ((par_hbm, par_ref), (len_hbm, len_ref), (new_hbm, new_ref))
    in_copies = [pltpu.make_async_copy(source, target, in_sem.at[at]) for at, (source, target) in enumerate(operands)]
    for copy in in_copies:
        copy.start()
    zeros[...] = jnp.zeros_like(zeros)
    for copy in in_copies:
        copy.wait()
    slots, owners = slots_of_children(par_ref, me)
    fresh = [new_ref[step].astype(jnp.float32) for step in range(STEPS)]
    for child in range(BEAMS):
        slot = slots[child]
        length = len_ref[owners[child]]
        first = length // PAGE
        last = (length + STEPS - 1) // PAGE

        def whole(index, carry, child=child, slot=slot):
            span = pl.ds(pl.multiple_of(index * PAGE, PAGE), PAGE)
            pltpu.make_async_copy(recv_ref.at[slot, span], cache_ref.at[child, span], out_sem).start()
            return carry

        def clear(index, carry, child=child):
            span = pl.ds(pl.multiple_of(index * PAGE, PAGE), PAGE)
            pltpu.make_async_copy(zeros, cache_ref.at[child, span], out_sem).start()
            return carry

        def fix(index, carry, child=child, slot=slot, length=length, first=first):
            at = pl.multiple_of(index * PAGE, PAGE)
            position = at + lax.broadcasted_iota(jnp.int32, (PAGE, 2 * HD), 0)
            page = recv_ref[slot, pl.ds(at, PAGE), :].astype(jnp.float32)
            page = jnp.where(position < length, page, 0.0)
            for step in range(STEPS):
                page = jnp.where(position == length + step, fresh[step][child:child + 1], page)
            edge[child * 2 + index - first] = page.astype(jnp.bfloat16)
            pltpu.make_async_copy(edge.at[child * 2 + index - first], cache_ref.at[child, pl.ds(at, PAGE)], out_sem).start()
            return carry

        lax.fori_loop(0, first, whole, 0)
        lax.fori_loop(last + 1, pages, clear, 0)
        lax.fori_loop(first, last + 1, fix, 0)

    rows = MOST * STEPS
    raw = []
    for distance in range(SPAN):
        part = raw_ref[distance].astype(jnp.float32)
        raw.append(jnp.concatenate([part[:rows], part[rows:]], axis=1))
    raw = jnp.concatenate(raw, axis=0).astype(jnp.bfloat16)
    row = lax.broadcasted_iota(jnp.int32, (BEAMS, SPAN * rows), 0)
    col = lax.broadcasted_iota(jnp.int32, (BEAMS, SPAN * rows), 1)
    slot_at = jnp.zeros_like(col)
    for child in range(BEAMS):
        slot_at = jnp.where(row == child, slots[child], slot_at)
    for step in range(STEPS):
        pick = jnp.where(col == slot_at * STEPS + step, 1.0, 0.0).astype(jnp.bfloat16)
        proj_ref[step] = jnp.dot(pick, raw, preferred_element_type=jnp.float32).astype(jnp.bfloat16)
    pltpu.make_async_copy(recv_ref, cache_ref, out_sem).wait()


def left_kernel(count, left_ref, got_ref, send_sem, recv_sem):
    me = lax.axis_index("dp")
    y = lax.rem(me, SPAN)
    targets = [me - y + lax.rem(y + ahead, SPAN) for ahead in (1, SPAN - 1)]
    barrier = pltpu.get_barrier_semaphore()
    for target in targets:
        pl.semaphore_signal(barrier, inc=1, device_id={"dp": target}, device_id_type=MESH)
    pl.semaphore_wait(barrier, 2)
    copies = []
    for side, target in enumerate(targets):
        copy = pltpu.make_async_remote_copy(
            src_ref=left_ref.at[side, pl.ds(0, count)], dst_ref=got_ref.at[side, pl.ds(0, count)],
            send_sem=send_sem.at[side], recv_sem=recv_sem.at[side],
            device_id={"dp": target}, device_id_type=MESH,
        )
        copy.start()
        copies.append(copy)
    for copy in copies:
        copy.wait()


def place_kernel(with_left, recv_ref, raw_ref, new_ref, meta_ref, *refs):
    left_ref = refs[0] if with_left else None
    proj_hbm, cache_ref, edge, zeros, proj_ref, out_sem, proj_sem = refs[-7:]
    total = recv_ref.shape[0]
    zeros[...] = jnp.zeros_like(zeros)
    fresh = [new_ref[step].astype(jnp.float32) for step in range(STEPS)]
    slots = [meta_ref[child * META + 6] for child in range(BEAMS)]
    per_child = cache_ref.shape[1]
    scale = GRAIN // TILE
    for child in range(BEAMS):
        length, start, split, again, until, third = (meta_ref[child * META + at] for at in range(6))
        first = length // TILE
        last = (length + STEPS - 1) // TILE
        until = jnp.minimum(until * scale, first) if with_left else first
        split = jnp.minimum(split * scale, until)

        def move(source, source_at, at, count, child=child):
            @pl.when(count > 0)
            def _():
                pltpu.make_async_copy(
                    source.at[pl.ds(source_at, count)], cache_ref.at[child, pl.ds(at, count)], out_sem
                ).start()

        move(recv_ref, start * scale, 0, split)
        move(recv_ref, again * scale, split, until - split)
        if with_left:
            move(left_ref, third * scale, until, first - until)
        move(zeros, 0, last + 1, per_child - 1 - last)
    for child in range(BEAMS):
        length, start, split, again, until, third = (meta_ref[child * META + at] for at in range(6))
        first = length // TILE
        last = (length + STEPS - 1) // TILE

        def fix(
            index, carry, child=child, length=length, first=first, start=start * scale, split=split * scale,
            again=again * scale, until=until * scale, third=third * scale,
        ):
            position = index * TILE + lax.broadcasted_iota(jnp.int32, (TILE, 2 * HD), 0)
            at = jnp.minimum(jnp.where(index < split, start + index, again + index - split), total - 1)
            part = recv_ref[at].astype(jnp.float32)
            if with_left:
                at = jnp.minimum(jnp.maximum(third + index - until, 0), left_ref.shape[0] - 1)
                part = jnp.where(index < until, part, left_ref[at].astype(jnp.float32))
            part = jnp.where(position < length, part, 0.0)
            for step in range(STEPS):
                part = jnp.where(position == length + step, fresh[step][child:child + 1], part)
            edge[child * 2 + index - first] = part.astype(jnp.bfloat16)
            pltpu.make_async_copy(edge.at[child * 2 + index - first], cache_ref.at[child, index], out_sem).start()
            return carry

        lax.fori_loop(first, last + 1, fix, 0)

    rows = MOST * STEPS
    raw = []
    for distance in range(SPAN):
        part = raw_ref[distance].astype(jnp.float32)
        raw.append(jnp.concatenate([part[:rows], part[rows:]], axis=1))
    raw = jnp.concatenate(raw, axis=0).astype(jnp.bfloat16)
    row = lax.broadcasted_iota(jnp.int32, (BEAMS, SPAN * rows), 0)
    col = lax.broadcasted_iota(jnp.int32, (BEAMS, SPAN * rows), 1)
    slot_at = jnp.zeros_like(col)
    for child in range(BEAMS):
        slot_at = jnp.where(row == child, slots[child], slot_at)
    for step in range(STEPS):
        pick = jnp.where(col == slot_at * STEPS + step, 1.0, 0.0).astype(jnp.bfloat16)
        proj_ref[step] = jnp.dot(pick, raw, preferred_element_type=jnp.float32).astype(jnp.bfloat16)
    proj_copy = pltpu.make_async_copy(proj_ref, proj_hbm, proj_sem)
    proj_copy.start()
    pltpu.make_async_copy(cache_ref, cache_ref, out_sem).wait()
    proj_copy.wait()


def local(shards, queries, new_kv, kv_pool, page_tables, lengths, parents, out_weight):
    wide = queries.shape[2]
    channels = kv_pool.shape[2]
    context = page_tables.shape[1] * kv_pool.shape[1]
    rows = MOST * STEPS
    vmem = pl.BlockSpec(memory_space=pltpu.VMEM)
    smem = pl.BlockSpec(memory_space=pltpu.SMEM)
    hbm = pl.BlockSpec(memory_space=pltpu.HBM)
    free = pl.BlockSpec(memory_space=pl.ANY)
    dma = pltpu.SemaphoreType.DMA
    bf16 = jnp.bfloat16

    def pinned(*operands):
        return [pltpu.with_memory_space_constraint(operand, pltpu.HBM) for operand in operands]

    grain_pool = kv_pool.reshape(-1, GRAIN, channels)
    with jax.named_scope("exchange"):
        recv, raw, left, meta, over = pl.pallas_call(
            exchange_kernel,
            out_shape=(
                jax.ShapeDtypeStruct((2 * LINK + MOST * PER_CHILD, GRAIN, channels), bf16),
                jax.ShapeDtypeStruct((SPAN, 2 * rows, wide // 2), bf16),
                jax.ShapeDtypeStruct((2, LEFT, GRAIN, channels), bf16),
                jax.ShapeDtypeStruct((BEAMS * META,), jnp.int32),
                jax.ShapeDtypeStruct((1,), jnp.int32),
            ),
            in_specs=[hbm] * 7,
            out_specs=(free, free, free, smem, smem),
            scratch_shapes=[
                pltpu.VMEM(queries.shape, bf16),
                pltpu.VMEM(new_kv.shape, bf16),
                pltpu.SMEM(page_tables.shape, jnp.int32),
                pltpu.SMEM(lengths.shape, jnp.int32),
                pltpu.SMEM(parents.shape, jnp.int32),
                pltpu.VMEM((1, *lengths.shape), jnp.int32),
                pltpu.VMEM((1, *parents.shape), jnp.int32),
                pltpu.VMEM(grain_pool.shape, bf16),
                pltpu.VMEM((shards, out_weight.shape[0], wide), bf16),
                pltpu.VMEM((SPAN, MOST * PER_CHILD, GRAIN, channels), bf16),
                pltpu.VMEM((2, FIRST, GRAIN, channels), bf16),
                pltpu.VMEM((2, FIRST, GRAIN, channels), bf16),
                pltpu.VMEM((2, REST, GRAIN, channels), bf16),
                pltpu.VMEM((2, LEFT, GRAIN, channels), bf16),
                pltpu.VMEM((SPAN, 2 * rows, (wide + channels) // 2), bf16),
                pltpu.VMEM((SPAN, 2 * rows, (wide + channels) // 2), bf16),
                pltpu.VMEM((SPAN * rows, wide), jnp.float32),
                pltpu.VMEM((shards, SPAN * rows, wide), bf16),
                pltpu.VMEM((shards, SPAN * rows, wide), bf16),
                pltpu.VMEM((SPAN, 2 * rows, wide // 2), bf16),
                pltpu.SMEM((SPAN * MOST,), jnp.int32),
                pltpu.SMEM((SPAN * MOST,), jnp.int32),
                dma((7,)), dma, dma((shards,)), dma((2,)), dma((3,)),
                dma((SPAN,)), dma((SPAN,)),
                dma((8,)), dma((8,)),
                dma((shards,)), dma((shards,)),
                dma((SPAN,)), dma((SPAN,)),
                pltpu.SemaphoreType.REGULAR,
            ],
            compiler_params=pltpu.CompilerParams(
                collective_id=0, has_side_effects=True, vmem_limit_bytes=48 * 1024 * 1024
            ),
            name="exchange",
        )(*pinned(queries, new_kv, grain_pool, page_tables, lengths, parents, out_weight))

    def place(*got):
        with jax.named_scope("place"):
            projected, cache = pl.pallas_call(
                functools.partial(place_kernel, len(got) > 0),
                out_shape=(
                    jax.ShapeDtypeStruct(queries.shape, bf16),
                    jax.ShapeDtypeStruct((BEAMS, context // TILE, TILE, channels), bf16),
                ),
                in_specs=[vmem, vmem, vmem, smem] + [vmem] * len(got),
                out_specs=(free, free),
                scratch_shapes=[
                    pltpu.VMEM((2 * BEAMS, TILE, channels), bf16),
                    pltpu.VMEM((context // TILE, TILE, channels), bf16),
                    pltpu.VMEM(queries.shape, bf16),
                    dma, dma,
                ],
                compiler_params=pltpu.CompilerParams(vmem_limit_bytes=24 * 1024 * 1024),
                name="place_left" if got else "place",
            )(recv.reshape(-1, TILE, channels), raw, new_kv, meta, *got)
            return projected, cache.reshape(BEAMS, context, channels)

    def placed():
        return place()

    def topped(count, number):
        with jax.named_scope("left"):
            got = pl.pallas_call(
                functools.partial(left_kernel, count),
                out_shape=jax.ShapeDtypeStruct(left.shape, bf16),
                in_specs=[free],
                out_specs=free,
                scratch_shapes=[dma((2,)), dma((2,))],
                compiler_params=pltpu.CompilerParams(
                    collective_id=number, has_side_effects=True, vmem_limit_bytes=4 * 1024 * 1024
                ),
                name="left",
            )(left)
        return place(got.reshape(-1, TILE, channels))

    def resent():
        with jax.named_scope("full"):
            whole = pl.pallas_call(
                full_kernel,
                out_shape=jax.ShapeDtypeStruct((SPAN, MOST * context, channels), bf16),
                in_specs=[hbm] * 3,
                out_specs=free,
                scratch_shapes=[
                    pltpu.SMEM(page_tables.shape, jnp.int32),
                    pltpu.SMEM(parents.shape, jnp.int32),
                    pltpu.VMEM(kv_pool.shape, bf16),
                    pltpu.VMEM((SPAN, MOST * context, channels), bf16),
                    dma((2,)), dma, dma((MOST,)),
                    dma((SPAN * MOST,)), dma((SPAN * MOST,)),
                ],
                compiler_params=pltpu.CompilerParams(
                    collective_id=1, has_side_effects=True, vmem_limit_bytes=24 * 1024 * 1024
                ),
                name="full",
            )(*pinned(kv_pool, page_tables, parents))
        with jax.named_scope("finish"):
            return pl.pallas_call(
                finish_kernel,
                out_shape=(
                    jax.ShapeDtypeStruct(queries.shape, bf16),
                    jax.ShapeDtypeStruct((BEAMS, context, channels), bf16),
                ),
                in_specs=[vmem, vmem, hbm, hbm, hbm],
                out_specs=(vmem, hbm),
                scratch_shapes=[
                    pltpu.VMEM(new_kv.shape, bf16),
                    pltpu.SMEM(lengths.shape, jnp.int32),
                    pltpu.SMEM(parents.shape, jnp.int32),
                    pltpu.VMEM((2 * BEAMS, PAGE, channels), bf16),
                    pltpu.VMEM((PAGE, channels), bf16),
                    dma((3,)), dma,
                ],
                compiler_params=pltpu.CompilerParams(vmem_limit_bytes=24 * 1024 * 1024),
                name="finish",
            )(whole.reshape(BEAMS, context, channels), raw, new_kv, lengths, parents)

    topping = [functools.partial(topped, count, 2 + at) for at, count in enumerate(TIERS)]
    return lax.switch(over[0], [placed, *topping, resent])


def solution(mesh):
    in_specs = (
        P(None, "dp", "tensor"),
        P(None, "dp", "tensor"),
        P("dp", None, "tensor"),
        P("dp", None),
        P(),
        P(),
        P("tensor", None),
    )
    out_specs = (P(None, "dp", "tensor"), P("dp", None, "tensor"))
    body = functools.partial(local, mesh.shape["tensor"])
    return jax.shard_map(body, mesh=mesh, in_specs=in_specs, out_specs=out_specs, check_vma=False)
```

```python
import functools

import jax
import jax.numpy as jnp
from jax import lax
from jax.experimental import pallas as pl
from jax.experimental.pallas import tpu as pltpu
from jax.sharding import PartitionSpec as P

HD = 128
SPAN = 4
MOST = 2
BEAMS = 8
STEPS = 4
PAGE = 128
PAGES = 8
GRAIN = 32
PER_CHILD = 32
PER_PAGE = PAGE // GRAIN
TILE = 16
VIA = 36
MORE = 16
REST = 36
TIERS = (4, 10, 24)
LEFT = TIERS[-1]
FIRST = VIA + MORE
LINK = FIRST + REST
META = 7
MESH = pl.DeviceIdType.MESH


def grains(length):
    return (length + (GRAIN - 1)) // GRAIN


def choose(values, index):
    out = values[0]
    for at in range(1, len(values)):
        out = jnp.where(index == at, values[at], out)
    return out


def balanced(up, far, down, keep_up, keep_down):
    least = [jnp.maximum(keep_up[i], far[i] - VIA) for i in range(SPAN)]
    most = [jnp.minimum(far[i] - keep_down[i], VIA) for i in range(SPAN)]
    via_up = [jnp.minimum(jnp.maximum(far[i] >> 1, least[i]), most[i]) for i in range(SPAN)]
    for at in range(SPAN):
        via_down = [far[i] - via_up[i] for i in range(SPAN)]
        nxt, prv = (at + 1) % SPAN, (at - 1) % SPAN
        load_up = jnp.maximum(up[at] + via_up[prv], up[nxt] + via_up[nxt])
        load_down = jnp.maximum(down[at] + via_down[nxt], down[prv] + via_down[prv])
        best = (load_down + far[at] - load_up) >> 1
        via_up[at] = jnp.minimum(jnp.maximum(best, least[at]), most[at])
    via_down = [far[i] - via_up[i] for i in range(SPAN)]
    return via_up, via_down


def planned(flows):
    names = ("up", "down", "far", "first", "second", "cut", "up_id", "down_id", "keep_up", "keep_down")
    plan = {name: [] for name in names}
    for at in range(SPAN):
        u0, u1, gu0, gu1 = flows[at][1]
        f0, f1, gf0, gf1 = flows[at][2]
        d0, d1, gd0, gd1 = flows[at][3]
        gu1 = jnp.where(u0 == u1, 0, gu1)
        gf1 = jnp.where(f0 == f1, 0, gf1)
        gd1 = jnp.where(d0 == d1, 0, gd1)

        def shared(parent, count, one, two):
            return jnp.where((parent == one) | (parent == two), count, 0)

        straight = shared(f0, gf0, u0, u1) + shared(f1, gf1, d0, d1)
        crossed = shared(f1, gf1, u0, u1) + shared(f0, gf0, d0, d1)
        swap = crossed > straight
        first, second = jnp.where(swap, f1, f0), jnp.where(swap, f0, f1)
        cut, rest = jnp.where(swap, gf1, gf0), jnp.where(swap, gf0, gf1)
        keep_up, keep_down = shared(first, cut, u0, u1), shared(second, rest, d0, d1)
        values = (
            gu0 + gu1 - keep_up, gd0 + gd1 - keep_down, gf0 + gf1, first, second, cut,
            jnp.where(keep_up > 0, first, -1), jnp.where(keep_down > 0, second, -1), keep_up, keep_down,
        )
        for name, value in zip(names, values):
            plan[name].append(value)
    plan["via_up"], plan["via_down"] = balanced(
        plan["up"], plan["far"], plan["down"], plan["keep_up"], plan["keep_down"]
    )
    return plan


def ring_plan(parents, lengths, ring):
    flows = [[None] * SPAN for _ in range(SPAN)]
    for target in range(SPAN):
        owners = [parents[(ring * SPAN + target) * BEAMS + child] for child in range(BEAMS)]
        sources = [(owner >> 3) & (SPAN - 1) for owner in owners]
        for at in range(SPAN):
            if at != target:
                one, two = owners[0], owners[0]
                for child in range(1, BEAMS):
                    two = jnp.where(sources[child] == at, owners[child], two)
                one = owners[BEAMS - 1]
                for child in range(BEAMS - 2, -1, -1):
                    one = jnp.where(sources[child] == at, owners[child], one)
                flows[at][(target - at) % SPAN] = (one, two, grains(lengths[one]), grains(lengths[two]))
    return {**planned(flows), "flows": flows}


def heaviest(parents, lengths, rings):
    beams = rings * SPAN * BEAMS
    counts = grains(lengths).astype(jnp.float32).astype(jnp.bfloat16)
    beam = lax.broadcasted_iota(jnp.int32, (beams, beams), 0)
    chosen = jnp.where(beam == parents, 1.0, 0.0).astype(jnp.bfloat16)
    counts = jnp.dot(jnp.broadcast_to(counts, (16, beams)), chosen, preferred_element_type=jnp.float32)[:1]
    lane = lax.broadcasted_iota(jnp.int32, (1, beams), 1)
    source = (parents // BEAMS) % SPAN
    rank = jnp.zeros_like(lane)
    for back in range(1, BEAMS):
        rank = rank + jnp.where((pltpu.roll(source, back, 1) == source) & (lane % BEAMS >= back), 1, 0)
    names = (parents % (SPAN * BEAMS)).astype(jnp.float32)
    rows = [
        jnp.where((source == at) & (rank == order), value, 0.0)
        for value in (names, counts) for at in range(SPAN) for order in range(MOST)
    ]
    rows = jnp.concatenate(rows, axis=0).astype(jnp.bfloat16)
    child = lax.broadcasted_iota(jnp.int32, (beams, 128), 0)
    ring = lax.broadcasted_iota(jnp.int32, (beams, 128), 1)
    flows = [[None] * SPAN for _ in range(SPAN)]
    for target in range(SPAN):
        member = (child // BEAMS % SPAN == target) & (child // (BEAMS * SPAN) == ring)
        member = jnp.where(member, 1.0, 0.0).astype(jnp.bfloat16)
        found = jnp.dot(rows, member, preferred_element_type=jnp.float32).astype(jnp.int32)
        for at in range(SPAN):
            wanted = (at * MOST, at * MOST + 1, (SPAN + at) * MOST, (SPAN + at) * MOST + 1)
            flows[at][(target - at) % SPAN] = tuple(found[one:one + 1] for one in wanted)
    plan = planned(flows)
    out = jnp.zeros_like(plan["far"][0])
    for at in range(SPAN):
        load_up = plan["up"][at] + plan["via_up"][at] + plan["via_up"][(at - 1) % SPAN]
        load_down = plan["down"][at] + plan["via_down"][at] + plan["via_down"][(at + 1) % SPAN]
        out = jnp.maximum(out, jnp.maximum(load_up, load_down))
    return jnp.max(out)


def slots_of_children(parents, me):
    taken = [jnp.int32(0) for _ in range(SPAN)]
    slots, owners = [], []
    for child in range(BEAMS):
        parent = parents[me * BEAMS + child]
        apart = jnp.bitwise_and(parent // BEAMS - me, SPAN - 1)
        slot = jnp.int32(0)
        for distance in range(SPAN):
            hit = apart == distance
            slot = jnp.where(hit, distance * MOST + taken[distance], slot)
            taken[distance] = taken[distance] + hit.astype(jnp.int32)
        slots.append(slot)
        owners.append(parent)
    return slots, owners


def served_beams(parents, me, target):
    count = jnp.int32(0)
    beams = [jnp.int32(0) for _ in range(MOST)]
    for child in range(BEAMS):
        parent = parents[target * BEAMS + child]
        hit = parent // BEAMS == me
        for rank in range(MOST):
            beams[rank] = jnp.where(hit & (count == rank), parent % BEAMS, beams[rank])
        count = count + hit.astype(jnp.int32)
    return beams


def exchange_kernel(
    q_hbm, new_hbm, pool_ref, table_hbm, len_hbm, par_hbm, w_ref,
    recv_ref, proj_ref, left_ref, meta_ref, over_ref,
    q_ref, new_ref, table_ref, len_ref, par_ref, len_row, par_row,
    pool_v, w_v, stage, first_send, first_recv, rest_send, left_send, q_send, q_recv, att, p_send, p_recv, r_send, lens, beams,
    in_sem, pool_sem, w_sem, own_sem, land_sem, qs_sem, qr_sem, bs_sem, br_sem, ps_sem, pr_sem, rs_sem, rr_sem, here_sem,
):
    me = lax.axis_index("dp")
    mine = lax.axis_index("tensor")
    shards = lax.axis_size("tensor")
    y = lax.rem(me, SPAN)
    base = me - y
    context = stage.shape[1] * GRAIN // MOST
    rings = lax.axis_size("dp") // SPAN
    wide = q_hbm.shape[2]
    heads = wide // HD
    rows = MOST * STEPS

    def peer(distance):
        return base + lax.rem(y + distance, SPAN)

    pairs = (
        (par_hbm, par_ref), (len_hbm, len_ref), (table_hbm, table_ref), (q_hbm, q_ref), (new_hbm, new_ref),
        (par_hbm, par_row.at[0]), (len_hbm, len_row.at[0]),
    )
    in_copies = [pltpu.make_async_copy(source, target, in_sem.at[at]) for at, (source, target) in enumerate(pairs)]
    pool_copy = pltpu.make_async_copy(pool_ref, pool_v, pool_sem)
    for copy in (*in_copies[:3], pool_copy, *in_copies[3:]):
        copy.start()
    barrier = pltpu.get_barrier_semaphore()
    for distance in range(1, SPAN):
        pl.semaphore_signal(barrier, inc=1, device_id={"dp": peer(distance)}, device_id_type=MESH)
    for other in range(1, shards):
        @pl.when(mine + other < shards)
        def _(other=other):
            pl.semaphore_signal(barrier, inc=1, device_id={"tensor": mine + other}, device_id_type=MESH)
    for copy in in_copies[:3]:
        copy.wait()

    plan = ring_plan(par_ref, len_ref, me >> 2)
    via_up, via_down = plan["via_up"], plan["via_down"]
    flows = {}
    for ahead in (1, 3):
        first, second, cut = (choose([plan["flows"][at][ahead][of] for at in range(SPAN)], y) for of in range(3))
        flows[ahead] = (first & 7, second & 7, cut)
    for ahead, kept in ((1, "up_id"), (3, "down_id")):
        first, second, cut = flows[ahead]
        flows[ahead] = (first, second, jnp.where(me * BEAMS + first == choose(plan[kept], y), 0, cut))
    flows[2] = (choose(plan["first"], y) & 7, choose(plan["second"], y) & 7, choose(plan["cut"], y))

    def grain_at(flow, number):
        first, second, cut = flow
        later = number >= cut
        number = jnp.where(later, number - cut, number)
        number = jnp.minimum(jnp.maximum(number, 0), PER_CHILD - 1)
        return table_ref[jnp.where(later, second, first), number >> 2] * PER_PAGE + (number & (PER_PAGE - 1))

    sides = (
        (flows[1], choose(via_up, y), jnp.int32(0), choose(via_up, (y - 1) & 3), peer(1)),
        (flows[3], choose(via_down, y), choose(via_up, y), choose(via_down, (y + 1) & 3), peer(3)),
    )
    pl.semaphore_wait(barrier, SPAN - 1 + mine)
    pool_copy.wait()
    b_copies = []
    cuts = (0, 12, VIA, FIRST)

    def send_part(part):
        for side, (flow, mine_via, skip, _, target) in enumerate(sides):
            def put(at, carry, side=side, flow=flow, mine_via=mine_via, skip=skip):
                for at in [4 * at + more for more in range(4)]:
                    far = at < mine_via
                    chosen = tuple(jnp.where(far, one, two) for one, two in zip(flows[2], flow))
                    number = jnp.where(far, skip + at, at - mine_via)
                    first_send[side, at] = pool_v[grain_at(chosen, number)]
                return carry

            lax.fori_loop(cuts[part] // 4, cuts[part + 1] // 4, put, 0)
            span = pl.ds(cuts[part], cuts[part + 1] - cuts[part])
            copy = pltpu.make_async_remote_copy(
                src_ref=first_send.at[side, span], dst_ref=first_recv.at[side, span],
                send_sem=bs_sem.at[side * 4 + part], recv_sem=br_sem.at[side * 4 + part],
                device_id={"dp": target}, device_id_type=MESH,
            )
            copy.start()
            b_copies.append(copy)

    send_part(0)
    for other in range(1, shards):
        @pl.when(mine >= other)
        def _(other=other):
            pl.semaphore_signal(here_sem, inc=1, device_id={"tensor": mine - other}, device_id_type=MESH)
    slots, owners = slots_of_children(par_ref, me)
    for copy in in_copies[3:5]:
        copy.wait()
    row = lax.broadcasted_iota(jnp.int32, (SPAN * rows, BEAMS), 0)
    col = lax.broadcasted_iota(jnp.int32, (SPAN * rows, BEAMS), 1)
    slot_at = jnp.zeros_like(col)
    for child in range(BEAMS):
        slot_at = jnp.where(col == child, slots[child], slot_at)
    q_sorted = jnp.zeros((SPAN * rows, wide), jnp.float32)
    new_sorted = jnp.zeros((SPAN * rows, 2 * HD), jnp.float32)
    for step in range(STEPS):
        pick = jnp.where((row // STEPS == slot_at) & (row % STEPS == step), 1.0, 0.0).astype(jnp.bfloat16)
        q_sorted += jnp.dot(pick, q_ref[step], preferred_element_type=jnp.float32)
        new_sorted += jnp.dot(pick, new_ref[step], preferred_element_type=jnp.float32)
    both = jnp.concatenate([q_sorted, new_sorted], axis=1)
    half = both.shape[1] // 2
    for distance in range(SPAN):
        part = both[distance * rows:(distance + 1) * rows]
        part = jnp.concatenate([part[:, :half], part[:, half:]], axis=0).astype(jnp.bfloat16)
        if distance == 0:
            q_recv[0] = part
        else:
            q_send[distance] = part
    q_copies = []
    for distance in range(1, SPAN):
        copy = pltpu.make_async_remote_copy(
            src_ref=q_send.at[distance], dst_ref=q_recv.at[distance],
            send_sem=qs_sem.at[distance], recv_sem=qr_sem.at[distance],
            device_id={"dp": peer(distance)}, device_id_type=MESH,
        )
        copy.start()
        q_copies.append(copy)
    send_part(1)
    send_part(2)
    for ahead in range(SPAN):
        served = served_beams(par_ref, me, peer(ahead))
        for rank in range(MOST):
            at = (SPAN - ahead) % SPAN * MOST + rank
            beams[at] = served[rank]
            lens[at] = len_ref[me * BEAMS + served[rank]]
    w_copies = []
    for block in range(shards):
        copy = pltpu.make_async_copy(w_ref.at[:, pl.ds(block * wide, wide)], w_v.at[block], w_sem.at[block])
        copy.start()
        w_copies.append(copy)

    def put_all(index, carry):
        slot = index // PAGES
        page = table_ref[beams[slot], index % PAGES]
        at = (index % (MOST * PAGES)) * PER_PAGE
        stage[index // (MOST * PAGES), pl.ds(at, PER_PAGE)] = pool_v[pl.ds(page * PER_PAGE, PER_PAGE)]
        return carry

    lax.fori_loop(0, SPAN * MOST * PAGES, put_all, 0)
    own_copy = pltpu.make_async_copy(stage.at[0], recv_ref.at[pl.ds(2 * LINK, MOST * PER_CHILD)], own_sem.at[0])
    own_copy.start()

    for copy in q_copies:
        copy.wait()

    def attend(distance):
        message = q_recv[distance].astype(jnp.float32)
        message = jnp.concatenate([message[:rows], message[rows:]], axis=1)
        q_rows = jnp.concatenate([message[:, h * HD:(h + 1) * HD] for h in range(heads)], axis=0).astype(jnp.bfloat16)
        fresh = message[:, wide:].astype(jnp.bfloat16)
        old_len = lens[distance * MOST]
        last_len = lens[distance * MOST + 1]
        contract = (((1,), (1,)), ((), ()))
        scale = HD ** -0.5
        half = MOST * PER_CHILD // 2
        keys = [stage[distance, pl.ds(rank * half, half), :, 0:HD].reshape(context, HD) for rank in range(MOST)]
        scores = [lax.dot_general(q_rows, key, contract, preferred_element_type=jnp.float32) for key in keys]
        rank_at = lax.broadcasted_iota(jnp.int32, scores[0].shape, 0) // STEPS % MOST
        scores = jnp.where(rank_at == 0, scores[0], scores[1]) * scale
        fresh_scores = lax.dot_general(q_rows, fresh[:, :HD], contract, preferred_element_type=jnp.float32) * scale
        position = lax.broadcasted_iota(jnp.int32, scores.shape, 1)
        limit = jnp.where(rank_at == 0, old_len, last_len)
        scores = jnp.where(position < limit, scores, -1e30)
        f_row = lax.broadcasted_iota(jnp.int32, fresh_scores.shape, 0)
        f_col = lax.broadcasted_iota(jnp.int32, fresh_scores.shape, 1)
        seen = (f_row // STEPS % MOST == f_col // STEPS) & (f_col % STEPS <= f_row % STEPS)
        fresh_scores = jnp.where(seen, fresh_scores, -1e30)
        top = jnp.maximum(jnp.max(scores, axis=1, keepdims=True), jnp.max(fresh_scores, axis=1, keepdims=True))
        exp_old = jnp.exp(scores - top)
        exp_new = jnp.exp(fresh_scores - top)
        total = jnp.sum(exp_old, axis=1, keepdims=True) + jnp.sum(exp_new, axis=1, keepdims=True)
        share = 1.0 / total
        w_old = (exp_old * share).astype(jnp.bfloat16)
        w_new = (exp_new * share).astype(jnp.bfloat16)
        values = [stage[distance, pl.ds(rank * half, half), :, HD:2 * HD].reshape(context, HD) for rank in range(MOST)]
        out = [jnp.dot(w_old, value, preferred_element_type=jnp.float32) for value in values]
        out = jnp.where(rank_at[:, :HD] == 0, out[0], out[1])
        out += jnp.dot(w_new, fresh[:, HD:], preferred_element_type=jnp.float32)
        out = jnp.concatenate([out[h * rows:(h + 1) * rows] for h in range(heads)], axis=1)
        att[pl.ds(pl.multiple_of(distance * rows, rows), rows), :] = out

    def attend_two(at, carry):
        attend(2 * at)
        attend(2 * at + 1)
        return carry

    lax.fori_loop(0, SPAN // 2, attend_two, 0)
    for copy in b_copies[:4]:
        copy.wait()
    more_copies = b_copies[4:]
    b_copies = []
    for side, (flow, mine_via, _, passed, target) in enumerate(sides):
        def put_passed(at, carry, side=side, flow=flow, mine_via=mine_via, passed=passed):
            for at in [4 * at + more for more in range(4)]:
                here = pool_v[grain_at(flow, FIRST - mine_via + at - passed)]
                rest_send[side, at] = jnp.where(at < passed, first_recv[side, at], here)
            return carry

        lax.fori_loop(0, REST // 4, put_passed, 0)
        copy = pltpu.make_async_remote_copy(
            src_ref=rest_send.at[side], dst_ref=recv_ref.at[pl.ds(side * LINK + FIRST, REST)],
            send_sem=bs_sem.at[side * 4 + 3], recv_sem=br_sem.at[side * 4 + 3],
            device_id={"dp": target}, device_id_type=MESH,
        )
        copy.start()
        b_copies.append(copy)
    attended = att[...].astype(jnp.bfloat16)
    for copy in w_copies:
        copy.wait()

    def p_copy(other):
        return pltpu.make_async_remote_copy(
            src_ref=p_send.at[other], dst_ref=p_recv.at[other],
            send_sem=ps_sem.at[other], recv_sem=pr_sem.at[other],
            device_id={"tensor": lax.rem(mine + other, shards)}, device_id_type=MESH,
        )

    def project(other, carry):
        product = jnp.dot(attended, w_v[lax.rem(mine + other, shards)], preferred_element_type=jnp.float32)
        p_send[other] = product.astype(jnp.bfloat16)
        p_copy(other).start()
        return carry

    @pl.when(mine < shards - 1)
    def _():
        pl.semaphore_wait(here_sem, shards - 1 - mine)

    lax.fori_loop(1, shards, project, 0)
    own = jnp.dot(attended, w_v[mine], preferred_element_type=jnp.float32)

    for copy in more_copies:
        copy.wait()
    for side in range(2):
        copy = pltpu.make_async_copy(first_recv.at[side], recv_ref.at[pl.ds(side * LINK, FIRST)], land_sem.at[side])
        copy.start()
        b_copies.append(copy)

    def gather_sums(other, total):
        p_copy(other).wait()
        return total + p_recv[other].astype(jnp.float32)

    summed = lax.fori_loop(1, shards, gather_sums, own)
    half = wide // 2
    r_copies = []
    for distance in range(SPAN):
        part = summed[distance * rows:(distance + 1) * rows]
        r_send[distance] = jnp.concatenate([part[:, :half], part[:, half:]], axis=0).astype(jnp.bfloat16)
        if distance == 0:
            copy = pltpu.make_async_copy(r_send.at[0], proj_ref.at[0], own_sem.at[1])
        else:
            copy = pltpu.make_async_remote_copy(
                src_ref=r_send.at[distance], dst_ref=proj_ref.at[distance],
                send_sem=rs_sem.at[distance], recv_sem=rr_sem.at[distance],
                device_id={"dp": peer(SPAN - distance)}, device_id_type=MESH,
            )
        copy.start()
        r_copies.append(copy)
    for copy in in_copies[5:]:
        copy.wait()
    load = heaviest(par_row[...], len_row[...], rings)
    over_ref[0] = sum(jnp.where(load > limit, 1, 0) for limit in (LINK, *(LINK + count for count in TIERS)))
    for side, (flow, mine_via, _, passed, _) in enumerate(sides):
        def put_left(at, carry, side=side, flow=flow, mine_via=mine_via, passed=passed):
            for at in [4 * at + more for more in range(4)]:
                left_send[side, at] = pool_v[grain_at(flow, LINK - mine_via - passed + at)]
            return carry

        lax.fori_loop(0, LEFT // 4, put_left, 0)
    left_copy = pltpu.make_async_copy(left_send, left_ref, land_sem.at[2])
    left_copy.start()
    for child in range(BEAMS):
        slot = slots[child]
        distance = slot >> 1
        length = len_ref[owners[child]]
        kept = jnp.where(distance == 3, choose(plan["up_id"], (y - 1) & 3), choose(plan["down_id"], (y + 1) & 3))
        before = jnp.int32(0)
        for other in range(BEAMS):
            if other != child:
                mate = (slots[other] >> 1 == distance) & (slots[other] < slot)
                counts = (owners[other] != owners[child]) & (owners[other] != kept)
                before = jnp.where(mate & counts, grains(len_ref[owners[other]]), before)
        far_before = jnp.where(owners[child] == choose(plan["first"], (y + 2) & 3), 0, choose(plan["cut"], (y + 2) & 3))
        before = jnp.where(distance == 2, far_before, before)
        from_up = choose(via_up, (y - 1) & 3), choose(via_up, (y + 2) & 3)
        from_down = choose(via_down, (y + 1) & 3), choose(via_down, (y + 2) & 3)
        near_via = jnp.where(distance == 3, from_up[0], from_down[0])
        near_pass = jnp.where(distance == 3, from_up[1], from_down[1])
        near_base = jnp.where(distance == 3, 0, LINK)
        split = jnp.where(distance == 2, from_up[1], FIRST - near_via) - before
        split = jnp.minimum(jnp.maximum(split, 0), PER_CHILD)
        start = jnp.where(distance == 2, FIRST + before, near_base + near_via + before)
        again = jnp.where(distance == 2, LINK + FIRST + before + split - from_up[1], start + split + near_pass)
        near = (distance == 1) | (distance == 3)
        until = LINK - near_via - near_pass - before
        until = jnp.where(near, jnp.minimum(jnp.maximum(until, 0), PER_CHILD), PER_CHILD)
        third = jnp.where(distance == 3, 0, LEFT) + near_via + near_pass + before + until - LINK
        held = near & (owners[child] == kept)
        kept_down = LINK + choose(via_down, (y + 1) & 3) - choose(plan["keep_down"], (y + 1) & 3)
        start = jnp.where(held, jnp.where(distance == 3, 0, kept_down), start)
        split = jnp.where(held, PER_CHILD, split)
        again = jnp.where(held, 0, again)
        until = jnp.where(held, PER_CHILD, until)
        third = jnp.where(held, 0, third)
        stays = distance == 0
        meta_ref[child * META] = length
        meta_ref[child * META + 1] = jnp.where(stays, 2 * LINK + (slot & 1) * PER_CHILD, start)
        meta_ref[child * META + 2] = jnp.where(stays, PER_CHILD, split)
        meta_ref[child * META + 3] = jnp.where(stays, 0, again)
        meta_ref[child * META + 4] = until
        meta_ref[child * META + 5] = jnp.where(near, third, 0)
        meta_ref[child * META + 6] = slot
    for copy in r_copies:
        copy.wait()
    for copy in b_copies:
        copy.wait()
    own_copy.wait()
    left_copy.wait()


def full_kernel(
    pool_ref, table_hbm, par_hbm, recv_ref,
    table_ref, par_ref, pool_v, stage,
    in_sem, pool_sem, own_sem, bs_sem, br_sem,
):
    me = lax.axis_index("dp")
    y = lax.rem(me, SPAN)
    base = me - y
    context = stage.shape[1] // MOST

    def peer(distance):
        return base + lax.rem(y + distance, SPAN)

    barrier = pltpu.get_barrier_semaphore()
    for distance in range(1, SPAN):
        pl.semaphore_signal(barrier, inc=1, device_id={"dp": peer(distance)}, device_id_type=MESH)
    in_copies = []
    for at, (source, target) in enumerate(((par_hbm, par_ref), (table_hbm, table_ref))):
        copy = pltpu.make_async_copy(source, target, in_sem.at[at])
        copy.start()
        in_copies.append(copy)
    pool_copy = pltpu.make_async_copy(pool_ref, pool_v, pool_sem)
    pool_copy.start()
    for copy in in_copies:
        copy.wait()
    pl.semaphore_wait(barrier, SPAN - 1)
    pool_copy.wait()
    copies = []
    for distance in (2, 1, 3, 0):
        served = served_beams(par_ref, me, peer(SPAN - distance))
        for rank in range(MOST):
            beam = served[rank]

            def put(index, carry, distance=distance, rank=rank, beam=beam):
                at = pl.multiple_of(rank * context + index * PAGE, PAGE)
                stage[distance, pl.ds(at, PAGE), :] = pool_v[table_ref[beam, index]]
                return carry

            lax.fori_loop(0, context // PAGE, put, 0)
            span = pl.ds(rank * context, context)
            if distance == 0:
                copy = pltpu.make_async_copy(stage.at[0, span], recv_ref.at[0, span], own_sem.at[rank])
            else:
                copy = pltpu.make_async_remote_copy(
                    src_ref=stage.at[distance, span], dst_ref=recv_ref.at[distance, span],
                    send_sem=bs_sem.at[distance * MOST + rank], recv_sem=br_sem.at[distance * MOST + rank],
                    device_id={"dp": peer(SPAN - distance)}, device_id_type=MESH,
                )
            copy.start()
            copies.append(copy)
    for copy in copies:
        copy.wait()


def finish_kernel(recv_ref, raw_ref, new_hbm, len_hbm, par_hbm, proj_ref, cache_ref, new_ref, len_ref, par_ref, edge, zeros, in_sem, out_sem):
    me = lax.axis_index("dp")
    pages = recv_ref.shape[1] // PAGE
    operands = ((par_hbm, par_ref), (len_hbm, len_ref), (new_hbm, new_ref))
    in_copies = [pltpu.make_async_copy(source, target, in_sem.at[at]) for at, (source, target) in enumerate(operands)]
    for copy in in_copies:
        copy.start()
    zeros[...] = jnp.zeros_like(zeros)
    for copy in in_copies:
        copy.wait()
    slots, owners = slots_of_children(par_ref, me)
    fresh = [new_ref[step].astype(jnp.float32) for step in range(STEPS)]
    for child in range(BEAMS):
        slot = slots[child]
        length = len_ref[owners[child]]
        first = length // PAGE
        last = (length + STEPS - 1) // PAGE

        def whole(index, carry, child=child, slot=slot):
            span = pl.ds(pl.multiple_of(index * PAGE, PAGE), PAGE)
            pltpu.make_async_copy(recv_ref.at[slot, span], cache_ref.at[child, span], out_sem).start()
            return carry

        def clear(index, carry, child=child):
            span = pl.ds(pl.multiple_of(index * PAGE, PAGE), PAGE)
            pltpu.make_async_copy(zeros, cache_ref.at[child, span], out_sem).start()
            return carry

        def fix(index, carry, child=child, slot=slot, length=length, first=first):
            at = pl.multiple_of(index * PAGE, PAGE)
            position = at + lax.broadcasted_iota(jnp.int32, (PAGE, 2 * HD), 0)
            page = recv_ref[slot, pl.ds(at, PAGE), :].astype(jnp.float32)
            page = jnp.where(position < length, page, 0.0)
            for step in range(STEPS):
                page = jnp.where(position == length + step, fresh[step][child:child + 1], page)
            edge[child * 2 + index - first] = page.astype(jnp.bfloat16)
            pltpu.make_async_copy(edge.at[child * 2 + index - first], cache_ref.at[child, pl.ds(at, PAGE)], out_sem).start()
            return carry

        lax.fori_loop(0, first, whole, 0)
        lax.fori_loop(last + 1, pages, clear, 0)
        lax.fori_loop(first, last + 1, fix, 0)

    rows = MOST * STEPS
    raw = []
    for distance in range(SPAN):
        part = raw_ref[distance].astype(jnp.float32)
        raw.append(jnp.concatenate([part[:rows], part[rows:]], axis=1))
    raw = jnp.concatenate(raw, axis=0).astype(jnp.bfloat16)
    row = lax.broadcasted_iota(jnp.int32, (BEAMS, SPAN * rows), 0)
    col = lax.broadcasted_iota(jnp.int32, (BEAMS, SPAN * rows), 1)
    slot_at = jnp.zeros_like(col)
    for child in range(BEAMS):
        slot_at = jnp.where(row == child, slots[child], slot_at)
    for step in range(STEPS):
        pick = jnp.where(col == slot_at * STEPS + step, 1.0, 0.0).astype(jnp.bfloat16)
        proj_ref[step] = jnp.dot(pick, raw, preferred_element_type=jnp.float32).astype(jnp.bfloat16)
    pltpu.make_async_copy(recv_ref, cache_ref, out_sem).wait()


def left_kernel(count, left_ref, got_ref, send_sem, recv_sem):
    me = lax.axis_index("dp")
    y = lax.rem(me, SPAN)
    targets = [me - y + lax.rem(y + ahead, SPAN) for ahead in (1, SPAN - 1)]
    barrier = pltpu.get_barrier_semaphore()
    for target in targets:
        pl.semaphore_signal(barrier, inc=1, device_id={"dp": target}, device_id_type=MESH)
    pl.semaphore_wait(barrier, 2)
    copies = []
    for side, target in enumerate(targets):
        copy = pltpu.make_async_remote_copy(
            src_ref=left_ref.at[side, pl.ds(0, count)], dst_ref=got_ref.at[side, pl.ds(0, count)],
            send_sem=send_sem.at[side], recv_sem=recv_sem.at[side],
            device_id={"dp": target}, device_id_type=MESH,
        )
        copy.start()
        copies.append(copy)
    for copy in copies:
        copy.wait()


def place_kernel(with_left, recv_ref, raw_ref, new_ref, meta_ref, *refs):
    left_ref = refs[0] if with_left else None
    proj_hbm, cache_ref, edge, zeros, proj_ref, out_sem, proj_sem = refs[-7:]
    total = recv_ref.shape[0]
    zeros[...] = jnp.zeros_like(zeros)
    fresh = [new_ref[step].astype(jnp.float32) for step in range(STEPS)]
    slots = [meta_ref[child * META + 6] for child in range(BEAMS)]
    per_child = cache_ref.shape[1]
    scale = GRAIN // TILE
    for child in range(BEAMS):
        length, start, split, again, until, third = (meta_ref[child * META + at] for at in range(6))
        first = length // TILE
        last = (length + STEPS - 1) // TILE
        until = jnp.minimum(until * scale, first) if with_left else first
        split = jnp.minimum(split * scale, until)

        def move(source, source_at, at, count, child=child):
            @pl.when(count > 0)
            def _():
                pltpu.make_async_copy(
                    source.at[pl.ds(source_at, count)], cache_ref.at[child, pl.ds(at, count)], out_sem
                ).start()

        move(recv_ref, start * scale, 0, split)
        move(recv_ref, again * scale, split, until - split)
        if with_left:
            move(left_ref, third * scale, until, first - until)
        move(zeros, 0, last + 1, per_child - 1 - last)
    for child in range(BEAMS):
        length, start, split, again, until, third = (meta_ref[child * META + at] for at in range(6))
        first = length // TILE
        last = (length + STEPS - 1) // TILE

        def fix(
            index, carry, child=child, length=length, first=first, start=start * scale, split=split * scale,
            again=again * scale, until=until * scale, third=third * scale,
        ):
            position = index * TILE + lax.broadcasted_iota(jnp.int32, (TILE, 2 * HD), 0)
            at = jnp.minimum(jnp.where(index < split, start + index, again + index - split), total - 1)
            part = recv_ref[at].astype(jnp.float32)
            if with_left:
                at = jnp.minimum(jnp.maximum(third + index - until, 0), left_ref.shape[0] - 1)
                part = jnp.where(index < until, part, left_ref[at].astype(jnp.float32))
            part = jnp.where(position < length, part, 0.0)
            for step in range(STEPS):
                part = jnp.where(position == length + step, fresh[step][child:child + 1], part)
            edge[child * 2 + index - first] = part.astype(jnp.bfloat16)
            pltpu.make_async_copy(edge.at[child * 2 + index - first], cache_ref.at[child, index], out_sem).start()
            return carry

        lax.fori_loop(first, last + 1, fix, 0)

    rows = MOST * STEPS
    raw = []
    for distance in range(SPAN):
        part = raw_ref[distance].astype(jnp.float32)
        raw.append(jnp.concatenate([part[:rows], part[rows:]], axis=1))
    raw = jnp.concatenate(raw, axis=0).astype(jnp.bfloat16)
    row = lax.broadcasted_iota(jnp.int32, (BEAMS, SPAN * rows), 0)
    col = lax.broadcasted_iota(jnp.int32, (BEAMS, SPAN * rows), 1)
    slot_at = jnp.zeros_like(col)
    for child in range(BEAMS):
        slot_at = jnp.where(row == child, slots[child], slot_at)
    for step in range(STEPS):
        pick = jnp.where(col == slot_at * STEPS + step, 1.0, 0.0).astype(jnp.bfloat16)
        proj_ref[step] = jnp.dot(pick, raw, preferred_element_type=jnp.float32).astype(jnp.bfloat16)
    proj_copy = pltpu.make_async_copy(proj_ref, proj_hbm, proj_sem)
    proj_copy.start()
    pltpu.make_async_copy(cache_ref, cache_ref, out_sem).wait()
    proj_copy.wait()


def local(shards, queries, new_kv, kv_pool, page_tables, lengths, parents, out_weight):
    wide = queries.shape[2]
    channels = kv_pool.shape[2]
    context = page_tables.shape[1] * kv_pool.shape[1]
    rows = MOST * STEPS
    vmem = pl.BlockSpec(memory_space=pltpu.VMEM)
    smem = pl.BlockSpec(memory_space=pltpu.SMEM)
    hbm = pl.BlockSpec(memory_space=pltpu.HBM)
    free = pl.BlockSpec(memory_space=pl.ANY)
    dma = pltpu.SemaphoreType.DMA
    bf16 = jnp.bfloat16

    def pinned(*operands):
        return [pltpu.with_memory_space_constraint(operand, pltpu.HBM) for operand in operands]

    grain_pool = kv_pool.reshape(-1, GRAIN, channels)
    with jax.named_scope("exchange"):
        recv, raw, left, meta, over = pl.pallas_call(
            exchange_kernel,
            out_shape=(
                jax.ShapeDtypeStruct((2 * LINK + MOST * PER_CHILD, GRAIN, channels), bf16),
                jax.ShapeDtypeStruct((SPAN, 2 * rows, wide // 2), bf16),
                jax.ShapeDtypeStruct((2, LEFT, GRAIN, channels), bf16),
                jax.ShapeDtypeStruct((BEAMS * META,), jnp.int32),
                jax.ShapeDtypeStruct((1,), jnp.int32),
            ),
            in_specs=[hbm] * 7,
            out_specs=(free, free, free, smem, smem),
            scratch_shapes=[
                pltpu.VMEM(queries.shape, bf16),
                pltpu.VMEM(new_kv.shape, bf16),
                pltpu.SMEM(page_tables.shape, jnp.int32),
                pltpu.SMEM(lengths.shape, jnp.int32),
                pltpu.SMEM(parents.shape, jnp.int32),
                pltpu.VMEM((1, *lengths.shape), jnp.int32),
                pltpu.VMEM((1, *parents.shape), jnp.int32),
                pltpu.VMEM(grain_pool.shape, bf16),
                pltpu.VMEM((shards, out_weight.shape[0], wide), bf16),
                pltpu.VMEM((SPAN, MOST * PER_CHILD, GRAIN, channels), bf16),
                pltpu.VMEM((2, FIRST, GRAIN, channels), bf16),
                pltpu.VMEM((2, FIRST, GRAIN, channels), bf16),
                pltpu.VMEM((2, REST, GRAIN, channels), bf16),
                pltpu.VMEM((2, LEFT, GRAIN, channels), bf16),
                pltpu.VMEM((SPAN, 2 * rows, (wide + channels) // 2), bf16),
                pltpu.VMEM((SPAN, 2 * rows, (wide + channels) // 2), bf16),
                pltpu.VMEM((SPAN * rows, wide), jnp.float32),
                pltpu.VMEM((shards, SPAN * rows, wide), bf16),
                pltpu.VMEM((shards, SPAN * rows, wide), bf16),
                pltpu.VMEM((SPAN, 2 * rows, wide // 2), bf16),
                pltpu.SMEM((SPAN * MOST,), jnp.int32),
                pltpu.SMEM((SPAN * MOST,), jnp.int32),
                dma((7,)), dma, dma((shards,)), dma((2,)), dma((3,)),
                dma((SPAN,)), dma((SPAN,)),
                dma((8,)), dma((8,)),
                dma((shards,)), dma((shards,)),
                dma((SPAN,)), dma((SPAN,)),
                pltpu.SemaphoreType.REGULAR,
            ],
            compiler_params=pltpu.CompilerParams(
                collective_id=0, has_side_effects=True, vmem_limit_bytes=48 * 1024 * 1024
            ),
            name="exchange",
        )(*pinned(queries, new_kv, grain_pool, page_tables, lengths, parents, out_weight))

    def place(*got):
        with jax.named_scope("place"):
            projected, cache = pl.pallas_call(
                functools.partial(place_kernel, len(got) > 0),
                out_shape=(
                    jax.ShapeDtypeStruct(queries.shape, bf16),
                    jax.ShapeDtypeStruct((BEAMS, context // TILE, TILE, channels), bf16),
                ),
                in_specs=[vmem, vmem, vmem, smem] + [vmem] * len(got),
                out_specs=(free, free),
                scratch_shapes=[
                    pltpu.VMEM((2 * BEAMS, TILE, channels), bf16),
                    pltpu.VMEM((context // TILE, TILE, channels), bf16),
                    pltpu.VMEM(queries.shape, bf16),
                    dma, dma,
                ],
                compiler_params=pltpu.CompilerParams(vmem_limit_bytes=24 * 1024 * 1024),
                name="place_left" if got else "place",
            )(recv.reshape(-1, TILE, channels), raw, new_kv, meta, *got)
            return projected, cache.reshape(BEAMS, context, channels)

    def placed():
        return place()

    def topped(count, number):
        with jax.named_scope("left"):
            got = pl.pallas_call(
                functools.partial(left_kernel, count),
                out_shape=jax.ShapeDtypeStruct(left.shape, bf16),
                in_specs=[free],
                out_specs=free,
                scratch_shapes=[dma((2,)), dma((2,))],
                compiler_params=pltpu.CompilerParams(
                    collective_id=number, has_side_effects=True, vmem_limit_bytes=4 * 1024 * 1024
                ),
                name="left",
            )(left)
        return place(got.reshape(-1, TILE, channels))

    def resent():
        with jax.named_scope("full"):
            whole = pl.pallas_call(
                full_kernel,
                out_shape=jax.ShapeDtypeStruct((SPAN, MOST * context, channels), bf16),
                in_specs=[hbm] * 3,
                out_specs=free,
                scratch_shapes=[
                    pltpu.SMEM(page_tables.shape, jnp.int32),
                    pltpu.SMEM(parents.shape, jnp.int32),
                    pltpu.VMEM(kv_pool.shape, bf16),
                    pltpu.VMEM((SPAN, MOST * context, channels), bf16),
                    dma((2,)), dma, dma((MOST,)),
                    dma((SPAN * MOST,)), dma((SPAN * MOST,)),
                ],
                compiler_params=pltpu.CompilerParams(
                    collective_id=1, has_side_effects=True, vmem_limit_bytes=24 * 1024 * 1024
                ),
                name="full",
            )(*pinned(kv_pool, page_tables, parents))
        with jax.named_scope("finish"):
            return pl.pallas_call(
                finish_kernel,
                out_shape=(
                    jax.ShapeDtypeStruct(queries.shape, bf16),
                    jax.ShapeDtypeStruct((BEAMS, context, channels), bf16),
                ),
                in_specs=[vmem, vmem, hbm, hbm, hbm],
                out_specs=(vmem, hbm),
                scratch_shapes=[
                    pltpu.VMEM(new_kv.shape, bf16),
                    pltpu.SMEM(lengths.shape, jnp.int32),
                    pltpu.SMEM(parents.shape, jnp.int32),
                    pltpu.VMEM((2 * BEAMS, PAGE, channels), bf16),
                    pltpu.VMEM((PAGE, channels), bf16),
                    dma((3,)), dma,
                ],
                compiler_params=pltpu.CompilerParams(vmem_limit_bytes=24 * 1024 * 1024),
                name="finish",
            )(whole.reshape(BEAMS, context, channels), raw, new_kv, lengths, parents)

    topping = [functools.partial(topped, count, 2 + at) for at, count in enumerate(TIERS)]
    return lax.switch(over[0], [placed, *topping, resent])


def solution(mesh):
    in_specs = (
        P(None, "dp", "tensor"),
        P(None, "dp", "tensor"),
        P("dp", None, "tensor"),
        P("dp", None),
        P(),
        P(),
        P("tensor", None),
    )
    out_specs = (P(None, "dp", "tensor"), P("dp", None, "tensor"))
    body = functools.partial(local, mesh.shape["tensor"])
    return jax.shard_map(body, mesh=mesh, in_specs=in_specs, out_specs=out_specs, check_vma=False)
```

```python
import functools

import jax
import jax.numpy as jnp
from jax import lax
from jax.experimental import pallas as pl
from jax.experimental.pallas import tpu as pltpu
from jax.sharding import PartitionSpec as P

HD = 128
SPAN = 4
MOST = 2
BEAMS = 8
STEPS = 4
PAGE = 128
PAGES = 8
GRAIN = 32
PER_CHILD = 32
PER_PAGE = PAGE // GRAIN
TILE = 16
VIA = 36
MORE = 16
REST = 36
TIERS = (4, 10, 24)
LEFT = TIERS[-1]
FIRST = VIA + MORE
LINK = FIRST + REST
META = 7
MESH = pl.DeviceIdType.MESH


def grains(length):
    return (length + (GRAIN - 1)) // GRAIN


def choose(values, index):
    out = values[0]
    for at in range(1, len(values)):
        out = jnp.where(index == at, values[at], out)
    return out


def balanced(up, far, down, keep_up, keep_down):
    least = [jnp.maximum(keep_up[i], far[i] - VIA) for i in range(SPAN)]
    most = [jnp.minimum(far[i] - keep_down[i], VIA) for i in range(SPAN)]
    via_up = [jnp.minimum(jnp.maximum(far[i] >> 1, least[i]), most[i]) for i in range(SPAN)]
    for at in range(SPAN):
        via_down = [far[i] - via_up[i] for i in range(SPAN)]
        nxt, prv = (at + 1) % SPAN, (at - 1) % SPAN
        load_up = jnp.maximum(up[at] + via_up[prv], up[nxt] + via_up[nxt])
        load_down = jnp.maximum(down[at] + via_down[nxt], down[prv] + via_down[prv])
        best = (load_down + far[at] - load_up) >> 1
        via_up[at] = jnp.minimum(jnp.maximum(best, least[at]), most[at])
    via_down = [far[i] - via_up[i] for i in range(SPAN)]
    return via_up, via_down


def planned(flows):
    names = ("up", "down", "far", "first", "second", "cut", "up_id", "down_id", "keep_up", "keep_down")
    plan = {name: [] for name in names}
    for at in range(SPAN):
        u0, u1, gu0, gu1 = flows[at][1]
        f0, f1, gf0, gf1 = flows[at][2]
        d0, d1, gd0, gd1 = flows[at][3]
        gu1 = jnp.where(u0 == u1, 0, gu1)
        gf1 = jnp.where(f0 == f1, 0, gf1)
        gd1 = jnp.where(d0 == d1, 0, gd1)

        def shared(parent, count, one, two):
            return jnp.where((parent == one) | (parent == two), count, 0)

        straight = shared(f0, gf0, u0, u1) + shared(f1, gf1, d0, d1)
        crossed = shared(f1, gf1, u0, u1) + shared(f0, gf0, d0, d1)
        swap = crossed > straight
        first, second = jnp.where(swap, f1, f0), jnp.where(swap, f0, f1)
        cut, rest = jnp.where(swap, gf1, gf0), jnp.where(swap, gf0, gf1)
        keep_up, keep_down = shared(first, cut, u0, u1), shared(second, rest, d0, d1)
        values = (
            gu0 + gu1 - keep_up, gd0 + gd1 - keep_down, gf0 + gf1, first, second, cut,
            jnp.where(keep_up > 0, first, -1), jnp.where(keep_down > 0, second, -1), keep_up, keep_down,
        )
        for name, value in zip(names, values):
            plan[name].append(value)
    plan["via_up"], plan["via_down"] = balanced(
        plan["up"], plan["far"], plan["down"], plan["keep_up"], plan["keep_down"]
    )
    return plan


def ring_plan(parents, lengths, ring):
    flows = [[None] * SPAN for _ in range(SPAN)]
    for target in range(SPAN):
        owners = [parents[(ring * SPAN + target) * BEAMS + child] for child in range(BEAMS)]
        sources = [(owner >> 3) & (SPAN - 1) for owner in owners]
        for at in range(SPAN):
            if at != target:
                one, two = owners[0], owners[0]
                for child in range(1, BEAMS):
                    two = jnp.where(sources[child] == at, owners[child], two)
                one = owners[BEAMS - 1]
                for child in range(BEAMS - 2, -1, -1):
                    one = jnp.where(sources[child] == at, owners[child], one)
                flows[at][(target - at) % SPAN] = (one, two, grains(lengths[one]), grains(lengths[two]))
    return {**planned(flows), "flows": flows}


def heaviest(parents, lengths, rings):
    beams = rings * SPAN * BEAMS
    counts = grains(lengths).astype(jnp.float32).astype(jnp.bfloat16)
    beam = lax.broadcasted_iota(jnp.int32, (beams, beams), 0)
    chosen = jnp.where(beam == parents, 1.0, 0.0).astype(jnp.bfloat16)
    counts = jnp.dot(jnp.broadcast_to(counts, (16, beams)), chosen, preferred_element_type=jnp.float32)[:1]
    lane = lax.broadcasted_iota(jnp.int32, (1, beams), 1)
    source = (parents // BEAMS) % SPAN
    rank = jnp.zeros_like(lane)
    for back in range(1, BEAMS):
        rank = rank + jnp.where((pltpu.roll(source, back, 1) == source) & (lane % BEAMS >= back), 1, 0)
    names = (parents % (SPAN * BEAMS)).astype(jnp.float32)
    rows = [
        jnp.where((source == at) & (rank == order), value, 0.0)
        for value in (names, counts) for at in range(SPAN) for order in range(MOST)
    ]
    rows = jnp.concatenate(rows, axis=0).astype(jnp.bfloat16)
    child = lax.broadcasted_iota(jnp.int32, (beams, 128), 0)
    ring = lax.broadcasted_iota(jnp.int32, (beams, 128), 1)
    flows = [[None] * SPAN for _ in range(SPAN)]
    for target in range(SPAN):
        member = (child // BEAMS % SPAN == target) & (child // (BEAMS * SPAN) == ring)
        member = jnp.where(member, 1.0, 0.0).astype(jnp.bfloat16)
        found = jnp.dot(rows, member, preferred_element_type=jnp.float32).astype(jnp.int32)
        for at in range(SPAN):
            wanted = (at * MOST, at * MOST + 1, (SPAN + at) * MOST, (SPAN + at) * MOST + 1)
            flows[at][(target - at) % SPAN] = tuple(found[one:one + 1] for one in wanted)
    plan = planned(flows)
    out = jnp.zeros_like(plan["far"][0])
    for at in range(SPAN):
        load_up = plan["up"][at] + plan["via_up"][at] + plan["via_up"][(at - 1) % SPAN]
        load_down = plan["down"][at] + plan["via_down"][at] + plan["via_down"][(at + 1) % SPAN]
        out = jnp.maximum(out, jnp.maximum(load_up, load_down))
    return jnp.max(out)


def slots_of_children(parents, me):
    taken = [jnp.int32(0) for _ in range(SPAN)]
    slots, owners = [], []
    for child in range(BEAMS):
        parent = parents[me * BEAMS + child]
        apart = jnp.bitwise_and(parent // BEAMS - me, SPAN - 1)
        slot = jnp.int32(0)
        for distance in range(SPAN):
            hit = apart == distance
            slot = jnp.where(hit, distance * MOST + taken[distance], slot)
            taken[distance] = taken[distance] + hit.astype(jnp.int32)
        slots.append(slot)
        owners.append(parent)
    return slots, owners


def served_beams(parents, me, target):
    count = jnp.int32(0)
    beams = [jnp.int32(0) for _ in range(MOST)]
    for child in range(BEAMS):
        parent = parents[target * BEAMS + child]
        hit = parent // BEAMS == me
        for rank in range(MOST):
            beams[rank] = jnp.where(hit & (count == rank), parent % BEAMS, beams[rank])
        count = count + hit.astype(jnp.int32)
    return beams


def exchange_kernel(
    q_hbm, new_hbm, pool_ref, table_hbm, len_hbm, par_hbm, w_ref,
    recv_ref, proj_ref, left_ref, meta_ref, over_ref,
    q_ref, new_ref, table_ref, len_ref, par_ref, len_row, par_row,
    pool_v, w_v, stage, first_send, first_recv, rest_send, left_send, q_send, q_recv, att, p_send, p_recv, r_send, lens, beams,
    in_sem, pool_sem, w_sem, own_sem, land_sem, qs_sem, qr_sem, bs_sem, br_sem, ps_sem, pr_sem, rs_sem, rr_sem, here_sem,
):
    me = lax.axis_index("dp")
    mine = lax.axis_index("tensor")
    shards = lax.axis_size("tensor")
    y = lax.rem(me, SPAN)
    base = me - y
    context = stage.shape[1] * GRAIN // MOST
    rings = lax.axis_size("dp") // SPAN
    wide = q_hbm.shape[2]
    heads = wide // HD
    rows = MOST * STEPS

    def peer(distance):
        return base + lax.rem(y + distance, SPAN)

    pairs = (
        (par_hbm, par_ref), (len_hbm, len_ref), (table_hbm, table_ref), (q_hbm, q_ref), (new_hbm, new_ref),
        (par_hbm, par_row.at[0]), (len_hbm, len_row.at[0]),
    )
    in_copies = [pltpu.make_async_copy(source, target, in_sem.at[at]) for at, (source, target) in enumerate(pairs)]
    pool_copy = pltpu.make_async_copy(pool_ref, pool_v, pool_sem)
    for copy in (*in_copies[:3], pool_copy, *in_copies[3:]):
        copy.start()
    barrier = pltpu.get_barrier_semaphore()
    for distance in range(1, SPAN):
        pl.semaphore_signal(barrier, inc=1, device_id={"dp": peer(distance)}, device_id_type=MESH)
    for other in range(1, shards):
        @pl.when(mine + other < shards)
        def _(other=other):
            pl.semaphore_signal(barrier, inc=1, device_id={"tensor": mine + other}, device_id_type=MESH)
    for copy in in_copies[:3]:
        copy.wait()

    plan = ring_plan(par_ref, len_ref, me >> 2)
    via_up, via_down = plan["via_up"], plan["via_down"]
    flows = {}
    for ahead in (1, 3):
        first, second, cut = (choose([plan["flows"][at][ahead][of] for at in range(SPAN)], y) for of in range(3))
        flows[ahead] = (first & 7, second & 7, cut)
    for ahead, kept in ((1, "up_id"), (3, "down_id")):
        first, second, cut = flows[ahead]
        flows[ahead] = (first, second, jnp.where(me * BEAMS + first == choose(plan[kept], y), 0, cut))
    flows[2] = (choose(plan["first"], y) & 7, choose(plan["second"], y) & 7, choose(plan["cut"], y))

    def grain_at(flow, number):
        first, second, cut = flow
        later = number >= cut
        number = jnp.where(later, number - cut, number)
        number = jnp.minimum(jnp.maximum(number, 0), PER_CHILD - 1)
        return table_ref[jnp.where(later, second, first), number >> 2] * PER_PAGE + (number & (PER_PAGE - 1))

    sides = (
        (flows[1], choose(via_up, y), jnp.int32(0), choose(via_up, (y - 1) & 3), peer(1)),
        (flows[3], choose(via_down, y), choose(via_up, y), choose(via_down, (y + 1) & 3), peer(3)),
    )
    pl.semaphore_wait(barrier, SPAN - 1 + mine)
    pool_copy.wait()
    b_copies = []
    cuts = (0, 12, VIA, FIRST)

    def send_part(part):
        for side, (flow, mine_via, skip, _, target) in enumerate(sides):
            def put(at, carry, side=side, flow=flow, mine_via=mine_via, skip=skip):
                for at in [4 * at + more for more in range(4)]:
                    far = at < mine_via
                    chosen = tuple(jnp.where(far, one, two) for one, two in zip(flows[2], flow))
                    number = jnp.where(far, skip + at, at - mine_via)
                    first_send[side, at] = pool_v[grain_at(chosen, number)]
                return carry

            lax.fori_loop(cuts[part] // 4, cuts[part + 1] // 4, put, 0)
            span = pl.ds(cuts[part], cuts[part + 1] - cuts[part])
            copy = pltpu.make_async_remote_copy(
                src_ref=first_send.at[side, span], dst_ref=first_recv.at[side, span],
                send_sem=bs_sem.at[side * 4 + part], recv_sem=br_sem.at[side * 4 + part],
                device_id={"dp": target}, device_id_type=MESH,
            )
            copy.start()
            b_copies.append(copy)

    send_part(0)
    for other in range(1, shards):
        @pl.when(mine >= other)
        def _(other=other):
            pl.semaphore_signal(here_sem, inc=1, device_id={"tensor": mine - other}, device_id_type=MESH)
    slots, owners = slots_of_children(par_ref, me)
    for copy in in_copies[3:5]:
        copy.wait()
    row = lax.broadcasted_iota(jnp.int32, (SPAN * rows, BEAMS), 0)
    col = lax.broadcasted_iota(jnp.int32, (SPAN * rows, BEAMS), 1)
    slot_at = jnp.zeros_like(col)
    for child in range(BEAMS):
        slot_at = jnp.where(col == child, slots[child], slot_at)
    q_sorted = jnp.zeros((SPAN * rows, wide), jnp.float32)
    new_sorted = jnp.zeros((SPAN * rows, 2 * HD), jnp.float32)
    for step in range(STEPS):
        pick = jnp.where((row // STEPS == slot_at) & (row % STEPS == step), 1.0, 0.0).astype(jnp.bfloat16)
        q_sorted += jnp.dot(pick, q_ref[step], preferred_element_type=jnp.float32)
        new_sorted += jnp.dot(pick, new_ref[step], preferred_element_type=jnp.float32)
    both = jnp.concatenate([q_sorted, new_sorted], axis=1)
    half = both.shape[1] // 2
    for distance in range(SPAN):
        part = both[distance * rows:(distance + 1) * rows]
        part = jnp.concatenate([part[:, :half], part[:, half:]], axis=0).astype(jnp.bfloat16)
        if distance == 0:
            q_recv[0] = part
        else:
            q_send[distance] = part
    q_copies = []
    for distance in range(1, SPAN):
        copy = pltpu.make_async_remote_copy(
            src_ref=q_send.at[distance], dst_ref=q_recv.at[distance],
            send_sem=qs_sem.at[distance], recv_sem=qr_sem.at[distance],
            device_id={"dp": peer(distance)}, device_id_type=MESH,
        )
        copy.start()
        q_copies.append(copy)
    send_part(1)
    send_part(2)
    for ahead in range(SPAN):
        served = served_beams(par_ref, me, peer(ahead))
        for rank in range(MOST):
            at = (SPAN - ahead) % SPAN * MOST + rank
            beams[at] = served[rank]
            lens[at] = len_ref[me * BEAMS + served[rank]]
    def put_all(index, carry):
        slot = index // PAGES
        page = table_ref[beams[slot], index % PAGES]
        at = (index % (MOST * PAGES)) * PER_PAGE
        stage[index // (MOST * PAGES), pl.ds(at, PER_PAGE)] = pool_v[pl.ds(page * PER_PAGE, PER_PAGE)]
        return carry

    lax.fori_loop(0, SPAN * MOST * PAGES, put_all, 0)
    own_copy = pltpu.make_async_copy(stage.at[0], recv_ref.at[pl.ds(2 * LINK, MOST * PER_CHILD)], own_sem.at[0])
    own_copy.start()

    for copy in q_copies:
        copy.wait()

    def attend(distance):
        message = q_recv[distance].astype(jnp.float32)
        message = jnp.concatenate([message[:rows], message[rows:]], axis=1)
        q_rows = jnp.concatenate([message[:, h * HD:(h + 1) * HD] for h in range(heads)], axis=0).astype(jnp.bfloat16)
        fresh = message[:, wide:].astype(jnp.bfloat16)
        old_len = lens[distance * MOST]
        last_len = lens[distance * MOST + 1]
        contract = (((1,), (1,)), ((), ()))
        scale = HD ** -0.5
        half = MOST * PER_CHILD // 2
        keys = [stage[distance, pl.ds(rank * half, half), :, 0:HD].reshape(context, HD) for rank in range(MOST)]
        scores = [lax.dot_general(q_rows, key, contract, preferred_element_type=jnp.float32) for key in keys]
        rank_at = lax.broadcasted_iota(jnp.int32, scores[0].shape, 0) // STEPS % MOST
        scores = jnp.where(rank_at == 0, scores[0], scores[1]) * scale
        fresh_scores = lax.dot_general(q_rows, fresh[:, :HD], contract, preferred_element_type=jnp.float32) * scale
        position = lax.broadcasted_iota(jnp.int32, scores.shape, 1)
        limit = jnp.where(rank_at == 0, old_len, last_len)
        scores = jnp.where(position < limit, scores, -1e30)
        f_row = lax.broadcasted_iota(jnp.int32, fresh_scores.shape, 0)
        f_col = lax.broadcasted_iota(jnp.int32, fresh_scores.shape, 1)
        seen = (f_row // STEPS % MOST == f_col // STEPS) & (f_col % STEPS <= f_row % STEPS)
        fresh_scores = jnp.where(seen, fresh_scores, -1e30)
        top = jnp.maximum(jnp.max(scores, axis=1, keepdims=True), jnp.max(fresh_scores, axis=1, keepdims=True))
        exp_old = jnp.exp(scores - top)
        exp_new = jnp.exp(fresh_scores - top)
        total = jnp.sum(exp_old, axis=1, keepdims=True) + jnp.sum(exp_new, axis=1, keepdims=True)
        share = 1.0 / total
        w_old = (exp_old * share).astype(jnp.bfloat16)
        w_new = (exp_new * share).astype(jnp.bfloat16)
        values = [stage[distance, pl.ds(rank * half, half), :, HD:2 * HD].reshape(context, HD) for rank in range(MOST)]
        out = [jnp.dot(w_old, value, preferred_element_type=jnp.float32) for value in values]
        out = jnp.where(rank_at[:, :HD] == 0, out[0], out[1])
        out += jnp.dot(w_new, fresh[:, HD:], preferred_element_type=jnp.float32)
        out = jnp.concatenate([out[h * rows:(h + 1) * rows] for h in range(heads)], axis=1)
        att[pl.ds(pl.multiple_of(distance * rows, rows), rows), :] = out

    def attend_two(at, carry):
        attend(2 * at)
        attend(2 * at + 1)
        return carry

    lax.fori_loop(0, SPAN // 2, attend_two, 0)
    def w_copy(other):
        block = lax.rem(mine + other, shards)
        source = w_ref.at[:, pl.ds(pl.multiple_of(block * wide, wide), wide)]
        return pltpu.make_async_copy(source, w_v.at[block], w_sem.at[block])

    for other in range(1, 4):
        w_copy(other).start()
    for copy in b_copies[:4]:
        copy.wait()
    more_copies = b_copies[4:]
    b_copies = []
    for side, (flow, mine_via, _, passed, target) in enumerate(sides):
        def put_passed(at, carry, side=side, flow=flow, mine_via=mine_via, passed=passed):
            for at in [4 * at + more for more in range(4)]:
                here = pool_v[grain_at(flow, FIRST - mine_via + at - passed)]
                rest_send[side, at] = jnp.where(at < passed, first_recv[side, at], here)
            return carry

        lax.fori_loop(0, REST // 4, put_passed, 0)
        copy = pltpu.make_async_remote_copy(
            src_ref=rest_send.at[side], dst_ref=recv_ref.at[pl.ds(side * LINK + FIRST, REST)],
            send_sem=bs_sem.at[side * 4 + 3], recv_sem=br_sem.at[side * 4 + 3],
            device_id={"dp": target}, device_id_type=MESH,
        )
        copy.start()
        b_copies.append(copy)
    attended = att[...].astype(jnp.bfloat16)

    def p_copy(other):
        return pltpu.make_async_remote_copy(
            src_ref=p_send.at[other], dst_ref=p_recv.at[other],
            send_sem=ps_sem.at[other], recv_sem=pr_sem.at[other],
            device_id={"tensor": lax.rem(mine + other, shards)}, device_id_type=MESH,
        )

    def project(other, carry):
        w_copy(other).wait()

        @pl.when(other + 3 <= shards)
        def _():
            w_copy(other + 3).start()

        product = jnp.dot(attended, w_v[lax.rem(mine + other, shards)], preferred_element_type=jnp.float32)
        p_send[other] = product.astype(jnp.bfloat16)
        p_copy(other).start()
        return carry

    @pl.when(mine < shards - 1)
    def _():
        pl.semaphore_wait(here_sem, shards - 1 - mine)

    lax.fori_loop(1, shards, project, 0)
    w_copy(shards).wait()
    own = jnp.dot(attended, w_v[mine], preferred_element_type=jnp.float32)

    for copy in more_copies:
        copy.wait()
    for side in range(2):
        copy = pltpu.make_async_copy(first_recv.at[side], recv_ref.at[pl.ds(side * LINK, FIRST)], land_sem.at[side])
        copy.start()
        b_copies.append(copy)

    def gather_sums(other, total):
        p_copy(other).wait()
        return total + p_recv[other].astype(jnp.float32)

    summed = lax.fori_loop(1, shards, gather_sums, own)
    half = wide // 2
    r_copies = []
    for distance in range(SPAN):
        part = summed[distance * rows:(distance + 1) * rows]
        r_send[distance] = jnp.concatenate([part[:, :half], part[:, half:]], axis=0).astype(jnp.bfloat16)
        if distance == 0:
            copy = pltpu.make_async_copy(r_send.at[0], proj_ref.at[0], own_sem.at[1])
        else:
            copy = pltpu.make_async_remote_copy(
                src_ref=r_send.at[distance], dst_ref=proj_ref.at[distance],
                send_sem=rs_sem.at[distance], recv_sem=rr_sem.at[distance],
                device_id={"dp": peer(SPAN - distance)}, device_id_type=MESH,
            )
        copy.start()
        r_copies.append(copy)
    for copy in in_copies[5:]:
        copy.wait()
    load = heaviest(par_row[...], len_row[...], rings)
    over_ref[0] = sum(jnp.where(load > limit, 1, 0) for limit in (LINK, *(LINK + count for count in TIERS)))
    for side, (flow, mine_via, _, passed, _) in enumerate(sides):
        def put_left(at, carry, side=side, flow=flow, mine_via=mine_via, passed=passed):
            for at in [4 * at + more for more in range(4)]:
                left_send[side, at] = pool_v[grain_at(flow, LINK - mine_via - passed + at)]
            return carry

        lax.fori_loop(0, LEFT // 4, put_left, 0)
    left_copy = pltpu.make_async_copy(left_send, left_ref, land_sem.at[2])
    left_copy.start()
    for child in range(BEAMS):
        slot = slots[child]
        distance = slot >> 1
        length = len_ref[owners[child]]
        kept = jnp.where(distance == 3, choose(plan["up_id"], (y - 1) & 3), choose(plan["down_id"], (y + 1) & 3))
        before = jnp.int32(0)
        for other in range(BEAMS):
            if other != child:
                mate = (slots[other] >> 1 == distance) & (slots[other] < slot)
                counts = (owners[other] != owners[child]) & (owners[other] != kept)
                before = jnp.where(mate & counts, grains(len_ref[owners[other]]), before)
        far_before = jnp.where(owners[child] == choose(plan["first"], (y + 2) & 3), 0, choose(plan["cut"], (y + 2) & 3))
        before = jnp.where(distance == 2, far_before, before)
        from_up = choose(via_up, (y - 1) & 3), choose(via_up, (y + 2) & 3)
        from_down = choose(via_down, (y + 1) & 3), choose(via_down, (y + 2) & 3)
        near_via = jnp.where(distance == 3, from_up[0], from_down[0])
        near_pass = jnp.where(distance == 3, from_up[1], from_down[1])
        near_base = jnp.where(distance == 3, 0, LINK)
        split = jnp.where(distance == 2, from_up[1], FIRST - near_via) - before
        split = jnp.minimum(jnp.maximum(split, 0), PER_CHILD)
        start = jnp.where(distance == 2, FIRST + before, near_base + near_via + before)
        again = jnp.where(distance == 2, LINK + FIRST + before + split - from_up[1], start + split + near_pass)
        near = (distance == 1) | (distance == 3)
        until = LINK - near_via - near_pass - before
        until = jnp.where(near, jnp.minimum(jnp.maximum(until, 0), PER_CHILD), PER_CHILD)
        third = jnp.where(distance == 3, 0, LEFT) + near_via + near_pass + before + until - LINK
        held = near & (owners[child] == kept)
        kept_down = LINK + choose(via_down, (y + 1) & 3) - choose(plan["keep_down"], (y + 1) & 3)
        start = jnp.where(held, jnp.where(distance == 3, 0, kept_down), start)
        split = jnp.where(held, PER_CHILD, split)
        again = jnp.where(held, 0, again)
        until = jnp.where(held, PER_CHILD, until)
        third = jnp.where(held, 0, third)
        stays = distance == 0
        meta_ref[child * META] = length
        meta_ref[child * META + 1] = jnp.where(stays, 2 * LINK + (slot & 1) * PER_CHILD, start)
        meta_ref[child * META + 2] = jnp.where(stays, PER_CHILD, split)
        meta_ref[child * META + 3] = jnp.where(stays, 0, again)
        meta_ref[child * META + 4] = until
        meta_ref[child * META + 5] = jnp.where(near, third, 0)
        meta_ref[child * META + 6] = slot
    for copy in r_copies:
        copy.wait()
    for copy in b_copies:
        copy.wait()
    own_copy.wait()
    left_copy.wait()


def full_kernel(
    pool_ref, table_hbm, par_hbm, recv_ref,
    table_ref, par_ref, pool_v, stage,
    in_sem, pool_sem, own_sem, bs_sem, br_sem,
):
    me = lax.axis_index("dp")
    y = lax.rem(me, SPAN)
    base = me - y
    context = stage.shape[1] // MOST

    def peer(distance):
        return base + lax.rem(y + distance, SPAN)

    barrier = pltpu.get_barrier_semaphore()
    for distance in range(1, SPAN):
        pl.semaphore_signal(barrier, inc=1, device_id={"dp": peer(distance)}, device_id_type=MESH)
    in_copies = []
    for at, (source, target) in enumerate(((par_hbm, par_ref), (table_hbm, table_ref))):
        copy = pltpu.make_async_copy(source, target, in_sem.at[at])
        copy.start()
        in_copies.append(copy)
    pool_copy = pltpu.make_async_copy(pool_ref, pool_v, pool_sem)
    pool_copy.start()
    for copy in in_copies:
        copy.wait()
    pl.semaphore_wait(barrier, SPAN - 1)
    pool_copy.wait()
    copies = []
    for distance in (2, 1, 3, 0):
        served = served_beams(par_ref, me, peer(SPAN - distance))
        for rank in range(MOST):
            beam = served[rank]

            def put(index, carry, distance=distance, rank=rank, beam=beam):
                at = pl.multiple_of(rank * context + index * PAGE, PAGE)
                stage[distance, pl.ds(at, PAGE), :] = pool_v[table_ref[beam, index]]
                return carry

            lax.fori_loop(0, context // PAGE, put, 0)
            span = pl.ds(rank * context, context)
            if distance == 0:
                copy = pltpu.make_async_copy(stage.at[0, span], recv_ref.at[0, span], own_sem.at[rank])
            else:
                copy = pltpu.make_async_remote_copy(
                    src_ref=stage.at[distance, span], dst_ref=recv_ref.at[distance, span],
                    send_sem=bs_sem.at[distance * MOST + rank], recv_sem=br_sem.at[distance * MOST + rank],
                    device_id={"dp": peer(SPAN - distance)}, device_id_type=MESH,
                )
            copy.start()
            copies.append(copy)
    for copy in copies:
        copy.wait()


def finish_kernel(recv_ref, raw_ref, new_hbm, len_hbm, par_hbm, proj_ref, cache_ref, new_ref, len_ref, par_ref, edge, zeros, in_sem, out_sem):
    me = lax.axis_index("dp")
    pages = recv_ref.shape[1] // PAGE
    operands = ((par_hbm, par_ref), (len_hbm, len_ref), (new_hbm, new_ref))
    in_copies = [pltpu.make_async_copy(source, target, in_sem.at[at]) for at, (source, target) in enumerate(operands)]
    for copy in in_copies:
        copy.start()
    zeros[...] = jnp.zeros_like(zeros)
    for copy in in_copies:
        copy.wait()
    slots, owners = slots_of_children(par_ref, me)
    fresh = [new_ref[step].astype(jnp.float32) for step in range(STEPS)]
    for child in range(BEAMS):
        slot = slots[child]
        length = len_ref[owners[child]]
        first = length // PAGE
        last = (length + STEPS - 1) // PAGE

        def whole(index, carry, child=child, slot=slot):
            span = pl.ds(pl.multiple_of(index * PAGE, PAGE), PAGE)
            pltpu.make_async_copy(recv_ref.at[slot, span], cache_ref.at[child, span], out_sem).start()
            return carry

        def clear(index, carry, child=child):
            span = pl.ds(pl.multiple_of(index * PAGE, PAGE), PAGE)
            pltpu.make_async_copy(zeros, cache_ref.at[child, span], out_sem).start()
            return carry

        def fix(index, carry, child=child, slot=slot, length=length, first=first):
            at = pl.multiple_of(index * PAGE, PAGE)
            position = at + lax.broadcasted_iota(jnp.int32, (PAGE, 2 * HD), 0)
            page = recv_ref[slot, pl.ds(at, PAGE), :].astype(jnp.float32)
            page = jnp.where(position < length, page, 0.0)
            for step in range(STEPS):
                page = jnp.where(position == length + step, fresh[step][child:child + 1], page)
            edge[child * 2 + index - first] = page.astype(jnp.bfloat16)
            pltpu.make_async_copy(edge.at[child * 2 + index - first], cache_ref.at[child, pl.ds(at, PAGE)], out_sem).start()
            return carry

        lax.fori_loop(0, first, whole, 0)
        lax.fori_loop(last + 1, pages, clear, 0)
        lax.fori_loop(first, last + 1, fix, 0)

    rows = MOST * STEPS
    raw = []
    for distance in range(SPAN):
        part = raw_ref[distance].astype(jnp.float32)
        raw.append(jnp.concatenate([part[:rows], part[rows:]], axis=1))
    raw = jnp.concatenate(raw, axis=0).astype(jnp.bfloat16)
    row = lax.broadcasted_iota(jnp.int32, (BEAMS, SPAN * rows), 0)
    col = lax.broadcasted_iota(jnp.int32, (BEAMS, SPAN * rows), 1)
    slot_at = jnp.zeros_like(col)
    for child in range(BEAMS):
        slot_at = jnp.where(row == child, slots[child], slot_at)
    for step in range(STEPS):
        pick = jnp.where(col == slot_at * STEPS + step, 1.0, 0.0).astype(jnp.bfloat16)
        proj_ref[step] = jnp.dot(pick, raw, preferred_element_type=jnp.float32).astype(jnp.bfloat16)
    pltpu.make_async_copy(recv_ref, cache_ref, out_sem).wait()


def left_kernel(count, left_ref, got_ref, send_sem, recv_sem):
    me = lax.axis_index("dp")
    y = lax.rem(me, SPAN)
    targets = [me - y + lax.rem(y + ahead, SPAN) for ahead in (1, SPAN - 1)]
    barrier = pltpu.get_barrier_semaphore()
    for target in targets:
        pl.semaphore_signal(barrier, inc=1, device_id={"dp": target}, device_id_type=MESH)
    pl.semaphore_wait(barrier, 2)
    copies = []
    for side, target in enumerate(targets):
        copy = pltpu.make_async_remote_copy(
            src_ref=left_ref.at[side, pl.ds(0, count)], dst_ref=got_ref.at[side, pl.ds(0, count)],
            send_sem=send_sem.at[side], recv_sem=recv_sem.at[side],
            device_id={"dp": target}, device_id_type=MESH,
        )
        copy.start()
        copies.append(copy)
    for copy in copies:
        copy.wait()


def place_kernel(with_left, recv_ref, raw_ref, new_ref, meta_ref, *refs):
    left_ref = refs[0] if with_left else None
    proj_hbm, cache_ref, edge, zeros, proj_ref, out_sem, proj_sem = refs[-7:]
    total = recv_ref.shape[0]
    zeros[...] = jnp.zeros_like(zeros)
    fresh = [new_ref[step].astype(jnp.float32) for step in range(STEPS)]
    slots = [meta_ref[child * META + 6] for child in range(BEAMS)]
    per_child = cache_ref.shape[1]
    scale = GRAIN // TILE
    for child in range(BEAMS):
        length, start, split, again, until, third = (meta_ref[child * META + at] for at in range(6))
        first = length // TILE
        last = (length + STEPS - 1) // TILE
        until = jnp.minimum(until * scale, first) if with_left else first
        split = jnp.minimum(split * scale, until)

        def move(source, source_at, at, count, child=child):
            @pl.when(count > 0)
            def _():
                pltpu.make_async_copy(
                    source.at[pl.ds(source_at, count)], cache_ref.at[child, pl.ds(at, count)], out_sem
                ).start()

        move(recv_ref, start * scale, 0, split)
        move(recv_ref, again * scale, split, until - split)
        if with_left:
            move(left_ref, third * scale, until, first - until)
        move(zeros, 0, last + 1, per_child - 1 - last)
    for child in range(BEAMS):
        length, start, split, again, until, third = (meta_ref[child * META + at] for at in range(6))
        first = length // TILE
        last = (length + STEPS - 1) // TILE

        def fix(
            index, carry, child=child, length=length, first=first, start=start * scale, split=split * scale,
            again=again * scale, until=until * scale, third=third * scale,
        ):
            position = index * TILE + lax.broadcasted_iota(jnp.int32, (TILE, 2 * HD), 0)
            at = jnp.minimum(jnp.where(index < split, start + index, again + index - split), total - 1)
            part = recv_ref[at].astype(jnp.float32)
            if with_left:
                at = jnp.minimum(jnp.maximum(third + index - until, 0), left_ref.shape[0] - 1)
                part = jnp.where(index < until, part, left_ref[at].astype(jnp.float32))
            part = jnp.where(position < length, part, 0.0)
            for step in range(STEPS):
                part = jnp.where(position == length + step, fresh[step][child:child + 1], part)
            edge[child * 2 + index - first] = part.astype(jnp.bfloat16)
            pltpu.make_async_copy(edge.at[child * 2 + index - first], cache_ref.at[child, index], out_sem).start()
            return carry

        lax.fori_loop(first, last + 1, fix, 0)

    rows = MOST * STEPS
    raw = []
    for distance in range(SPAN):
        part = raw_ref[distance].astype(jnp.float32)
        raw.append(jnp.concatenate([part[:rows], part[rows:]], axis=1))
    raw = jnp.concatenate(raw, axis=0).astype(jnp.bfloat16)
    row = lax.broadcasted_iota(jnp.int32, (BEAMS, SPAN * rows), 0)
    col = lax.broadcasted_iota(jnp.int32, (BEAMS, SPAN * rows), 1)
    slot_at = jnp.zeros_like(col)
    for child in range(BEAMS):
        slot_at = jnp.where(row == child, slots[child], slot_at)
    for step in range(STEPS):
        pick = jnp.where(col == slot_at * STEPS + step, 1.0, 0.0).astype(jnp.bfloat16)
        proj_ref[step] = jnp.dot(pick, raw, preferred_element_type=jnp.float32).astype(jnp.bfloat16)
    proj_copy = pltpu.make_async_copy(proj_ref, proj_hbm, proj_sem)
    proj_copy.start()
    pltpu.make_async_copy(cache_ref, cache_ref, out_sem).wait()
    proj_copy.wait()


def local(shards, queries, new_kv, kv_pool, page_tables, lengths, parents, out_weight):
    wide = queries.shape[2]
    channels = kv_pool.shape[2]
    context = page_tables.shape[1] * kv_pool.shape[1]
    rows = MOST * STEPS
    vmem = pl.BlockSpec(memory_space=pltpu.VMEM)
    smem = pl.BlockSpec(memory_space=pltpu.SMEM)
    hbm = pl.BlockSpec(memory_space=pltpu.HBM)
    free = pl.BlockSpec(memory_space=pl.ANY)
    dma = pltpu.SemaphoreType.DMA
    bf16 = jnp.bfloat16

    def pinned(*operands):
        return [pltpu.with_memory_space_constraint(operand, pltpu.HBM) for operand in operands]

    grain_pool = kv_pool.reshape(-1, GRAIN, channels)
    with jax.named_scope("exchange"):
        recv, raw, left, meta, over = pl.pallas_call(
            exchange_kernel,
            out_shape=(
                jax.ShapeDtypeStruct((2 * LINK + MOST * PER_CHILD, GRAIN, channels), bf16),
                jax.ShapeDtypeStruct((SPAN, 2 * rows, wide // 2), bf16),
                jax.ShapeDtypeStruct((2, LEFT, GRAIN, channels), bf16),
                jax.ShapeDtypeStruct((BEAMS * META,), jnp.int32),
                jax.ShapeDtypeStruct((1,), jnp.int32),
            ),
            in_specs=[hbm] * 7,
            out_specs=(free, free, free, smem, smem),
            scratch_shapes=[
                pltpu.VMEM(queries.shape, bf16),
                pltpu.VMEM(new_kv.shape, bf16),
                pltpu.SMEM(page_tables.shape, jnp.int32),
                pltpu.SMEM(lengths.shape, jnp.int32),
                pltpu.SMEM(parents.shape, jnp.int32),
                pltpu.VMEM((1, *lengths.shape), jnp.int32),
                pltpu.VMEM((1, *parents.shape), jnp.int32),
                pltpu.VMEM(grain_pool.shape, bf16),
                pltpu.VMEM((shards, out_weight.shape[0], wide), bf16),
                pltpu.VMEM((SPAN, MOST * PER_CHILD, GRAIN, channels), bf16),
                pltpu.VMEM((2, FIRST, GRAIN, channels), bf16),
                pltpu.VMEM((2, FIRST, GRAIN, channels), bf16),
                pltpu.VMEM((2, REST, GRAIN, channels), bf16),
                pltpu.VMEM((2, LEFT, GRAIN, channels), bf16),
                pltpu.VMEM((SPAN, 2 * rows, (wide + channels) // 2), bf16),
                pltpu.VMEM((SPAN, 2 * rows, (wide + channels) // 2), bf16),
                pltpu.VMEM((SPAN * rows, wide), jnp.float32),
                pltpu.VMEM((shards, SPAN * rows, wide), bf16),
                pltpu.VMEM((shards, SPAN * rows, wide), bf16),
                pltpu.VMEM((SPAN, 2 * rows, wide // 2), bf16),
                pltpu.SMEM((SPAN * MOST,), jnp.int32),
                pltpu.SMEM((SPAN * MOST,), jnp.int32),
                dma((7,)), dma, dma((shards,)), dma((2,)), dma((3,)),
                dma((SPAN,)), dma((SPAN,)),
                dma((8,)), dma((8,)),
                dma((shards,)), dma((shards,)),
                dma((SPAN,)), dma((SPAN,)),
                pltpu.SemaphoreType.REGULAR,
            ],
            compiler_params=pltpu.CompilerParams(
                collective_id=0, has_side_effects=True, vmem_limit_bytes=48 * 1024 * 1024
            ),
            name="exchange",
        )(*pinned(queries, new_kv, grain_pool, page_tables, lengths, parents, out_weight))

    def place(*got):
        with jax.named_scope("place"):
            projected, cache = pl.pallas_call(
                functools.partial(place_kernel, len(got) > 0),
                out_shape=(
                    jax.ShapeDtypeStruct(queries.shape, bf16),
                    jax.ShapeDtypeStruct((BEAMS, context // TILE, TILE, channels), bf16),
                ),
                in_specs=[vmem, vmem, vmem, smem] + [vmem] * len(got),
                out_specs=(free, free),
                scratch_shapes=[
                    pltpu.VMEM((2 * BEAMS, TILE, channels), bf16),
                    pltpu.VMEM((context // TILE, TILE, channels), bf16),
                    pltpu.VMEM(queries.shape, bf16),
                    dma, dma,
                ],
                compiler_params=pltpu.CompilerParams(vmem_limit_bytes=24 * 1024 * 1024),
                name="place_left" if got else "place",
            )(recv.reshape(-1, TILE, channels), raw, new_kv, meta, *got)
            return projected, cache.reshape(BEAMS, context, channels)

    def placed():
        return place()

    def topped(count, number):
        with jax.named_scope("left"):
            got = pl.pallas_call(
                functools.partial(left_kernel, count),
                out_shape=jax.ShapeDtypeStruct(left.shape, bf16),
                in_specs=[free],
                out_specs=free,
                scratch_shapes=[dma((2,)), dma((2,))],
                compiler_params=pltpu.CompilerParams(
                    collective_id=number, has_side_effects=True, vmem_limit_bytes=4 * 1024 * 1024
                ),
                name="left",
            )(left)
        return place(got.reshape(-1, TILE, channels))

    def resent():
        with jax.named_scope("full"):
            whole = pl.pallas_call(
                full_kernel,
                out_shape=jax.ShapeDtypeStruct((SPAN, MOST * context, channels), bf16),
                in_specs=[hbm] * 3,
                out_specs=free,
                scratch_shapes=[
                    pltpu.SMEM(page_tables.shape, jnp.int32),
                    pltpu.SMEM(parents.shape, jnp.int32),
                    pltpu.VMEM(kv_pool.shape, bf16),
                    pltpu.VMEM((SPAN, MOST * context, channels), bf16),
                    dma((2,)), dma, dma((MOST,)),
                    dma((SPAN * MOST,)), dma((SPAN * MOST,)),
                ],
                compiler_params=pltpu.CompilerParams(
                    collective_id=1, has_side_effects=True, vmem_limit_bytes=24 * 1024 * 1024
                ),
                name="full",
            )(*pinned(kv_pool, page_tables, parents))
        with jax.named_scope("finish"):
            return pl.pallas_call(
                finish_kernel,
                out_shape=(
                    jax.ShapeDtypeStruct(queries.shape, bf16),
                    jax.ShapeDtypeStruct((BEAMS, context, channels), bf16),
                ),
                in_specs=[vmem, vmem, hbm, hbm, hbm],
                out_specs=(vmem, hbm),
                scratch_shapes=[
                    pltpu.VMEM(new_kv.shape, bf16),
                    pltpu.SMEM(lengths.shape, jnp.int32),
                    pltpu.SMEM(parents.shape, jnp.int32),
                    pltpu.VMEM((2 * BEAMS, PAGE, channels), bf16),
                    pltpu.VMEM((PAGE, channels), bf16),
                    dma((3,)), dma,
                ],
                compiler_params=pltpu.CompilerParams(vmem_limit_bytes=24 * 1024 * 1024),
                name="finish",
            )(whole.reshape(BEAMS, context, channels), raw, new_kv, lengths, parents)

    topping = [functools.partial(topped, count, 2 + at) for at, count in enumerate(TIERS)]
    return lax.switch(over[0], [placed, *topping, resent])


def solution(mesh):
    in_specs = (
        P(None, "dp", "tensor"),
        P(None, "dp", "tensor"),
        P("dp", None, "tensor"),
        P("dp", None),
        P(),
        P(),
        P("tensor", None),
    )
    out_specs = (P(None, "dp", "tensor"), P("dp", None, "tensor"))
    body = functools.partial(local, mesh.shape["tensor"])
    return jax.shard_map(body, mesh=mesh, in_specs=in_specs, out_specs=out_specs, check_vma=False)
```

```python
import functools

import jax
import jax.numpy as jnp
from jax import lax
from jax.experimental import pallas as pl
from jax.experimental.pallas import tpu as pltpu
from jax.sharding import PartitionSpec as P

HD = 128
SPAN = 4
MOST = 2
BEAMS = 8
STEPS = 4
PAGE = 128
PAGES = 8
GRAIN = 16
PER_CHILD = 64
PER_PAGE = PAGE // GRAIN
PAGE_BITS = PER_PAGE.bit_length() - 1
TILE = 16
VIA = 72
MORE = 28
REST = 72
TIERS = (8, 20, 48)
LEFT = TIERS[-1]
FIRST = VIA + MORE
LINK = FIRST + REST
META = 7
MESH = pl.DeviceIdType.MESH


def grains(length):
    return (length + (GRAIN - 1)) // GRAIN


def choose(values, index):
    out = values[0]
    for at in range(1, len(values)):
        out = jnp.where(index == at, values[at], out)
    return out


def balanced(up, far, down, keep_up, keep_down):
    least = [jnp.maximum(keep_up[i], far[i] - VIA) for i in range(SPAN)]
    most = [jnp.minimum(far[i] - keep_down[i], VIA) for i in range(SPAN)]
    via_up = [jnp.minimum(jnp.maximum(far[i] >> 1, least[i]), most[i]) for i in range(SPAN)]
    for at in (*range(SPAN), *range(SPAN)):
        via_down = [far[i] - via_up[i] for i in range(SPAN)]
        nxt, prv = (at + 1) % SPAN, (at - 1) % SPAN
        load_up = jnp.maximum(up[at] + via_up[prv], up[nxt] + via_up[nxt])
        load_down = jnp.maximum(down[at] + via_down[nxt], down[prv] + via_down[prv])
        best = (load_down + far[at] - load_up) >> 1
        via_up[at] = jnp.minimum(jnp.maximum(best, least[at]), most[at])
    via_down = [far[i] - via_up[i] for i in range(SPAN)]
    return via_up, via_down


def planned(flows):
    names = ("up", "down", "far", "first", "second", "cut", "up_id", "down_id", "keep_up", "keep_down")
    plan = {name: [] for name in names}
    for at in range(SPAN):
        u0, u1, gu0, gu1 = flows[at][1]
        f0, f1, gf0, gf1 = flows[at][2]
        d0, d1, gd0, gd1 = flows[at][3]
        gu1 = jnp.where(u0 == u1, 0, gu1)
        gf1 = jnp.where(f0 == f1, 0, gf1)
        gd1 = jnp.where(d0 == d1, 0, gd1)

        def shared(parent, count, one, two):
            return jnp.where((parent == one) | (parent == two), count, 0)

        straight = shared(f0, gf0, u0, u1) + shared(f1, gf1, d0, d1)
        crossed = shared(f1, gf1, u0, u1) + shared(f0, gf0, d0, d1)
        swap = crossed > straight
        first, second = jnp.where(swap, f1, f0), jnp.where(swap, f0, f1)
        cut, rest = jnp.where(swap, gf1, gf0), jnp.where(swap, gf0, gf1)
        keep_up, keep_down = shared(first, cut, u0, u1), shared(second, rest, d0, d1)
        values = (
            gu0 + gu1 - keep_up, gd0 + gd1 - keep_down, gf0 + gf1, first, second, cut,
            jnp.where(keep_up > 0, first, -1), jnp.where(keep_down > 0, second, -1), keep_up, keep_down,
        )
        for name, value in zip(names, values):
            plan[name].append(value)
    plan["via_up"], plan["via_down"] = balanced(
        plan["up"], plan["far"], plan["down"], plan["keep_up"], plan["keep_down"]
    )
    return plan


def ring_plan(parents, lengths, ring):
    flows = [[None] * SPAN for _ in range(SPAN)]
    for target in range(SPAN):
        owners = [parents[(ring * SPAN + target) * BEAMS + child] for child in range(BEAMS)]
        sources = [(owner >> 3) & (SPAN - 1) for owner in owners]
        for at in range(SPAN):
            if at != target:
                one, two = owners[0], owners[0]
                for child in range(1, BEAMS):
                    two = jnp.where(sources[child] == at, owners[child], two)
                one = owners[BEAMS - 1]
                for child in range(BEAMS - 2, -1, -1):
                    one = jnp.where(sources[child] == at, owners[child], one)
                flows[at][(target - at) % SPAN] = (one, two, grains(lengths[one]), grains(lengths[two]))
    return {**planned(flows), "flows": flows}


def heaviest(parents, lengths, rings):
    beams = rings * SPAN * BEAMS
    counts = grains(lengths).astype(jnp.float32).astype(jnp.bfloat16)
    beam = lax.broadcasted_iota(jnp.int32, (beams, beams), 0)
    chosen = jnp.where(beam == parents, 1.0, 0.0).astype(jnp.bfloat16)
    counts = jnp.dot(jnp.broadcast_to(counts, (16, beams)), chosen, preferred_element_type=jnp.float32)[:1]
    lane = lax.broadcasted_iota(jnp.int32, (1, beams), 1)
    source = (parents // BEAMS) % SPAN
    rank = jnp.zeros_like(lane)
    for back in range(1, BEAMS):
        rank = rank + jnp.where((pltpu.roll(source, back, 1) == source) & (lane % BEAMS >= back), 1, 0)
    names = (parents % (SPAN * BEAMS)).astype(jnp.float32)
    rows = [
        jnp.where((source == at) & (rank == order), value, 0.0)
        for value in (names, counts) for at in range(SPAN) for order in range(MOST)
    ]
    rows = jnp.concatenate(rows, axis=0).astype(jnp.bfloat16)
    child = lax.broadcasted_iota(jnp.int32, (beams, 128), 0)
    ring = lax.broadcasted_iota(jnp.int32, (beams, 128), 1)
    flows = [[None] * SPAN for _ in range(SPAN)]
    for target in range(SPAN):
        member = (child // BEAMS % SPAN == target) & (child // (BEAMS * SPAN) == ring)
        member = jnp.where(member, 1.0, 0.0).astype(jnp.bfloat16)
        found = jnp.dot(rows, member, preferred_element_type=jnp.float32).astype(jnp.int32)
        for at in range(SPAN):
            wanted = (at * MOST, at * MOST + 1, (SPAN + at) * MOST, (SPAN + at) * MOST + 1)
            flows[at][(target - at) % SPAN] = tuple(found[one:one + 1] for one in wanted)
    plan = planned(flows)
    out = jnp.zeros_like(plan["far"][0])
    for at in range(SPAN):
        load_up = plan["up"][at] + plan["via_up"][at] + plan["via_up"][(at - 1) % SPAN]
        load_down = plan["down"][at] + plan["via_down"][at] + plan["via_down"][(at + 1) % SPAN]
        out = jnp.maximum(out, jnp.maximum(load_up, load_down))
    return jnp.max(out)


def slots_of_children(parents, me):
    taken = [jnp.int32(0) for _ in range(SPAN)]
    slots, owners = [], []
    for child in range(BEAMS):
        parent = parents[me * BEAMS + child]
        apart = jnp.bitwise_and(parent // BEAMS - me, SPAN - 1)
        slot = jnp.int32(0)
        for distance in range(SPAN):
            hit = apart == distance
            slot = jnp.where(hit, distance * MOST + taken[distance], slot)
            taken[distance] = taken[distance] + hit.astype(jnp.int32)
        slots.append(slot)
        owners.append(parent)
    return slots, owners


def served_beams(parents, me, target):
    count = jnp.int32(0)
    beams = [jnp.int32(0) for _ in range(MOST)]
    for child in range(BEAMS):
        parent = parents[target * BEAMS + child]
        hit = parent // BEAMS == me
        for rank in range(MOST):
            beams[rank] = jnp.where(hit & (count == rank), parent % BEAMS, beams[rank])
        count = count + hit.astype(jnp.int32)
    return beams


def exchange_kernel(
    q_hbm, new_hbm, pool_ref, table_hbm, len_hbm, par_hbm, w_ref,
    recv_ref, proj_ref, left_ref, meta_ref, over_ref,
    q_ref, new_ref, table_ref, len_ref, par_ref, len_row, par_row,
    pool_v, w_v, stage, first_send, first_recv, rest_send, left_send, q_send, q_recv, att, p_send, p_recv, r_send, lens, beams,
    in_sem, pool_sem, w_sem, own_sem, land_sem, qs_sem, qr_sem, bs_sem, br_sem, ps_sem, pr_sem, rs_sem, rr_sem, here_sem,
):
    me = lax.axis_index("dp")
    mine = lax.axis_index("tensor")
    shards = lax.axis_size("tensor")
    y = lax.rem(me, SPAN)
    base = me - y
    context = stage.shape[1] * GRAIN // MOST
    rings = lax.axis_size("dp") // SPAN
    wide = q_hbm.shape[2]
    heads = wide // HD
    rows = MOST * STEPS

    def peer(distance):
        return base + lax.rem(y + distance, SPAN)

    pairs = (
        (par_hbm, par_ref), (len_hbm, len_ref), (table_hbm, table_ref), (q_hbm, q_ref), (new_hbm, new_ref),
        (par_hbm, par_row.at[0]), (len_hbm, len_row.at[0]),
    )
    in_copies = [pltpu.make_async_copy(source, target, in_sem.at[at]) for at, (source, target) in enumerate(pairs)]
    pool_copy = pltpu.make_async_copy(pool_ref, pool_v, pool_sem)
    for copy in (*in_copies[:3], pool_copy, *in_copies[3:]):
        copy.start()
    barrier = pltpu.get_barrier_semaphore()
    for distance in range(1, SPAN):
        pl.semaphore_signal(barrier, inc=1, device_id={"dp": peer(distance)}, device_id_type=MESH)
    for other in range(1, shards):
        @pl.when(mine + other < shards)
        def _(other=other):
            pl.semaphore_signal(barrier, inc=1, device_id={"tensor": mine + other}, device_id_type=MESH)
    for copy in in_copies[:3]:
        copy.wait()

    plan = ring_plan(par_ref, len_ref, me >> 2)
    via_up, via_down = plan["via_up"], plan["via_down"]
    flows = {}
    for ahead in (1, 3):
        first, second, cut = (choose([plan["flows"][at][ahead][of] for at in range(SPAN)], y) for of in range(3))
        flows[ahead] = (first & 7, second & 7, cut)
    for ahead, kept in ((1, "up_id"), (3, "down_id")):
        first, second, cut = flows[ahead]
        flows[ahead] = (first, second, jnp.where(me * BEAMS + first == choose(plan[kept], y), 0, cut))
    flows[2] = (choose(plan["first"], y) & 7, choose(plan["second"], y) & 7, choose(plan["cut"], y))

    def grain_at(flow, number):
        first, second, cut = flow
        later = number >= cut
        number = jnp.where(later, number - cut, number)
        number = jnp.minimum(jnp.maximum(number, 0), PER_CHILD - 1)
        return table_ref[jnp.where(later, second, first), number >> PAGE_BITS] * PER_PAGE + (number & (PER_PAGE - 1))

    sides = (
        (flows[1], choose(via_up, y), jnp.int32(0), choose(via_up, (y - 1) & 3), peer(1)),
        (flows[3], choose(via_down, y), choose(via_up, y), choose(via_down, (y + 1) & 3), peer(3)),
    )
    pl.semaphore_wait(barrier, SPAN - 1 + mine)
    pool_copy.wait()
    b_copies = []
    cuts = (0, 24, VIA, FIRST)

    def send_part(part):
        for side, (flow, mine_via, skip, _, target) in enumerate(sides):
            def put(at, carry, side=side, flow=flow, mine_via=mine_via, skip=skip):
                for at in [4 * at + more for more in range(4)]:
                    far = at < mine_via
                    chosen = tuple(jnp.where(far, one, two) for one, two in zip(flows[2], flow))
                    number = jnp.where(far, skip + at, at - mine_via)
                    first_send[side, at] = pool_v[grain_at(chosen, number)]
                return carry

            lax.fori_loop(cuts[part] // 4, cuts[part + 1] // 4, put, 0)
            span = pl.ds(cuts[part], cuts[part + 1] - cuts[part])
            copy = pltpu.make_async_remote_copy(
                src_ref=first_send.at[side, span], dst_ref=first_recv.at[side, span],
                send_sem=bs_sem.at[side * 4 + part], recv_sem=br_sem.at[side * 4 + part],
                device_id={"dp": target}, device_id_type=MESH,
            )
            copy.start()
            b_copies.append(copy)

    send_part(0)
    for other in range(1, shards):
        @pl.when(mine >= other)
        def _(other=other):
            pl.semaphore_signal(here_sem, inc=1, device_id={"tensor": mine - other}, device_id_type=MESH)
    slots, owners = slots_of_children(par_ref, me)
    for copy in in_copies[3:5]:
        copy.wait()
    row = lax.broadcasted_iota(jnp.int32, (SPAN * rows, BEAMS), 0)
    col = lax.broadcasted_iota(jnp.int32, (SPAN * rows, BEAMS), 1)
    slot_at = jnp.zeros_like(col)
    for child in range(BEAMS):
        slot_at = jnp.where(col == child, slots[child], slot_at)
    q_sorted = jnp.zeros((SPAN * rows, wide), jnp.float32)
    new_sorted = jnp.zeros((SPAN * rows, 2 * HD), jnp.float32)
    for step in range(STEPS):
        pick = jnp.where((row // STEPS == slot_at) & (row % STEPS == step), 1.0, 0.0).astype(jnp.bfloat16)
        q_sorted += jnp.dot(pick, q_ref[step], preferred_element_type=jnp.float32)
        new_sorted += jnp.dot(pick, new_ref[step], preferred_element_type=jnp.float32)
    both = jnp.concatenate([q_sorted, new_sorted], axis=1)
    half = both.shape[1] // 2
    for distance in range(SPAN):
        part = both[distance * rows:(distance + 1) * rows]
        part = jnp.concatenate([part[:, :half], part[:, half:]], axis=0).astype(jnp.bfloat16)
        if distance == 0:
            q_recv[0] = part
        else:
            q_send[distance] = part
    q_copies = []
    for distance in range(1, SPAN):
        copy = pltpu.make_async_remote_copy(
            src_ref=q_send.at[distance], dst_ref=q_recv.at[distance],
            send_sem=qs_sem.at[distance], recv_sem=qr_sem.at[distance],
            device_id={"dp": peer(distance)}, device_id_type=MESH,
        )
        copy.start()
        q_copies.append(copy)
    send_part(1)
    send_part(2)
    for ahead in range(SPAN):
        served = served_beams(par_ref, me, peer(ahead))
        for rank in range(MOST):
            at = (SPAN - ahead) % SPAN * MOST + rank
            beams[at] = served[rank]
            lens[at] = len_ref[me * BEAMS + served[rank]]
    w_copies = []
    for block in range(shards):
        copy = pltpu.make_async_copy(w_ref.at[:, pl.ds(block * wide, wide)], w_v.at[block], w_sem.at[block])
        copy.start()
        w_copies.append(copy)

    def put_all(index, carry):
        slot = index // PAGES
        page = table_ref[beams[slot], index % PAGES]
        at = (index % (MOST * PAGES)) * PER_PAGE
        stage[index // (MOST * PAGES), pl.ds(at, PER_PAGE)] = pool_v[pl.ds(page * PER_PAGE, PER_PAGE)]
        return carry

    lax.fori_loop(0, SPAN * MOST * PAGES, put_all, 0)
    own_copy = pltpu.make_async_copy(stage.at[0], recv_ref.at[pl.ds(2 * LINK, MOST * PER_CHILD)], own_sem.at[0])
    own_copy.start()

    for copy in q_copies:
        copy.wait()

    def attend(distance):
        message = q_recv[distance].astype(jnp.float32)
        message = jnp.concatenate([message[:rows], message[rows:]], axis=1)
        q_rows = jnp.concatenate([message[:, h * HD:(h + 1) * HD] for h in range(heads)], axis=0).astype(jnp.bfloat16)
        fresh = message[:, wide:].astype(jnp.bfloat16)
        old_len = lens[distance * MOST]
        last_len = lens[distance * MOST + 1]
        contract = (((1,), (1,)), ((), ()))
        scale = HD ** -0.5
        half = MOST * PER_CHILD // 2
        keys = [stage[distance, pl.ds(rank * half, half), :, 0:HD].reshape(context, HD) for rank in range(MOST)]
        scores = [lax.dot_general(q_rows, key, contract, preferred_element_type=jnp.float32) for key in keys]
        rank_at = lax.broadcasted_iota(jnp.int32, scores[0].shape, 0) // STEPS % MOST
        scores = jnp.where(rank_at == 0, scores[0], scores[1]) * scale
        fresh_scores = lax.dot_general(q_rows, fresh[:, :HD], contract, preferred_element_type=jnp.float32) * scale
        position = lax.broadcasted_iota(jnp.int32, scores.shape, 1)
        limit = jnp.where(rank_at == 0, old_len, last_len)
        scores = jnp.where(position < limit, scores, -1e30)
        f_row = lax.broadcasted_iota(jnp.int32, fresh_scores.shape, 0)
        f_col = lax.broadcasted_iota(jnp.int32, fresh_scores.shape, 1)
        seen = (f_row // STEPS % MOST == f_col // STEPS) & (f_col % STEPS <= f_row % STEPS)
        fresh_scores = jnp.where(seen, fresh_scores, -1e30)
        top = jnp.maximum(jnp.max(scores, axis=1, keepdims=True), jnp.max(fresh_scores, axis=1, keepdims=True))
        exp_old = jnp.exp(scores - top)
        exp_new = jnp.exp(fresh_scores - top)
        total = jnp.sum(exp_old, axis=1, keepdims=True) + jnp.sum(exp_new, axis=1, keepdims=True)
        share = 1.0 / total
        w_old = (exp_old * share).astype(jnp.bfloat16)
        w_new = (exp_new * share).astype(jnp.bfloat16)
        values = [stage[distance, pl.ds(rank * half, half), :, HD:2 * HD].reshape(context, HD) for rank in range(MOST)]
        out = [jnp.dot(w_old, value, preferred_element_type=jnp.float32) for value in values]
        out = jnp.where(rank_at[:, :HD] == 0, out[0], out[1])
        out += jnp.dot(w_new, fresh[:, HD:], preferred_element_type=jnp.float32)
        out = jnp.concatenate([out[h * rows:(h + 1) * rows] for h in range(heads)], axis=1)
        att[pl.ds(pl.multiple_of(distance * rows, rows), rows), :] = out

    def attend_two(at, carry):
        attend(2 * at)
        attend(2 * at + 1)
        return carry

    lax.fori_loop(0, SPAN // 2, attend_two, 0)
    for copy in b_copies[:4]:
        copy.wait()
    more_copies = b_copies[4:]
    b_copies = []
    for side, (flow, mine_via, _, passed, target) in enumerate(sides):
        def put_passed(at, carry, side=side, flow=flow, mine_via=mine_via, passed=passed):
            for at in [4 * at + more for more in range(4)]:
                here = pool_v[grain_at(flow, FIRST - mine_via + at - passed)]
                rest_send[side, at] = jnp.where(at < passed, first_recv[side, at], here)
            return carry

        lax.fori_loop(0, REST // 4, put_passed, 0)
        copy = pltpu.make_async_remote_copy(
            src_ref=rest_send.at[side], dst_ref=recv_ref.at[pl.ds(side * LINK + FIRST, REST)],
            send_sem=bs_sem.at[side * 4 + 3], recv_sem=br_sem.at[side * 4 + 3],
            device_id={"dp": target}, device_id_type=MESH,
        )
        copy.start()
        b_copies.append(copy)
    attended = att[...].astype(jnp.bfloat16)
    for copy in w_copies:
        copy.wait()

    def p_copy(other):
        return pltpu.make_async_remote_copy(
            src_ref=p_send.at[other], dst_ref=p_recv.at[other],
            send_sem=ps_sem.at[other], recv_sem=pr_sem.at[other],
            device_id={"tensor": lax.rem(mine + other, shards)}, device_id_type=MESH,
        )

    def project(other, carry):
        product = jnp.dot(attended, w_v[lax.rem(mine + other, shards)], preferred_element_type=jnp.float32)
        p_send[other] = product.astype(jnp.bfloat16)
        p_copy(other).start()
        return carry

    @pl.when(mine < shards - 1)
    def _():
        pl.semaphore_wait(here_sem, shards - 1 - mine)

    lax.fori_loop(1, shards, project, 0)
    own = jnp.dot(attended, w_v[mine], preferred_element_type=jnp.float32)

    for copy in more_copies:
        copy.wait()
    for side in range(2):
        copy = pltpu.make_async_copy(first_recv.at[side], recv_ref.at[pl.ds(side * LINK, FIRST)], land_sem.at[side])
        copy.start()
        b_copies.append(copy)

    def gather_sums(other, total):
        p_copy(other).wait()
        return total + p_recv[other].astype(jnp.float32)

    summed = lax.fori_loop(1, shards, gather_sums, own)
    half = wide // 2
    r_copies = []
    for distance in range(SPAN):
        part = summed[distance * rows:(distance + 1) * rows]
        r_send[distance] = jnp.concatenate([part[:, :half], part[:, half:]], axis=0).astype(jnp.bfloat16)
        if distance == 0:
            copy = pltpu.make_async_copy(r_send.at[0], proj_ref.at[0], own_sem.at[1])
        else:
            copy = pltpu.make_async_remote_copy(
                src_ref=r_send.at[distance], dst_ref=proj_ref.at[distance],
                send_sem=rs_sem.at[distance], recv_sem=rr_sem.at[distance],
                device_id={"dp": peer(SPAN - distance)}, device_id_type=MESH,
            )
        copy.start()
        r_copies.append(copy)
    for copy in in_copies[5:]:
        copy.wait()
    load = heaviest(par_row[...], len_row[...], rings)
    over_ref[0] = sum(jnp.where(load > limit, 1, 0) for limit in (LINK, *(LINK + count for count in TIERS)))
    for side, (flow, mine_via, _, passed, _) in enumerate(sides):
        def put_left(at, carry, side=side, flow=flow, mine_via=mine_via, passed=passed):
            for at in [4 * at + more for more in range(4)]:
                left_send[side, at] = pool_v[grain_at(flow, LINK - mine_via - passed + at)]
            return carry

        lax.fori_loop(0, LEFT // 4, put_left, 0)
    left_copy = pltpu.make_async_copy(left_send, left_ref, land_sem.at[2])
    left_copy.start()
    for child in range(BEAMS):
        slot = slots[child]
        distance = slot >> 1
        length = len_ref[owners[child]]
        kept = jnp.where(distance == 3, choose(plan["up_id"], (y - 1) & 3), choose(plan["down_id"], (y + 1) & 3))
        before = jnp.int32(0)
        for other in range(BEAMS):
            if other != child:
                mate = (slots[other] >> 1 == distance) & (slots[other] < slot)
                counts = (owners[other] != owners[child]) & (owners[other] != kept)
                before = jnp.where(mate & counts, grains(len_ref[owners[other]]), before)
        far_before = jnp.where(owners[child] == choose(plan["first"], (y + 2) & 3), 0, choose(plan["cut"], (y + 2) & 3))
        before = jnp.where(distance == 2, far_before, before)
        from_up = choose(via_up, (y - 1) & 3), choose(via_up, (y + 2) & 3)
        from_down = choose(via_down, (y + 1) & 3), choose(via_down, (y + 2) & 3)
        near_via = jnp.where(distance == 3, from_up[0], from_down[0])
        near_pass = jnp.where(distance == 3, from_up[1], from_down[1])
        near_base = jnp.where(distance == 3, 0, LINK)
        split = jnp.where(distance == 2, from_up[1], FIRST - near_via) - before
        split = jnp.minimum(jnp.maximum(split, 0), PER_CHILD)
        start = jnp.where(distance == 2, FIRST + before, near_base + near_via + before)
        again = jnp.where(distance == 2, LINK + FIRST + before + split - from_up[1], start + split + near_pass)
        near = (distance == 1) | (distance == 3)
        until = LINK - near_via - near_pass - before
        until = jnp.where(near, jnp.minimum(jnp.maximum(until, 0), PER_CHILD), PER_CHILD)
        third = jnp.where(distance == 3, 0, LEFT) + near_via + near_pass + before + until - LINK
        held = near & (owners[child] == kept)
        kept_down = LINK + choose(via_down, (y + 1) & 3) - choose(plan["keep_down"], (y + 1) & 3)
        start = jnp.where(held, jnp.where(distance == 3, 0, kept_down), start)
        split = jnp.where(held, PER_CHILD, split)
        again = jnp.where(held, 0, again)
        until = jnp.where(held, PER_CHILD, until)
        third = jnp.where(held, 0, third)
        stays = distance == 0
        meta_ref[child * META] = length
        meta_ref[child * META + 1] = jnp.where(stays, 2 * LINK + (slot & 1) * PER_CHILD, start)
        meta_ref[child * META + 2] = jnp.where(stays, PER_CHILD, split)
        meta_ref[child * META + 3] = jnp.where(stays, 0, again)
        meta_ref[child * META + 4] = until
        meta_ref[child * META + 5] = jnp.where(near, third, 0)
        meta_ref[child * META + 6] = slot
    for copy in r_copies:
        copy.wait()
    for copy in b_copies:
        copy.wait()
    own_copy.wait()
    left_copy.wait()


def full_kernel(
    pool_ref, table_hbm, par_hbm, recv_ref,
    table_ref, par_ref, pool_v, stage,
    in_sem, pool_sem, own_sem, bs_sem, br_sem,
):
    me = lax.axis_index("dp")
    y = lax.rem(me, SPAN)
    base = me - y
    context = stage.shape[1] // MOST

    def peer(distance):
        return base + lax.rem(y + distance, SPAN)

    barrier = pltpu.get_barrier_semaphore()
    for distance in range(1, SPAN):
        pl.semaphore_signal(barrier, inc=1, device_id={"dp": peer(distance)}, device_id_type=MESH)
    in_copies = []
    for at, (source, target) in enumerate(((par_hbm, par_ref), (table_hbm, table_ref))):
        copy = pltpu.make_async_copy(source, target, in_sem.at[at])
        copy.start()
        in_copies.append(copy)
    pool_copy = pltpu.make_async_copy(pool_ref, pool_v, pool_sem)
    pool_copy.start()
    for copy in in_copies:
        copy.wait()
    pl.semaphore_wait(barrier, SPAN - 1)
    pool_copy.wait()
    copies = []
    for distance in (2, 1, 3, 0):
        served = served_beams(par_ref, me, peer(SPAN - distance))
        for rank in range(MOST):
            beam = served[rank]

            def put(index, carry, distance=distance, rank=rank, beam=beam):
                at = pl.multiple_of(rank * context + index * PAGE, PAGE)
                stage[distance, pl.ds(at, PAGE), :] = pool_v[table_ref[beam, index]]
                return carry

            lax.fori_loop(0, context // PAGE, put, 0)
            span = pl.ds(rank * context, context)
            if distance == 0:
                copy = pltpu.make_async_copy(stage.at[0, span], recv_ref.at[0, span], own_sem.at[rank])
            else:
                copy = pltpu.make_async_remote_copy(
                    src_ref=stage.at[distance, span], dst_ref=recv_ref.at[distance, span],
                    send_sem=bs_sem.at[distance * MOST + rank], recv_sem=br_sem.at[distance * MOST + rank],
                    device_id={"dp": peer(SPAN - distance)}, device_id_type=MESH,
                )
            copy.start()
            copies.append(copy)
    for copy in copies:
        copy.wait()


def finish_kernel(recv_ref, raw_ref, new_hbm, len_hbm, par_hbm, proj_ref, cache_ref, new_ref, len_ref, par_ref, edge, zeros, in_sem, out_sem):
    me = lax.axis_index("dp")
    pages = recv_ref.shape[1] // PAGE
    operands = ((par_hbm, par_ref), (len_hbm, len_ref), (new_hbm, new_ref))
    in_copies = [pltpu.make_async_copy(source, target, in_sem.at[at]) for at, (source, target) in enumerate(operands)]
    for copy in in_copies:
        copy.start()
    zeros[...] = jnp.zeros_like(zeros)
    for copy in in_copies:
        copy.wait()
    slots, owners = slots_of_children(par_ref, me)
    fresh = [new_ref[step].astype(jnp.float32) for step in range(STEPS)]
    for child in range(BEAMS):
        slot = slots[child]
        length = len_ref[owners[child]]
        first = length // PAGE
        last = (length + STEPS - 1) // PAGE

        def whole(index, carry, child=child, slot=slot):
            span = pl.ds(pl.multiple_of(index * PAGE, PAGE), PAGE)
            pltpu.make_async_copy(recv_ref.at[slot, span], cache_ref.at[child, span], out_sem).start()
            return carry

        def clear(index, carry, child=child):
            span = pl.ds(pl.multiple_of(index * PAGE, PAGE), PAGE)
            pltpu.make_async_copy(zeros, cache_ref.at[child, span], out_sem).start()
            return carry

        def fix(index, carry, child=child, slot=slot, length=length, first=first):
            at = pl.multiple_of(index * PAGE, PAGE)
            position = at + lax.broadcasted_iota(jnp.int32, (PAGE, 2 * HD), 0)
            page = recv_ref[slot, pl.ds(at, PAGE), :].astype(jnp.float32)
            page = jnp.where(position < length, page, 0.0)
            for step in range(STEPS):
                page = jnp.where(position == length + step, fresh[step][child:child + 1], page)
            edge[child * 2 + index - first] = page.astype(jnp.bfloat16)
            pltpu.make_async_copy(edge.at[child * 2 + index - first], cache_ref.at[child, pl.ds(at, PAGE)], out_sem).start()
            return carry

        lax.fori_loop(0, first, whole, 0)
        lax.fori_loop(last + 1, pages, clear, 0)
        lax.fori_loop(first, last + 1, fix, 0)

    rows = MOST * STEPS
    raw = []
    for distance in range(SPAN):
        part = raw_ref[distance].astype(jnp.float32)
        raw.append(jnp.concatenate([part[:rows], part[rows:]], axis=1))
    raw = jnp.concatenate(raw, axis=0).astype(jnp.bfloat16)
    row = lax.broadcasted_iota(jnp.int32, (BEAMS, SPAN * rows), 0)
    col = lax.broadcasted_iota(jnp.int32, (BEAMS, SPAN * rows), 1)
    slot_at = jnp.zeros_like(col)
    for child in range(BEAMS):
        slot_at = jnp.where(row == child, slots[child], slot_at)
    for step in range(STEPS):
        pick = jnp.where(col == slot_at * STEPS + step, 1.0, 0.0).astype(jnp.bfloat16)
        proj_ref[step] = jnp.dot(pick, raw, preferred_element_type=jnp.float32).astype(jnp.bfloat16)
    pltpu.make_async_copy(recv_ref, cache_ref, out_sem).wait()


def left_kernel(count, left_ref, got_ref, send_sem, recv_sem):
    me = lax.axis_index("dp")
    y = lax.rem(me, SPAN)
    targets = [me - y + lax.rem(y + ahead, SPAN) for ahead in (1, SPAN - 1)]
    barrier = pltpu.get_barrier_semaphore()
    for target in targets:
        pl.semaphore_signal(barrier, inc=1, device_id={"dp": target}, device_id_type=MESH)
    pl.semaphore_wait(barrier, 2)
    copies = []
    for side, target in enumerate(targets):
        copy = pltpu.make_async_remote_copy(
            src_ref=left_ref.at[side, pl.ds(0, count)], dst_ref=got_ref.at[side, pl.ds(0, count)],
            send_sem=send_sem.at[side], recv_sem=recv_sem.at[side],
            device_id={"dp": target}, device_id_type=MESH,
        )
        copy.start()
        copies.append(copy)
    for copy in copies:
        copy.wait()


def place_kernel(with_left, recv_ref, raw_ref, new_ref, meta_ref, *refs):
    left_ref = refs[0] if with_left else None
    proj_hbm, cache_ref, edge, zeros, proj_ref, out_sem, proj_sem = refs[-7:]
    total = recv_ref.shape[0]
    zeros[...] = jnp.zeros_like(zeros)
    fresh = [new_ref[step].astype(jnp.float32) for step in range(STEPS)]
    slots = [meta_ref[child * META + 6] for child in range(BEAMS)]
    per_child = cache_ref.shape[1]
    scale = GRAIN // TILE
    for child in range(BEAMS):
        length, start, split, again, until, third = (meta_ref[child * META + at] for at in range(6))
        first = length // TILE
        last = (length + STEPS - 1) // TILE
        until = jnp.minimum(until * scale, first) if with_left else first
        split = jnp.minimum(split * scale, until)

        def move(source, source_at, at, count, child=child):
            @pl.when(count > 0)
            def _():
                pltpu.make_async_copy(
                    source.at[pl.ds(source_at, count)], cache_ref.at[child, pl.ds(at, count)], out_sem
                ).start()

        move(recv_ref, start * scale, 0, split)
        move(recv_ref, again * scale, split, until - split)
        if with_left:
            move(left_ref, third * scale, until, first - until)
        move(zeros, 0, last + 1, per_child - 1 - last)
    for child in range(BEAMS):
        length, start, split, again, until, third = (meta_ref[child * META + at] for at in range(6))
        first = length // TILE
        last = (length + STEPS - 1) // TILE

        def fix(
            index, carry, child=child, length=length, first=first, start=start * scale, split=split * scale,
            again=again * scale, until=until * scale, third=third * scale,
        ):
            position = index * TILE + lax.broadcasted_iota(jnp.int32, (TILE, 2 * HD), 0)
            at = jnp.minimum(jnp.where(index < split, start + index, again + index - split), total - 1)
            part = recv_ref[at].astype(jnp.float32)
            if with_left:
                at = jnp.minimum(jnp.maximum(third + index - until, 0), left_ref.shape[0] - 1)
                part = jnp.where(index < until, part, left_ref[at].astype(jnp.float32))
            part = jnp.where(position < length, part, 0.0)
            for step in range(STEPS):
                part = jnp.where(position == length + step, fresh[step][child:child + 1], part)
            edge[child * 2 + index - first] = part.astype(jnp.bfloat16)
            pltpu.make_async_copy(edge.at[child * 2 + index - first], cache_ref.at[child, index], out_sem).start()
            return carry

        lax.fori_loop(first, last + 1, fix, 0)

    rows = MOST * STEPS
    raw = []
    for distance in range(SPAN):
        part = raw_ref[distance].astype(jnp.float32)
        raw.append(jnp.concatenate([part[:rows], part[rows:]], axis=1))
    raw = jnp.concatenate(raw, axis=0).astype(jnp.bfloat16)
    row = lax.broadcasted_iota(jnp.int32, (BEAMS, SPAN * rows), 0)
    col = lax.broadcasted_iota(jnp.int32, (BEAMS, SPAN * rows), 1)
    slot_at = jnp.zeros_like(col)
    for child in range(BEAMS):
        slot_at = jnp.where(row == child, slots[child], slot_at)
    for step in range(STEPS):
        pick = jnp.where(col == slot_at * STEPS + step, 1.0, 0.0).astype(jnp.bfloat16)
        proj_ref[step] = jnp.dot(pick, raw, preferred_element_type=jnp.float32).astype(jnp.bfloat16)
    proj_copy = pltpu.make_async_copy(proj_ref, proj_hbm, proj_sem)
    proj_copy.start()
    pltpu.make_async_copy(cache_ref, cache_ref, out_sem).wait()
    proj_copy.wait()


def local(shards, queries, new_kv, kv_pool, page_tables, lengths, parents, out_weight):
    wide = queries.shape[2]
    channels = kv_pool.shape[2]
    context = page_tables.shape[1] * kv_pool.shape[1]
    rows = MOST * STEPS
    vmem = pl.BlockSpec(memory_space=pltpu.VMEM)
    smem = pl.BlockSpec(memory_space=pltpu.SMEM)
    hbm = pl.BlockSpec(memory_space=pltpu.HBM)
    free = pl.BlockSpec(memory_space=pl.ANY)
    dma = pltpu.SemaphoreType.DMA
    bf16 = jnp.bfloat16

    def pinned(*operands):
        return [pltpu.with_memory_space_constraint(operand, pltpu.HBM) for operand in operands]

    grain_pool = kv_pool.reshape(-1, GRAIN, channels)
    with jax.named_scope("exchange"):
        recv, raw, left, meta, over = pl.pallas_call(
            exchange_kernel,
            out_shape=(
                jax.ShapeDtypeStruct((2 * LINK + MOST * PER_CHILD, GRAIN, channels), bf16),
                jax.ShapeDtypeStruct((SPAN, 2 * rows, wide // 2), bf16),
                jax.ShapeDtypeStruct((2, LEFT, GRAIN, channels), bf16),
                jax.ShapeDtypeStruct((BEAMS * META,), jnp.int32),
                jax.ShapeDtypeStruct((1,), jnp.int32),
            ),
            in_specs=[hbm] * 7,
            out_specs=(free, free, free, smem, smem),
            scratch_shapes=[
                pltpu.VMEM(queries.shape, bf16),
                pltpu.VMEM(new_kv.shape, bf16),
                pltpu.SMEM(page_tables.shape, jnp.int32),
                pltpu.SMEM(lengths.shape, jnp.int32),
                pltpu.SMEM(parents.shape, jnp.int32),
                pltpu.VMEM((1, *lengths.shape), jnp.int32),
                pltpu.VMEM((1, *parents.shape), jnp.int32),
                pltpu.VMEM(grain_pool.shape, bf16),
                pltpu.VMEM((shards, out_weight.shape[0], wide), bf16),
                pltpu.VMEM((SPAN, MOST * PER_CHILD, GRAIN, channels), bf16),
                pltpu.VMEM((2, FIRST, GRAIN, channels), bf16),
                pltpu.VMEM((2, FIRST, GRAIN, channels), bf16),
                pltpu.VMEM((2, REST, GRAIN, channels), bf16),
                pltpu.VMEM((2, LEFT, GRAIN, channels), bf16),
                pltpu.VMEM((SPAN, 2 * rows, (wide + channels) // 2), bf16),
                pltpu.VMEM((SPAN, 2 * rows, (wide + channels) // 2), bf16),
                pltpu.VMEM((SPAN * rows, wide), jnp.float32),
                pltpu.VMEM((shards, SPAN * rows, wide), bf16),
                pltpu.VMEM((shards, SPAN * rows, wide), bf16),
                pltpu.VMEM((SPAN, 2 * rows, wide // 2), bf16),
                pltpu.SMEM((SPAN * MOST,), jnp.int32),
                pltpu.SMEM((SPAN * MOST,), jnp.int32),
                dma((7,)), dma, dma((shards,)), dma((2,)), dma((3,)),
                dma((SPAN,)), dma((SPAN,)),
                dma((8,)), dma((8,)),
                dma((shards,)), dma((shards,)),
                dma((SPAN,)), dma((SPAN,)),
                pltpu.SemaphoreType.REGULAR,
            ],
            compiler_params=pltpu.CompilerParams(
                collective_id=0, has_side_effects=True, vmem_limit_bytes=48 * 1024 * 1024
            ),
            name="exchange",
        )(*pinned(queries, new_kv, grain_pool, page_tables, lengths, parents, out_weight))

    def place(*got):
        with jax.named_scope("place"):
            projected, cache = pl.pallas_call(
                functools.partial(place_kernel, len(got) > 0),
                out_shape=(
                    jax.ShapeDtypeStruct(queries.shape, bf16),
                    jax.ShapeDtypeStruct((BEAMS, context // TILE, TILE, channels), bf16),
                ),
                in_specs=[vmem, vmem, vmem, smem] + [vmem] * len(got),
                out_specs=(free, free),
                scratch_shapes=[
                    pltpu.VMEM((2 * BEAMS, TILE, channels), bf16),
                    pltpu.VMEM((context // TILE, TILE, channels), bf16),
                    pltpu.VMEM(queries.shape, bf16),
                    dma, dma,
                ],
                compiler_params=pltpu.CompilerParams(vmem_limit_bytes=24 * 1024 * 1024),
                name="place_left" if got else "place",
            )(recv.reshape(-1, TILE, channels), raw, new_kv, meta, *got)
            return projected, cache.reshape(BEAMS, context, channels)

    def placed():
        return place()

    def topped(count, number):
        with jax.named_scope("left"):
            got = pl.pallas_call(
                functools.partial(left_kernel, count),
                out_shape=jax.ShapeDtypeStruct(left.shape, bf16),
                in_specs=[free],
                out_specs=free,
                scratch_shapes=[dma((2,)), dma((2,))],
                compiler_params=pltpu.CompilerParams(
                    collective_id=number, has_side_effects=True, vmem_limit_bytes=4 * 1024 * 1024
                ),
                name="left",
            )(left)
        return place(got.reshape(-1, TILE, channels))

    def resent():
        with jax.named_scope("full"):
            whole = pl.pallas_call(
                full_kernel,
                out_shape=jax.ShapeDtypeStruct((SPAN, MOST * context, channels), bf16),
                in_specs=[hbm] * 3,
                out_specs=free,
                scratch_shapes=[
                    pltpu.SMEM(page_tables.shape, jnp.int32),
                    pltpu.SMEM(parents.shape, jnp.int32),
                    pltpu.VMEM(kv_pool.shape, bf16),
                    pltpu.VMEM((SPAN, MOST * context, channels), bf16),
                    dma((2,)), dma, dma((MOST,)),
                    dma((SPAN * MOST,)), dma((SPAN * MOST,)),
                ],
                compiler_params=pltpu.CompilerParams(
                    collective_id=1, has_side_effects=True, vmem_limit_bytes=24 * 1024 * 1024
                ),
                name="full",
            )(*pinned(kv_pool, page_tables, parents))
        with jax.named_scope("finish"):
            return pl.pallas_call(
                finish_kernel,
                out_shape=(
                    jax.ShapeDtypeStruct(queries.shape, bf16),
                    jax.ShapeDtypeStruct((BEAMS, context, channels), bf16),
                ),
                in_specs=[vmem, vmem, hbm, hbm, hbm],
                out_specs=(vmem, hbm),
                scratch_shapes=[
                    pltpu.VMEM(new_kv.shape, bf16),
                    pltpu.SMEM(lengths.shape, jnp.int32),
                    pltpu.SMEM(parents.shape, jnp.int32),
                    pltpu.VMEM((2 * BEAMS, PAGE, channels), bf16),
                    pltpu.VMEM((PAGE, channels), bf16),
                    dma((3,)), dma,
                ],
                compiler_params=pltpu.CompilerParams(vmem_limit_bytes=24 * 1024 * 1024),
                name="finish",
            )(whole.reshape(BEAMS, context, channels), raw, new_kv, lengths, parents)

    topping = [functools.partial(topped, count, 2 + at) for at, count in enumerate(TIERS)]
    return lax.switch(over[0], [placed, *topping, resent])


def solution(mesh):
    in_specs = (
        P(None, "dp", "tensor"),
        P(None, "dp", "tensor"),
        P("dp", None, "tensor"),
        P("dp", None),
        P(),
        P(),
        P("tensor", None),
    )
    out_specs = (P(None, "dp", "tensor"), P("dp", None, "tensor"))
    body = functools.partial(local, mesh.shape["tensor"])
    return jax.shard_map(body, mesh=mesh, in_specs=in_specs, out_specs=out_specs, check_vma=False)
```

```python
import functools

import jax
import jax.numpy as jnp
from jax import lax
from jax.experimental import pallas as pl
from jax.experimental.pallas import tpu as pltpu
from jax.sharding import PartitionSpec as P

HD = 128
SPAN = 4
MOST = 2
BEAMS = 8
STEPS = 4
PAGE = 128
PAGES = 8
GRAIN = 16
PER_CHILD = 64
PER_PAGE = PAGE // GRAIN
PAGE_BITS = PER_PAGE.bit_length() - 1
TILE = 16
VIA = 72
MORE = 28
REST = 72
TIERS = (8, 20, 48)
LEFT = TIERS[-1]
FIRST = VIA + MORE
LINK = FIRST + REST
META = 7
MESH = pl.DeviceIdType.MESH


def grains(length):
    return (length + (GRAIN - 1)) // GRAIN


def choose(values, index):
    out = values[0]
    for at in range(1, len(values)):
        out = jnp.where(index == at, values[at], out)
    return out


def balanced(up, far, down, keep_up, keep_down):
    least = [jnp.maximum(keep_up[i], far[i] - VIA) for i in range(SPAN)]
    most = [jnp.minimum(far[i] - keep_down[i], VIA) for i in range(SPAN)]
    via_up = [jnp.minimum(jnp.maximum(far[i] >> 1, least[i]), most[i]) for i in range(SPAN)]
    for at in (*range(SPAN), *range(SPAN)):
        via_down = [far[i] - via_up[i] for i in range(SPAN)]
        nxt, prv = (at + 1) % SPAN, (at - 1) % SPAN
        load_up = jnp.maximum(up[at] + via_up[prv], up[nxt] + via_up[nxt])
        load_down = jnp.maximum(down[at] + via_down[nxt], down[prv] + via_down[prv])
        best = (load_down + far[at] - load_up) >> 1
        via_up[at] = jnp.minimum(jnp.maximum(best, least[at]), most[at])
    via_down = [far[i] - via_up[i] for i in range(SPAN)]
    return via_up, via_down


def planned(flows):
    names = ("up", "down", "far", "first", "second", "cut", "up_id", "down_id", "keep_up", "keep_down")
    plan = {name: [] for name in names}
    for at in range(SPAN):
        u0, u1, gu0, gu1 = flows[at][1]
        f0, f1, gf0, gf1 = flows[at][2]
        d0, d1, gd0, gd1 = flows[at][3]
        gu1 = jnp.where(u0 == u1, 0, gu1)
        gf1 = jnp.where(f0 == f1, 0, gf1)
        gd1 = jnp.where(d0 == d1, 0, gd1)

        def shared(parent, count, one, two):
            return jnp.where((parent == one) | (parent == two), count, 0)

        straight = shared(f0, gf0, u0, u1) + shared(f1, gf1, d0, d1)
        crossed = shared(f1, gf1, u0, u1) + shared(f0, gf0, d0, d1)
        swap = crossed > straight
        first, second = jnp.where(swap, f1, f0), jnp.where(swap, f0, f1)
        cut, rest = jnp.where(swap, gf1, gf0), jnp.where(swap, gf0, gf1)
        keep_up, keep_down = shared(first, cut, u0, u1), shared(second, rest, d0, d1)
        values = (
            gu0 + gu1 - keep_up, gd0 + gd1 - keep_down, gf0 + gf1, first, second, cut,
            jnp.where(keep_up > 0, first, -1), jnp.where(keep_down > 0, second, -1), keep_up, keep_down,
        )
        for name, value in zip(names, values):
            plan[name].append(value)
    plan["via_up"], plan["via_down"] = balanced(
        plan["up"], plan["far"], plan["down"], plan["keep_up"], plan["keep_down"]
    )
    return plan


def ring_plan(parents, lengths, ring):
    flows = [[None] * SPAN for _ in range(SPAN)]
    for target in range(SPAN):
        owners = [parents[(ring * SPAN + target) * BEAMS + child] for child in range(BEAMS)]
        sources = [(owner >> 3) & (SPAN - 1) for owner in owners]
        for at in range(SPAN):
            if at != target:
                one, two = owners[0], owners[0]
                for child in range(1, BEAMS):
                    two = jnp.where(sources[child] == at, owners[child], two)
                one = owners[BEAMS - 1]
                for child in range(BEAMS - 2, -1, -1):
                    one = jnp.where(sources[child] == at, owners[child], one)
                flows[at][(target - at) % SPAN] = (one, two, grains(lengths[one]), grains(lengths[two]))
    return {**planned(flows), "flows": flows}


def heaviest(parents, lengths, rings):
    beams = rings * SPAN * BEAMS
    counts = grains(lengths).astype(jnp.float32).astype(jnp.bfloat16)
    beam = lax.broadcasted_iota(jnp.int32, (beams, beams), 0)
    chosen = jnp.where(beam == parents, 1.0, 0.0).astype(jnp.bfloat16)
    counts = jnp.dot(jnp.broadcast_to(counts, (16, beams)), chosen, preferred_element_type=jnp.float32)[:1]
    lane = lax.broadcasted_iota(jnp.int32, (1, beams), 1)
    source = (parents // BEAMS) % SPAN
    rank = jnp.zeros_like(lane)
    for back in range(1, BEAMS):
        rank = rank + jnp.where((pltpu.roll(source, back, 1) == source) & (lane % BEAMS >= back), 1, 0)
    names = (parents % (SPAN * BEAMS)).astype(jnp.float32)
    rows = [
        jnp.where((source == at) & (rank == order), value, 0.0)
        for value in (names, counts) for at in range(SPAN) for order in range(MOST)
    ]
    rows = jnp.concatenate(rows, axis=0).astype(jnp.bfloat16)
    child = lax.broadcasted_iota(jnp.int32, (beams, 128), 0)
    ring = lax.broadcasted_iota(jnp.int32, (beams, 128), 1)
    flows = [[None] * SPAN for _ in range(SPAN)]
    for target in range(SPAN):
        member = (child // BEAMS % SPAN == target) & (child // (BEAMS * SPAN) == ring)
        member = jnp.where(member, 1.0, 0.0).astype(jnp.bfloat16)
        found = jnp.dot(rows, member, preferred_element_type=jnp.float32).astype(jnp.int32)
        for at in range(SPAN):
            wanted = (at * MOST, at * MOST + 1, (SPAN + at) * MOST, (SPAN + at) * MOST + 1)
            flows[at][(target - at) % SPAN] = tuple(found[one:one + 1] for one in wanted)
    plan = planned(flows)
    out = jnp.zeros_like(plan["far"][0])
    for at in range(SPAN):
        load_up = plan["up"][at] + plan["via_up"][at] + plan["via_up"][(at - 1) % SPAN]
        load_down = plan["down"][at] + plan["via_down"][at] + plan["via_down"][(at + 1) % SPAN]
        out = jnp.maximum(out, jnp.maximum(load_up, load_down))
    return jnp.max(out)


def slots_of_children(parents, me):
    taken = [jnp.int32(0) for _ in range(SPAN)]
    slots, owners = [], []
    for child in range(BEAMS):
        parent = parents[me * BEAMS + child]
        apart = jnp.bitwise_and(parent // BEAMS - me, SPAN - 1)
        slot = jnp.int32(0)
        for distance in range(SPAN):
            hit = apart == distance
            slot = jnp.where(hit, distance * MOST + taken[distance], slot)
            taken[distance] = taken[distance] + hit.astype(jnp.int32)
        slots.append(slot)
        owners.append(parent)
    return slots, owners


def served_beams(parents, me, target):
    count = jnp.int32(0)
    beams = [jnp.int32(0) for _ in range(MOST)]
    for child in range(BEAMS):
        parent = parents[target * BEAMS + child]
        hit = parent // BEAMS == me
        for rank in range(MOST):
            beams[rank] = jnp.where(hit & (count == rank), parent % BEAMS, beams[rank])
        count = count + hit.astype(jnp.int32)
    return beams


def exchange_kernel(
    q_hbm, new_hbm, pool_ref, table_hbm, len_hbm, par_hbm, w_ref,
    recv_ref, proj_ref, left_ref, meta_ref, over_ref,
    q_ref, new_ref, table_ref, len_ref, par_ref, len_row, par_row,
    pool_v, w_v, stage, first_send, first_recv, rest_send, left_send, q_send, q_recv, att, p_send, p_recv, r_send, lens, beams,
    in_sem, pool_sem, w_sem, own_sem, land_sem, qs_sem, qr_sem, bs_sem, br_sem, ps_sem, pr_sem, rs_sem, rr_sem, here_sem,
):
    me = lax.axis_index("dp")
    mine = lax.axis_index("tensor")
    shards = lax.axis_size("tensor")
    y = lax.rem(me, SPAN)
    base = me - y
    context = stage.shape[1] * GRAIN // MOST
    rings = lax.axis_size("dp") // SPAN
    wide = q_hbm.shape[2]
    heads = wide // HD
    rows = MOST * STEPS

    def peer(distance):
        return base + lax.rem(y + distance, SPAN)

    pairs = (
        (par_hbm, par_ref), (len_hbm, len_ref), (table_hbm, table_ref), (q_hbm, q_ref), (new_hbm, new_ref),
        (par_hbm, par_row.at[0]), (len_hbm, len_row.at[0]),
    )
    in_copies = [pltpu.make_async_copy(source, target, in_sem.at[at]) for at, (source, target) in enumerate(pairs)]
    pool_copy = pltpu.make_async_copy(pool_ref, pool_v, pool_sem)
    for copy in (*in_copies[:3], pool_copy, *in_copies[3:]):
        copy.start()
    barrier = pltpu.get_barrier_semaphore()
    for distance in range(1, SPAN):
        pl.semaphore_signal(barrier, inc=1, device_id={"dp": peer(distance)}, device_id_type=MESH)
    for other in range(1, shards):
        @pl.when(mine + other < shards)
        def _(other=other):
            pl.semaphore_signal(barrier, inc=1, device_id={"tensor": mine + other}, device_id_type=MESH)
    for copy in in_copies[:3]:
        copy.wait()

    slots, owners = slots_of_children(par_ref, me)
    for copy in in_copies[3:5]:
        copy.wait()
    row = lax.broadcasted_iota(jnp.int32, (SPAN * rows, BEAMS), 0)
    col = lax.broadcasted_iota(jnp.int32, (SPAN * rows, BEAMS), 1)
    slot_at = jnp.zeros_like(col)
    for child in range(BEAMS):
        slot_at = jnp.where(col == child, slots[child], slot_at)
    q_sorted = jnp.zeros((SPAN * rows, wide), jnp.float32)
    new_sorted = jnp.zeros((SPAN * rows, 2 * HD), jnp.float32)
    for step in range(STEPS):
        pick = jnp.where((row // STEPS == slot_at) & (row % STEPS == step), 1.0, 0.0).astype(jnp.bfloat16)
        q_sorted += jnp.dot(pick, q_ref[step], preferred_element_type=jnp.float32)
        new_sorted += jnp.dot(pick, new_ref[step], preferred_element_type=jnp.float32)
    both = jnp.concatenate([q_sorted, new_sorted], axis=1)
    half = both.shape[1] // 2
    for distance in range(SPAN):
        part = both[distance * rows:(distance + 1) * rows]
        part = jnp.concatenate([part[:, :half], part[:, half:]], axis=0).astype(jnp.bfloat16)
        if distance == 0:
            q_recv[0] = part
        else:
            q_send[distance] = part

    plan = ring_plan(par_ref, len_ref, me >> 2)
    via_up, via_down = plan["via_up"], plan["via_down"]
    flows = {}
    for ahead in (1, 3):
        first, second, cut = (choose([plan["flows"][at][ahead][of] for at in range(SPAN)], y) for of in range(3))
        flows[ahead] = (first & 7, second & 7, cut)
    for ahead, kept in ((1, "up_id"), (3, "down_id")):
        first, second, cut = flows[ahead]
        flows[ahead] = (first, second, jnp.where(me * BEAMS + first == choose(plan[kept], y), 0, cut))
    flows[2] = (choose(plan["first"], y) & 7, choose(plan["second"], y) & 7, choose(plan["cut"], y))

    def grain_at(flow, number):
        first, second, cut = flow
        later = number >= cut
        number = jnp.where(later, number - cut, number)
        number = jnp.minimum(jnp.maximum(number, 0), PER_CHILD - 1)
        return table_ref[jnp.where(later, second, first), number >> PAGE_BITS] * PER_PAGE + (number & (PER_PAGE - 1))

    sides = (
        (flows[1], choose(via_up, y), jnp.int32(0), choose(via_up, (y - 1) & 3), peer(1)),
        (flows[3], choose(via_down, y), choose(via_up, y), choose(via_down, (y + 1) & 3), peer(3)),
    )
    pl.semaphore_wait(barrier, SPAN - 1 + mine)
    q_copies = []
    for distance in range(1, SPAN):
        copy = pltpu.make_async_remote_copy(
            src_ref=q_send.at[distance], dst_ref=q_recv.at[distance],
            send_sem=qs_sem.at[distance], recv_sem=qr_sem.at[distance],
            device_id={"dp": peer(distance)}, device_id_type=MESH,
        )
        copy.start()
        q_copies.append(copy)
    pool_copy.wait()
    b_copies = []
    cuts = (0, 24, VIA, FIRST)

    def send_part(part):
        for side, (flow, mine_via, skip, _, target) in enumerate(sides):
            def put(at, carry, side=side, flow=flow, mine_via=mine_via, skip=skip):
                for at in [4 * at + more for more in range(4)]:
                    far = at < mine_via
                    chosen = tuple(jnp.where(far, one, two) for one, two in zip(flows[2], flow))
                    number = jnp.where(far, skip + at, at - mine_via)
                    first_send[side, at] = pool_v[grain_at(chosen, number)]
                return carry

            lax.fori_loop(cuts[part] // 4, cuts[part + 1] // 4, put, 0)
            span = pl.ds(cuts[part], cuts[part + 1] - cuts[part])
            copy = pltpu.make_async_remote_copy(
                src_ref=first_send.at[side, span], dst_ref=first_recv.at[side, span],
                send_sem=bs_sem.at[side * 4 + part], recv_sem=br_sem.at[side * 4 + part],
                device_id={"dp": target}, device_id_type=MESH,
            )
            copy.start()
            b_copies.append(copy)

    send_part(0)
    for other in range(1, shards):
        @pl.when(mine >= other)
        def _(other=other):
            pl.semaphore_signal(here_sem, inc=1, device_id={"tensor": mine - other}, device_id_type=MESH)
    send_part(1)
    send_part(2)
    for ahead in range(SPAN):
        served = served_beams(par_ref, me, peer(ahead))
        for rank in range(MOST):
            at = (SPAN - ahead) % SPAN * MOST + rank
            beams[at] = served[rank]
            lens[at] = len_ref[me * BEAMS + served[rank]]
    w_copies = []
    for block in range(shards):
        copy = pltpu.make_async_copy(w_ref.at[:, pl.ds(block * wide, wide)], w_v.at[block], w_sem.at[block])
        copy.start()
        w_copies.append(copy)

    def put_all(index, carry):
        slot = index // PAGES
        page = table_ref[beams[slot], index % PAGES]
        at = (index % (MOST * PAGES)) * PER_PAGE
        stage[index // (MOST * PAGES), pl.ds(at, PER_PAGE)] = pool_v[pl.ds(page * PER_PAGE, PER_PAGE)]
        return carry

    lax.fori_loop(0, SPAN * MOST * PAGES, put_all, 0)
    own_copy = pltpu.make_async_copy(stage.at[0], recv_ref.at[pl.ds(2 * LINK, MOST * PER_CHILD)], own_sem.at[0])
    own_copy.start()

    for copy in q_copies:
        copy.wait()

    def attend(distance):
        message = q_recv[distance].astype(jnp.float32)
        message = jnp.concatenate([message[:rows], message[rows:]], axis=1)
        q_rows = jnp.concatenate([message[:, h * HD:(h + 1) * HD] for h in range(heads)], axis=0).astype(jnp.bfloat16)
        fresh = message[:, wide:].astype(jnp.bfloat16)
        old_len = lens[distance * MOST]
        last_len = lens[distance * MOST + 1]
        contract = (((1,), (1,)), ((), ()))
        scale = HD ** -0.5
        half = MOST * PER_CHILD // 2
        keys = [stage[distance, pl.ds(rank * half, half), :, 0:HD].reshape(context, HD) for rank in range(MOST)]
        scores = [lax.dot_general(q_rows, key, contract, preferred_element_type=jnp.float32) for key in keys]
        rank_at = lax.broadcasted_iota(jnp.int32, scores[0].shape, 0) // STEPS % MOST
        scores = jnp.where(rank_at == 0, scores[0], scores[1]) * scale
        fresh_scores = lax.dot_general(q_rows, fresh[:, :HD], contract, preferred_element_type=jnp.float32) * scale
        position = lax.broadcasted_iota(jnp.int32, scores.shape, 1)
        limit = jnp.where(rank_at == 0, old_len, last_len)
        scores = jnp.where(position < limit, scores, -1e30)
        f_row = lax.broadcasted_iota(jnp.int32, fresh_scores.shape, 0)
        f_col = lax.broadcasted_iota(jnp.int32, fresh_scores.shape, 1)
        seen = (f_row // STEPS % MOST == f_col // STEPS) & (f_col % STEPS <= f_row % STEPS)
        fresh_scores = jnp.where(seen, fresh_scores, -1e30)
        top = jnp.maximum(jnp.max(scores, axis=1, keepdims=True), jnp.max(fresh_scores, axis=1, keepdims=True))
        exp_old = jnp.exp(scores - top)
        exp_new = jnp.exp(fresh_scores - top)
        total = jnp.sum(exp_old, axis=1, keepdims=True) + jnp.sum(exp_new, axis=1, keepdims=True)
        share = 1.0 / total
        w_old = (exp_old * share).astype(jnp.bfloat16)
        w_new = (exp_new * share).astype(jnp.bfloat16)
        values = [stage[distance, pl.ds(rank * half, half), :, HD:2 * HD].reshape(context, HD) for rank in range(MOST)]
        out = [jnp.dot(w_old, value, preferred_element_type=jnp.float32) for value in values]
        out = jnp.where(rank_at[:, :HD] == 0, out[0], out[1])
        out += jnp.dot(w_new, fresh[:, HD:], preferred_element_type=jnp.float32)
        out = jnp.concatenate([out[h * rows:(h + 1) * rows] for h in range(heads)], axis=1)
        att[pl.ds(pl.multiple_of(distance * rows, rows), rows), :] = out

    def attend_two(at, carry):
        attend(2 * at)
        attend(2 * at + 1)
        return carry

    lax.fori_loop(0, SPAN // 2, attend_two, 0)
    for copy in b_copies[:4]:
        copy.wait()
    more_copies = b_copies[4:]
    b_copies = []
    for side, (flow, mine_via, _, passed, target) in enumerate(sides):
        def put_passed(at, carry, side=side, flow=flow, mine_via=mine_via, passed=passed):
            for at in [4 * at + more for more in range(4)]:
                here = pool_v[grain_at(flow, FIRST - mine_via + at - passed)]
                rest_send[side, at] = jnp.where(at < passed, first_recv[side, at], here)
            return carry

        lax.fori_loop(0, REST // 4, put_passed, 0)
        copy = pltpu.make_async_remote_copy(
            src_ref=rest_send.at[side], dst_ref=recv_ref.at[pl.ds(side * LINK + FIRST, REST)],
            send_sem=bs_sem.at[side * 4 + 3], recv_sem=br_sem.at[side * 4 + 3],
            device_id={"dp": target}, device_id_type=MESH,
        )
        copy.start()
        b_copies.append(copy)
    attended = att[...].astype(jnp.bfloat16)
    for copy in w_copies:
        copy.wait()

    def p_copy(other):
        return pltpu.make_async_remote_copy(
            src_ref=p_send.at[other], dst_ref=p_recv.at[other],
            send_sem=ps_sem.at[other], recv_sem=pr_sem.at[other],
            device_id={"tensor": lax.rem(mine + other, shards)}, device_id_type=MESH,
        )

    def project(other, carry):
        product = jnp.dot(attended, w_v[lax.rem(mine + other, shards)], preferred_element_type=jnp.float32)
        p_send[other] = product.astype(jnp.bfloat16)
        p_copy(other).start()
        return carry

    @pl.when(mine < shards - 1)
    def _():
        pl.semaphore_wait(here_sem, shards - 1 - mine)

    lax.fori_loop(1, shards, project, 0)
    own = jnp.dot(attended, w_v[mine], preferred_element_type=jnp.float32)

    for copy in more_copies:
        copy.wait()
    for side in range(2):
        copy = pltpu.make_async_copy(first_recv.at[side], recv_ref.at[pl.ds(side * LINK, FIRST)], land_sem.at[side])
        copy.start()
        b_copies.append(copy)

    def gather_sums(other, total):
        p_copy(other).wait()
        return total + p_recv[other].astype(jnp.float32)

    summed = lax.fori_loop(1, shards, gather_sums, own)
    half = wide // 2
    r_copies = []
    for distance in range(SPAN):
        part = summed[distance * rows:(distance + 1) * rows]
        r_send[distance] = jnp.concatenate([part[:, :half], part[:, half:]], axis=0).astype(jnp.bfloat16)
        if distance == 0:
            copy = pltpu.make_async_copy(r_send.at[0], proj_ref.at[0], own_sem.at[1])
        else:
            copy = pltpu.make_async_remote_copy(
                src_ref=r_send.at[distance], dst_ref=proj_ref.at[distance],
                send_sem=rs_sem.at[distance], recv_sem=rr_sem.at[distance],
                device_id={"dp": peer(SPAN - distance)}, device_id_type=MESH,
            )
        copy.start()
        r_copies.append(copy)
    for copy in in_copies[5:]:
        copy.wait()
    load = heaviest(par_row[...], len_row[...], rings)
    over_ref[0] = sum(jnp.where(load > limit, 1, 0) for limit in (LINK, *(LINK + count for count in TIERS)))
    for side, (flow, mine_via, _, passed, _) in enumerate(sides):
        def put_left(at, carry, side=side, flow=flow, mine_via=mine_via, passed=passed):
            for at in [4 * at + more for more in range(4)]:
                left_send[side, at] = pool_v[grain_at(flow, LINK - mine_via - passed + at)]
            return carry

        lax.fori_loop(0, LEFT // 4, put_left, 0)
    left_copy = pltpu.make_async_copy(left_send, left_ref, land_sem.at[2])
    left_copy.start()
    for child in range(BEAMS):
        slot = slots[child]
        distance = slot >> 1
        length = len_ref[owners[child]]
        kept = jnp.where(distance == 3, choose(plan["up_id"], (y - 1) & 3), choose(plan["down_id"], (y + 1) & 3))
        before = jnp.int32(0)
        for other in range(BEAMS):
            if other != child:
                mate = (slots[other] >> 1 == distance) & (slots[other] < slot)
                counts = (owners[other] != owners[child]) & (owners[other] != kept)
                before = jnp.where(mate & counts, grains(len_ref[owners[other]]), before)
        far_before = jnp.where(owners[child] == choose(plan["first"], (y + 2) & 3), 0, choose(plan["cut"], (y + 2) & 3))
        before = jnp.where(distance == 2, far_before, before)
        from_up = choose(via_up, (y - 1) & 3), choose(via_up, (y + 2) & 3)
        from_down = choose(via_down, (y + 1) & 3), choose(via_down, (y + 2) & 3)
        near_via = jnp.where(distance == 3, from_up[0], from_down[0])
        near_pass = jnp.where(distance == 3, from_up[1], from_down[1])
        near_base = jnp.where(distance == 3, 0, LINK)
        split = jnp.where(distance == 2, from_up[1], FIRST - near_via) - before
        split = jnp.minimum(jnp.maximum(split, 0), PER_CHILD)
        start = jnp.where(distance == 2, FIRST + before, near_base + near_via + before)
        again = jnp.where(distance == 2, LINK + FIRST + before + split - from_up[1], start + split + near_pass)
        near = (distance == 1) | (distance == 3)
        until = LINK - near_via - near_pass - before
        until = jnp.where(near, jnp.minimum(jnp.maximum(until, 0), PER_CHILD), PER_CHILD)
        third = jnp.where(distance == 3, 0, LEFT) + near_via + near_pass + before + until - LINK
        held = near & (owners[child] == kept)
        kept_down = LINK + choose(via_down, (y + 1) & 3) - choose(plan["keep_down"], (y + 1) & 3)
        start = jnp.where(held, jnp.where(distance == 3, 0, kept_down), start)
        split = jnp.where(held, PER_CHILD, split)
        again = jnp.where(held, 0, again)
        until = jnp.where(held, PER_CHILD, until)
        third = jnp.where(held, 0, third)
        stays = distance == 0
        meta_ref[child * META] = length
        meta_ref[child * META + 1] = jnp.where(stays, 2 * LINK + (slot & 1) * PER_CHILD, start)
        meta_ref[child * META + 2] = jnp.where(stays, PER_CHILD, split)
        meta_ref[child * META + 3] = jnp.where(stays, 0, again)
        meta_ref[child * META + 4] = until
        meta_ref[child * META + 5] = jnp.where(near, third, 0)
        meta_ref[child * META + 6] = slot
    for copy in r_copies:
        copy.wait()
    for copy in b_copies:
        copy.wait()
    own_copy.wait()
    left_copy.wait()


def full_kernel(
    pool_ref, table_hbm, par_hbm, recv_ref,
    table_ref, par_ref, pool_v, stage,
    in_sem, pool_sem, own_sem, bs_sem, br_sem,
):
    me = lax.axis_index("dp")
    y = lax.rem(me, SPAN)
    base = me - y
    context = stage.shape[1] // MOST

    def peer(distance):
        return base + lax.rem(y + distance, SPAN)

    barrier = pltpu.get_barrier_semaphore()
    for distance in range(1, SPAN):
        pl.semaphore_signal(barrier, inc=1, device_id={"dp": peer(distance)}, device_id_type=MESH)
    in_copies = []
    for at, (source, target) in enumerate(((par_hbm, par_ref), (table_hbm, table_ref))):
        copy = pltpu.make_async_copy(source, target, in_sem.at[at])
        copy.start()
        in_copies.append(copy)
    pool_copy = pltpu.make_async_copy(pool_ref, pool_v, pool_sem)
    pool_copy.start()
    for copy in in_copies:
        copy.wait()
    pl.semaphore_wait(barrier, SPAN - 1)
    pool_copy.wait()
    copies = []
    for distance in (2, 1, 3, 0):
        served = served_beams(par_ref, me, peer(SPAN - distance))
        for rank in range(MOST):
            beam = served[rank]

            def put(index, carry, distance=distance, rank=rank, beam=beam):
                at = pl.multiple_of(rank * context + index * PAGE, PAGE)
                stage[distance, pl.ds(at, PAGE), :] = pool_v[table_ref[beam, index]]
                return carry

            lax.fori_loop(0, context // PAGE, put, 0)
            span = pl.ds(rank * context, context)
            if distance == 0:
                copy = pltpu.make_async_copy(stage.at[0, span], recv_ref.at[0, span], own_sem.at[rank])
            else:
                copy = pltpu.make_async_remote_copy(
                    src_ref=stage.at[distance, span], dst_ref=recv_ref.at[distance, span],
                    send_sem=bs_sem.at[distance * MOST + rank], recv_sem=br_sem.at[distance * MOST + rank],
                    device_id={"dp": peer(SPAN - distance)}, device_id_type=MESH,
                )
            copy.start()
            copies.append(copy)
    for copy in copies:
        copy.wait()


def finish_kernel(recv_ref, raw_ref, new_hbm, len_hbm, par_hbm, proj_ref, cache_ref, new_ref, len_ref, par_ref, edge, zeros, in_sem, out_sem):
    me = lax.axis_index("dp")
    pages = recv_ref.shape[1] // PAGE
    operands = ((par_hbm, par_ref), (len_hbm, len_ref), (new_hbm, new_ref))
    in_copies = [pltpu.make_async_copy(source, target, in_sem.at[at]) for at, (source, target) in enumerate(operands)]
    for copy in in_copies:
        copy.start()
    zeros[...] = jnp.zeros_like(zeros)
    for copy in in_copies:
        copy.wait()
    slots, owners = slots_of_children(par_ref, me)
    fresh = [new_ref[step].astype(jnp.float32) for step in range(STEPS)]
    for child in range(BEAMS):
        slot = slots[child]
        length = len_ref[owners[child]]
        first = length // PAGE
        last = (length + STEPS - 1) // PAGE

        def whole(index, carry, child=child, slot=slot):
            span = pl.ds(pl.multiple_of(index * PAGE, PAGE), PAGE)
            pltpu.make_async_copy(recv_ref.at[slot, span], cache_ref.at[child, span], out_sem).start()
            return carry

        def clear(index, carry, child=child):
            span = pl.ds(pl.multiple_of(index * PAGE, PAGE), PAGE)
            pltpu.make_async_copy(zeros, cache_ref.at[child, span], out_sem).start()
            return carry

        def fix(index, carry, child=child, slot=slot, length=length, first=first):
            at = pl.multiple_of(index * PAGE, PAGE)
            position = at + lax.broadcasted_iota(jnp.int32, (PAGE, 2 * HD), 0)
            page = recv_ref[slot, pl.ds(at, PAGE), :].astype(jnp.float32)
            page = jnp.where(position < length, page, 0.0)
            for step in range(STEPS):
                page = jnp.where(position == length + step, fresh[step][child:child + 1], page)
            edge[child * 2 + index - first] = page.astype(jnp.bfloat16)
            pltpu.make_async_copy(edge.at[child * 2 + index - first], cache_ref.at[child, pl.ds(at, PAGE)], out_sem).start()
            return carry

        lax.fori_loop(0, first, whole, 0)
        lax.fori_loop(last + 1, pages, clear, 0)
        lax.fori_loop(first, last + 1, fix, 0)

    rows = MOST * STEPS
    raw = []
    for distance in range(SPAN):
        part = raw_ref[distance].astype(jnp.float32)
        raw.append(jnp.concatenate([part[:rows], part[rows:]], axis=1))
    raw = jnp.concatenate(raw, axis=0).astype(jnp.bfloat16)
    row = lax.broadcasted_iota(jnp.int32, (BEAMS, SPAN * rows), 0)
    col = lax.broadcasted_iota(jnp.int32, (BEAMS, SPAN * rows), 1)
    slot_at = jnp.zeros_like(col)
    for child in range(BEAMS):
        slot_at = jnp.where(row == child, slots[child], slot_at)
    for step in range(STEPS):
        pick = jnp.where(col == slot_at * STEPS + step, 1.0, 0.0).astype(jnp.bfloat16)
        proj_ref[step] = jnp.dot(pick, raw, preferred_element_type=jnp.float32).astype(jnp.bfloat16)
    pltpu.make_async_copy(recv_ref, cache_ref, out_sem).wait()


def left_kernel(count, left_ref, got_ref, send_sem, recv_sem):
    me = lax.axis_index("dp")
    y = lax.rem(me, SPAN)
    targets = [me - y + lax.rem(y + ahead, SPAN) for ahead in (1, SPAN - 1)]
    barrier = pltpu.get_barrier_semaphore()
    for target in targets:
        pl.semaphore_signal(barrier, inc=1, device_id={"dp": target}, device_id_type=MESH)
    pl.semaphore_wait(barrier, 2)
    copies = []
    for side, target in enumerate(targets):
        copy = pltpu.make_async_remote_copy(
            src_ref=left_ref.at[side, pl.ds(0, count)], dst_ref=got_ref.at[side, pl.ds(0, count)],
            send_sem=send_sem.at[side], recv_sem=recv_sem.at[side],
            device_id={"dp": target}, device_id_type=MESH,
        )
        copy.start()
        copies.append(copy)
    for copy in copies:
        copy.wait()


def place_kernel(with_left, recv_ref, raw_ref, new_ref, meta_ref, *refs):
    left_ref = refs[0] if with_left else None
    proj_hbm, cache_ref, edge, zeros, proj_ref, out_sem, proj_sem = refs[-7:]
    total = recv_ref.shape[0]
    zeros[...] = jnp.zeros_like(zeros)
    fresh = [new_ref[step].astype(jnp.float32) for step in range(STEPS)]
    slots = [meta_ref[child * META + 6] for child in range(BEAMS)]
    per_child = cache_ref.shape[1]
    scale = GRAIN // TILE
    for child in range(BEAMS):
        length, start, split, again, until, third = (meta_ref[child * META + at] for at in range(6))
        first = length // TILE
        last = (length + STEPS - 1) // TILE
        until = jnp.minimum(until * scale, first) if with_left else first
        split = jnp.minimum(split * scale, until)

        def move(source, source_at, at, count, child=child):
            @pl.when(count > 0)
            def _():
                pltpu.make_async_copy(
                    source.at[pl.ds(source_at, count)], cache_ref.at[child, pl.ds(at, count)], out_sem
                ).start()

        move(recv_ref, start * scale, 0, split)
        move(recv_ref, again * scale, split, until - split)
        if with_left:
            move(left_ref, third * scale, until, first - until)
        move(zeros, 0, last + 1, per_child - 1 - last)
    for child in range(BEAMS):
        length, start, split, again, until, third = (meta_ref[child * META + at] for at in range(6))
        first = length // TILE
        last = (length + STEPS - 1) // TILE

        def fix(
            index, carry, child=child, length=length, first=first, start=start * scale, split=split * scale,
            again=again * scale, until=until * scale, third=third * scale,
        ):
            position = index * TILE + lax.broadcasted_iota(jnp.int32, (TILE, 2 * HD), 0)
            at = jnp.minimum(jnp.where(index < split, start + index, again + index - split), total - 1)
            part = recv_ref[at].astype(jnp.float32)
            if with_left:
                at = jnp.minimum(jnp.maximum(third + index - until, 0), left_ref.shape[0] - 1)
                part = jnp.where(index < until, part, left_ref[at].astype(jnp.float32))
            part = jnp.where(position < length, part, 0.0)
            for step in range(STEPS):
                part = jnp.where(position == length + step, fresh[step][child:child + 1], part)
            edge[child * 2 + index - first] = part.astype(jnp.bfloat16)
            pltpu.make_async_copy(edge.at[child * 2 + index - first], cache_ref.at[child, index], out_sem).start()
            return carry

        lax.fori_loop(first, last + 1, fix, 0)

    rows = MOST * STEPS
    raw = []
    for distance in range(SPAN):
        part = raw_ref[distance].astype(jnp.float32)
        raw.append(jnp.concatenate([part[:rows], part[rows:]], axis=1))
    raw = jnp.concatenate(raw, axis=0).astype(jnp.bfloat16)
    row = lax.broadcasted_iota(jnp.int32, (BEAMS, SPAN * rows), 0)
    col = lax.broadcasted_iota(jnp.int32, (BEAMS, SPAN * rows), 1)
    slot_at = jnp.zeros_like(col)
    for child in range(BEAMS):
        slot_at = jnp.where(row == child, slots[child], slot_at)
    for step in range(STEPS):
        pick = jnp.where(col == slot_at * STEPS + step, 1.0, 0.0).astype(jnp.bfloat16)
        proj_ref[step] = jnp.dot(pick, raw, preferred_element_type=jnp.float32).astype(jnp.bfloat16)
    proj_copy = pltpu.make_async_copy(proj_ref, proj_hbm, proj_sem)
    proj_copy.start()
    pltpu.make_async_copy(cache_ref, cache_ref, out_sem).wait()
    proj_copy.wait()


def local(shards, queries, new_kv, kv_pool, page_tables, lengths, parents, out_weight):
    wide = queries.shape[2]
    channels = kv_pool.shape[2]
    context = page_tables.shape[1] * kv_pool.shape[1]
    rows = MOST * STEPS
    vmem = pl.BlockSpec(memory_space=pltpu.VMEM)
    smem = pl.BlockSpec(memory_space=pltpu.SMEM)
    hbm = pl.BlockSpec(memory_space=pltpu.HBM)
    free = pl.BlockSpec(memory_space=pl.ANY)
    dma = pltpu.SemaphoreType.DMA
    bf16 = jnp.bfloat16

    def pinned(*operands):
        return [pltpu.with_memory_space_constraint(operand, pltpu.HBM) for operand in operands]

    grain_pool = kv_pool.reshape(-1, GRAIN, channels)
    with jax.named_scope("exchange"):
        recv, raw, left, meta, over = pl.pallas_call(
            exchange_kernel,
            out_shape=(
                jax.ShapeDtypeStruct((2 * LINK + MOST * PER_CHILD, GRAIN, channels), bf16),
                jax.ShapeDtypeStruct((SPAN, 2 * rows, wide // 2), bf16),
                jax.ShapeDtypeStruct((2, LEFT, GRAIN, channels), bf16),
                jax.ShapeDtypeStruct((BEAMS * META,), jnp.int32),
                jax.ShapeDtypeStruct((1,), jnp.int32),
            ),
            in_specs=[hbm] * 7,
            out_specs=(free, free, free, smem, smem),
            scratch_shapes=[
                pltpu.VMEM(queries.shape, bf16),
                pltpu.VMEM(new_kv.shape, bf16),
                pltpu.SMEM(page_tables.shape, jnp.int32),
                pltpu.SMEM(lengths.shape, jnp.int32),
                pltpu.SMEM(parents.shape, jnp.int32),
                pltpu.VMEM((1, *lengths.shape), jnp.int32),
                pltpu.VMEM((1, *parents.shape), jnp.int32),
                pltpu.VMEM(grain_pool.shape, bf16),
                pltpu.VMEM((shards, out_weight.shape[0], wide), bf16),
                pltpu.VMEM((SPAN, MOST * PER_CHILD, GRAIN, channels), bf16),
                pltpu.VMEM((2, FIRST, GRAIN, channels), bf16),
                pltpu.VMEM((2, FIRST, GRAIN, channels), bf16),
                pltpu.VMEM((2, REST, GRAIN, channels), bf16),
                pltpu.VMEM((2, LEFT, GRAIN, channels), bf16),
                pltpu.VMEM((SPAN, 2 * rows, (wide + channels) // 2), bf16),
                pltpu.VMEM((SPAN, 2 * rows, (wide + channels) // 2), bf16),
                pltpu.VMEM((SPAN * rows, wide), jnp.float32),
                pltpu.VMEM((shards, SPAN * rows, wide), bf16),
                pltpu.VMEM((shards, SPAN * rows, wide), bf16),
                pltpu.VMEM((SPAN, 2 * rows, wide // 2), bf16),
                pltpu.SMEM((SPAN * MOST,), jnp.int32),
                pltpu.SMEM((SPAN * MOST,), jnp.int32),
                dma((7,)), dma, dma((shards,)), dma((2,)), dma((3,)),
                dma((SPAN,)), dma((SPAN,)),
                dma((8,)), dma((8,)),
                dma((shards,)), dma((shards,)),
                dma((SPAN,)), dma((SPAN,)),
                pltpu.SemaphoreType.REGULAR,
            ],
            compiler_params=pltpu.CompilerParams(
                collective_id=0, has_side_effects=True, vmem_limit_bytes=48 * 1024 * 1024
            ),
            name="exchange",
        )(*pinned(queries, new_kv, grain_pool, page_tables, lengths, parents, out_weight))

    def place(*got):
        with jax.named_scope("place"):
            projected, cache = pl.pallas_call(
                functools.partial(place_kernel, len(got) > 0),
                out_shape=(
                    jax.ShapeDtypeStruct(queries.shape, bf16),
                    jax.ShapeDtypeStruct((BEAMS, context // TILE, TILE, channels), bf16),
                ),
                in_specs=[vmem, vmem, vmem, smem] + [vmem] * len(got),
                out_specs=(free, free),
                scratch_shapes=[
                    pltpu.VMEM((2 * BEAMS, TILE, channels), bf16),
                    pltpu.VMEM((context // TILE, TILE, channels), bf16),
                    pltpu.VMEM(queries.shape, bf16),
                    dma, dma,
                ],
                compiler_params=pltpu.CompilerParams(vmem_limit_bytes=24 * 1024 * 1024),
                name="place_left" if got else "place",
            )(recv.reshape(-1, TILE, channels), raw, new_kv, meta, *got)
            return projected, cache.reshape(BEAMS, context, channels)

    def placed():
        return place()

    def topped(count, number):
        with jax.named_scope("left"):
            got = pl.pallas_call(
                functools.partial(left_kernel, count),
                out_shape=jax.ShapeDtypeStruct(left.shape, bf16),
                in_specs=[free],
                out_specs=free,
                scratch_shapes=[dma((2,)), dma((2,))],
                compiler_params=pltpu.CompilerParams(
                    collective_id=number, has_side_effects=True, vmem_limit_bytes=4 * 1024 * 1024
                ),
                name="left",
            )(left)
        return place(got.reshape(-1, TILE, channels))

    def resent():
        with jax.named_scope("full"):
            whole = pl.pallas_call(
                full_kernel,
                out_shape=jax.ShapeDtypeStruct((SPAN, MOST * context, channels), bf16),
                in_specs=[hbm] * 3,
                out_specs=free,
                scratch_shapes=[
                    pltpu.SMEM(page_tables.shape, jnp.int32),
                    pltpu.SMEM(parents.shape, jnp.int32),
                    pltpu.VMEM(kv_pool.shape, bf16),
                    pltpu.VMEM((SPAN, MOST * context, channels), bf16),
                    dma((2,)), dma, dma((MOST,)),
                    dma((SPAN * MOST,)), dma((SPAN * MOST,)),
                ],
                compiler_params=pltpu.CompilerParams(
                    collective_id=1, has_side_effects=True, vmem_limit_bytes=24 * 1024 * 1024
                ),
                name="full",
            )(*pinned(kv_pool, page_tables, parents))
        with jax.named_scope("finish"):
            return pl.pallas_call(
                finish_kernel,
                out_shape=(
                    jax.ShapeDtypeStruct(queries.shape, bf16),
                    jax.ShapeDtypeStruct((BEAMS, context, channels), bf16),
                ),
                in_specs=[vmem, vmem, hbm, hbm, hbm],
                out_specs=(vmem, hbm),
                scratch_shapes=[
                    pltpu.VMEM(new_kv.shape, bf16),
                    pltpu.SMEM(lengths.shape, jnp.int32),
                    pltpu.SMEM(parents.shape, jnp.int32),
                    pltpu.VMEM((2 * BEAMS, PAGE, channels), bf16),
                    pltpu.VMEM((PAGE, channels), bf16),
                    dma((3,)), dma,
                ],
                compiler_params=pltpu.CompilerParams(vmem_limit_bytes=24 * 1024 * 1024),
                name="finish",
            )(whole.reshape(BEAMS, context, channels), raw, new_kv, lengths, parents)

    topping = [functools.partial(topped, count, 2 + at) for at, count in enumerate(TIERS)]
    return lax.switch(over[0], [placed, *topping, resent])


def solution(mesh):
    in_specs = (
        P(None, "dp", "tensor"),
        P(None, "dp", "tensor"),
        P("dp", None, "tensor"),
        P("dp", None),
        P(),
        P(),
        P("tensor", None),
    )
    out_specs = (P(None, "dp", "tensor"), P("dp", None, "tensor"))
    body = functools.partial(local, mesh.shape["tensor"])
    return jax.shard_map(body, mesh=mesh, in_specs=in_specs, out_specs=out_specs, check_vma=False)
```

```python
import functools

import jax
import jax.numpy as jnp
from jax import lax
from jax.experimental import pallas as pl
from jax.experimental.pallas import tpu as pltpu
from jax.sharding import PartitionSpec as P

HD = 128
SPAN = 4
MOST = 2
BEAMS = 8
STEPS = 4
PAGE = 128
PAGES = 8
GRAIN = 16
PER_CHILD = 64
PER_PAGE = PAGE // GRAIN
PAGE_BITS = PER_PAGE.bit_length() - 1
TILE = 16
VIA = 72
MORE = 28
REST = 72
TIERS = (8, 20, 48)
LEFT = TIERS[-1]
FIRST = VIA + MORE
LINK = FIRST + REST
META = 7
MESH = pl.DeviceIdType.MESH


def grains(length):
    return (length + (GRAIN - 1)) // GRAIN


def choose(values, index):
    out = values[0]
    for at in range(1, len(values)):
        out = jnp.where(index == at, values[at], out)
    return out


def balanced(up, far, down, keep_up, keep_down):
    least = [jnp.maximum(keep_up[i], far[i] - VIA) for i in range(SPAN)]
    most = [jnp.minimum(far[i] - keep_down[i], VIA) for i in range(SPAN)]
    via_up = [jnp.minimum(jnp.maximum(far[i] >> 1, least[i]), most[i]) for i in range(SPAN)]
    for at in (*range(SPAN), *range(SPAN)):
        via_down = [far[i] - via_up[i] for i in range(SPAN)]
        nxt, prv = (at + 1) % SPAN, (at - 1) % SPAN
        load_up = jnp.maximum(up[at] + via_up[prv], up[nxt] + via_up[nxt])
        load_down = jnp.maximum(down[at] + via_down[nxt], down[prv] + via_down[prv])
        best = (load_down + far[at] - load_up) >> 1
        via_up[at] = jnp.minimum(jnp.maximum(best, least[at]), most[at])
    via_down = [far[i] - via_up[i] for i in range(SPAN)]
    return via_up, via_down


def planned(flows):
    names = ("up", "down", "far", "first", "second", "cut", "up_id", "down_id", "keep_up", "keep_down")
    plan = {name: [] for name in names}
    for at in range(SPAN):
        u0, u1, gu0, gu1 = flows[at][1]
        f0, f1, gf0, gf1 = flows[at][2]
        d0, d1, gd0, gd1 = flows[at][3]
        gu1 = jnp.where(u0 == u1, 0, gu1)
        gf1 = jnp.where(f0 == f1, 0, gf1)
        gd1 = jnp.where(d0 == d1, 0, gd1)

        def shared(parent, count, one, two):
            return jnp.where((parent == one) | (parent == two), count, 0)

        straight = shared(f0, gf0, u0, u1) + shared(f1, gf1, d0, d1)
        crossed = shared(f1, gf1, u0, u1) + shared(f0, gf0, d0, d1)
        swap = crossed > straight
        first, second = jnp.where(swap, f1, f0), jnp.where(swap, f0, f1)
        cut, rest = jnp.where(swap, gf1, gf0), jnp.where(swap, gf0, gf1)
        keep_up, keep_down = shared(first, cut, u0, u1), shared(second, rest, d0, d1)
        values = (
            gu0 + gu1 - keep_up, gd0 + gd1 - keep_down, gf0 + gf1, first, second, cut,
            jnp.where(keep_up > 0, first, -1), jnp.where(keep_down > 0, second, -1), keep_up, keep_down,
        )
        for name, value in zip(names, values):
            plan[name].append(value)
    plan["via_up"], plan["via_down"] = balanced(
        plan["up"], plan["far"], plan["down"], plan["keep_up"], plan["keep_down"]
    )
    return plan


def ring_plan(parents, lengths, ring):
    flows = [[None] * SPAN for _ in range(SPAN)]
    for target in range(SPAN):
        owners = [parents[(ring * SPAN + target) * BEAMS + child] for child in range(BEAMS)]
        sources = [(owner >> 3) & (SPAN - 1) for owner in owners]
        for at in range(SPAN):
            if at != target:
                one, two = owners[0], owners[0]
                for child in range(1, BEAMS):
                    two = jnp.where(sources[child] == at, owners[child], two)
                one = owners[BEAMS - 1]
                for child in range(BEAMS - 2, -1, -1):
                    one = jnp.where(sources[child] == at, owners[child], one)
                flows[at][(target - at) % SPAN] = (one, two, grains(lengths[one]), grains(lengths[two]))
    return {**planned(flows), "flows": flows}


def heaviest(parents, lengths, rings):
    beams = rings * SPAN * BEAMS
    counts = grains(lengths).astype(jnp.float32).astype(jnp.bfloat16)
    beam = lax.broadcasted_iota(jnp.int32, (beams, beams), 0)
    chosen = jnp.where(beam == parents, 1.0, 0.0).astype(jnp.bfloat16)
    counts = jnp.dot(jnp.broadcast_to(counts, (16, beams)), chosen, preferred_element_type=jnp.float32)[:1]
    lane = lax.broadcasted_iota(jnp.int32, (1, beams), 1)
    source = (parents // BEAMS) % SPAN
    rank = jnp.zeros_like(lane)
    for back in range(1, BEAMS):
        rank = rank + jnp.where((pltpu.roll(source, back, 1) == source) & (lane % BEAMS >= back), 1, 0)
    names = (parents % (SPAN * BEAMS)).astype(jnp.float32)
    rows = [
        jnp.where((source == at) & (rank == order), value, 0.0)
        for value in (names, counts) for at in range(SPAN) for order in range(MOST)
    ]
    rows = jnp.concatenate(rows, axis=0).astype(jnp.bfloat16)
    child = lax.broadcasted_iota(jnp.int32, (beams, 128), 0)
    ring = lax.broadcasted_iota(jnp.int32, (beams, 128), 1)
    flows = [[None] * SPAN for _ in range(SPAN)]
    for target in range(SPAN):
        member = (child // BEAMS % SPAN == target) & (child // (BEAMS * SPAN) == ring)
        member = jnp.where(member, 1.0, 0.0).astype(jnp.bfloat16)
        found = jnp.dot(rows, member, preferred_element_type=jnp.float32).astype(jnp.int32)
        for at in range(SPAN):
            wanted = (at * MOST, at * MOST + 1, (SPAN + at) * MOST, (SPAN + at) * MOST + 1)
            flows[at][(target - at) % SPAN] = tuple(found[one:one + 1] for one in wanted)
    plan = planned(flows)
    out = jnp.zeros_like(plan["far"][0])
    for at in range(SPAN):
        load_up = plan["up"][at] + plan["via_up"][at] + plan["via_up"][(at - 1) % SPAN]
        load_down = plan["down"][at] + plan["via_down"][at] + plan["via_down"][(at + 1) % SPAN]
        out = jnp.maximum(out, jnp.maximum(load_up, load_down))
    return jnp.max(out)


def slots_of_children(parents, me):
    taken = [jnp.int32(0) for _ in range(SPAN)]
    slots, owners = [], []
    for child in range(BEAMS):
        parent = parents[me * BEAMS + child]
        apart = jnp.bitwise_and(parent // BEAMS - me, SPAN - 1)
        slot = jnp.int32(0)
        for distance in range(SPAN):
            hit = apart == distance
            slot = jnp.where(hit, distance * MOST + taken[distance], slot)
            taken[distance] = taken[distance] + hit.astype(jnp.int32)
        slots.append(slot)
        owners.append(parent)
    return slots, owners


def served_beams(parents, me, target):
    count = jnp.int32(0)
    beams = [jnp.int32(0) for _ in range(MOST)]
    for child in range(BEAMS):
        parent = parents[target * BEAMS + child]
        hit = parent // BEAMS == me
        for rank in range(MOST):
            beams[rank] = jnp.where(hit & (count == rank), parent % BEAMS, beams[rank])
        count = count + hit.astype(jnp.int32)
    return beams


def exchange_kernel(
    q_hbm, new_hbm, pool_ref, table_hbm, len_hbm, par_hbm, w_ref,
    recv_ref, proj_ref, left_ref, meta_ref, over_ref,
    q_ref, new_ref, table_ref, len_ref, par_ref, len_row, par_row,
    pool_v, w_v, stage, first_send, first_recv, rest_send, left_send, q_send, q_recv, att, p_send, p_recv, r_send, lens, beams,
    in_sem, pool_sem, w_sem, own_sem, land_sem, qs_sem, qr_sem, bs_sem, br_sem, ps_sem, pr_sem, rs_sem, rr_sem, here_sem,
):
    me = lax.axis_index("dp")
    mine = lax.axis_index("tensor")
    shards = lax.axis_size("tensor")
    y = lax.rem(me, SPAN)
    base = me - y
    context = stage.shape[1] * GRAIN // MOST
    rings = lax.axis_size("dp") // SPAN
    wide = q_hbm.shape[2]
    heads = wide // HD
    rows = MOST * STEPS

    def peer(distance):
        return base + lax.rem(y + distance, SPAN)

    pairs = (
        (par_hbm, par_ref), (len_hbm, len_ref), (table_hbm, table_ref), (q_hbm, q_ref), (new_hbm, new_ref),
        (par_hbm, par_row.at[0]), (len_hbm, len_row.at[0]),
    )
    in_copies = [pltpu.make_async_copy(source, target, in_sem.at[at]) for at, (source, target) in enumerate(pairs)]
    pool_copy = pltpu.make_async_copy(pool_ref, pool_v, pool_sem)
    for copy in (*in_copies[:3], pool_copy, *in_copies[3:]):
        copy.start()
    barrier = pltpu.get_barrier_semaphore()
    for distance in range(1, SPAN):
        pl.semaphore_signal(barrier, inc=1, device_id={"dp": peer(distance)}, device_id_type=MESH)
    for other in range(1, shards):
        @pl.when(mine + other < shards)
        def _(other=other):
            pl.semaphore_signal(barrier, inc=1, device_id={"tensor": mine + other}, device_id_type=MESH)
    for copy in in_copies[:3]:
        copy.wait()

    slots, owners = slots_of_children(par_ref, me)
    for copy in in_copies[3:5]:
        copy.wait()
    row = lax.broadcasted_iota(jnp.int32, (SPAN * rows, BEAMS), 0)
    col = lax.broadcasted_iota(jnp.int32, (SPAN * rows, BEAMS), 1)
    slot_at = jnp.zeros_like(col)
    for child in range(BEAMS):
        slot_at = jnp.where(col == child, slots[child], slot_at)
    q_sorted = jnp.zeros((SPAN * rows, wide), jnp.float32)
    new_sorted = jnp.zeros((SPAN * rows, 2 * HD), jnp.float32)
    for step in range(STEPS):
        pick = jnp.where((row // STEPS == slot_at) & (row % STEPS == step), 1.0, 0.0).astype(jnp.bfloat16)
        q_sorted += jnp.dot(pick, q_ref[step], preferred_element_type=jnp.float32)
        new_sorted += jnp.dot(pick, new_ref[step], preferred_element_type=jnp.float32)
    both = jnp.concatenate([q_sorted, new_sorted], axis=1)
    half = both.shape[1] // 2
    for distance in range(SPAN):
        part = both[distance * rows:(distance + 1) * rows]
        part = jnp.concatenate([part[:, :half], part[:, half:]], axis=0).astype(jnp.bfloat16)
        if distance == 0:
            q_recv[0] = part
        else:
            q_send[distance] = part

    plan = ring_plan(par_ref, len_ref, me >> 2)
    via_up, via_down = plan["via_up"], plan["via_down"]
    flows = {}
    for ahead in (1, 3):
        first, second, cut = (choose([plan["flows"][at][ahead][of] for at in range(SPAN)], y) for of in range(3))
        flows[ahead] = (first & 7, second & 7, cut)
    for ahead, kept in ((1, "up_id"), (3, "down_id")):
        first, second, cut = flows[ahead]
        flows[ahead] = (first, second, jnp.where(me * BEAMS + first == choose(plan[kept], y), 0, cut))
    flows[2] = (choose(plan["first"], y) & 7, choose(plan["second"], y) & 7, choose(plan["cut"], y))

    def grain_at(flow, number):
        first, second, cut = flow
        later = number >= cut
        number = jnp.where(later, number - cut, number)
        number = jnp.minimum(jnp.maximum(number, 0), PER_CHILD - 1)
        return table_ref[jnp.where(later, second, first), number >> PAGE_BITS] * PER_PAGE + (number & (PER_PAGE - 1))

    sides = (
        (flows[1], choose(via_up, y), jnp.int32(0), choose(via_up, (y - 1) & 3), peer(1)),
        (flows[3], choose(via_down, y), choose(via_up, y), choose(via_down, (y + 1) & 3), peer(3)),
    )
    pl.semaphore_wait(barrier, SPAN - 1 + mine)
    q_copies = []
    for distance in range(1, SPAN):
        copy = pltpu.make_async_remote_copy(
            src_ref=q_send.at[distance], dst_ref=q_recv.at[distance],
            send_sem=qs_sem.at[distance], recv_sem=qr_sem.at[distance],
            device_id={"dp": peer(distance)}, device_id_type=MESH,
        )
        copy.start()
        q_copies.append(copy)
    pool_copy.wait()
    b_copies = []
    cuts = (0, 12, VIA, FIRST)

    def send_part(part):
        for side, (flow, mine_via, skip, _, target) in enumerate(sides):
            def put(at, carry, side=side, flow=flow, mine_via=mine_via, skip=skip):
                for at in [4 * at + more for more in range(4)]:
                    far = at < mine_via
                    chosen = tuple(jnp.where(far, one, two) for one, two in zip(flows[2], flow))
                    number = jnp.where(far, skip + at, at - mine_via)
                    first_send[side, at] = pool_v[grain_at(chosen, number)]
                return carry

            lax.fori_loop(cuts[part] // 4, cuts[part + 1] // 4, put, 0)
            span = pl.ds(cuts[part], cuts[part + 1] - cuts[part])
            copy = pltpu.make_async_remote_copy(
                src_ref=first_send.at[side, span], dst_ref=first_recv.at[side, span],
                send_sem=bs_sem.at[side * 4 + part], recv_sem=br_sem.at[side * 4 + part],
                device_id={"dp": target}, device_id_type=MESH,
            )
            copy.start()
            b_copies.append(copy)

    send_part(0)
    send_part(1)
    send_part(2)
    for other in range(1, shards):
        @pl.when(mine >= other)
        def _(other=other):
            pl.semaphore_signal(here_sem, inc=1, device_id={"tensor": mine - other}, device_id_type=MESH)
    for ahead in range(SPAN):
        served = served_beams(par_ref, me, peer(ahead))
        for rank in range(MOST):
            at = (SPAN - ahead) % SPAN * MOST + rank
            beams[at] = served[rank]
            lens[at] = len_ref[me * BEAMS + served[rank]]
    w_copies = []
    for block in range(shards):
        copy = pltpu.make_async_copy(w_ref.at[:, pl.ds(block * wide, wide)], w_v.at[block], w_sem.at[block])
        copy.start()
        w_copies.append(copy)

    def put_all(index, carry):
        slot = index // PAGES
        page = table_ref[beams[slot], index % PAGES]
        at = (index % (MOST * PAGES)) * PER_PAGE
        stage[index // (MOST * PAGES), pl.ds(at, PER_PAGE)] = pool_v[pl.ds(page * PER_PAGE, PER_PAGE)]
        return carry

    lax.fori_loop(0, SPAN * MOST * PAGES, put_all, 0)
    own_copy = pltpu.make_async_copy(stage.at[0], recv_ref.at[pl.ds(2 * LINK, MOST * PER_CHILD)], own_sem.at[0])
    own_copy.start()

    for copy in q_copies:
        copy.wait()

    def attend(distance):
        message = q_recv[distance].astype(jnp.float32)
        message = jnp.concatenate([message[:rows], message[rows:]], axis=1)
        q_rows = jnp.concatenate([message[:, h * HD:(h + 1) * HD] for h in range(heads)], axis=0).astype(jnp.bfloat16)
        fresh = message[:, wide:].astype(jnp.bfloat16)
        old_len = lens[distance * MOST]
        last_len = lens[distance * MOST + 1]
        contract = (((1,), (1,)), ((), ()))
        scale = HD ** -0.5
        half = MOST * PER_CHILD // 2
        keys = [stage[distance, pl.ds(rank * half, half), :, 0:HD].reshape(context, HD) for rank in range(MOST)]
        scores = [lax.dot_general(q_rows, key, contract, preferred_element_type=jnp.float32) for key in keys]
        rank_at = lax.broadcasted_iota(jnp.int32, scores[0].shape, 0) // STEPS % MOST
        scores = jnp.where(rank_at == 0, scores[0], scores[1]) * scale
        fresh_scores = lax.dot_general(q_rows, fresh[:, :HD], contract, preferred_element_type=jnp.float32) * scale
        position = lax.broadcasted_iota(jnp.int32, scores.shape, 1)
        limit = jnp.where(rank_at == 0, old_len, last_len)
        scores = jnp.where(position < limit, scores, -1e30)
        f_row = lax.broadcasted_iota(jnp.int32, fresh_scores.shape, 0)
        f_col = lax.broadcasted_iota(jnp.int32, fresh_scores.shape, 1)
        seen = (f_row // STEPS % MOST == f_col // STEPS) & (f_col % STEPS <= f_row % STEPS)
        fresh_scores = jnp.where(seen, fresh_scores, -1e30)
        top = jnp.maximum(jnp.max(scores, axis=1, keepdims=True), jnp.max(fresh_scores, axis=1, keepdims=True))
        exp_old = jnp.exp(scores - top)
        exp_new = jnp.exp(fresh_scores - top)
        total = jnp.sum(exp_old, axis=1, keepdims=True) + jnp.sum(exp_new, axis=1, keepdims=True)
        share = 1.0 / total
        w_old = (exp_old * share).astype(jnp.bfloat16)
        w_new = (exp_new * share).astype(jnp.bfloat16)
        values = [stage[distance, pl.ds(rank * half, half), :, HD:2 * HD].reshape(context, HD) for rank in range(MOST)]
        out = [jnp.dot(w_old, value, preferred_element_type=jnp.float32) for value in values]
        out = jnp.where(rank_at[:, :HD] == 0, out[0], out[1])
        out += jnp.dot(w_new, fresh[:, HD:], preferred_element_type=jnp.float32)
        out = jnp.concatenate([out[h * rows:(h + 1) * rows] for h in range(heads)], axis=1)
        att[pl.ds(pl.multiple_of(distance * rows, rows), rows), :] = out

    def attend_two(at, carry):
        attend(2 * at)
        attend(2 * at + 1)
        return carry

    lax.fori_loop(0, SPAN // 2, attend_two, 0)
    for copy in b_copies[:4]:
        copy.wait()
    more_copies = b_copies[4:]
    b_copies = []
    for side, (flow, mine_via, _, passed, target) in enumerate(sides):
        def put_passed(at, carry, side=side, flow=flow, mine_via=mine_via, passed=passed):
            for at in [4 * at + more for more in range(4)]:
                here = pool_v[grain_at(flow, FIRST - mine_via + at - passed)]
                rest_send[side, at] = jnp.where(at < passed, first_recv[side, at], here)
            return carry

        lax.fori_loop(0, REST // 4, put_passed, 0)
        copy = pltpu.make_async_remote_copy(
            src_ref=rest_send.at[side], dst_ref=recv_ref.at[pl.ds(side * LINK + FIRST, REST)],
            send_sem=bs_sem.at[side * 4 + 3], recv_sem=br_sem.at[side * 4 + 3],
            device_id={"dp": target}, device_id_type=MESH,
        )
        copy.start()
        b_copies.append(copy)
    attended = att[...].astype(jnp.bfloat16)
    for copy in w_copies:
        copy.wait()

    def p_copy(other):
        return pltpu.make_async_remote_copy(
            src_ref=p_send.at[other], dst_ref=p_recv.at[other],
            send_sem=ps_sem.at[other], recv_sem=pr_sem.at[other],
            device_id={"tensor": lax.rem(mine + other, shards)}, device_id_type=MESH,
        )

    def project(other, carry):
        product = jnp.dot(attended, w_v[lax.rem(mine + other, shards)], preferred_element_type=jnp.float32)
        p_send[other] = product.astype(jnp.bfloat16)
        p_copy(other).start()
        return carry

    @pl.when(mine < shards - 1)
    def _():
        pl.semaphore_wait(here_sem, shards - 1 - mine)

    lax.fori_loop(1, shards, project, 0)
    own = jnp.dot(attended, w_v[mine], preferred_element_type=jnp.float32)

    for copy in more_copies:
        copy.wait()
    for side in range(2):
        copy = pltpu.make_async_copy(first_recv.at[side], recv_ref.at[pl.ds(side * LINK, FIRST)], land_sem.at[side])
        copy.start()
        b_copies.append(copy)

    def gather_sums(other, total):
        p_copy(other).wait()
        return total + p_recv[other].astype(jnp.float32)

    summed = lax.fori_loop(1, shards, gather_sums, own)
    half = wide // 2
    r_copies = []
    for distance in range(SPAN):
        part = summed[distance * rows:(distance + 1) * rows]
        r_send[distance] = jnp.concatenate([part[:, :half], part[:, half:]], axis=0).astype(jnp.bfloat16)
        if distance == 0:
            copy = pltpu.make_async_copy(r_send.at[0], proj_ref.at[0], own_sem.at[1])
        else:
            copy = pltpu.make_async_remote_copy(
                src_ref=r_send.at[distance], dst_ref=proj_ref.at[distance],
                send_sem=rs_sem.at[distance], recv_sem=rr_sem.at[distance],
                device_id={"dp": peer(SPAN - distance)}, device_id_type=MESH,
            )
        copy.start()
        r_copies.append(copy)
    for copy in in_copies[5:]:
        copy.wait()
    load = heaviest(par_row[...], len_row[...], rings)
    over_ref[0] = sum(jnp.where(load > limit, 1, 0) for limit in (LINK, *(LINK + count for count in TIERS)))
    for side, (flow, mine_via, _, passed, _) in enumerate(sides):
        def put_left(at, carry, side=side, flow=flow, mine_via=mine_via, passed=passed):
            for at in [4 * at + more for more in range(4)]:
                left_send[side, at] = pool_v[grain_at(flow, LINK - mine_via - passed + at)]
            return carry

        lax.fori_loop(0, LEFT // 4, put_left, 0)
    left_copy = pltpu.make_async_copy(left_send, left_ref, land_sem.at[2])
    left_copy.start()
    for child in range(BEAMS):
        slot = slots[child]
        distance = slot >> 1
        length = len_ref[owners[child]]
        kept = jnp.where(distance == 3, choose(plan["up_id"], (y - 1) & 3), choose(plan["down_id"], (y + 1) & 3))
        before = jnp.int32(0)
        for other in range(BEAMS):
            if other != child:
                mate = (slots[other] >> 1 == distance) & (slots[other] < slot)
                counts = (owners[other] != owners[child]) & (owners[other] != kept)
                before = jnp.where(mate & counts, grains(len_ref[owners[other]]), before)
        far_before = jnp.where(owners[child] == choose(plan["first"], (y + 2) & 3), 0, choose(plan["cut"], (y + 2) & 3))
        before = jnp.where(distance == 2, far_before, before)
        from_up = choose(via_up, (y - 1) & 3), choose(via_up, (y + 2) & 3)
        from_down = choose(via_down, (y + 1) & 3), choose(via_down, (y + 2) & 3)
        near_via = jnp.where(distance == 3, from_up[0], from_down[0])
        near_pass = jnp.where(distance == 3, from_up[1], from_down[1])
        near_base = jnp.where(distance == 3, 0, LINK)
        split = jnp.where(distance == 2, from_up[1], FIRST - near_via) - before
        split = jnp.minimum(jnp.maximum(split, 0), PER_CHILD)
        start = jnp.where(distance == 2, FIRST + before, near_base + near_via + before)
        again = jnp.where(distance == 2, LINK + FIRST + before + split - from_up[1], start + split + near_pass)
        near = (distance == 1) | (distance == 3)
        until = LINK - near_via - near_pass - before
        until = jnp.where(near, jnp.minimum(jnp.maximum(until, 0), PER_CHILD), PER_CHILD)
        third = jnp.where(distance == 3, 0, LEFT) + near_via + near_pass + before + until - LINK
        held = near & (owners[child] == kept)
        kept_down = LINK + choose(via_down, (y + 1) & 3) - choose(plan["keep_down"], (y + 1) & 3)
        start = jnp.where(held, jnp.where(distance == 3, 0, kept_down), start)
        split = jnp.where(held, PER_CHILD, split)
        again = jnp.where(held, 0, again)
        until = jnp.where(held, PER_CHILD, until)
        third = jnp.where(held, 0, third)
        stays = distance == 0
        meta_ref[child * META] = length
        meta_ref[child * META + 1] = jnp.where(stays, 2 * LINK + (slot & 1) * PER_CHILD, start)
        meta_ref[child * META + 2] = jnp.where(stays, PER_CHILD, split)
        meta_ref[child * META + 3] = jnp.where(stays, 0, again)
        meta_ref[child * META + 4] = until
        meta_ref[child * META + 5] = jnp.where(near, third, 0)
        meta_ref[child * META + 6] = slot
    for copy in r_copies:
        copy.wait()
    for copy in b_copies:
        copy.wait()
    own_copy.wait()
    left_copy.wait()


def full_kernel(
    pool_ref, table_hbm, par_hbm, recv_ref,
    table_ref, par_ref, pool_v, stage,
    in_sem, pool_sem, own_sem, bs_sem, br_sem,
):
    me = lax.axis_index("dp")
    y = lax.rem(me, SPAN)
    base = me - y
    context = stage.shape[1] // MOST

    def peer(distance):
        return base + lax.rem(y + distance, SPAN)

    barrier = pltpu.get_barrier_semaphore()
    for distance in range(1, SPAN):
        pl.semaphore_signal(barrier, inc=1, device_id={"dp": peer(distance)}, device_id_type=MESH)
    in_copies = []
    for at, (source, target) in enumerate(((par_hbm, par_ref), (table_hbm, table_ref))):
        copy = pltpu.make_async_copy(source, target, in_sem.at[at])
        copy.start()
        in_copies.append(copy)
    pool_copy = pltpu.make_async_copy(pool_ref, pool_v, pool_sem)
    pool_copy.start()
    for copy in in_copies:
        copy.wait()
    pl.semaphore_wait(barrier, SPAN - 1)
    pool_copy.wait()
    copies = []
    for distance in (2, 1, 3, 0):
        served = served_beams(par_ref, me, peer(SPAN - distance))
        for rank in range(MOST):
            beam = served[rank]

            def put(index, carry, distance=distance, rank=rank, beam=beam):
                at = pl.multiple_of(rank * context + index * PAGE, PAGE)
                stage[distance, pl.ds(at, PAGE), :] = pool_v[table_ref[beam, index]]
                return carry

            lax.fori_loop(0, context // PAGE, put, 0)
            span = pl.ds(rank * context, context)
            if distance == 0:
                copy = pltpu.make_async_copy(stage.at[0, span], recv_ref.at[0, span], own_sem.at[rank])
            else:
                copy = pltpu.make_async_remote_copy(
                    src_ref=stage.at[distance, span], dst_ref=recv_ref.at[distance, span],
                    send_sem=bs_sem.at[distance * MOST + rank], recv_sem=br_sem.at[distance * MOST + rank],
                    device_id={"dp": peer(SPAN - distance)}, device_id_type=MESH,
                )
            copy.start()
            copies.append(copy)
    for copy in copies:
        copy.wait()


def finish_kernel(recv_ref, raw_ref, new_hbm, len_hbm, par_hbm, proj_ref, cache_ref, new_ref, len_ref, par_ref, edge, zeros, in_sem, out_sem):
    me = lax.axis_index("dp")
    pages = recv_ref.shape[1] // PAGE
    operands = ((par_hbm, par_ref), (len_hbm, len_ref), (new_hbm, new_ref))
    in_copies = [pltpu.make_async_copy(source, target, in_sem.at[at]) for at, (source, target) in enumerate(operands)]
    for copy in in_copies:
        copy.start()
    zeros[...] = jnp.zeros_like(zeros)
    for copy in in_copies:
        copy.wait()
    slots, owners = slots_of_children(par_ref, me)
    fresh = [new_ref[step].astype(jnp.float32) for step in range(STEPS)]
    for child in range(BEAMS):
        slot = slots[child]
        length = len_ref[owners[child]]
        first = length // PAGE
        last = (length + STEPS - 1) // PAGE

        def whole(index, carry, child=child, slot=slot):
            span = pl.ds(pl.multiple_of(index * PAGE, PAGE), PAGE)
            pltpu.make_async_copy(recv_ref.at[slot, span], cache_ref.at[child, span], out_sem).start()
            return carry

        def clear(index, carry, child=child):
            span = pl.ds(pl.multiple_of(index * PAGE, PAGE), PAGE)
            pltpu.make_async_copy(zeros, cache_ref.at[child, span], out_sem).start()
            return carry

        def fix(index, carry, child=child, slot=slot, length=length, first=first):
            at = pl.multiple_of(index * PAGE, PAGE)
            position = at + lax.broadcasted_iota(jnp.int32, (PAGE, 2 * HD), 0)
            page = recv_ref[slot, pl.ds(at, PAGE), :].astype(jnp.float32)
            page = jnp.where(position < length, page, 0.0)
            for step in range(STEPS):
                page = jnp.where(position == length + step, fresh[step][child:child + 1], page)
            edge[child * 2 + index - first] = page.astype(jnp.bfloat16)
            pltpu.make_async_copy(edge.at[child * 2 + index - first], cache_ref.at[child, pl.ds(at, PAGE)], out_sem).start()
            return carry

        lax.fori_loop(0, first, whole, 0)
        lax.fori_loop(last + 1, pages, clear, 0)
        lax.fori_loop(first, last + 1, fix, 0)

    rows = MOST * STEPS
    raw = []
    for distance in range(SPAN):
        part = raw_ref[distance].astype(jnp.float32)
        raw.append(jnp.concatenate([part[:rows], part[rows:]], axis=1))
    raw = jnp.concatenate(raw, axis=0).astype(jnp.bfloat16)
    row = lax.broadcasted_iota(jnp.int32, (BEAMS, SPAN * rows), 0)
    col = lax.broadcasted_iota(jnp.int32, (BEAMS, SPAN * rows), 1)
    slot_at = jnp.zeros_like(col)
    for child in range(BEAMS):
        slot_at = jnp.where(row == child, slots[child], slot_at)
    for step in range(STEPS):
        pick = jnp.where(col == slot_at * STEPS + step, 1.0, 0.0).astype(jnp.bfloat16)
        proj_ref[step] = jnp.dot(pick, raw, preferred_element_type=jnp.float32).astype(jnp.bfloat16)
    pltpu.make_async_copy(recv_ref, cache_ref, out_sem).wait()


def left_kernel(count, left_ref, got_ref, send_sem, recv_sem):
    me = lax.axis_index("dp")
    y = lax.rem(me, SPAN)
    targets = [me - y + lax.rem(y + ahead, SPAN) for ahead in (1, SPAN - 1)]
    barrier = pltpu.get_barrier_semaphore()
    for target in targets:
        pl.semaphore_signal(barrier, inc=1, device_id={"dp": target}, device_id_type=MESH)
    pl.semaphore_wait(barrier, 2)
    copies = []
    for side, target in enumerate(targets):
        copy = pltpu.make_async_remote_copy(
            src_ref=left_ref.at[side, pl.ds(0, count)], dst_ref=got_ref.at[side, pl.ds(0, count)],
            send_sem=send_sem.at[side], recv_sem=recv_sem.at[side],
            device_id={"dp": target}, device_id_type=MESH,
        )
        copy.start()
        copies.append(copy)
    for copy in copies:
        copy.wait()


def place_kernel(with_left, recv_ref, raw_ref, new_ref, meta_ref, *refs):
    left_ref = refs[0] if with_left else None
    proj_hbm, cache_ref, edge, zeros, proj_ref, out_sem, proj_sem = refs[-7:]
    total = recv_ref.shape[0]
    zeros[...] = jnp.zeros_like(zeros)
    fresh = [new_ref[step].astype(jnp.float32) for step in range(STEPS)]
    slots = [meta_ref[child * META + 6] for child in range(BEAMS)]
    per_child = cache_ref.shape[1]
    scale = GRAIN // TILE
    for child in range(BEAMS):
        length, start, split, again, until, third = (meta_ref[child * META + at] for at in range(6))
        first = length // TILE
        last = (length + STEPS - 1) // TILE
        until = jnp.minimum(until * scale, first) if with_left else first
        split = jnp.minimum(split * scale, until)

        def move(source, source_at, at, count, child=child):
            @pl.when(count > 0)
            def _():
                pltpu.make_async_copy(
                    source.at[pl.ds(source_at, count)], cache_ref.at[child, pl.ds(at, count)], out_sem
                ).start()

        move(recv_ref, start * scale, 0, split)
        move(recv_ref, again * scale, split, until - split)
        if with_left:
            move(left_ref, third * scale, until, first - until)
        move(zeros, 0, last + 1, per_child - 1 - last)
    for child in range(BEAMS):
        length, start, split, again, until, third = (meta_ref[child * META + at] for at in range(6))
        first = length // TILE
        last = (length + STEPS - 1) // TILE

        def fix(
            index, carry, child=child, length=length, first=first, start=start * scale, split=split * scale,
            again=again * scale, until=until * scale, third=third * scale,
        ):
            position = index * TILE + lax.broadcasted_iota(jnp.int32, (TILE, 2 * HD), 0)
            at = jnp.minimum(jnp.where(index < split, start + index, again + index - split), total - 1)
            part = recv_ref[at].astype(jnp.float32)
            if with_left:
                at = jnp.minimum(jnp.maximum(third + index - until, 0), left_ref.shape[0] - 1)
                part = jnp.where(index < until, part, left_ref[at].astype(jnp.float32))
            part = jnp.where(position < length, part, 0.0)
            for step in range(STEPS):
                part = jnp.where(position == length + step, fresh[step][child:child + 1], part)
            edge[child * 2 + index - first] = part.astype(jnp.bfloat16)
            pltpu.make_async_copy(edge.at[child * 2 + index - first], cache_ref.at[child, index], out_sem).start()
            return carry

        lax.fori_loop(first, last + 1, fix, 0)

    rows = MOST * STEPS
    raw = []
    for distance in range(SPAN):
        part = raw_ref[distance].astype(jnp.float32)
        raw.append(jnp.concatenate([part[:rows], part[rows:]], axis=1))
    raw = jnp.concatenate(raw, axis=0).astype(jnp.bfloat16)
    row = lax.broadcasted_iota(jnp.int32, (BEAMS, SPAN * rows), 0)
    col = lax.broadcasted_iota(jnp.int32, (BEAMS, SPAN * rows), 1)
    slot_at = jnp.zeros_like(col)
    for child in range(BEAMS):
        slot_at = jnp.where(row == child, slots[child], slot_at)
    for step in range(STEPS):
        pick = jnp.where(col == slot_at * STEPS + step, 1.0, 0.0).astype(jnp.bfloat16)
        proj_ref[step] = jnp.dot(pick, raw, preferred_element_type=jnp.float32).astype(jnp.bfloat16)
    proj_copy = pltpu.make_async_copy(proj_ref, proj_hbm, proj_sem)
    proj_copy.start()
    pltpu.make_async_copy(cache_ref, cache_ref, out_sem).wait()
    proj_copy.wait()


def local(shards, queries, new_kv, kv_pool, page_tables, lengths, parents, out_weight):
    wide = queries.shape[2]
    channels = kv_pool.shape[2]
    context = page_tables.shape[1] * kv_pool.shape[1]
    rows = MOST * STEPS
    vmem = pl.BlockSpec(memory_space=pltpu.VMEM)
    smem = pl.BlockSpec(memory_space=pltpu.SMEM)
    hbm = pl.BlockSpec(memory_space=pltpu.HBM)
    free = pl.BlockSpec(memory_space=pl.ANY)
    dma = pltpu.SemaphoreType.DMA
    bf16 = jnp.bfloat16

    def pinned(*operands):
        return [pltpu.with_memory_space_constraint(operand, pltpu.HBM) for operand in operands]

    grain_pool = kv_pool.reshape(-1, GRAIN, channels)
    with jax.named_scope("exchange"):
        recv, raw, left, meta, over = pl.pallas_call(
            exchange_kernel,
            out_shape=(
                jax.ShapeDtypeStruct((2 * LINK + MOST * PER_CHILD, GRAIN, channels), bf16),
                jax.ShapeDtypeStruct((SPAN, 2 * rows, wide // 2), bf16),
                jax.ShapeDtypeStruct((2, LEFT, GRAIN, channels), bf16),
                jax.ShapeDtypeStruct((BEAMS * META,), jnp.int32),
                jax.ShapeDtypeStruct((1,), jnp.int32),
            ),
            in_specs=[hbm] * 7,
            out_specs=(free, free, free, smem, smem),
            scratch_shapes=[
                pltpu.VMEM(queries.shape, bf16),
                pltpu.VMEM(new_kv.shape, bf16),
                pltpu.SMEM(page_tables.shape, jnp.int32),
                pltpu.SMEM(lengths.shape, jnp.int32),
                pltpu.SMEM(parents.shape, jnp.int32),
                pltpu.VMEM((1, *lengths.shape), jnp.int32),
                pltpu.VMEM((1, *parents.shape), jnp.int32),
                pltpu.VMEM(grain_pool.shape, bf16),
                pltpu.VMEM((shards, out_weight.shape[0], wide), bf16),
                pltpu.VMEM((SPAN, MOST * PER_CHILD, GRAIN, channels), bf16),
                pltpu.VMEM((2, FIRST, GRAIN, channels), bf16),
                pltpu.VMEM((2, FIRST, GRAIN, channels), bf16),
                pltpu.VMEM((2, REST, GRAIN, channels), bf16),
                pltpu.VMEM((2, LEFT, GRAIN, channels), bf16),
                pltpu.VMEM((SPAN, 2 * rows, (wide + channels) // 2), bf16),
                pltpu.VMEM((SPAN, 2 * rows, (wide + channels) // 2), bf16),
                pltpu.VMEM((SPAN * rows, wide), jnp.float32),
                pltpu.VMEM((shards, SPAN * rows, wide), bf16),
                pltpu.VMEM((shards, SPAN * rows, wide), bf16),
                pltpu.VMEM((SPAN, 2 * rows, wide // 2), bf16),
                pltpu.SMEM((SPAN * MOST,), jnp.int32),
                pltpu.SMEM((SPAN * MOST,), jnp.int32),
                dma((7,)), dma, dma((shards,)), dma((2,)), dma((3,)),
                dma((SPAN,)), dma((SPAN,)),
                dma((8,)), dma((8,)),
                dma((shards,)), dma((shards,)),
                dma((SPAN,)), dma((SPAN,)),
                pltpu.SemaphoreType.REGULAR,
            ],
            compiler_params=pltpu.CompilerParams(
                collective_id=0, has_side_effects=True, vmem_limit_bytes=48 * 1024 * 1024
            ),
            name="exchange",
        )(*pinned(queries, new_kv, grain_pool, page_tables, lengths, parents, out_weight))

    def place(*got):
        with jax.named_scope("place"):
            projected, cache = pl.pallas_call(
                functools.partial(place_kernel, len(got) > 0),
                out_shape=(
                    jax.ShapeDtypeStruct(queries.shape, bf16),
                    jax.ShapeDtypeStruct((BEAMS, context // TILE, TILE, channels), bf16),
                ),
                in_specs=[vmem, vmem, vmem, smem] + [vmem] * len(got),
                out_specs=(free, free),
                scratch_shapes=[
                    pltpu.VMEM((2 * BEAMS, TILE, channels), bf16),
                    pltpu.VMEM((context // TILE, TILE, channels), bf16),
                    pltpu.VMEM(queries.shape, bf16),
                    dma, dma,
                ],
                compiler_params=pltpu.CompilerParams(vmem_limit_bytes=24 * 1024 * 1024),
                name="place_left" if got else "place",
            )(recv.reshape(-1, TILE, channels), raw, new_kv, meta, *got)
            return projected, cache.reshape(BEAMS, context, channels)

    def placed():
        return place()

    def topped(count, number):
        with jax.named_scope("left"):
            got = pl.pallas_call(
                functools.partial(left_kernel, count),
                out_shape=jax.ShapeDtypeStruct(left.shape, bf16),
                in_specs=[free],
                out_specs=free,
                scratch_shapes=[dma((2,)), dma((2,))],
                compiler_params=pltpu.CompilerParams(
                    collective_id=number, has_side_effects=True, vmem_limit_bytes=4 * 1024 * 1024
                ),
                name="left",
            )(left)
        return place(got.reshape(-1, TILE, channels))

    def resent():
        with jax.named_scope("full"):
            whole = pl.pallas_call(
                full_kernel,
                out_shape=jax.ShapeDtypeStruct((SPAN, MOST * context, channels), bf16),
                in_specs=[hbm] * 3,
                out_specs=free,
                scratch_shapes=[
                    pltpu.SMEM(page_tables.shape, jnp.int32),
                    pltpu.SMEM(parents.shape, jnp.int32),
                    pltpu.VMEM(kv_pool.shape, bf16),
                    pltpu.VMEM((SPAN, MOST * context, channels), bf16),
                    dma((2,)), dma, dma((MOST,)),
                    dma((SPAN * MOST,)), dma((SPAN * MOST,)),
                ],
                compiler_params=pltpu.CompilerParams(
                    collective_id=1, has_side_effects=True, vmem_limit_bytes=24 * 1024 * 1024
                ),
                name="full",
            )(*pinned(kv_pool, page_tables, parents))
        with jax.named_scope("finish"):
            return pl.pallas_call(
                finish_kernel,
                out_shape=(
                    jax.ShapeDtypeStruct(queries.shape, bf16),
                    jax.ShapeDtypeStruct((BEAMS, context, channels), bf16),
                ),
                in_specs=[vmem, vmem, hbm, hbm, hbm],
                out_specs=(vmem, hbm),
                scratch_shapes=[
                    pltpu.VMEM(new_kv.shape, bf16),
                    pltpu.SMEM(lengths.shape, jnp.int32),
                    pltpu.SMEM(parents.shape, jnp.int32),
                    pltpu.VMEM((2 * BEAMS, PAGE, channels), bf16),
                    pltpu.VMEM((PAGE, channels), bf16),
                    dma((3,)), dma,
                ],
                compiler_params=pltpu.CompilerParams(vmem_limit_bytes=24 * 1024 * 1024),
                name="finish",
            )(whole.reshape(BEAMS, context, channels), raw, new_kv, lengths, parents)

    topping = [functools.partial(topped, count, 2 + at) for at, count in enumerate(TIERS)]
    return lax.switch(over[0], [placed, *topping, resent])


def solution(mesh):
    in_specs = (
        P(None, "dp", "tensor"),
        P(None, "dp", "tensor"),
        P("dp", None, "tensor"),
        P("dp", None),
        P(),
        P(),
        P("tensor", None),
    )
    out_specs = (P(None, "dp", "tensor"), P("dp", None, "tensor"))
    body = functools.partial(local, mesh.shape["tensor"])
    return jax.shard_map(body, mesh=mesh, in_specs=in_specs, out_specs=out_specs, check_vma=False)
```
